128 devices in a mesh: tm: 32 (over x, z, y_lo), cell: 4 (over y_hi, core).
Axes of the slice: x: 4, y: 4 (y_hi: 2, y_lo: 2; y = y_hi * 2 + y_lo), z: 4, core: 2. Of those that a mesh axis runs over, the one named last changes fastest.
Arguments:
- embedding: bfloat16 [32, 196608], P(None, ('tm', 'cell')), may hold values from -4 to 4, as said below
- counts: int32 [32], replicated, may hold values from 384 to 6144, as said below
Outputs:
- gradient: float32 [32, 196608], P(None, ('tm', 'cell'))
The draws below stay inside these ranges and needn't reach their ends.
Inputs may be any that keep to these rules, and one draw needn't show every extreme that they name: Time point t has counts[t] live cells in the first counts[t] of its 6144 slots; the other slots are padding. `embedding`: values of order one.
All inputs are finite; a program needn't handle non-finite values.
Results may differ from the reference program's by a relative error of at most 0.0013.
Values may be sent and summed in bfloat16 or wider, within the bound.
No kernel may reach another device: no remote copies, remote signals or barrier semaphores. Data moves between devices by JAX's collectives and lax.ppermute only.
A program may use at most 128 MiB of HBM per device.

```python
import jax
import jax.numpy as jnp
from jax import lax

EMB = 32
CAP_DEV = 1536
SWEEPS = 2
ADJOINT = 2
CAP = 6144
TIMES = 32


def draw_embedding(key, part):
    key = jax.random.fold_in(key, 7)
    noise_key, cell_key, feat_key = jax.random.split(key, 3)
    cell_total = TIMES * CAP
    cell_scale = jnp.exp(jax.random.uniform(cell_key, (1, cell_total), minval=-0.5, maxval=0.5))
    feat_scale = jnp.exp(jax.random.uniform(feat_key, (EMB, 1), minval=-0.5, maxval=0.5))
    values = 0.2 * jax.random.normal(noise_key, (EMB, cell_total)) * cell_scale * feat_scale
    return jnp.clip(values, -4.0, 4.0).astype(jnp.bfloat16)


def draw_counts(key, part):
    key = jax.random.fold_in(key, 11)
    value_key, order_key = jax.random.split(key)
    lowest = CAP // 16
    highest = CAP // 2 + CAP // 8
    values = jax.random.randint(value_key, (TIMES,), lowest, highest + 1)
    order = jax.random.permutation(order_key, TIMES)
    values = values.at[order[0]].set(CAP)
    values = values.at[order[1]].set(lowest)
    return values.astype(jnp.int32)


def setup_inputs(seed: int = 0) -> dict:
    arg_keys = jax.random.split(jax.random.key(seed), 3)
    return {
        "embedding": draw_embedding(jax.random.fold_in(arg_keys[2], 71), 0),
        "counts": draw_counts(jax.random.fold_in(arg_keys[2], 71), 0),
    }


ENTROPY = 0.25
PENALTY = 5.0
DAMPING = PENALTY / (PENALTY + ENTROPY)
MASKED = -1.0e30


def cost_tile(sources, targets, source_sq, target_sq):
    products = lax.dot_general(sources, targets, (((0,), (0,)), ((), ())), preferred_element_type=jnp.float32)
    return source_sq[:, None] + target_sq[None, :] - 2.0 * products


def lse_combine(first, second):
    top_value = jnp.maximum(first[0], second[0])
    summed = first[1] * jnp.exp(first[0] - top_value) + second[1] * jnp.exp(second[0] - top_value)
    return top_value, summed


def pair_grads(sources, targets, source_live, target_live):
    slots = sources.shape[1]
    step_rows = CAP_DEV // max(1, CAP_DEV // 768)
    num_blocks = slots // step_rows
    block_ids = jnp.arange(num_blocks, dtype=jnp.int32)
    source_f32 = sources.astype(jnp.float32)
    target_f32 = targets.astype(jnp.float32)
    source_sq = jnp.sum(source_f32 * source_f32, axis=0)
    target_sq = jnp.sum(target_f32 * target_f32, axis=0)

    def rows_of(vector, block_index):
        return lax.dynamic_slice_in_dim(vector, block_index * step_rows, step_rows, 0)

    def tile(block_index):
        start = block_index * step_rows
        piece = lax.dynamic_slice_in_dim(sources, start, step_rows, 1)
        live_part = rows_of(source_live, block_index)
        mask = live_part[:, None] & target_live[None, :]
        return mask, cost_tile(piece, targets, rows_of(source_sq, block_index), target_sq)

    def column_log(source_pot):
        def visit(carry, block_index):
            mask, cost = tile(block_index)
            scores = jnp.where(mask, (rows_of(source_pot, block_index)[:, None] - cost) / ENTROPY, MASKED)
            block_top = jnp.max(scores, axis=0)
            block_sum = jnp.sum(jnp.exp(scores - block_top[None, :]), axis=0)
            return lse_combine(carry, (block_top, block_sum)), None
        start_pair = (jnp.full((slots,), MASKED, jnp.float32), jnp.zeros((slots,), jnp.float32))
        result, _ = lax.scan(visit, start_pair, block_ids)
        return result[0] + jnp.log(result[1])

    def row_log(target_pot):
        def visit(block_index):
            mask, cost = tile(block_index)
            scores = jnp.where(mask, (target_pot[None, :] - cost) / ENTROPY, MASKED)
            block_top = jnp.max(scores, axis=1)
            return block_top + jnp.log(jnp.sum(jnp.exp(scores - block_top[:, None]), axis=1))
        return lax.map(visit, block_ids).reshape(slots)

    source_pot = jnp.zeros((slots,), jnp.float32)
    target_pot = jnp.zeros((slots,), jnp.float32)
    last_rows = jnp.zeros((slots,), jnp.float32)
    for sweep in range(SWEEPS):
        target_pot = jnp.where(target_live, -DAMPING * ENTROPY * column_log(source_pot), 0.0)
        last_rows = row_log(target_pot)
        source_pot = jnp.where(source_live, -DAMPING * ENTROPY * last_rows, 0.0)
    final_cols = column_log(source_pot)

    def kernels(block_index):
        mask, cost = tile(block_index)
        src_pot = rows_of(source_pot, block_index)
        src_log = rows_of(last_rows, block_index)
        plan = jnp.where(mask, jnp.exp((src_pot[:, None] + target_pot[None, :] - cost) / ENTROPY), 0.0)
        row_kernel = jnp.where(mask, jnp.exp((target_pot[None, :] - cost) / ENTROPY - src_log[:, None]), 0.0)
        col_kernel = jnp.where(mask, jnp.exp((src_pot[:, None] - cost) / ENTROPY - final_cols[None, :]), 0.0)
        return cost, plan, row_kernel, col_kernel

    def stats_visit(carry, block_index):
        cost, plan, row_kernel, col_kernel = kernels(block_index)
        weighted = plan * cost / ENTROPY
        return carry + jnp.sum(weighted, axis=0), jnp.sum(weighted, axis=1)

    target_push, pushes = lax.scan(stats_visit, jnp.zeros((slots,), jnp.float32), block_ids)
    source_push = pushes.reshape(slots)
    source_adj, target_adj = source_push, target_push
    for step_k in range(ADJOINT):
        def adj_visit(carry, block_index):
            cost, plan, row_kernel, col_kernel = kernels(block_index)
            new_rows = rows_of(source_push, block_index) - DAMPING * jnp.sum(col_kernel * target_adj[None, :], axis=1)
            return carry + jnp.sum(row_kernel * rows_of(source_adj, block_index)[:, None], axis=0), new_rows
        pulled, new_rows = lax.scan(adj_visit, jnp.zeros((slots,), jnp.float32), block_ids)
        source_adj, target_adj = new_rows.reshape(slots), target_push - DAMPING * pulled

    def grad_visit(carry, block_index):
        cost, plan, row_kernel, col_kernel = kernels(block_index)
        adj_rows = rows_of(source_adj, block_index)
        cost_grad = plan * (1.0 - cost / ENTROPY) + DAMPING * (adj_rows[:, None] * row_kernel + target_adj[None, :] * col_kernel)
        rounded = cost_grad.astype(jnp.bfloat16)
        row_total = jnp.sum(cost_grad, axis=1)
        pulled_rows = lax.dot_general(targets, rounded, (((1,), (1,)), ((), ())), preferred_element_type=jnp.float32)
        src_cols = lax.dynamic_slice_in_dim(source_f32, block_index * step_rows, step_rows, 1)
        source_grad = 2.0 * (src_cols * row_total[None, :] - pulled_rows)
        piece = lax.dynamic_slice_in_dim(sources, block_index * step_rows, step_rows, 1)
        pulled_cols = lax.dot_general(piece, rounded, (((1,), (0,)), ((), ())), preferred_element_type=jnp.float32)
        return (carry[0] + jnp.sum(cost_grad, axis=0), carry[1] + pulled_cols), source_grad

    start_pair = (jnp.zeros((slots,), jnp.float32), jnp.zeros((EMB, slots), jnp.float32))
    (col_total, pulled_total), source_grads = lax.scan(grad_visit, start_pair, block_ids)
    source_grad = jnp.transpose(source_grads, (1, 0, 2)).reshape(EMB, slots)
    target_grad = 2.0 * (target_f32 * col_total[None, :] - pulled_total)
    return source_grad, target_grad


def reference(embedding, counts):
    blocks = embedding.reshape(EMB, TIMES, CAP)
    slot_ids = jnp.arange(CAP, dtype=jnp.int32)

    def one_pair(index):
        sources = lax.dynamic_index_in_dim(blocks, index, 1, keepdims=False)
        targets = lax.dynamic_index_in_dim(blocks, index + 1, 1, keepdims=False)
        count_here = lax.dynamic_index_in_dim(counts, index, 0, keepdims=False)
        count_next = lax.dynamic_index_in_dim(counts, index + 1, 0, keepdims=False)
        return pair_grads(sources, targets, slot_ids < count_here, slot_ids < count_next)

    source_grads, target_grads = lax.map(one_pair, jnp.arange(TIMES - 1, dtype=jnp.int32))
    empty = jnp.zeros((1, EMB, CAP), jnp.float32)
    total = jnp.concatenate([source_grads, empty], axis=0) + jnp.concatenate([empty, target_grads], axis=0)
    return jnp.transpose(total, (1, 0, 2)).reshape(EMB, TIMES * CAP)
```

```python
import functools

import jax
import jax.numpy as jnp
from jax import lax
from jax.experimental import pallas as pl
from jax.experimental.pallas import tpu as pltpu
from jax.sharding import PartitionSpec as P

ENTROPY = 0.25
PENALTY = 5.0
DAMPING = PENALTY / (PENALTY + ENTROPY)
MASKED = -1e30
SQ_SCALE = 1.0 / ENTROPY
DOT_SCALE = 2.0 / ENTROPY
TINY = 1e-37
SHIFT = 44.0
LOWEST = 1e-24

ROWS = 256
COLS = 512
LANES = 128
DEPTH = 128
F32 = jnp.float32
BF16 = jnp.bfloat16


def split3(value):
    high = value.astype(BF16).astype(F32)
    rest = value - high
    middle = rest.astype(BF16).astype(F32)
    return high, middle, rest - middle


def write_augmented(out_ref, start, feats, pot, is_row):
    n = feats.shape[1]
    cols = pl.ds(start, n)
    scaled = feats.astype(F32) * DOT_SCALE if is_row else feats
    out_ref[0:32, cols] = scaled.astype(out_ref.dtype)
    first = 0 if is_row else 3
    ones_from = 3 if is_row else 0
    row = lax.broadcasted_iota(jnp.int32, (16, n), 0)
    tail = jnp.where((row >= ones_from) & (row < ones_from + 3), 1.0, 0.0)
    for k, piece in enumerate(split3(pot)):
        tail = jnp.where(row == first + k, piece, tail)
    out_ref[32:48, cols] = tail.astype(out_ref.dtype)
    out_ref[48:128, cols] = jnp.zeros((80, n), out_ref.dtype)


def square_sum(feats):
    wide = feats.astype(F32)
    return jnp.sum(wide * wide, axis=0, keepdims=True)


def live_pot(feats, start, count):
    ids = start + lax.broadcasted_iota(jnp.int32, (1, feats.shape[1]), 1)
    return jnp.where(ids < count, -SQ_SCALE * square_sum(feats), MASKED)


def aligned(index, size):
    return pl.multiple_of(index * size, size)


def around(counts):
    size = counts.shape[0]
    time, member = lax.axis_index("tm"), lax.axis_index("cell")
    before = jnp.where(time > 0, counts[jnp.maximum(time - 1, 0)], 0)
    after = jnp.where(time + 1 < size, counts[jnp.minimum(time + 1, size - 1)], 0)
    return before, counts[time], after, member


def row_steps(count_here, count_next, member, group):
    blocks = pl.cdiv(count_here, LANES)
    mine = jnp.maximum((blocks - member + group - 1) // group, 0)
    per_step = ROWS // LANES
    steps = (mine + per_step - 1) // per_step
    return jnp.where(count_next > 0, steps, 0)


def col_steps(count):
    return (count + COLS - 1) // COLS


LTS = COLS // LANES
SUB = 32
WIDE = 1536


def scores(xa, ya_ref, c, cols=COLS):
    return jnp.dot(xa, ya_ref[:, pl.ds(aligned(c, cols), cols)], preferred_element_type=F32)


def piped(count, matmul, work, first_ref, second_ref, load=None, store=None):
    load = load or (lambda c: None)
    store = store or (lambda c, state: None)
    first_ref[...] = matmul(0)

    def pair(i, _):
        here, there = 2 * i, 2 * i + 1
        states = load(here), load(there)
        second_ref[...] = matmul(there)
        one = work(here, first_ref, states[0])
        first_ref[...] = matmul(jnp.minimum(there + 1, count - 1))
        two = work(there, second_ref, states[1])
        store(here, one)
        store(there, two)
        return 0

    lax.fori_loop(0, count // 2, pair, 0)

    @pl.when(count % 2 == 1)
    def _():
        store(count - 1, work(count - 1, first_ref, load(count - 1)))


def adder(acc_refs):
    def store(c, sums):
        for k, acc_ref in enumerate(acc_refs):
            lts = len(sums[k])
            for lt in range(lts):
                acc_ref[:, lane_tile(c, lt, lts)] += sums[k][lt]

    return store


def lane_tile(c, lt, lts=LTS):
    return pl.ds(aligned(c * lts + lt, LANES), LANES)


def piece_of(z_ref, rg, lt, size=SUB):
    return z_ref[rg : rg + size, lt * LANES : (lt + 1) * LANES]


def in_steps(total, visit):
    for start in range(0, total, WIDE):
        visit(start, slice(start, start + WIDE))


def kernel_a(
    counts, x0, x1, x2, x3, y0, y1, y2, y3,
    xg_ref, yg_ref, xa_ref, gb_ref, log_ref,
    ya_ref, xat_ref, za_ref, zb_ref, top_ref, sum_ref,
):
    _, count_here, count_next, member = around(counts)
    group = 4
    nb = row_steps(count_here, count_next, member, group)
    nc = col_steps(count_next)
    local = x0.shape[1]
    for k, (x_ref, y_ref) in enumerate(((x0, y0), (x1, y1), (x2, y2), (x3, y3))):
        place = pl.ds(aligned(member ^ k, local), local)
        xg_ref[:, place] = x_ref[...]
        yg_ref[:, place] = y_ref[...]
    for k in range(local // LANES):
        block_id = group * k + member
        piece = xg_ref[:, pl.ds(aligned(block_id, LANES), LANES)]
        pot = live_pot(piece, block_id * LANES, count_here) + SHIFT
        write_augmented(xat_ref, k * LANES, piece, pot, True)
        xa_ref[k * LANES : (k + 1) * LANES, :] = jnp.transpose(
            xat_ref[:, k * LANES : (k + 1) * LANES]
        ).astype(BF16)
    sum_ref[...] = jnp.zeros_like(sum_ref)

    def prepare(start, cols):
        feats = yg_ref[:, cols]
        pot = live_pot(feats, start, count_next)
        gb_ref[:, cols] = pot
        write_augmented(ya_ref, start, feats, pot, False)

    in_steps(group * local, prepare)

    def exact():
        top_ref[...] = jnp.full(top_ref.shape, MASKED, F32)
        sum_ref[...] = jnp.zeros_like(sum_ref)

        def row_visit(b, _):
            xa = xa_ref[pl.ds(aligned(b, ROWS), ROWS), :]

            def load(c):
                return [(top_ref[:, lane_tile(c, lt)], sum_ref[:, lane_tile(c, lt)]) for lt in range(LTS)]

            def work(c, z_ref, state):
                after = []
                for lt, (old, total) in enumerate(state):
                    tile = z_ref[:, lt * LANES : (lt + 1) * LANES].reshape(ROWS // 8, 8, LANES)
                    top = jnp.maximum(old, jnp.max(tile, axis=0))
                    total = total * jnp.exp(old - top) + jnp.sum(jnp.exp(tile - top[None]), axis=0)
                    after.append((top, total))
                return after

            def store(c, state):
                for lt, (top, total) in enumerate(state):
                    top_ref[:, lane_tile(c, lt)] = top
                    sum_ref[:, lane_tile(c, lt)] = total

            piped(nc, lambda c: scores(xa, ya_ref, c), work, za_ref, zb_ref, load, store)
            return 0

        lax.fori_loop(0, nb, row_visit, 0)
        tops = top_ref[...]
        top = jnp.max(tops, axis=0, keepdims=True)
        total = jnp.sum(sum_ref[...] * jnp.exp(tops - top), axis=0, keepdims=True)
        log_ref[...] = top + jnp.log(jnp.maximum(total, TINY)) - SHIFT

    thin = 2 * LANES

    def quick_visit(b, _):
        halves = [xa_ref[pl.ds(aligned(2 * b + k, ROWS // 2), ROWS // 2), :] for k in range(2)]

        def tile_sums(c, tiles):
            for t in range(tiles):
                totals = [jnp.zeros((8, LANES), F32) for _ in range(2)]
                for half in halves:
                    z = scores(half, ya_ref, c * tiles + t, thin)
                    for lt in range(2):
                        p = jnp.exp(z[:, lt * LANES : (lt + 1) * LANES])
                        totals[lt] = totals[lt] + jnp.sum(p.reshape(ROWS // 16, 8, LANES), axis=0)
                for lt in range(2):
                    sum_ref[:, lane_tile(c * tiles + t, lt, 2)] += totals[lt]

        def pair(i, _):
            tile_sums(i, 4)
            return 0

        lax.fori_loop(0, nc // 2, pair, 0)

        @pl.when(nc % 2 == 1)
        def _():
            tile_sums(nc - 1, 2)

        return 0

    lax.fori_loop(0, nb, quick_visit, 0)
    total = jnp.sum(sum_ref[...], axis=0, keepdims=True)
    log_ref[...] = jnp.where(total > 0.0, jnp.log(jnp.maximum(total, TINY)) - SHIFT, MASKED)
    ids = lax.broadcasted_iota(jnp.int32, total.shape, 1)
    lowest = jnp.min(jnp.where(ids < count_next, total, 1.0))

    @pl.when((lowest < LOWEST) & (nb > 0))
    def _():
        exact()


def column_sums(c, z_ref, _):
    rows, cols = z_ref.shape
    sums = []
    for lt in range(cols // LANES):
        p = jnp.exp(z_ref[:, lt * LANES : (lt + 1) * LANES])
        sums.append(jnp.sum(p.reshape(rows // 8, 8, LANES), axis=0))
    return [sums]


def row_adder(sum_ref, push_ref=None, g_ref=None):
    def first(c, z_ref, kept):
        for rg in range(0, ROWS, SUB):
            rows = slice(rg, rg + SUB)
            total = sum_ref[rows, :]
            push = push_ref[rows, :] if push_ref is not None else None
            for lt in range(LTS):
                z = piece_of(z_ref, rg, lt)
                p = jnp.exp(z)
                total = total + p
                kept[0][rows, lane_tile(c, lt)] = p.astype(kept[0].dtype)
                if push is not None:
                    part = p * (g_ref[:, lane_tile(c, lt)] - z)
                    push = push + part
                    kept[1][rows, lane_tile(c, lt)] = part.astype(kept[1].dtype)
            sum_ref[rows, :] = total
            if push is not None:
                push_ref[rows, :] = push

    return first


def column_parts(c, plan):
    sums = [[jnp.zeros((8, LANES), F32) for _ in range(LTS)] for _ in plan]
    for rg in range(0, ROWS, 8):
        for k, (kept_ref, weight_ref) in enumerate(plan):
            scale = weight_ref[rg : rg + 8, :]
            for lt in range(LTS):
                sums[k][lt] = sums[k][lt] + scale * kept_ref[rg : rg + 8, lane_tile(c, lt)]
    return sums


def two_stage(nb, nc, first, finish, second, store, matmul_of, buffers, kept):
    def stage(b, now, before):
        matmul = matmul_of(b)

        def work(c, z_ref, _):
            first(c, z_ref, now)
            return second(c, before) if before else None

        piped(nc, matmul, work, *buffers, store=store if before else None)
        finish(b)

    def tail(before):
        def pair(i, _):
            one, two = second(2 * i, before), second(2 * i + 1, before)
            store(2 * i, one)
            store(2 * i + 1, two)
            return 0

        lax.fori_loop(0, nc // 2, pair, 0)

        @pl.when(nc % 2 == 1)
        def _():
            store(nc - 1, second(nc - 1, before))

    even, odd = kept

    @pl.when(nb > 0)
    def _():
        stage(0, even, None)

    def visit(b, _):
        @pl.when(b % 2 == 1)
        def _():
            stage(b, odd, even)

        @pl.when(b % 2 == 0)
        def _():
            stage(b, even, odd)

        return 0

    lax.fori_loop(1, nb, visit, 0)

    @pl.when((nb > 0) & (nb % 2 == 1))
    def _():
        tail(even)

    @pl.when((nb > 0) & (nb % 2 == 0))
    def _():
        tail(odd)


def col_tile(c):
    return pl.ds(aligned(c, COLS), COLS)


def split2(value):
    high = value.astype(BF16).astype(F32)
    return high, value - high


def turned_weights(columns):
    lane = lax.broadcasted_iota(jnp.int32, (ROWS, LANES), 1)
    packed = jnp.zeros((ROWS, LANES), F32)
    for at, column in columns:
        packed = jnp.where(lane == at, column, packed)
    return jnp.transpose(packed)


def sweep(quick, exact, low_ref, lost=None):
    low_ref[...] = jnp.ones_like(low_ref)
    quick()
    again = jnp.min(low_ref[...]) < LOWEST
    if lost is not None:
        again = again | lost()

    @pl.when(again)
    def _():
        exact()


def row_lse(xa, ya_ref, nc, buffers, top_ref, sum_ref, push_ref=None, g_ref=None):
    top_ref[...] = jnp.full(top_ref.shape, MASKED, F32)
    sum_ref[...] = jnp.zeros_like(sum_ref)
    if push_ref is not None:
        push_ref[...] = jnp.zeros_like(push_ref)

    def work(c, z_ref, _):
        for rg in range(0, ROWS, SUB):
            rows = slice(rg, rg + SUB)
            old = top_ref[rows, :]
            pieces = [piece_of(z_ref, rg, lt) for lt in range(LTS)]
            top = old
            for z in pieces:
                top = jnp.maximum(top, z)
            fade = jnp.exp(old - top)
            total = sum_ref[rows, :] * fade
            push = push_ref[rows, :] * fade if push_ref is not None else None
            for lt, z in enumerate(pieces):
                p = jnp.exp(z - top)
                total = total + p
                if push is not None:
                    push = push + p * (g_ref[:, lane_tile(c, lt)] - z)
            top_ref[rows, :] = top
            sum_ref[rows, :] = total
            if push is not None:
                push_ref[rows, :] = push

    piped(nc, lambda c: scores(xa, ya_ref, c), work, *buffers)
    tops = top_ref[...]
    top = jnp.max(tops, axis=1, keepdims=True)
    fade = jnp.exp(tops - top)
    total = jnp.sum(sum_ref[...] * fade, axis=1, keepdims=True)
    if push_ref is None:
        return top, total
    return top, total, jnp.sum(push_ref[...] * fade, axis=1, keepdims=True)


def row_potential(xa):
    lane = lax.broadcasted_iota(jnp.int32, (ROWS, LANES), 1)
    wide = xa.astype(F32)
    old = jnp.sum(jnp.where((lane >= 32) & (lane < 35), wide, 0.0), axis=1, keepdims=True)
    return lane, wide, old


def with_row_potential(lane, wide, pot):
    high, middle, low = split3(pot)
    new = jnp.where(lane == 32, high, jnp.where(lane == 33, middle, jnp.where(lane == 34, low, wide)))
    return new.astype(BF16)


def kernel_b(counts, xa_ref, yg_ref, gb_ref, l0, l1, l2, l3, g_ref, col_ref, ya_ref, za_ref, zb_ref, p_ref, q_ref, top_ref, sum_ref, weight_ref, low_ref, most_ref, acc_ref):
    _, count_here, count_next, member = around(counts)
    nb = row_steps(count_here, count_next, member, 4)
    nc = col_steps(count_next)

    def prepare(start, cols):
        logs = [ref[:, cols] for ref in (l0, l1, l2, l3)]
        top = jnp.maximum(jnp.maximum(logs[0], logs[1]), jnp.maximum(logs[2], logs[3]))
        total = sum(jnp.exp(one - top) for one in logs)
        ids = start + lax.broadcasted_iota(jnp.int32, (1, WIDE), 1)
        pot = jnp.where(ids < count_next, -DAMPING * (top + jnp.log(total)), 0.0)
        g_ref[:, cols] = pot
        write_augmented(ya_ref, start, yg_ref[:, cols], pot + gb_ref[:, cols], False)

    in_steps(yg_ref.shape[1], prepare)

    buffers = za_ref, zb_ref

    def quick():
        acc_ref[...] = jnp.zeros_like(acc_ref)

        def matmul_of(b):
            sum_ref[...] = jnp.zeros_like(sum_ref)
            xa = xa_ref[pl.ds(aligned(b, ROWS), ROWS), :]
            return lambda c: scores(xa, ya_ref, c)

        def finish(b):
            lane, wide, old = row_potential(xa_ref[pl.ds(aligned(b, ROWS), ROWS), :])
            live = old > 0.5 * MASKED
            total = jnp.sum(sum_ref[...], axis=1, keepdims=True)
            low_ref[...] = jnp.minimum(low_ref[...], jnp.where(live, total, 1.0))
            pot = -DAMPING * (jnp.log(jnp.maximum(total, TINY)) - SHIFT)
            weight = jnp.where(live, jnp.exp(pot - SHIFT), 0.0)
            weight_ref[...] = jnp.broadcast_to(weight, weight_ref.shape)
            most_ref[...] = jnp.maximum(most_ref[...], weight)

        two_stage(
            nb, nc, row_adder(sum_ref), finish, lambda c, kept: column_parts(c, [(kept[0], weight_ref)]),
            adder([acc_ref]), matmul_of, buffers, ((p_ref,), (q_ref,)),
        )

    def exact():
        acc_ref[...] = jnp.zeros_like(acc_ref)

        def row_visit(b, _):
            xa = xa_ref[pl.ds(aligned(b, ROWS), ROWS), :]
            lane, wide, old = row_potential(xa)
            live = old > 0.5 * MASKED
            top, total = row_lse(xa, ya_ref, nc, buffers, top_ref, sum_ref)
            pot = -DAMPING * (top + jnp.log(total) - SHIFT)
            xb = with_row_potential(lane, wide, jnp.where(live, pot + old - SHIFT, MASKED))
            piped(nc, lambda c: scores(xb, ya_ref, c), column_sums, *buffers, store=adder([acc_ref]))
            return 0

        lax.fori_loop(0, nb, row_visit, 0)

    def lost():
        total = jnp.sum(acc_ref[...], axis=0, keepdims=True)
        ids = lax.broadcasted_iota(jnp.int32, total.shape, 1)
        least = jnp.min(jnp.where((ids < count_next) & (nb > 0), total, 1.0))
        return least < jnp.max(most_ref[...]) * 2.0**-91

    most_ref[...] = jnp.zeros_like(most_ref)
    sweep(quick, exact, low_ref, lost)
    col_ref[...] = jnp.sum(acc_ref[...], axis=0, keepdims=True)


def kernel_c(
    counts, xa_ref, yg_ref, gb_ref, g_ref, c0, c1, c2, c3,
    xb_ref, aux_ref, g2_ref, col_ref,
    ya_ref, za_ref, zb_ref, p_ref, w_ref, q_ref, v_ref, top_ref, sum_ref, push_ref, adj_ref, low_ref, cost_ref, weight_ref, acc_ref, acc0_ref, acc1_ref, acc2_ref,
):
    _, count_here, count_next, member = around(counts)
    nb = row_steps(count_here, count_next, member, 4)
    nc = col_steps(count_next)

    def prepare(start, cols):
        total = (c0[:, cols] + c1[:, cols]) + (c2[:, cols] + c3[:, cols])
        ids = start + lax.broadcasted_iota(jnp.int32, (1, WIDE), 1)
        log = jnp.log(jnp.maximum(total, TINY)) - g_ref[:, cols]
        pot = jnp.where(ids < count_next, -DAMPING * log, 0.0)
        g2_ref[:, cols] = pot
        write_augmented(ya_ref, start, yg_ref[:, cols], pot + gb_ref[:, cols], False)

    in_steps(yg_ref.shape[1], prepare)

    buffers = za_ref, zb_ref
    accs = acc0_ref, acc1_ref, acc2_ref

    ids = lax.broadcasted_iota(jnp.int32, g_ref.shape, 1)
    centre = jnp.sum(jnp.where(ids < count_next, g_ref[...], 0.0), axis=1, keepdims=True)
    centre = centre / (DAMPING * jnp.maximum(count_next, 1).astype(F32)) + 3.0
    cost_ref[...] = g2_ref[...] + (SHIFT - centre)

    def close_rows(b, top, total, push):
        rows_here = pl.ds(aligned(b, ROWS), ROWS)
        lane, wide, old = row_potential(xa_ref[rows_here, :])
        live = old > 0.5 * MASKED
        total = jnp.maximum(total, TINY)
        row_log = top + jnp.log(total) - SHIFT
        pot = jnp.where(live, -DAMPING * row_log, 0.0)
        row_sum = jnp.where(live, jnp.exp(row_log + pot), 0.0)
        adjoint = jnp.where(live, push / total + centre, 0.0)
        inverse = jnp.where(row_sum > 0.0, 1.0 / jnp.maximum(row_sum, TINY), 0.0)
        full = jnp.where(live, pot + old - SHIFT, MASKED)
        xb = with_row_potential(lane, wide, full)
        xb_ref[rows_here, :] = xb
        aux = jnp.where(lane == 0, adjoint, jnp.where(lane == 1, inverse, jnp.where(lane == 2, pot, full)))
        aux_ref[rows_here, :] = aux
        return live, pot, adjoint, xb

    def quick():
        acc_ref[...] = jnp.zeros_like(acc_ref)

        def matmul_of(b):
            sum_ref[...] = jnp.zeros_like(sum_ref)
            push_ref[...] = jnp.zeros_like(push_ref)
            xa = xa_ref[pl.ds(aligned(b, ROWS), ROWS), :]
            return lambda c: scores(xa, ya_ref, c)

        def finish(b):
            total = jnp.sum(sum_ref[...], axis=1, keepdims=True)
            push = jnp.sum(push_ref[...], axis=1, keepdims=True)
            live, pot, adjoint, _ = close_rows(b, 0.0, total, push)
            low_ref[...] = jnp.minimum(low_ref[...], jnp.where(live, total, 1.0))
            weight = jnp.where(live, jnp.exp(pot - SHIFT), 0.0)
            pieces = (*split2(weight), *split2(weight * adjoint))
            weight_ref[...] = turned_weights(list(enumerate(pieces)))[0:16, :].astype(BF16)

        def second(c, kept):
            weights = weight_ref[...]
            plan = jnp.dot(weights, kept[0][:, col_tile(c)], preferred_element_type=F32)
            cost = jnp.dot(weights, kept[1][:, col_tile(c)], preferred_element_type=F32)
            return plan, cost

        def store(c, sums):
            acc_ref[0:16, col_tile(c)] += sums[0]
            acc_ref[16:32, col_tile(c)] += sums[1]

        two_stage(
            nb, nc, row_adder(sum_ref, push_ref, cost_ref), finish, second, store, matmul_of, buffers,
            ((p_ref, w_ref), (q_ref, v_ref)),
        )
        acc0_ref[0:1, :] = acc_ref[0:1, :] + acc_ref[1:2, :]
        acc1_ref[0:1, :] = acc_ref[16:17, :] + acc_ref[17:18, :]
        acc2_ref[0:1, :] = acc_ref[2:3, :] + acc_ref[3:4, :]
        for ref in accs:
            ref[1:8, :] = jnp.zeros((7, ref.shape[1]), F32)

    def exact():
        for ref in accs:
            ref[...] = jnp.zeros_like(ref)

        def row_visit(b, _):
            xa = xa_ref[pl.ds(aligned(b, ROWS), ROWS), :]
            top, total, push = row_lse(xa, ya_ref, nc, buffers, top_ref, sum_ref, push_ref, cost_ref)
            _, pot, adjoint, xb = close_rows(b, top, total, push)
            top_ref[...] = jnp.broadcast_to(pot - SHIFT, top_ref.shape)
            adj_ref[...] = jnp.broadcast_to(adjoint, adj_ref.shape)

            def work(c, z_ref, _):
                sums = [[jnp.zeros((8, LANES), F32) for _ in range(LTS)] for _ in range(3)]
                for rg in range(0, ROWS, 8):
                    pot_here = top_ref[rg : rg + 8, :]
                    adj_here = adj_ref[rg : rg + 8, :]
                    for lt in range(LTS):
                        tile = piece_of(z_ref, rg, lt, 8)
                        p = jnp.exp(tile)
                        sums[0][lt] = sums[0][lt] + p
                        sums[1][lt] = sums[1][lt] + p * (cost_ref[:, lane_tile(c, lt)] + (pot_here - tile))
                        sums[2][lt] = sums[2][lt] + p * adj_here
                return sums

            piped(nc, lambda c: scores(xb, ya_ref, c), work, *buffers, store=adder(accs))
            return 0

        lax.fori_loop(0, nb, row_visit, 0)

    sweep(quick, exact, low_ref)
    mass = jnp.sum(acc0_ref[...], axis=0, keepdims=True)
    slots = mass.shape[1]
    col_ref[:, 0:slots] = mass
    push = jnp.sum(acc1_ref[...], axis=0, keepdims=True)
    col_ref[:, slots : 2 * slots] = push + centre * mass
    col_ref[:, 2 * slots :] = jnp.sum(acc2_ref[...], axis=0, keepdims=True)


def kernel_d(
    counts, xb_ref, aux_ref, yg_ref, gb_ref, g2_ref, s0, s1, s2, s3,
    stat_ref, send_ref,
    ya_ref, za_ref, zb_ref, p_ref, q_ref, values_ref, sum_ref, weight_ref, acc_ref,
):
    _, count_here, count_next, member = around(counts)
    nb = row_steps(count_here, count_next, member, 4)
    nc = col_steps(count_next)
    slots = yg_ref.shape[1]
    local = xb_ref.shape[0]
    acc_ref[...] = jnp.zeros_like(acc_ref)

    def prepare(start, cols):
        mass, push, pulled = (
            (s0[:, part] + s1[:, part]) + (s2[:, part] + s3[:, part])
            for part in (pl.ds(start + k * slots, WIDE) for k in range(3))
        )
        inverse = jnp.where(mass > 0.0, 1.0 / jnp.maximum(mass, TINY), 0.0)
        pot = g2_ref[:, cols]
        over, later = push * inverse, (push - DAMPING * pulled) * inverse
        stat_ref[0:1, cols] = pot + gb_ref[:, cols]
        stat_ref[1:2, cols] = over
        stat_ref[2:3, cols] = pot
        stat_ref[3:8, cols] = jnp.zeros((5, WIDE), F32)
        row = lax.broadcasted_iota(jnp.int32, (16, WIDE), 0)
        values = jnp.where(row == 0, 1.0, 0.0)
        for k, piece in enumerate((*split2(over), *split2(later))):
            values = jnp.where(row == k + 1, piece, values)
        values_ref[:, cols] = values.astype(BF16)
        write_augmented(ya_ref, start, yg_ref[:, cols], pot + gb_ref[:, cols], False)

    in_steps(slots, prepare)
    rest = 2 * slots
    send_ref[:, rest : rest + local] = jnp.full((1, local), MASKED, F32)
    send_ref[:, rest + local :] = jnp.zeros((1, local), F32)

    def matmul_of(b):
        sum_ref[...] = jnp.zeros_like(sum_ref)
        xb = xb_ref[pl.ds(aligned(b, ROWS), ROWS), :]
        return lambda c: scores(xb, ya_ref, c)

    def first(c, z_ref, kept):
        rounded = []
        for rg in range(0, ROWS, SUB):
            line = []
            for lt in range(LTS):
                p = jnp.exp(piece_of(z_ref, rg, lt)).astype(BF16)
                kept[0][rg : rg + SUB, lane_tile(c, lt)] = p
                line.append(p)
            rounded.append(jnp.concatenate(line, axis=1))
        sum_ref[...] += lax.dot_general(
            jnp.concatenate(rounded, axis=0), values_ref[:, col_tile(c)], (((1,), (1,)), ((), ())),
            preferred_element_type=F32,
        )

    def finish(b):
        sums = sum_ref[...]
        inverse = jnp.where(sums[:, 0:1] > 0.0, 1.0 / jnp.maximum(sums[:, 0:1], TINY), 0.0)
        middle, last = sums[:, 1:2] + sums[:, 2:3], sums[:, 3:4] + sums[:, 4:5]
        aux = aux_ref[pl.ds(aligned(b, ROWS), ROWS), :]
        start_adj, pot, full = aux[:, 0:1], aux[:, 2:3], aux[:, 3:4]
        middle_adj = start_adj - DAMPING * middle * inverse
        last_adj = start_adj - DAMPING * last * inverse
        alpha = 1.0 + DAMPING * last_adj - pot
        high, low = split2(middle_adj)
        packed = turned_weights([(0, full), (1, alpha), (8, jnp.ones_like(high)), (9, high), (10, low)])
        weight_ref[...] = packed[8:24, :].astype(BF16)
        send_ref[:, pl.ds(aligned(b + rest // ROWS, ROWS), ROWS)] = packed[0:1, :]
        send_ref[:, pl.ds(aligned(b + (rest + local) // ROWS, ROWS), ROWS)] = packed[1:2, :]

    def second(c, kept):
        return jnp.dot(weight_ref[...], kept[0][:, col_tile(c)], preferred_element_type=F32)

    def store(c, sums):
        acc_ref[:, col_tile(c)] += sums

    two_stage(
        nb, nc, first, finish, second, store, matmul_of, (za_ref, zb_ref), ((p_ref,), (q_ref,)),
    )
    send_ref[:, 0:slots] = acc_ref[0:1, :]
    send_ref[:, slots:rest] = acc_ref[1:2, :] + acc_ref[2:3, :]


def kernel_f(counts, p0, p1, p2, p3, stat_ref, col_ref, mine_ref, early_ref, parts_ref):
    member = lax.axis_index("cell")
    slots, local = stat_ref.shape[1], mine_ref.shape[1]
    for k, ref in enumerate((p0, p1, p2, p3)):
        parts_ref[member ^ k] = ref[...]
    mass, total = (
        (p0[:, part] + p1[:, part]) + (p2[:, part] + p3[:, part]) for part in (slice(0, slots), slice(slots, 2 * slots))
    )
    inverse = jnp.where(mass > 0.0, 1.0 / jnp.maximum(mass, TINY), 0.0)
    last = stat_ref[1:2, :] - DAMPING * total * inverse
    col_ref[0:1, :] = stat_ref[0:1, :]
    col_ref[1:2, :] = DAMPING * last - stat_ref[2:3, :]
    for block in range(slots // LANES):
        owner, place = block % 4, block // 4
        lanes = slice(block * LANES, (block + 1) * LANES)
        for k in range(2):
            at = 2 * slots + k * local + place * LANES
            early_ref[k : k + 1, lanes] = parts_ref[owner, :, at : at + LANES]
    here = pl.ds(aligned(member, local), local)
    mine_ref[...] = early_ref[:, here]
    early_ref[:, slots:] = col_ref[:, here]


def kernel_e(
    counts, *refs, earlier,
):
    own_ref, rowpot_ref, other_ref, colpot_ref = refs[:4]
    base_ref = refs[4] if earlier else None
    out_ref, xw_ref, tile_ref, ys_ref, beta_ref, za_ref, zb_ref, pull_ref, sum_ref = refs[5 if earlier else 4 :]
    local, slots = own_ref.shape[1], other_ref.shape[1]
    before, here, after, member = around(counts)
    count_rows = jnp.clip(here - member * local, 0, local)
    count_cols = before if earlier else after
    if earlier:
        own_at = slots
    else:
        own_at = 0
    nc = col_steps(count_cols)
    nb = jnp.where(count_cols > 0, (count_rows + ROWS - 1) // ROWS, 0)
    out_ref[...] = base_ref[...] if earlier else jnp.zeros_like(out_ref)

    def prepare(c, _):
        cols = pl.ds(aligned(c, COLS), COLS)
        write_augmented(tile_ref, 0, other_ref[:, cols], colpot_ref[0:1, cols], False)
        ys_ref[cols, :] = jnp.transpose(tile_ref[...]).astype(BF16)
        beta_ref[cols, :] = jnp.transpose(jnp.broadcast_to(colpot_ref[1:2, cols], (LANES, COLS)))
        return 0

    @pl.when(nb > 0)
    def _():
        lax.fori_loop(0, nc, prepare, 0)

    def row_visit(b, _):
        rows_here = pl.ds(aligned(b, ROWS), ROWS)
        own = own_ref[:, rows_here]
        own_pots = pl.ds(aligned(b + own_at // ROWS, ROWS), ROWS)
        write_augmented(xw_ref, 0, own, rowpot_ref[0:1, own_pots], True)
        xw = xw_ref[...]
        alpha = rowpot_ref[1:2, own_pots]
        sum_ref[...] = jnp.zeros_like(sum_ref)
        pull_ref[...] = jnp.zeros_like(pull_ref)

        def matmul(c):
            return jnp.dot(ys_ref[pl.ds(aligned(c, COLS), COLS), :], xw, preferred_element_type=F32)

        def work(c, z_ref, _):
            rounded = []
            sums = [jnp.zeros((8, LANES), F32) for _ in range(ROWS // LANES)]
            for jg in range(0, COLS, 16):
                beta = beta_ref[pl.ds(pl.multiple_of(c * COLS + jg, 16), 16), :]
                line = []
                for lt in range(ROWS // LANES):
                    tile = piece_of(z_ref, jg, lt, 16)
                    grad = jnp.exp(tile) * (tile + (alpha[:, lt * LANES : (lt + 1) * LANES] + beta))
                    sums[lt] = sums[lt] + (grad[0:8] + grad[8:16])
                    line.append(grad.astype(BF16))
                rounded.append(jnp.concatenate(line, axis=1))
            for lt in range(ROWS // LANES):
                sum_ref[:, lt * LANES : (lt + 1) * LANES] += sums[lt]
            feats = other_ref[:, pl.ds(aligned(c, COLS), COLS)]
            pull_ref[...] += jnp.dot(feats, jnp.concatenate(rounded, axis=0), preferred_element_type=F32)

        piped(nc, matmul, work, za_ref, zb_ref)
        total = jnp.sum(sum_ref[...], axis=0, keepdims=True)
        out_ref[:, rows_here] += 2.0 * (own.astype(F32) * total - pull_ref[...])
        return 0

    lax.fori_loop(0, nb, row_visit, 0)


def run(body, name, outs, scratch, limit, counts, *operands, flops=0):
    vmem = pl.BlockSpec(memory_space=pltpu.VMEM)
    return pl.pallas_call(
        body,
        name=name,
        out_shape=outs,
        in_specs=[pl.BlockSpec(memory_space=pltpu.SMEM)] + [vmem] * len(operands),
        out_specs=jax.tree.map(lambda _: vmem, outs),
        scratch_shapes=scratch,
        compiler_params=pltpu.CompilerParams(vmem_limit_bytes=limit * 1024 * 1024),
        cost_estimate=pl.CostEstimate(flops=flops, bytes_accessed=4_000_000, transcendentals=9_000_000),
    )(counts, *operands)


def shape(*dims, dtype=F32):
    return jax.ShapeDtypeStruct(dims, dtype)


def shifted(block, distance):
    size = lax.axis_size("tm")
    route = [(i - distance, i) for i in range(size) if 0 <= i - distance < size]
    return lax.ppermute(block, "tm", route)


def swapped(block, k):
    return lax.ppermute(block, "cell", [(i, i ^ k) for i in range(lax.axis_size("cell"))])


def exchanged(block):
    near = swapped(block, 1)
    far = swapped(block, 2)
    return [block, near, far, swapped(far, 1)]


def per_device(embedding, counts):
    feat_dim, local = embedding.shape
    group = lax.axis_size("cell")
    slots = local * group

    target_parts = exchanged(shifted(embedding, -1))
    source_parts = exchanged(embedding)

    flops = 2 * local * slots * DEPTH
    aug = pltpu.VMEM((DEPTH, slots), BF16)
    narrow = pltpu.VMEM((ROWS, LANES), F32)
    wide = pltpu.VMEM((ROWS, slots), F32)
    half = pltpu.VMEM((ROWS, slots), BF16)
    turned_rows = pltpu.VMEM((16, ROWS), BF16)
    buffers = [pltpu.VMEM((ROWS, COLS), F32)] * 2
    long = pltpu.VMEM((8, slots), F32)
    grouped, targets, xa, gb, log = run(
        kernel_a, "column_log",
        (
            shape(feat_dim, slots, dtype=BF16), shape(feat_dim, slots, dtype=BF16),
            shape(local, DEPTH, dtype=BF16), shape(1, slots), shape(1, slots),
        ),
        [aug, pltpu.VMEM((DEPTH, local), F32), *buffers, long, long],
        16, counts, *source_parts, *target_parts, flops=flops,
    )
    logs = exchanged(log)
    g1, col1 = run(
        kernel_b, "first_sweep",
        (shape(1, slots), shape(1, slots)),
        [aug, *buffers, wide, wide, narrow, narrow, narrow, narrow, narrow, long],
        24, counts, xa, targets, gb, *logs, flops=2 * flops,
    )
    grouped, col1 = lax.optimization_barrier((grouped, col1))
    earlier = shifted(grouped, 1)
    xb, aux, g2, stats = run(
        kernel_c, "second_sweep",
        (shape(local, DEPTH, dtype=BF16), shape(local, LANES), shape(1, slots), shape(1, 3 * slots)),
        [
            aug, *buffers, half, half, half, half, narrow, narrow, narrow, narrow, narrow,
            pltpu.VMEM((1, slots), F32), turned_rows, pltpu.VMEM((32, slots), F32), long, long, long,
        ],
        28, counts, xa, targets, gb, g1, *exchanged(col1), flops=2 * flops,
    )
    xb, earlier = lax.optimization_barrier((xb, earlier))
    stat, send = run(
        kernel_d, "adjoint",
        (shape(8, slots), shape(1, 2 * slots + 2 * local)),
        [
            aug, *buffers, half, half, pltpu.VMEM((16, slots), BF16), pltpu.VMEM((ROWS, 16), F32), turned_rows,
            pltpu.VMEM((16, slots), F32),
        ],
        20, counts, xb, aux, targets, gb, g2, *exchanged(stats), flops=2 * flops,
    )
    col_pair, rows_mine, early = run(
        kernel_f, "assemble",
        (shape(2, slots), shape(2, local), shape(2, slots + local)),
        [pltpu.VMEM((group, 1, 2 * slots + 2 * local), F32)],
        8, counts, *exchanged(send), stat,
    )
    early = shifted(early, 1)

    turned = [pltpu.VMEM((COLS, ROWS), F32)] * 2
    scratch_e = [
        pltpu.VMEM((DEPTH, ROWS), BF16), pltpu.VMEM((DEPTH, COLS), F32), pltpu.VMEM((slots, DEPTH), BF16),
        pltpu.VMEM((slots, LANES), F32), *turned, pltpu.VMEM((feat_dim, ROWS), F32), pltpu.VMEM((8, ROWS), F32),
    ]
    source_grad = run(
        functools.partial(kernel_e, earlier=False), "source_gradient", shape(feat_dim, local), scratch_e,
        16, counts, embedding, rows_mine, targets, col_pair, flops=2 * flops,
    )
    return run(
        functools.partial(kernel_e, earlier=True), "target_gradient", shape(feat_dim, local), scratch_e,
        16, counts, embedding, early, earlier, early, source_grad, flops=2 * flops,
    )


def solution(mesh):
    in_specs = (P(None, ("tm", "cell")), P())
    out_specs = P(None, ("tm", "cell"))
    return jax.shard_map(
        per_device, mesh=mesh, in_specs=in_specs, out_specs=out_specs, check_vma=False
    )
```

```python
import functools

import jax
import jax.numpy as jnp
from jax import lax
from jax.experimental import pallas as pl
from jax.experimental.pallas import tpu as pltpu
from jax.sharding import PartitionSpec as P

ENTROPY = 0.25
PENALTY = 5.0
DAMPING = PENALTY / (PENALTY + ENTROPY)
MASKED = -1e30
SQ_SCALE = 1.0 / ENTROPY
DOT_SCALE = 2.0 / ENTROPY
TINY = 1e-37
SHIFT = 44.0
LOWEST = 1e-24

ROWS = 256
COLS = 512
LANES = 128
DEPTH = 128
F32 = jnp.float32
BF16 = jnp.bfloat16


def split3(value):
    high = value.astype(BF16).astype(F32)
    rest = value - high
    middle = rest.astype(BF16).astype(F32)
    return high, middle, rest - middle


def write_augmented(out_ref, start, feats, pot, is_row):
    n = feats.shape[1]
    cols = pl.ds(start, n)
    scaled = feats.astype(F32) * DOT_SCALE if is_row else feats
    out_ref[0:32, cols] = scaled.astype(out_ref.dtype)
    first = 0 if is_row else 3
    ones_from = 3 if is_row else 0
    row = lax.broadcasted_iota(jnp.int32, (16, n), 0)
    tail = jnp.where((row >= ones_from) & (row < ones_from + 3), 1.0, 0.0)
    for k, piece in enumerate(split3(pot)):
        tail = jnp.where(row == first + k, piece, tail)
    out_ref[32:48, cols] = tail.astype(out_ref.dtype)
    out_ref[48:128, cols] = jnp.zeros((80, n), out_ref.dtype)


def square_sum(feats):
    wide = feats.astype(F32)
    return jnp.sum(wide * wide, axis=0, keepdims=True)


def live_pot(feats, start, count):
    ids = start + lax.broadcasted_iota(jnp.int32, (1, feats.shape[1]), 1)
    return jnp.where(ids < count, -SQ_SCALE * square_sum(feats), MASKED)


def aligned(index, size):
    return pl.multiple_of(index * size, size)


def around(counts):
    size = counts.shape[0]
    time, member = lax.axis_index("tm"), lax.axis_index("cell")
    before = jnp.where(time > 0, counts[jnp.maximum(time - 1, 0)], 0)
    after = jnp.where(time + 1 < size, counts[jnp.minimum(time + 1, size - 1)], 0)
    return before, counts[time], after, member


def row_steps(count_here, count_next, member, group):
    blocks = pl.cdiv(count_here, LANES)
    mine = jnp.maximum((blocks - member + group - 1) // group, 0)
    per_step = ROWS // LANES
    steps = (mine + per_step - 1) // per_step
    return jnp.where(count_next > 0, steps, 0)


def col_steps(count):
    return (count + COLS - 1) // COLS


LTS = COLS // LANES
SUB = 32
WIDE = 1536


def scores(xa, ya_ref, c, cols=COLS):
    return jnp.dot(xa, ya_ref[:, pl.ds(aligned(c, cols), cols)], preferred_element_type=F32)


def piped(count, matmul, work, first_ref, second_ref, load=None, store=None):
    load = load or (lambda c: None)
    store = store or (lambda c, state: None)
    first_ref[...] = matmul(0)

    def pair(i, _):
        here, there = 2 * i, 2 * i + 1
        states = load(here), load(there)
        second_ref[...] = matmul(there)
        one = work(here, first_ref, states[0])
        first_ref[...] = matmul(jnp.minimum(there + 1, count - 1))
        two = work(there, second_ref, states[1])
        store(here, one)
        store(there, two)
        return 0

    lax.fori_loop(0, count // 2, pair, 0)

    @pl.when(count % 2 == 1)
    def _():
        store(count - 1, work(count - 1, first_ref, load(count - 1)))


def adder(acc_refs):
    def store(c, sums):
        for k, acc_ref in enumerate(acc_refs):
            lts = len(sums[k])
            for lt in range(lts):
                acc_ref[:, lane_tile(c, lt, lts)] += sums[k][lt]

    return store


def lane_tile(c, lt, lts=LTS):
    return pl.ds(aligned(c * lts + lt, LANES), LANES)


def piece_of(z_ref, rg, lt, size=SUB):
    return z_ref[rg : rg + size, lt * LANES : (lt + 1) * LANES]


def in_steps(total, visit):
    for start in range(0, total, WIDE):
        visit(start, slice(start, start + WIDE))


def kernel_a(
    counts, x0, x1, x2, x3, y0, y1, y2, y3,
    xg_ref, yg_ref, xa_ref, gb_ref, log_ref,
    ya_ref, xat_ref, za_ref, zb_ref, top_ref, sum_ref,
):
    _, count_here, count_next, member = around(counts)
    group = 4
    nb = row_steps(count_here, count_next, member, group)
    nc = col_steps(count_next)
    local = x0.shape[1]
    for k, (x_ref, y_ref) in enumerate(((x0, y0), (x1, y1), (x2, y2), (x3, y3))):
        place = pl.ds(aligned(member ^ k, local), local)
        xg_ref[:, place] = x_ref[...]
        yg_ref[:, place] = y_ref[...]
    for k in range(local // LANES):
        block_id = group * k + member
        piece = xg_ref[:, pl.ds(aligned(block_id, LANES), LANES)]
        pot = live_pot(piece, block_id * LANES, count_here) + SHIFT
        write_augmented(xat_ref, k * LANES, piece, pot, True)
        xa_ref[k * LANES : (k + 1) * LANES, :] = jnp.transpose(
            xat_ref[:, k * LANES : (k + 1) * LANES]
        ).astype(BF16)
    sum_ref[...] = jnp.zeros_like(sum_ref)

    def prepare(start, cols):
        feats = yg_ref[:, cols]
        pot = live_pot(feats, start, count_next)
        gb_ref[:, cols] = pot
        write_augmented(ya_ref, start, feats, pot, False)

    in_steps(group * local, prepare)

    def exact():
        top_ref[...] = jnp.full(top_ref.shape, MASKED, F32)
        sum_ref[...] = jnp.zeros_like(sum_ref)

        def row_visit(b, _):
            xa = xa_ref[pl.ds(aligned(b, ROWS), ROWS), :]

            def load(c):
                return [(top_ref[:, lane_tile(c, lt)], sum_ref[:, lane_tile(c, lt)]) for lt in range(LTS)]

            def work(c, z_ref, state):
                after = []
                for lt, (old, total) in enumerate(state):
                    tile = z_ref[:, lt * LANES : (lt + 1) * LANES].reshape(ROWS // 8, 8, LANES)
                    top = jnp.maximum(old, jnp.max(tile, axis=0))
                    total = total * jnp.exp(old - top) + jnp.sum(jnp.exp(tile - top[None]), axis=0)
                    after.append((top, total))
                return after

            def store(c, state):
                for lt, (top, total) in enumerate(state):
                    top_ref[:, lane_tile(c, lt)] = top
                    sum_ref[:, lane_tile(c, lt)] = total

            piped(nc, lambda c: scores(xa, ya_ref, c), work, za_ref, zb_ref, load, store)
            return 0

        lax.fori_loop(0, nb, row_visit, 0)
        tops = top_ref[...]
        top = jnp.max(tops, axis=0, keepdims=True)
        total = jnp.sum(sum_ref[...] * jnp.exp(tops - top), axis=0, keepdims=True)
        log_ref[...] = top + jnp.log(jnp.maximum(total, TINY)) - SHIFT

    thin = 2 * LANES

    def quick_visit(b, _):
        halves = [xa_ref[pl.ds(aligned(2 * b + k, ROWS // 2), ROWS // 2), :] for k in range(2)]

        def tile_sums(c, tiles):
            for t in range(tiles):
                totals = [jnp.zeros((8, LANES), F32) for _ in range(2)]
                for half in halves:
                    z = scores(half, ya_ref, c * tiles + t, thin)
                    for lt in range(2):
                        p = jnp.exp(z[:, lt * LANES : (lt + 1) * LANES])
                        totals[lt] = totals[lt] + jnp.sum(p.reshape(ROWS // 16, 8, LANES), axis=0)
                for lt in range(2):
                    sum_ref[:, lane_tile(c * tiles + t, lt, 2)] += totals[lt]

        def pair(i, _):
            tile_sums(i, 4)
            return 0

        lax.fori_loop(0, nc // 2, pair, 0)

        @pl.when(nc % 2 == 1)
        def _():
            tile_sums(nc - 1, 2)

        return 0

    lax.fori_loop(0, nb, quick_visit, 0)
    total = jnp.sum(sum_ref[...], axis=0, keepdims=True)
    log_ref[...] = jnp.where(total > 0.0, jnp.log(jnp.maximum(total, TINY)) - SHIFT, MASKED)
    ids = lax.broadcasted_iota(jnp.int32, total.shape, 1)
    lowest = jnp.min(jnp.where(ids < count_next, total, 1.0))

    @pl.when((lowest < LOWEST) & (nb > 0))
    def _():
        exact()


def column_sums(c, z_ref, _):
    rows, cols = z_ref.shape
    sums = []
    for lt in range(cols // LANES):
        p = jnp.exp(z_ref[:, lt * LANES : (lt + 1) * LANES])
        sums.append(jnp.sum(p.reshape(rows // 8, 8, LANES), axis=0))
    return [sums]


def row_adder(sum_ref, push_ref=None, g_ref=None):
    def first(c, scores_of, kept):
        half = ROWS // 2
        for start in range(0, ROWS, half):
            scored = scores_of(c, start, half)
            for rg in range(0, half, SUB):
                rows = slice(start + rg, start + rg + SUB)
                total = sum_ref[rows, :]
                push = push_ref[rows, :] if push_ref is not None else None
                for lt in range(LTS):
                    z = piece_of(scored, rg, lt)
                    p = jnp.exp(z)
                    total = total + p
                    kept[0][rows, lane_tile(c, lt)] = p.astype(kept[0].dtype)
                    if push is not None:
                        part = p * (g_ref[:, lane_tile(c, lt)] - z)
                        push = push + part
                        kept[1][rows, lane_tile(c, lt)] = part.astype(kept[1].dtype)
                sum_ref[rows, :] = total
                if push is not None:
                    push_ref[rows, :] = push

    return first


def column_parts(c, plan):
    sums = [[jnp.zeros((8, LANES), F32) for _ in range(LTS)] for _ in plan]
    for rg in range(0, ROWS, 8):
        for k, (kept_ref, weight_ref) in enumerate(plan):
            scale = weight_ref[rg : rg + 8, :]
            for lt in range(LTS):
                sums[k][lt] = sums[k][lt] + scale * kept_ref[rg : rg + 8, lane_tile(c, lt)]
    return sums


def two_stage(nb, nc, first, finish, second, store, matmul_of, buffers, kept):
    def stage(b, now, before):
        matmul = matmul_of(b)

        def work(c, z, _):
            first(c, z, now)
            return second(c, before) if before else None

        if buffers is None:
            in_pairs(lambda c: work(c, matmul, None), store if before else None)
        else:
            piped(nc, matmul, work, *buffers, store=store if before else None)
        finish(b)

    def in_pairs(visit, put):
        put = put or (lambda c, sums: None)

        def pair(i, _):
            one, two = visit(2 * i), visit(2 * i + 1)
            put(2 * i, one)
            put(2 * i + 1, two)
            return 0

        lax.fori_loop(0, nc // 2, pair, 0)

        @pl.when(nc % 2 == 1)
        def _():
            put(nc - 1, visit(nc - 1))

    def tail(before):
        in_pairs(lambda c: second(c, before), store)

    even, odd = kept

    @pl.when(nb > 0)
    def _():
        stage(0, even, None)

    def visit(b, _):
        @pl.when(b % 2 == 1)
        def _():
            stage(b, odd, even)

        @pl.when(b % 2 == 0)
        def _():
            stage(b, even, odd)

        return 0

    lax.fori_loop(1, nb, visit, 0)

    @pl.when((nb > 0) & (nb % 2 == 1))
    def _():
        tail(even)

    @pl.when((nb > 0) & (nb % 2 == 0))
    def _():
        tail(odd)


def col_tile(c):
    return pl.ds(aligned(c, COLS), COLS)


def split2(value):
    high = value.astype(BF16).astype(F32)
    return high, value - high


def turned_weights(columns):
    lane = lax.broadcasted_iota(jnp.int32, (ROWS, LANES), 1)
    packed = jnp.zeros((ROWS, LANES), F32)
    for at, column in columns:
        packed = jnp.where(lane == at, column, packed)
    return jnp.transpose(packed)


def sweep(quick, exact, low_ref, lost=None):
    low_ref[...] = jnp.ones_like(low_ref)
    quick()
    again = jnp.min(low_ref[...]) < LOWEST
    if lost is not None:
        again = again | lost()

    @pl.when(again)
    def _():
        exact()


def row_lse(xa, ya_ref, nc, buffers, top_ref, sum_ref, push_ref=None, g_ref=None):
    top_ref[...] = jnp.full(top_ref.shape, MASKED, F32)
    sum_ref[...] = jnp.zeros_like(sum_ref)
    if push_ref is not None:
        push_ref[...] = jnp.zeros_like(push_ref)

    def work(c, z_ref, _):
        for rg in range(0, ROWS, SUB):
            rows = slice(rg, rg + SUB)
            old = top_ref[rows, :]
            pieces = [piece_of(z_ref, rg, lt) for lt in range(LTS)]
            top = old
            for z in pieces:
                top = jnp.maximum(top, z)
            fade = jnp.exp(old - top)
            total = sum_ref[rows, :] * fade
            push = push_ref[rows, :] * fade if push_ref is not None else None
            for lt, z in enumerate(pieces):
                p = jnp.exp(z - top)
                total = total + p
                if push is not None:
                    push = push + p * (g_ref[:, lane_tile(c, lt)] - z)
            top_ref[rows, :] = top
            sum_ref[rows, :] = total
            if push is not None:
                push_ref[rows, :] = push

    piped(nc, lambda c: scores(xa, ya_ref, c), work, *buffers)
    tops = top_ref[...]
    top = jnp.max(tops, axis=1, keepdims=True)
    fade = jnp.exp(tops - top)
    total = jnp.sum(sum_ref[...] * fade, axis=1, keepdims=True)
    if push_ref is None:
        return top, total
    return top, total, jnp.sum(push_ref[...] * fade, axis=1, keepdims=True)


def row_potential(xa):
    lane = lax.broadcasted_iota(jnp.int32, (ROWS, LANES), 1)
    wide = xa.astype(F32)
    old = jnp.sum(jnp.where((lane >= 32) & (lane < 35), wide, 0.0), axis=1, keepdims=True)
    return lane, wide, old


def with_row_potential(lane, wide, pot):
    high, middle, low = split3(pot)
    new = jnp.where(lane == 32, high, jnp.where(lane == 33, middle, jnp.where(lane == 34, low, wide)))
    return new.astype(BF16)


def kernel_b(counts, xa_ref, yg_ref, gb_ref, l0, l1, l2, l3, g_ref, col_ref, ya_ref, za_ref, zb_ref, p_ref, q_ref, top_ref, sum_ref, weight_ref, low_ref, most_ref, acc_ref):
    _, count_here, count_next, member = around(counts)
    nb = row_steps(count_here, count_next, member, 4)
    nc = col_steps(count_next)

    def prepare(start, cols):
        logs = [ref[:, cols] for ref in (l0, l1, l2, l3)]
        top = jnp.maximum(jnp.maximum(logs[0], logs[1]), jnp.maximum(logs[2], logs[3]))
        total = sum(jnp.exp(one - top) for one in logs)
        ids = start + lax.broadcasted_iota(jnp.int32, (1, WIDE), 1)
        pot = jnp.where(ids < count_next, -DAMPING * (top + jnp.log(total)), 0.0)
        g_ref[:, cols] = pot
        write_augmented(ya_ref, start, yg_ref[:, cols], pot + gb_ref[:, cols], False)

    in_steps(yg_ref.shape[1], prepare)

    buffers = za_ref, zb_ref

    def quick():
        acc_ref[...] = jnp.zeros_like(acc_ref)

        def matmul_of(b):
            sum_ref[...] = jnp.zeros_like(sum_ref)
            return lambda c, start, size: scores(
                xa_ref[pl.ds(pl.multiple_of(b * ROWS + start, size), size), :], ya_ref, c
            )

        def finish(b):
            lane, wide, old = row_potential(xa_ref[pl.ds(aligned(b, ROWS), ROWS), :])
            live = old > 0.5 * MASKED
            total = jnp.sum(sum_ref[...], axis=1, keepdims=True)
            low_ref[...] = jnp.minimum(low_ref[...], jnp.where(live, total, 1.0))
            pot = -DAMPING * (jnp.log(jnp.maximum(total, TINY)) - SHIFT)
            weight = jnp.where(live, jnp.exp(pot - SHIFT), 0.0)
            weight_ref[...] = jnp.broadcast_to(weight, weight_ref.shape)
            most_ref[...] = jnp.maximum(most_ref[...], weight)

        two_stage(
            nb, nc, row_adder(sum_ref), finish, lambda c, kept: column_parts(c, [(kept[0], weight_ref)]),
            adder([acc_ref]), matmul_of, None, ((p_ref,), (q_ref,)),
        )

    def exact():
        acc_ref[...] = jnp.zeros_like(acc_ref)

        def row_visit(b, _):
            xa = xa_ref[pl.ds(aligned(b, ROWS), ROWS), :]
            lane, wide, old = row_potential(xa)
            live = old > 0.5 * MASKED
            top, total = row_lse(xa, ya_ref, nc, buffers, top_ref, sum_ref)
            pot = -DAMPING * (top + jnp.log(total) - SHIFT)
            xb = with_row_potential(lane, wide, jnp.where(live, pot + old - SHIFT, MASKED))
            piped(nc, lambda c: scores(xb, ya_ref, c), column_sums, *buffers, store=adder([acc_ref]))
            return 0

        lax.fori_loop(0, nb, row_visit, 0)

    def lost():
        total = jnp.sum(acc_ref[...], axis=0, keepdims=True)
        ids = lax.broadcasted_iota(jnp.int32, total.shape, 1)
        least = jnp.min(jnp.where((ids < count_next) & (nb > 0), total, 1.0))
        return least < jnp.max(most_ref[...]) * 2.0**-91

    most_ref[...] = jnp.zeros_like(most_ref)
    sweep(quick, exact, low_ref, lost)
    col_ref[...] = jnp.sum(acc_ref[...], axis=0, keepdims=True)


def kernel_c(
    counts, xa_ref, yg_ref, gb_ref, g_ref, c0, c1, c2, c3,
    xb_ref, aux_ref, g2_ref, col_ref,
    ya_ref, za_ref, zb_ref, p_ref, w_ref, q_ref, v_ref, top_ref, sum_ref, push_ref, adj_ref, low_ref, cost_ref, weight_ref, acc_ref, acc0_ref, acc1_ref, acc2_ref,
):
    _, count_here, count_next, member = around(counts)
    nb = row_steps(count_here, count_next, member, 4)
    nc = col_steps(count_next)

    def prepare(start, cols):
        total = (c0[:, cols] + c1[:, cols]) + (c2[:, cols] + c3[:, cols])
        ids = start + lax.broadcasted_iota(jnp.int32, (1, WIDE), 1)
        log = jnp.log(jnp.maximum(total, TINY)) - g_ref[:, cols]
        pot = jnp.where(ids < count_next, -DAMPING * log, 0.0)
        g2_ref[:, cols] = pot
        write_augmented(ya_ref, start, yg_ref[:, cols], pot + gb_ref[:, cols], False)

    in_steps(yg_ref.shape[1], prepare)

    buffers = za_ref, zb_ref
    accs = acc0_ref, acc1_ref, acc2_ref

    ids = lax.broadcasted_iota(jnp.int32, g_ref.shape, 1)
    centre = jnp.sum(jnp.where(ids < count_next, g_ref[...], 0.0), axis=1, keepdims=True)
    centre = centre / (DAMPING * jnp.maximum(count_next, 1).astype(F32)) + 3.0
    cost_ref[...] = g2_ref[...] + (SHIFT - centre)

    def close_rows(b, top, total, push):
        rows_here = pl.ds(aligned(b, ROWS), ROWS)
        lane, wide, old = row_potential(xa_ref[rows_here, :])
        live = old > 0.5 * MASKED
        total = jnp.maximum(total, TINY)
        row_log = top + jnp.log(total) - SHIFT
        pot = jnp.where(live, -DAMPING * row_log, 0.0)
        row_sum = jnp.where(live, jnp.exp(row_log + pot), 0.0)
        adjoint = jnp.where(live, push / total + centre, 0.0)
        inverse = jnp.where(row_sum > 0.0, 1.0 / jnp.maximum(row_sum, TINY), 0.0)
        full = jnp.where(live, pot + old - SHIFT, MASKED)
        xb = with_row_potential(lane, wide, full)
        xb_ref[rows_here, :] = xb
        aux = jnp.where(lane == 0, adjoint, jnp.where(lane == 1, inverse, jnp.where(lane == 2, pot, full)))
        aux_ref[rows_here, :] = aux
        return live, pot, adjoint, xb

    def quick():
        acc_ref[...] = jnp.zeros_like(acc_ref)

        def matmul_of(b):
            sum_ref[...] = jnp.zeros_like(sum_ref)
            push_ref[...] = jnp.zeros_like(push_ref)
            return lambda c, start, size: scores(
                xa_ref[pl.ds(pl.multiple_of(b * ROWS + start, size), size), :], ya_ref, c
            )

        def finish(b):
            total = jnp.sum(sum_ref[...], axis=1, keepdims=True)
            push = jnp.sum(push_ref[...], axis=1, keepdims=True)
            live, pot, adjoint, _ = close_rows(b, 0.0, total, push)
            low_ref[...] = jnp.minimum(low_ref[...], jnp.where(live, total, 1.0))
            weight = jnp.where(live, jnp.exp(pot - SHIFT), 0.0)
            pieces = (*split2(weight), *split2(weight * adjoint))
            weight_ref[...] = turned_weights(list(enumerate(pieces)))[0:16, :].astype(BF16)

        def second(c, kept):
            weights = weight_ref[...]
            plan = jnp.dot(weights, kept[0][:, col_tile(c)], preferred_element_type=F32)
            cost = jnp.dot(weights, kept[1][:, col_tile(c)], preferred_element_type=F32)
            return plan, cost

        def store(c, sums):
            acc_ref[0:16, col_tile(c)] += sums[0]
            acc_ref[16:32, col_tile(c)] += sums[1]

        two_stage(
            nb, nc, row_adder(sum_ref, push_ref, cost_ref), finish, second, store, matmul_of, None,
            ((p_ref, w_ref), (q_ref, v_ref)),
        )
        acc0_ref[0:1, :] = acc_ref[0:1, :] + acc_ref[1:2, :]
        acc1_ref[0:1, :] = acc_ref[16:17, :] + acc_ref[17:18, :]
        acc2_ref[0:1, :] = acc_ref[2:3, :] + acc_ref[3:4, :]
        for ref in accs:
            ref[1:8, :] = jnp.zeros((7, ref.shape[1]), F32)

    def exact():
        for ref in accs:
            ref[...] = jnp.zeros_like(ref)

        def row_visit(b, _):
            xa = xa_ref[pl.ds(aligned(b, ROWS), ROWS), :]
            top, total, push = row_lse(xa, ya_ref, nc, buffers, top_ref, sum_ref, push_ref, cost_ref)
            _, pot, adjoint, xb = close_rows(b, top, total, push)
            top_ref[...] = jnp.broadcast_to(pot - SHIFT, top_ref.shape)
            adj_ref[...] = jnp.broadcast_to(adjoint, adj_ref.shape)

            def work(c, z_ref, _):
                sums = [[jnp.zeros((8, LANES), F32) for _ in range(LTS)] for _ in range(3)]
                for rg in range(0, ROWS, 8):
                    pot_here = top_ref[rg : rg + 8, :]
                    adj_here = adj_ref[rg : rg + 8, :]
                    for lt in range(LTS):
                        tile = piece_of(z_ref, rg, lt, 8)
                        p = jnp.exp(tile)
                        sums[0][lt] = sums[0][lt] + p
                        sums[1][lt] = sums[1][lt] + p * (cost_ref[:, lane_tile(c, lt)] + (pot_here - tile))
                        sums[2][lt] = sums[2][lt] + p * adj_here
                return sums

            piped(nc, lambda c: scores(xb, ya_ref, c), work, *buffers, store=adder(accs))
            return 0

        lax.fori_loop(0, nb, row_visit, 0)

    sweep(quick, exact, low_ref)
    mass = jnp.sum(acc0_ref[...], axis=0, keepdims=True)
    slots = mass.shape[1]
    col_ref[:, 0:slots] = mass
    push = jnp.sum(acc1_ref[...], axis=0, keepdims=True)
    col_ref[:, slots : 2 * slots] = push + centre * mass
    col_ref[:, 2 * slots :] = jnp.sum(acc2_ref[...], axis=0, keepdims=True)


def kernel_d(
    counts, xb_ref, aux_ref, yg_ref, gb_ref, g2_ref, s0, s1, s2, s3,
    stat_ref, send_ref,
    ya_ref, za_ref, zb_ref, p_ref, q_ref, first_ref, second_ref, weight_ref, acc_ref,
):
    _, count_here, count_next, member = around(counts)
    nb = row_steps(count_here, count_next, member, 4)
    nc = col_steps(count_next)
    slots = yg_ref.shape[1]
    local = xb_ref.shape[0]
    acc_ref[...] = jnp.zeros_like(acc_ref)

    def prepare(start, cols):
        mass, push, pulled = (
            (s0[:, part] + s1[:, part]) + (s2[:, part] + s3[:, part])
            for part in (pl.ds(start + k * slots, WIDE) for k in range(3))
        )
        inverse = jnp.where(mass > 0.0, 1.0 / jnp.maximum(mass, TINY), 0.0)
        pot = g2_ref[:, cols]
        stat_ref[0:1, cols] = pot + gb_ref[:, cols]
        stat_ref[1:2, cols] = push * inverse
        stat_ref[2:3, cols] = (push - DAMPING * pulled) * inverse
        stat_ref[3:4, cols] = inverse
        stat_ref[4:5, cols] = pot
        stat_ref[5:8, cols] = jnp.zeros((3, WIDE), F32)
        write_augmented(ya_ref, start, yg_ref[:, cols], pot + gb_ref[:, cols], False)

    in_steps(slots, prepare)
    send_ref[:, slots : slots + local] = jnp.full((1, local), MASKED, F32)
    send_ref[:, slots + local :] = jnp.zeros((1, local), F32)

    def matmul_of(b):
        first_ref[...] = jnp.zeros_like(first_ref)
        second_ref[...] = jnp.zeros_like(second_ref)
        xb = xb_ref[pl.ds(aligned(b, ROWS), ROWS), :]
        return lambda c: scores(xb, ya_ref, c)

    def sums(c, z_ref, kept):
        for rg in range(0, ROWS, SUB):
            rows = slice(rg, rg + SUB)
            first = first_ref[rows, :]
            second = second_ref[rows, :]
            for lt in range(LTS):
                p = jnp.exp(piece_of(z_ref, rg, lt))
                kept[0][rows, lane_tile(c, lt)] = p
                first = first + p * stat_ref[1:2, lane_tile(c, lt)]
                second = second + p * stat_ref[2:3, lane_tile(c, lt)]
            first_ref[rows, :] = first
            second_ref[rows, :] = second

    def finish(b):
        first = jnp.sum(first_ref[...], axis=1, keepdims=True)
        second = jnp.sum(second_ref[...], axis=1, keepdims=True)
        aux = aux_ref[pl.ds(aligned(b, ROWS), ROWS), :]
        start_adj, inverse, pot, full = aux[:, 0:1], aux[:, 1:2], aux[:, 2:3], aux[:, 3:4]
        middle_adj = start_adj - DAMPING * first * inverse
        last_adj = start_adj - DAMPING * second * inverse
        weight_ref[...] = jnp.broadcast_to(middle_adj, weight_ref.shape)
        alpha = 1.0 + DAMPING * last_adj - pot
        lane = lax.broadcasted_iota(jnp.int32, (ROWS, LANES), 1)
        packed = jnp.transpose(jnp.where(lane == 0, full, alpha))
        send_ref[:, pl.ds(aligned(b + slots // ROWS, ROWS), ROWS)] = packed[0:1, :]
        send_ref[:, pl.ds(aligned(b + (slots + local) // ROWS, ROWS), ROWS)] = packed[1:2, :]

    two_stage(
        nb, nc, sums, finish, lambda c, kept: column_parts(c, [(kept[0], weight_ref)]), adder([acc_ref]), matmul_of,
        (za_ref, zb_ref), ((p_ref,), (q_ref,)),
    )
    send_ref[:, 0:slots] = jnp.sum(acc_ref[...], axis=0, keepdims=True)


def kernel_f(counts, p0, p1, p2, p3, stat_ref, col_ref, mine_ref, early_ref, parts_ref):
    member = lax.axis_index("cell")
    slots, local = stat_ref.shape[1], mine_ref.shape[1]
    for k, ref in enumerate((p0, p1, p2, p3)):
        parts_ref[member ^ k] = ref[...]
    total = (p0[:, 0:slots] + p1[:, 0:slots]) + (p2[:, 0:slots] + p3[:, 0:slots])
    last = stat_ref[1:2, :] - DAMPING * total * stat_ref[3:4, :]
    col_ref[0:1, :] = stat_ref[0:1, :]
    col_ref[1:2, :] = DAMPING * last - stat_ref[4:5, :]
    for block in range(slots // LANES):
        owner, place = block % 4, block // 4
        lanes = slice(block * LANES, (block + 1) * LANES)
        for k in range(2):
            at = slots + k * local + place * LANES
            early_ref[k : k + 1, lanes] = parts_ref[owner, :, at : at + LANES]
    here = pl.ds(aligned(member, local), local)
    mine_ref[...] = early_ref[:, here]
    early_ref[:, slots:] = col_ref[:, here]


def kernel_e(
    counts, *refs, earlier,
):
    own_ref, rowpot_ref, other_ref, colpot_ref = refs[:4]
    base_ref = refs[4] if earlier else None
    out_ref, xw_ref, tile_ref, ys_ref, beta_ref, za_ref, zb_ref, pull_ref, sum_ref = refs[5 if earlier else 4 :]
    local, slots = own_ref.shape[1], other_ref.shape[1]
    before, here, after, member = around(counts)
    count_rows = jnp.clip(here - member * local, 0, local)
    count_cols = before if earlier else after
    if earlier:
        own_at = slots
    else:
        own_at = 0
    nc = col_steps(count_cols)
    nb = jnp.where(count_cols > 0, (count_rows + ROWS - 1) // ROWS, 0)
    out_ref[...] = base_ref[...] if earlier else jnp.zeros_like(out_ref)

    def prepare(c, _):
        cols = pl.ds(aligned(c, COLS), COLS)
        write_augmented(tile_ref, 0, other_ref[:, cols], colpot_ref[0:1, cols], False)
        ys_ref[cols, :] = jnp.transpose(tile_ref[...]).astype(BF16)
        beta_ref[cols, :] = jnp.transpose(jnp.broadcast_to(colpot_ref[1:2, cols], (LANES, COLS)))
        return 0

    @pl.when(nb > 0)
    def _():
        lax.fori_loop(0, nc, prepare, 0)

    def row_visit(b, _):
        rows_here = pl.ds(aligned(b, ROWS), ROWS)
        own = own_ref[:, rows_here]
        own_pots = pl.ds(aligned(b + own_at // ROWS, ROWS), ROWS)
        write_augmented(xw_ref, 0, own, rowpot_ref[0:1, own_pots], True)
        xw = xw_ref[...]
        alpha = rowpot_ref[1:2, own_pots]
        sum_ref[...] = jnp.zeros_like(sum_ref)
        pull_ref[...] = jnp.zeros_like(pull_ref)

        def matmul(c):
            return jnp.dot(ys_ref[pl.ds(aligned(c, COLS), COLS), :], xw, preferred_element_type=F32)

        def work(c, z_ref, _):
            rounded = []
            sums = [jnp.zeros((8, LANES), F32) for _ in range(ROWS // LANES)]
            for jg in range(0, COLS, 16):
                beta = beta_ref[pl.ds(pl.multiple_of(c * COLS + jg, 16), 16), :]
                line = []
                for lt in range(ROWS // LANES):
                    tile = piece_of(z_ref, jg, lt, 16)
                    grad = jnp.exp(tile) * (tile + (alpha[:, lt * LANES : (lt + 1) * LANES] + beta))
                    sums[lt] = sums[lt] + (grad[0:8] + grad[8:16])
                    line.append(grad.astype(BF16))
                rounded.append(jnp.concatenate(line, axis=1))
            for lt in range(ROWS // LANES):
                sum_ref[:, lt * LANES : (lt + 1) * LANES] += sums[lt]
            feats = other_ref[:, pl.ds(aligned(c, COLS), COLS)]
            pull_ref[...] += jnp.dot(feats, jnp.concatenate(rounded, axis=0), preferred_element_type=F32)

        piped(nc, matmul, work, za_ref, zb_ref)
        total = jnp.sum(sum_ref[...], axis=0, keepdims=True)
        out_ref[:, rows_here] += 2.0 * (own.astype(F32) * total - pull_ref[...])
        return 0

    lax.fori_loop(0, nb, row_visit, 0)


def run(body, name, outs, scratch, limit, counts, *operands, flops=0):
    vmem = pl.BlockSpec(memory_space=pltpu.VMEM)
    return pl.pallas_call(
        body,
        name=name,
        out_shape=outs,
        in_specs=[pl.BlockSpec(memory_space=pltpu.SMEM)] + [vmem] * len(operands),
        out_specs=jax.tree.map(lambda _: vmem, outs),
        scratch_shapes=scratch,
        compiler_params=pltpu.CompilerParams(vmem_limit_bytes=limit * 1024 * 1024),
        cost_estimate=pl.CostEstimate(flops=flops, bytes_accessed=4_000_000, transcendentals=9_000_000),
    )(counts, *operands)


def shape(*dims, dtype=F32):
    return jax.ShapeDtypeStruct(dims, dtype)


def shifted(block, distance):
    size = lax.axis_size("tm")
    route = [(i - distance, i) for i in range(size) if 0 <= i - distance < size]
    return lax.ppermute(block, "tm", route)


def swapped(block, k):
    return lax.ppermute(block, "cell", [(i, i ^ k) for i in range(lax.axis_size("cell"))])


def exchanged(block):
    near = swapped(block, 1)
    far = swapped(block, 2)
    return [block, near, far, swapped(far, 1)]


def per_device(embedding, counts):
    feat_dim, local = embedding.shape
    group = lax.axis_size("cell")
    slots = local * group

    target_parts = exchanged(shifted(embedding, -1))
    source_parts = exchanged(embedding)

    flops = 2 * local * slots * DEPTH
    aug = pltpu.VMEM((DEPTH, slots), BF16)
    narrow = pltpu.VMEM((ROWS, LANES), F32)
    wide = pltpu.VMEM((ROWS, slots), F32)
    half = pltpu.VMEM((ROWS, slots), BF16)
    turned_rows = pltpu.VMEM((16, ROWS), BF16)
    buffers = [pltpu.VMEM((ROWS, COLS), F32)] * 2
    long = pltpu.VMEM((8, slots), F32)
    grouped, targets, xa, gb, log = run(
        kernel_a, "column_log",
        (
            shape(feat_dim, slots, dtype=BF16), shape(feat_dim, slots, dtype=BF16),
            shape(local, DEPTH, dtype=BF16), shape(1, slots), shape(1, slots),
        ),
        [aug, pltpu.VMEM((DEPTH, local), F32), *buffers, long, long],
        16, counts, *source_parts, *target_parts, flops=flops,
    )
    logs = exchanged(log)
    g1, col1 = run(
        kernel_b, "first_sweep",
        (shape(1, slots), shape(1, slots)),
        [aug, *buffers, wide, wide, narrow, narrow, narrow, narrow, narrow, long],
        24, counts, xa, targets, gb, *logs, flops=2 * flops,
    )
    grouped, col1 = lax.optimization_barrier((grouped, col1))
    earlier = shifted(grouped, 1)
    xb, aux, g2, stats = run(
        kernel_c, "second_sweep",
        (shape(local, DEPTH, dtype=BF16), shape(local, LANES), shape(1, slots), shape(1, 3 * slots)),
        [
            aug, *buffers, half, half, half, half, narrow, narrow, narrow, narrow, narrow,
            pltpu.VMEM((1, slots), F32), turned_rows, pltpu.VMEM((32, slots), F32), long, long, long,
        ],
        28, counts, xa, targets, gb, g1, *exchanged(col1), flops=2 * flops,
    )
    xb, earlier = lax.optimization_barrier((xb, earlier))
    stat, send = run(
        kernel_d, "adjoint",
        (shape(8, slots), shape(1, slots + 2 * local)),
        [aug, *buffers, wide, wide, narrow, narrow, narrow, long],
        24, counts, xb, aux, targets, gb, g2, *exchanged(stats), flops=2 * flops,
    )
    col_pair, rows_mine, early = run(
        kernel_f, "assemble",
        (shape(2, slots), shape(2, local), shape(2, slots + local)),
        [pltpu.VMEM((group, 1, slots + 2 * local), F32)],
        8, counts, *exchanged(send), stat,
    )
    early = shifted(early, 1)

    turned = [pltpu.VMEM((COLS, ROWS), F32)] * 2
    scratch_e = [
        pltpu.VMEM((DEPTH, ROWS), BF16), pltpu.VMEM((DEPTH, COLS), F32), pltpu.VMEM((slots, DEPTH), BF16),
        pltpu.VMEM((slots, LANES), F32), *turned, pltpu.VMEM((feat_dim, ROWS), F32), pltpu.VMEM((8, ROWS), F32),
    ]
    source_grad = run(
        functools.partial(kernel_e, earlier=False), "source_gradient", shape(feat_dim, local), scratch_e,
        16, counts, embedding, rows_mine, targets, col_pair, flops=2 * flops,
    )
    return run(
        functools.partial(kernel_e, earlier=True), "target_gradient", shape(feat_dim, local), scratch_e,
        16, counts, embedding, early, earlier, early, source_grad, flops=2 * flops,
    )


def solution(mesh):
    in_specs = (P(None, ("tm", "cell")), P())
    out_specs = P(None, ("tm", "cell"))
    return jax.shard_map(
        per_device, mesh=mesh, in_specs=in_specs, out_specs=out_specs, check_vma=False
    )
```

```python
import functools

import jax
import jax.numpy as jnp
from jax import lax
from jax.experimental import pallas as pl
from jax.experimental.pallas import tpu as pltpu
from jax.sharding import PartitionSpec as P

ENTROPY = 0.25
PENALTY = 5.0
DAMPING = PENALTY / (PENALTY + ENTROPY)
MASKED = -1e30
SQ_SCALE = 1.0 / ENTROPY
DOT_SCALE = 2.0 / ENTROPY
TINY = 1e-37
SHIFT = 44.0
LOWEST = 1e-24

ROWS = 256
COLS = 512
LANES = 128
DEPTH = 128
F32 = jnp.float32
BF16 = jnp.bfloat16


def split3(value):
    high = value.astype(BF16).astype(F32)
    rest = value - high
    middle = rest.astype(BF16).astype(F32)
    return high, middle, rest - middle


def write_augmented(out_ref, start, feats, pot, is_row):
    n = feats.shape[1]
    cols = pl.ds(start, n)
    scaled = feats.astype(F32) * DOT_SCALE if is_row else feats
    out_ref[0:32, cols] = scaled.astype(out_ref.dtype)
    first = 0 if is_row else 3
    ones_from = 3 if is_row else 0
    row = lax.broadcasted_iota(jnp.int32, (16, n), 0)
    tail = jnp.where((row >= ones_from) & (row < ones_from + 3), 1.0, 0.0)
    for k, piece in enumerate(split3(pot)):
        tail = jnp.where(row == first + k, piece, tail)
    out_ref[32:48, cols] = tail.astype(out_ref.dtype)
    out_ref[48:128, cols] = jnp.zeros((80, n), out_ref.dtype)


def square_sum(feats):
    wide = feats.astype(F32)
    return jnp.sum(wide * wide, axis=0, keepdims=True)


def live_pot(feats, start, count):
    ids = start + lax.broadcasted_iota(jnp.int32, (1, feats.shape[1]), 1)
    return jnp.where(ids < count, -SQ_SCALE * square_sum(feats), MASKED)


def aligned(index, size):
    return pl.multiple_of(index * size, size)


def around(counts):
    size = counts.shape[0]
    time, member = lax.axis_index("tm"), lax.axis_index("cell")
    before = jnp.where(time > 0, counts[jnp.maximum(time - 1, 0)], 0)
    after = jnp.where(time + 1 < size, counts[jnp.minimum(time + 1, size - 1)], 0)
    return before, counts[time], after, member


def row_steps(count_here, count_next, member, group):
    blocks = pl.cdiv(count_here, LANES)
    mine = jnp.maximum((blocks - member + group - 1) // group, 0)
    per_step = ROWS // LANES
    steps = (mine + per_step - 1) // per_step
    return jnp.where(count_next > 0, steps, 0)


def col_steps(count):
    return (count + COLS - 1) // COLS


LTS = COLS // LANES
SUB = 32
WIDE = 1536


def scores(xa, ya_ref, c, cols=COLS):
    return jnp.dot(xa, ya_ref[:, pl.ds(aligned(c, cols), cols)], preferred_element_type=F32)


def piped(count, matmul, work, first_ref, second_ref, load=None, store=None):
    load = load or (lambda c: None)
    store = store or (lambda c, state: None)
    first_ref[...] = matmul(0)

    def pair(i, _):
        here, there = 2 * i, 2 * i + 1
        states = load(here), load(there)
        second_ref[...] = matmul(there)
        one = work(here, first_ref, states[0])
        first_ref[...] = matmul(jnp.minimum(there + 1, count - 1))
        two = work(there, second_ref, states[1])
        store(here, one)
        store(there, two)
        return 0

    lax.fori_loop(0, count // 2, pair, 0)

    @pl.when(count % 2 == 1)
    def _():
        store(count - 1, work(count - 1, first_ref, load(count - 1)))


def adder(acc_refs):
    def store(c, sums):
        for k, acc_ref in enumerate(acc_refs):
            lts = len(sums[k])
            for lt in range(lts):
                acc_ref[:, lane_tile(c, lt, lts)] += sums[k][lt]

    return store


def lane_tile(c, lt, lts=LTS):
    return pl.ds(aligned(c * lts + lt, LANES), LANES)


def piece_of(z_ref, rg, lt, size=SUB):
    return z_ref[rg : rg + size, lt * LANES : (lt + 1) * LANES]


def in_steps(total, visit):
    for start in range(0, total, WIDE):
        visit(start, slice(start, start + WIDE))


def kernel_a(
    counts, x0, x1, x2, x3, y0, y1, y2, y3,
    xg_ref, yg_ref, xa_ref, gb_ref, log_ref,
    ya_ref, xat_ref, za_ref, zb_ref, top_ref, sum_ref,
):
    _, count_here, count_next, member = around(counts)
    group = 4
    nb = row_steps(count_here, count_next, member, group)
    nc = col_steps(count_next)
    local = x0.shape[1]
    for k, (x_ref, y_ref) in enumerate(((x0, y0), (x1, y1), (x2, y2), (x3, y3))):
        place = pl.ds(aligned(member ^ k, local), local)
        xg_ref[:, place] = x_ref[...]
        yg_ref[:, place] = y_ref[...]
    for k in range(local // LANES):
        block_id = group * k + member
        piece = xg_ref[:, pl.ds(aligned(block_id, LANES), LANES)]
        pot = live_pot(piece, block_id * LANES, count_here) + SHIFT
        write_augmented(xat_ref, k * LANES, piece, pot, True)
        xa_ref[k * LANES : (k + 1) * LANES, :] = jnp.transpose(
            xat_ref[:, k * LANES : (k + 1) * LANES]
        ).astype(BF16)
    sum_ref[...] = jnp.zeros_like(sum_ref)

    def prepare(start, cols):
        feats = yg_ref[:, cols]
        pot = live_pot(feats, start, count_next)
        gb_ref[:, cols] = pot
        write_augmented(ya_ref, start, feats, pot, False)

    in_steps(group * local, prepare)

    def exact():
        top_ref[...] = jnp.full(top_ref.shape, MASKED, F32)
        sum_ref[...] = jnp.zeros_like(sum_ref)

        def row_visit(b, _):
            xa = xa_ref[pl.ds(aligned(b, ROWS), ROWS), :]

            def load(c):
                return [(top_ref[:, lane_tile(c, lt)], sum_ref[:, lane_tile(c, lt)]) for lt in range(LTS)]

            def work(c, z_ref, state):
                after = []
                for lt, (old, total) in enumerate(state):
                    tile = z_ref[:, lt * LANES : (lt + 1) * LANES].reshape(ROWS // 8, 8, LANES)
                    top = jnp.maximum(old, jnp.max(tile, axis=0))
                    total = total * jnp.exp(old - top) + jnp.sum(jnp.exp(tile - top[None]), axis=0)
                    after.append((top, total))
                return after

            def store(c, state):
                for lt, (top, total) in enumerate(state):
                    top_ref[:, lane_tile(c, lt)] = top
                    sum_ref[:, lane_tile(c, lt)] = total

            piped(nc, lambda c: scores(xa, ya_ref, c), work, za_ref, zb_ref, load, store)
            return 0

        lax.fori_loop(0, nb, row_visit, 0)
        tops = top_ref[...]
        top = jnp.max(tops, axis=0, keepdims=True)
        total = jnp.sum(sum_ref[...] * jnp.exp(tops - top), axis=0, keepdims=True)
        log_ref[...] = top + jnp.log(jnp.maximum(total, TINY)) - SHIFT

    thin = 2 * LANES

    def quick_visit(b, _):
        halves = [xa_ref[pl.ds(aligned(2 * b + k, ROWS // 2), ROWS // 2), :] for k in range(2)]

        def tile_sums(c, tiles):
            for t in range(tiles):
                totals = [jnp.zeros((8, LANES), F32) for _ in range(2)]
                for half in halves:
                    z = scores(half, ya_ref, c * tiles + t, thin)
                    for lt in range(2):
                        p = jnp.exp(z[:, lt * LANES : (lt + 1) * LANES])
                        totals[lt] = totals[lt] + jnp.sum(p.reshape(ROWS // 16, 8, LANES), axis=0)
                for lt in range(2):
                    sum_ref[:, lane_tile(c * tiles + t, lt, 2)] += totals[lt]

        def pair(i, _):
            tile_sums(i, 4)
            return 0

        lax.fori_loop(0, nc // 2, pair, 0)

        @pl.when(nc % 2 == 1)
        def _():
            tile_sums(nc - 1, 2)

        return 0

    lax.fori_loop(0, nb, quick_visit, 0)
    total = jnp.sum(sum_ref[...], axis=0, keepdims=True)
    log_ref[...] = jnp.where(total > 0.0, jnp.log(jnp.maximum(total, TINY)) - SHIFT, MASKED)
    ids = lax.broadcasted_iota(jnp.int32, total.shape, 1)
    lowest = jnp.min(jnp.where(ids < count_next, total, 1.0))

    @pl.when((lowest < LOWEST) & (nb > 0))
    def _():
        exact()


def column_sums(c, z_ref, _):
    rows, cols = z_ref.shape
    sums = []
    for lt in range(cols // LANES):
        p = jnp.exp(z_ref[:, lt * LANES : (lt + 1) * LANES])
        sums.append(jnp.sum(p.reshape(rows // 8, 8, LANES), axis=0))
    return [sums]


def row_adder(sum_ref, push_ref=None, g_ref=None):
    def first(c, scores_of, kept):
        half = ROWS // 2
        for start in range(0, ROWS, half):
            scored = scores_of(c, start, half)
            for rg in range(0, half, SUB):
                rows = slice(start + rg, start + rg + SUB)
                total = sum_ref[rows, :]
                push = push_ref[rows, :] if push_ref is not None else None
                for lt in range(LTS):
                    z = piece_of(scored, rg, lt)
                    p = jnp.exp(z)
                    total = total + p
                    kept[0][rows, lane_tile(c, lt)] = p.astype(kept[0].dtype)
                    if push is not None:
                        part = p * (g_ref[:, lane_tile(c, lt)] - z)
                        push = push + part
                        kept[1][rows, lane_tile(c, lt)] = part.astype(kept[1].dtype)
                sum_ref[rows, :] = total
                if push is not None:
                    push_ref[rows, :] = push

    return first


def column_parts(c, plan):
    sums = [[jnp.zeros((8, LANES), F32) for _ in range(LTS)] for _ in plan]
    for rg in range(0, ROWS, 8):
        for k, (kept_ref, weight_ref) in enumerate(plan):
            scale = weight_ref[rg : rg + 8, :]
            for lt in range(LTS):
                sums[k][lt] = sums[k][lt] + scale * kept_ref[rg : rg + 8, lane_tile(c, lt)]
    return sums


def two_stage(nb, nc, first, finish, second, store, matmul_of, buffers, kept):
    def stage(b, now, before):
        matmul = matmul_of(b)

        def work(c, z, _):
            first(c, z, now)
            return second(c, before) if before else None

        if buffers is None:
            in_pairs(lambda c: work(c, matmul, None), store if before else None)
        else:
            piped(nc, matmul, work, *buffers, store=store if before else None)
        finish(b)

    def in_pairs(visit, put):
        put = put or (lambda c, sums: None)

        def pair(i, _):
            one, two = visit(2 * i), visit(2 * i + 1)
            put(2 * i, one)
            put(2 * i + 1, two)
            return 0

        lax.fori_loop(0, nc // 2, pair, 0)

        @pl.when(nc % 2 == 1)
        def _():
            put(nc - 1, visit(nc - 1))

    def tail(before):
        in_pairs(lambda c: second(c, before), store)

    even, odd = kept

    @pl.when(nb > 0)
    def _():
        stage(0, even, None)

    def visit(b, _):
        @pl.when(b % 2 == 1)
        def _():
            stage(b, odd, even)

        @pl.when(b % 2 == 0)
        def _():
            stage(b, even, odd)

        return 0

    lax.fori_loop(1, nb, visit, 0)

    @pl.when((nb > 0) & (nb % 2 == 1))
    def _():
        tail(even)

    @pl.when((nb > 0) & (nb % 2 == 0))
    def _():
        tail(odd)


def col_tile(c):
    return pl.ds(aligned(c, COLS), COLS)


def split2(value):
    high = value.astype(BF16).astype(F32)
    return high, value - high


def turned_weights(columns):
    lane = lax.broadcasted_iota(jnp.int32, (ROWS, LANES), 1)
    packed = jnp.zeros((ROWS, LANES), F32)
    for at, column in columns:
        packed = jnp.where(lane == at, column, packed)
    return jnp.transpose(packed)


def sweep(quick, exact, low_ref, lost=None):
    low_ref[...] = jnp.ones_like(low_ref)
    quick()
    again = jnp.min(low_ref[...]) < LOWEST
    if lost is not None:
        again = again | lost()

    @pl.when(again)
    def _():
        exact()


def row_lse(xa, ya_ref, nc, buffers, top_ref, sum_ref, push_ref=None, g_ref=None):
    top_ref[...] = jnp.full(top_ref.shape, MASKED, F32)
    sum_ref[...] = jnp.zeros_like(sum_ref)
    if push_ref is not None:
        push_ref[...] = jnp.zeros_like(push_ref)

    def work(c, z_ref, _):
        for rg in range(0, ROWS, SUB):
            rows = slice(rg, rg + SUB)
            old = top_ref[rows, :]
            pieces = [piece_of(z_ref, rg, lt) for lt in range(LTS)]
            top = old
            for z in pieces:
                top = jnp.maximum(top, z)
            fade = jnp.exp(old - top)
            total = sum_ref[rows, :] * fade
            push = push_ref[rows, :] * fade if push_ref is not None else None
            for lt, z in enumerate(pieces):
                p = jnp.exp(z - top)
                total = total + p
                if push is not None:
                    push = push + p * (g_ref[:, lane_tile(c, lt)] - z)
            top_ref[rows, :] = top
            sum_ref[rows, :] = total
            if push is not None:
                push_ref[rows, :] = push

    piped(nc, lambda c: scores(xa, ya_ref, c), work, *buffers)
    tops = top_ref[...]
    top = jnp.max(tops, axis=1, keepdims=True)
    fade = jnp.exp(tops - top)
    total = jnp.sum(sum_ref[...] * fade, axis=1, keepdims=True)
    if push_ref is None:
        return top, total
    return top, total, jnp.sum(push_ref[...] * fade, axis=1, keepdims=True)


def row_potential(xa):
    lane = lax.broadcasted_iota(jnp.int32, (ROWS, LANES), 1)
    wide = xa.astype(F32)
    old = jnp.sum(jnp.where((lane >= 32) & (lane < 35), wide, 0.0), axis=1, keepdims=True)
    return lane, wide, old


def with_row_potential(lane, wide, pot):
    high, middle, low = split3(pot)
    new = jnp.where(lane == 32, high, jnp.where(lane == 33, middle, jnp.where(lane == 34, low, wide)))
    return new.astype(BF16)


def kernel_b(counts, xa_ref, yg_ref, gb_ref, l0, l1, l2, l3, g_ref, col_ref, ya_ref, za_ref, zb_ref, p_ref, q_ref, top_ref, sum_ref, weight_ref, low_ref, most_ref, acc_ref):
    _, count_here, count_next, member = around(counts)
    nb = row_steps(count_here, count_next, member, 4)
    nc = col_steps(count_next)

    def prepare(start, cols):
        logs = [ref[:, cols] for ref in (l0, l1, l2, l3)]
        top = jnp.maximum(jnp.maximum(logs[0], logs[1]), jnp.maximum(logs[2], logs[3]))
        total = sum(jnp.exp(one - top) for one in logs)
        ids = start + lax.broadcasted_iota(jnp.int32, (1, WIDE), 1)
        pot = jnp.where(ids < count_next, -DAMPING * (top + jnp.log(total)), 0.0)
        g_ref[:, cols] = pot
        write_augmented(ya_ref, start, yg_ref[:, cols], pot + gb_ref[:, cols], False)

    in_steps(yg_ref.shape[1], prepare)

    buffers = za_ref, zb_ref

    def quick():
        acc_ref[...] = jnp.zeros_like(acc_ref)

        def matmul_of(b):
            sum_ref[...] = jnp.zeros_like(sum_ref)
            return lambda c, start, size: scores(
                xa_ref[pl.ds(pl.multiple_of(b * ROWS + start, size), size), :], ya_ref, c
            )

        def finish(b):
            lane, wide, old = row_potential(xa_ref[pl.ds(aligned(b, ROWS), ROWS), :])
            live = old > 0.5 * MASKED
            total = jnp.sum(sum_ref[...], axis=1, keepdims=True)
            low_ref[...] = jnp.minimum(low_ref[...], jnp.where(live, total, 1.0))
            pot = -DAMPING * (jnp.log(jnp.maximum(total, TINY)) - SHIFT)
            weight = jnp.where(live, jnp.exp(pot - SHIFT), 0.0)
            weight_ref[...] = jnp.broadcast_to(weight, weight_ref.shape)
            most_ref[...] = jnp.maximum(most_ref[...], weight)

        two_stage(
            nb, nc, row_adder(sum_ref), finish, lambda c, kept: column_parts(c, [(kept[0], weight_ref)]),
            adder([acc_ref]), matmul_of, None, ((p_ref,), (q_ref,)),
        )

    def exact():
        acc_ref[...] = jnp.zeros_like(acc_ref)

        def row_visit(b, _):
            xa = xa_ref[pl.ds(aligned(b, ROWS), ROWS), :]
            lane, wide, old = row_potential(xa)
            live = old > 0.5 * MASKED
            top, total = row_lse(xa, ya_ref, nc, buffers, top_ref, sum_ref)
            pot = -DAMPING * (top + jnp.log(total) - SHIFT)
            xb = with_row_potential(lane, wide, jnp.where(live, pot + old - SHIFT, MASKED))
            piped(nc, lambda c: scores(xb, ya_ref, c), column_sums, *buffers, store=adder([acc_ref]))
            return 0

        lax.fori_loop(0, nb, row_visit, 0)

    def lost():
        total = jnp.sum(acc_ref[...], axis=0, keepdims=True)
        ids = lax.broadcasted_iota(jnp.int32, total.shape, 1)
        least = jnp.min(jnp.where((ids < count_next) & (nb > 0), total, 1.0))
        return least < jnp.max(most_ref[...]) * 2.0**-91

    most_ref[...] = jnp.zeros_like(most_ref)
    sweep(quick, exact, low_ref, lost)
    col_ref[...] = jnp.sum(acc_ref[...], axis=0, keepdims=True)


def kernel_c(
    counts, xa_ref, yg_ref, gb_ref, g_ref, c0, c1, c2, c3,
    xb_ref, aux_ref, g2_ref, col_ref,
    ya_ref, za_ref, zb_ref, p_ref, w_ref, q_ref, v_ref, top_ref, sum_ref, push_ref, adj_ref, low_ref, cost_ref, weight_ref, acc_ref, acc0_ref, acc1_ref, acc2_ref,
):
    _, count_here, count_next, member = around(counts)
    nb = row_steps(count_here, count_next, member, 4)
    nc = col_steps(count_next)

    def prepare(start, cols):
        total = (c0[:, cols] + c1[:, cols]) + (c2[:, cols] + c3[:, cols])
        ids = start + lax.broadcasted_iota(jnp.int32, (1, WIDE), 1)
        log = jnp.log(jnp.maximum(total, TINY)) - g_ref[:, cols]
        pot = jnp.where(ids < count_next, -DAMPING * log, 0.0)
        g2_ref[:, cols] = pot
        write_augmented(ya_ref, start, yg_ref[:, cols], pot + gb_ref[:, cols], False)

    in_steps(yg_ref.shape[1], prepare)

    buffers = za_ref, zb_ref
    accs = acc0_ref, acc1_ref, acc2_ref

    ids = lax.broadcasted_iota(jnp.int32, g_ref.shape, 1)
    centre = jnp.sum(jnp.where(ids < count_next, g_ref[...], 0.0), axis=1, keepdims=True)
    centre = centre / (DAMPING * jnp.maximum(count_next, 1).astype(F32)) + 3.0
    cost_ref[...] = g2_ref[...] + (SHIFT - centre)

    def close_rows(b, top, total, push):
        rows_here = pl.ds(aligned(b, ROWS), ROWS)
        lane, wide, old = row_potential(xa_ref[rows_here, :])
        live = old > 0.5 * MASKED
        total = jnp.maximum(total, TINY)
        row_log = top + jnp.log(total) - SHIFT
        pot = jnp.where(live, -DAMPING * row_log, 0.0)
        row_sum = jnp.where(live, jnp.exp(row_log + pot), 0.0)
        adjoint = jnp.where(live, push / total + centre, 0.0)
        inverse = jnp.where(row_sum > 0.0, 1.0 / jnp.maximum(row_sum, TINY), 0.0)
        full = jnp.where(live, pot + old - SHIFT, MASKED)
        xb = with_row_potential(lane, wide, full)
        xb_ref[rows_here, :] = xb
        aux = jnp.where(lane == 0, adjoint, jnp.where(lane == 1, inverse, jnp.where(lane == 2, pot, full)))
        aux_ref[rows_here, :] = aux
        return live, pot, adjoint, xb

    def quick():
        acc_ref[...] = jnp.zeros_like(acc_ref)

        def matmul_of(b):
            sum_ref[...] = jnp.zeros_like(sum_ref)
            push_ref[...] = jnp.zeros_like(push_ref)
            return lambda c, start, size: scores(
                xa_ref[pl.ds(pl.multiple_of(b * ROWS + start, size), size), :], ya_ref, c
            )

        def finish(b):
            total = jnp.sum(sum_ref[...], axis=1, keepdims=True)
            push = jnp.sum(push_ref[...], axis=1, keepdims=True)
            live, pot, adjoint, _ = close_rows(b, 0.0, total, push)
            low_ref[...] = jnp.minimum(low_ref[...], jnp.where(live, total, 1.0))
            weight = jnp.where(live, jnp.exp(pot - SHIFT), 0.0)
            pieces = (*split2(weight), *split2(weight * adjoint))
            weight_ref[...] = turned_weights(list(enumerate(pieces)))[0:16, :].astype(BF16)

        def second(c, kept):
            weights = weight_ref[...]
            plan = jnp.dot(weights, kept[0][:, col_tile(c)], preferred_element_type=F32)
            cost = jnp.dot(weights, kept[1][:, col_tile(c)], preferred_element_type=F32)
            return plan, cost

        def store(c, sums):
            acc_ref[0:16, col_tile(c)] += sums[0]
            acc_ref[16:32, col_tile(c)] += sums[1]

        two_stage(
            nb, nc, row_adder(sum_ref, push_ref, cost_ref), finish, second, store, matmul_of, None,
            ((p_ref, w_ref), (q_ref, v_ref)),
        )
        acc0_ref[0:1, :] = acc_ref[0:1, :] + acc_ref[1:2, :]
        acc1_ref[0:1, :] = acc_ref[16:17, :] + acc_ref[17:18, :]
        acc2_ref[0:1, :] = acc_ref[2:3, :] + acc_ref[3:4, :]
        for ref in accs:
            ref[1:8, :] = jnp.zeros((7, ref.shape[1]), F32)

    def exact():
        for ref in accs:
            ref[...] = jnp.zeros_like(ref)

        def row_visit(b, _):
            xa = xa_ref[pl.ds(aligned(b, ROWS), ROWS), :]
            top, total, push = row_lse(xa, ya_ref, nc, buffers, top_ref, sum_ref, push_ref, cost_ref)
            _, pot, adjoint, xb = close_rows(b, top, total, push)
            top_ref[...] = jnp.broadcast_to(pot - SHIFT, top_ref.shape)
            adj_ref[...] = jnp.broadcast_to(adjoint, adj_ref.shape)

            def work(c, z_ref, _):
                sums = [[jnp.zeros((8, LANES), F32) for _ in range(LTS)] for _ in range(3)]
                for rg in range(0, ROWS, 8):
                    pot_here = top_ref[rg : rg + 8, :]
                    adj_here = adj_ref[rg : rg + 8, :]
                    for lt in range(LTS):
                        tile = piece_of(z_ref, rg, lt, 8)
                        p = jnp.exp(tile)
                        sums[0][lt] = sums[0][lt] + p
                        sums[1][lt] = sums[1][lt] + p * (cost_ref[:, lane_tile(c, lt)] + (pot_here - tile))
                        sums[2][lt] = sums[2][lt] + p * adj_here
                return sums

            piped(nc, lambda c: scores(xb, ya_ref, c), work, *buffers, store=adder(accs))
            return 0

        lax.fori_loop(0, nb, row_visit, 0)

    sweep(quick, exact, low_ref)
    mass = jnp.sum(acc0_ref[...], axis=0, keepdims=True)
    slots = mass.shape[1]
    col_ref[:, 0:slots] = mass
    push = jnp.sum(acc1_ref[...], axis=0, keepdims=True)
    col_ref[:, slots : 2 * slots] = push + centre * mass
    col_ref[:, 2 * slots :] = jnp.sum(acc2_ref[...], axis=0, keepdims=True)


def kernel_d(
    counts, xb_ref, aux_ref, yg_ref, gb_ref, g2_ref, s0, s1, s2, s3,
    stat_ref, send_ref,
    ya_ref, p_ref, q_ref, first_ref, second_ref, weight_ref, acc_ref,
):
    _, count_here, count_next, member = around(counts)
    nb = row_steps(count_here, count_next, member, 4)
    nc = col_steps(count_next)
    slots = yg_ref.shape[1]
    local = xb_ref.shape[0]
    acc_ref[...] = jnp.zeros_like(acc_ref)

    def prepare(start, cols):
        mass, push, pulled = (
            (s0[:, part] + s1[:, part]) + (s2[:, part] + s3[:, part])
            for part in (pl.ds(start + k * slots, WIDE) for k in range(3))
        )
        inverse = jnp.where(mass > 0.0, 1.0 / jnp.maximum(mass, TINY), 0.0)
        pot = g2_ref[:, cols]
        stat_ref[0:1, cols] = pot + gb_ref[:, cols]
        stat_ref[1:2, cols] = push * inverse
        stat_ref[2:3, cols] = (push - DAMPING * pulled) * inverse
        stat_ref[3:4, cols] = inverse
        stat_ref[4:5, cols] = pot
        stat_ref[5:8, cols] = jnp.zeros((3, WIDE), F32)
        write_augmented(ya_ref, start, yg_ref[:, cols], pot + gb_ref[:, cols], False)

    in_steps(slots, prepare)
    send_ref[:, slots : slots + local] = jnp.full((1, local), MASKED, F32)
    send_ref[:, slots + local :] = jnp.zeros((1, local), F32)

    def matmul_of(b):
        first_ref[...] = jnp.zeros_like(first_ref)
        second_ref[...] = jnp.zeros_like(second_ref)
        return lambda c, start, size: scores(
            xb_ref[pl.ds(pl.multiple_of(b * ROWS + start, size), size), :], ya_ref, c
        )

    def sums(c, scores_of, kept):
        half = ROWS // 2
        for start in range(0, ROWS, half):
            scored = scores_of(c, start, half)
            for rg in range(0, half, SUB):
                rows = slice(start + rg, start + rg + SUB)
                first = first_ref[rows, :]
                second = second_ref[rows, :]
                for lt in range(LTS):
                    p = jnp.exp(piece_of(scored, rg, lt))
                    kept[0][rows, lane_tile(c, lt)] = p
                    first = first + p * stat_ref[1:2, lane_tile(c, lt)]
                    second = second + p * stat_ref[2:3, lane_tile(c, lt)]
                first_ref[rows, :] = first
                second_ref[rows, :] = second

    def finish(b):
        first = jnp.sum(first_ref[...], axis=1, keepdims=True)
        second = jnp.sum(second_ref[...], axis=1, keepdims=True)
        aux = aux_ref[pl.ds(aligned(b, ROWS), ROWS), :]
        start_adj, inverse, pot, full = aux[:, 0:1], aux[:, 1:2], aux[:, 2:3], aux[:, 3:4]
        middle_adj = start_adj - DAMPING * first * inverse
        last_adj = start_adj - DAMPING * second * inverse
        weight_ref[...] = jnp.broadcast_to(middle_adj, weight_ref.shape)
        alpha = 1.0 + DAMPING * last_adj - pot
        lane = lax.broadcasted_iota(jnp.int32, (ROWS, LANES), 1)
        packed = jnp.transpose(jnp.where(lane == 0, full, alpha))
        send_ref[:, pl.ds(aligned(b + slots // ROWS, ROWS), ROWS)] = packed[0:1, :]
        send_ref[:, pl.ds(aligned(b + (slots + local) // ROWS, ROWS), ROWS)] = packed[1:2, :]

    two_stage(
        nb, nc, sums, finish, lambda c, kept: column_parts(c, [(kept[0], weight_ref)]), adder([acc_ref]), matmul_of,
        None, ((p_ref,), (q_ref,)),
    )
    send_ref[:, 0:slots] = jnp.sum(acc_ref[...], axis=0, keepdims=True)


def kernel_f(counts, p0, p1, p2, p3, stat_ref, col_ref, mine_ref, early_ref, parts_ref):
    member = lax.axis_index("cell")
    slots, local = stat_ref.shape[1], mine_ref.shape[1]
    for k, ref in enumerate((p0, p1, p2, p3)):
        parts_ref[member ^ k] = ref[...]
    total = (p0[:, 0:slots] + p1[:, 0:slots]) + (p2[:, 0:slots] + p3[:, 0:slots])
    last = stat_ref[1:2, :] - DAMPING * total * stat_ref[3:4, :]
    col_ref[0:1, :] = stat_ref[0:1, :]
    col_ref[1:2, :] = DAMPING * last - stat_ref[4:5, :]
    for block in range(slots // LANES):
        owner, place = block % 4, block // 4
        lanes = slice(block * LANES, (block + 1) * LANES)
        for k in range(2):
            at = slots + k * local + place * LANES
            early_ref[k : k + 1, lanes] = parts_ref[owner, :, at : at + LANES]
    here = pl.ds(aligned(member, local), local)
    mine_ref[...] = early_ref[:, here]
    early_ref[:, slots:] = col_ref[:, here]


def kernel_e(
    counts, *refs, earlier,
):
    own_ref, rowpot_ref, other_ref, colpot_ref = refs[:4]
    base_ref = refs[4] if earlier else None
    out_ref, xw_ref, tile_ref, ys_ref, beta_ref, pull_ref, sum_ref = refs[5 if earlier else 4 :]
    local, slots = own_ref.shape[1], other_ref.shape[1]
    before, here, after, member = around(counts)
    count_rows = jnp.clip(here - member * local, 0, local)
    count_cols = before if earlier else after
    if earlier:
        own_at = slots
    else:
        own_at = 0
    nc = col_steps(count_cols)
    nb = jnp.where(count_cols > 0, (count_rows + ROWS - 1) // ROWS, 0)
    out_ref[...] = base_ref[...] if earlier else jnp.zeros_like(out_ref)

    def prepare(c, _):
        cols = pl.ds(aligned(c, COLS), COLS)
        write_augmented(tile_ref, 0, other_ref[:, cols], colpot_ref[0:1, cols], False)
        ys_ref[cols, :] = jnp.transpose(tile_ref[...]).astype(BF16)
        beta_ref[cols, :] = jnp.transpose(jnp.broadcast_to(colpot_ref[1:2, cols], (LANES, COLS)))
        return 0

    @pl.when(nb > 0)
    def _():
        lax.fori_loop(0, nc, prepare, 0)

    def row_visit(b, _):
        rows_here = pl.ds(aligned(b, ROWS), ROWS)
        own = own_ref[:, rows_here]
        own_pots = pl.ds(aligned(b + own_at // ROWS, ROWS), ROWS)
        write_augmented(xw_ref, 0, own, rowpot_ref[0:1, own_pots], True)
        xw = xw_ref[...]
        alpha = rowpot_ref[1:2, own_pots]
        sum_ref[...] = jnp.zeros_like(sum_ref)
        pull_ref[...] = jnp.zeros_like(pull_ref)

        def step(c, part):
            rounded = []
            sums = [jnp.zeros((8, LANES), F32) for _ in range(ROWS // LANES)]
            for first in range(0, 2 * LANES, LANES):
                start = pl.multiple_of(c * COLS + part * 2 * LANES + first, LANES)
                z = jnp.dot(ys_ref[pl.ds(start, LANES), :], xw, preferred_element_type=F32)
                for jg in range(0, LANES, 16):
                    beta = beta_ref[pl.ds(pl.multiple_of(start + jg, 16), 16), :]
                    line = []
                    for lt in range(ROWS // LANES):
                        tile = piece_of(z, jg, lt, 16)
                        grad = jnp.exp(tile) * (tile + (alpha[:, lt * LANES : (lt + 1) * LANES] + beta))
                        sums[lt] = sums[lt] + (grad[0:8] + grad[8:16])
                        line.append(grad.astype(BF16))
                    rounded.append(jnp.concatenate(line, axis=1))
            feats = other_ref[:, pl.ds(pl.multiple_of(c * COLS + part * 2 * LANES, 2 * LANES), 2 * LANES)]
            return sums, jnp.dot(feats, jnp.concatenate(rounded, axis=0), preferred_element_type=F32)

        def visit(cs):
            parts = [step(c, part) for c in cs for part in range(COLS // (2 * LANES))]
            for lt in range(ROWS // LANES):
                sum_ref[:, lt * LANES : (lt + 1) * LANES] += sum(sums[lt] for sums, _ in parts)
            pull_ref[...] += sum(pulled for _, pulled in parts)

        def pair(i, _):
            visit((2 * i, 2 * i + 1))
            return 0

        lax.fori_loop(0, nc // 2, pair, 0)

        @pl.when(nc % 2 == 1)
        def _():
            visit((nc - 1,))

        total = jnp.sum(sum_ref[...], axis=0, keepdims=True)
        out_ref[:, rows_here] += 2.0 * (own.astype(F32) * total - pull_ref[...])
        return 0

    lax.fori_loop(0, nb, row_visit, 0)


def run(body, name, outs, scratch, limit, counts, *operands, flops=0):
    vmem = pl.BlockSpec(memory_space=pltpu.VMEM)
    return pl.pallas_call(
        body,
        name=name,
        out_shape=outs,
        in_specs=[pl.BlockSpec(memory_space=pltpu.SMEM)] + [vmem] * len(operands),
        out_specs=jax.tree.map(lambda _: vmem, outs),
        scratch_shapes=scratch,
        compiler_params=pltpu.CompilerParams(vmem_limit_bytes=limit * 1024 * 1024),
        cost_estimate=pl.CostEstimate(flops=flops, bytes_accessed=4_000_000, transcendentals=9_000_000),
    )(counts, *operands)


def shape(*dims, dtype=F32):
    return jax.ShapeDtypeStruct(dims, dtype)


def shifted(block, distance):
    size = lax.axis_size("tm")
    route = [(i - distance, i) for i in range(size) if 0 <= i - distance < size]
    return lax.ppermute(block, "tm", route)


def from_later(block, k):
    times, size = lax.axis_size("tm"), lax.axis_size("cell")
    route = [((t + 1) * size + (i ^ k), t * size + i) for t in range(times - 1) for i in range(size)]
    return lax.ppermute(block, ("tm", "cell"), route)


def swapped(block, k):
    return lax.ppermute(block, "cell", [(i, i ^ k) for i in range(lax.axis_size("cell"))])


def exchanged(block):
    near = swapped(block, 1)
    far = swapped(block, 2)
    return [block, near, far, swapped(far, 1)]


def per_device(embedding, counts):
    feat_dim, local = embedding.shape
    group = lax.axis_size("cell")
    slots = local * group

    ahead, ahead_far = from_later(embedding, 0), from_later(embedding, 2)
    source_parts = exchanged(embedding)
    target_parts = [ahead, swapped(ahead, 1), ahead_far, swapped(ahead_far, 1)]

    flops = 2 * local * slots * DEPTH
    aug = pltpu.VMEM((DEPTH, slots), BF16)
    narrow = pltpu.VMEM((ROWS, LANES), F32)
    wide = pltpu.VMEM((ROWS, slots), F32)
    half = pltpu.VMEM((ROWS, slots), BF16)
    turned_rows = pltpu.VMEM((16, ROWS), BF16)
    buffers = [pltpu.VMEM((ROWS, COLS), F32)] * 2
    long = pltpu.VMEM((8, slots), F32)
    grouped, targets, xa, gb, log = run(
        kernel_a, "column_log",
        (
            shape(feat_dim, slots, dtype=BF16), shape(feat_dim, slots, dtype=BF16),
            shape(local, DEPTH, dtype=BF16), shape(1, slots), shape(1, slots),
        ),
        [aug, pltpu.VMEM((DEPTH, local), F32), *buffers, long, long],
        16, counts, *source_parts, *target_parts, flops=flops,
    )
    logs = exchanged(log)
    g1, col1 = run(
        kernel_b, "first_sweep",
        (shape(1, slots), shape(1, slots)),
        [aug, *buffers, wide, wide, narrow, narrow, narrow, narrow, narrow, long],
        24, counts, xa, targets, gb, *logs, flops=2 * flops,
    )
    grouped, col1 = lax.optimization_barrier((grouped, col1))
    earlier = shifted(grouped, 1)
    xb, aux, g2, stats = run(
        kernel_c, "second_sweep",
        (shape(local, DEPTH, dtype=BF16), shape(local, LANES), shape(1, slots), shape(1, 3 * slots)),
        [
            aug, *buffers, half, half, half, half, narrow, narrow, narrow, narrow, narrow,
            pltpu.VMEM((1, slots), F32), turned_rows, pltpu.VMEM((32, slots), F32), long, long, long,
        ],
        28, counts, xa, targets, gb, g1, *exchanged(col1), flops=2 * flops,
    )
    xb, earlier = lax.optimization_barrier((xb, earlier))
    stat, send = run(
        kernel_d, "adjoint",
        (shape(8, slots), shape(1, slots + 2 * local)),
        [aug, wide, wide, narrow, narrow, narrow, long],
        24, counts, xb, aux, targets, gb, g2, *exchanged(stats), flops=2 * flops,
    )
    col_pair, rows_mine, early = run(
        kernel_f, "assemble",
        (shape(2, slots), shape(2, local), shape(2, slots + local)),
        [pltpu.VMEM((group, 1, slots + 2 * local), F32)],
        8, counts, *exchanged(send), stat,
    )
    early = shifted(early, 1)

    scratch_e = [
        pltpu.VMEM((DEPTH, ROWS), BF16), pltpu.VMEM((DEPTH, COLS), F32), pltpu.VMEM((slots, DEPTH), BF16),
        pltpu.VMEM((slots, LANES), F32), pltpu.VMEM((feat_dim, ROWS), F32), pltpu.VMEM((8, ROWS), F32),
    ]
    source_grad = run(
        functools.partial(kernel_e, earlier=False), "source_gradient", shape(feat_dim, local), scratch_e,
        16, counts, embedding, rows_mine, targets, col_pair, flops=2 * flops,
    )
    return run(
        functools.partial(kernel_e, earlier=True), "target_gradient", shape(feat_dim, local), scratch_e,
        16, counts, embedding, early, earlier, early, source_grad, flops=2 * flops,
    )


def solution(mesh):
    in_specs = (P(None, ("tm", "cell")), P())
    out_specs = P(None, ("tm", "cell"))
    return jax.shard_map(
        per_device, mesh=mesh, in_specs=in_specs, out_specs=out_specs, check_vma=False
    )
```

```python
import functools

import jax
import jax.numpy as jnp
from jax import lax
from jax.experimental import pallas as pl
from jax.experimental.pallas import tpu as pltpu
from jax.sharding import PartitionSpec as P

ENTROPY = 0.25
PENALTY = 5.0
DAMPING = PENALTY / (PENALTY + ENTROPY)
MASKED = -1e30
SQ_SCALE = 1.0 / ENTROPY
DOT_SCALE = 2.0 / ENTROPY
TINY = 1e-37
SHIFT = 44.0
LOWEST = 1e-24

ROWS = 256
COLS = 512
LANES = 128
DEPTH = 128
F32 = jnp.float32
BF16 = jnp.bfloat16


def split3(value):
    high = value.astype(BF16).astype(F32)
    rest = value - high
    middle = rest.astype(BF16).astype(F32)
    return high, middle, rest - middle


def write_augmented(out_ref, start, feats, pot, is_row):
    n = feats.shape[1]
    cols = pl.ds(start, n)
    scaled = feats.astype(F32) * DOT_SCALE if is_row else feats
    out_ref[0:32, cols] = scaled.astype(out_ref.dtype)
    first = 0 if is_row else 3
    ones_from = 3 if is_row else 0
    row = lax.broadcasted_iota(jnp.int32, (16, n), 0)
    tail = jnp.where((row >= ones_from) & (row < ones_from + 3), 1.0, 0.0)
    for k, piece in enumerate(split3(pot)):
        tail = jnp.where(row == first + k, piece, tail)
    out_ref[32:48, cols] = tail.astype(out_ref.dtype)
    out_ref[48:128, cols] = jnp.zeros((80, n), out_ref.dtype)


def square_sum(feats):
    wide = feats.astype(F32)
    return jnp.sum(wide * wide, axis=0, keepdims=True)


def live_pot(feats, start, count):
    ids = start + lax.broadcasted_iota(jnp.int32, (1, feats.shape[1]), 1)
    return jnp.where(ids < count, -SQ_SCALE * square_sum(feats), MASKED)


def aligned(index, size):
    return pl.multiple_of(index * size, size)


def around(counts):
    size = counts.shape[0]
    time, member = lax.axis_index("tm"), lax.axis_index("cell")
    before = jnp.where(time > 0, counts[jnp.maximum(time - 1, 0)], 0)
    after = jnp.where(time + 1 < size, counts[jnp.minimum(time + 1, size - 1)], 0)
    return before, counts[time], after, member


def row_blocks(count_here, count_next, member, group):
    blocks = pl.cdiv(count_here, LANES)
    mine = jnp.maximum((blocks - member + group - 1) // group, 0)
    return jnp.where(count_next > 0, mine, 0)


def live_rows(start, member, count, group=4):
    row = lax.broadcasted_iota(jnp.int32, (ROWS, 1), 0)
    slot = (group * (start // LANES) + member) * LANES + row
    return slot + jnp.where(row >= LANES, (group - 1) * LANES, 0) < count


def col_steps(count):
    return (count + COLS - 1) // COLS


LTS = COLS // LANES
SUB = 32
WIDE = 1536


def scores(xa, ya_ref, c, cols=COLS):
    return jnp.dot(xa, ya_ref[:, pl.ds(aligned(c, cols), cols)], preferred_element_type=F32)


def piped(count, matmul, work, first_ref, second_ref, load=None, store=None):
    load = load or (lambda c: None)
    store = store or (lambda c, state: None)
    first_ref[...] = matmul(0)

    def pair(i, _):
        here, there = 2 * i, 2 * i + 1
        states = load(here), load(there)
        second_ref[...] = matmul(there)
        one = work(here, first_ref, states[0])
        first_ref[...] = matmul(jnp.minimum(there + 1, count - 1))
        two = work(there, second_ref, states[1])
        store(here, one)
        store(there, two)
        return 0

    lax.fori_loop(0, count // 2, pair, 0)

    @pl.when(count % 2 == 1)
    def _():
        store(count - 1, work(count - 1, first_ref, load(count - 1)))


def adder(acc_refs):
    def store(c, sums):
        for k, acc_ref in enumerate(acc_refs):
            lts = len(sums[k])
            for lt in range(lts):
                acc_ref[:, lane_tile(c, lt, lts)] += sums[k][lt]

    return store


def lane_tile(c, lt, lts=LTS):
    return pl.ds(aligned(c * lts + lt, LANES), LANES)


def piece_of(z_ref, rg, lt, size=SUB):
    return z_ref[rg : rg + size, lt * LANES : (lt + 1) * LANES]


def in_steps(total, visit):
    for start in range(0, total, WIDE):
        visit(start, slice(start, start + WIDE))


def kernel_a(
    counts, x0, x1, x2, x3, y0, y1, y2, y3,
    xg_ref, yg_ref, xa_ref, gb_ref, log_ref,
    ya_ref, xat_ref, za_ref, zb_ref, top_ref, sum_ref,
):
    _, count_here, count_next, member = around(counts)
    group = 4
    mine = row_blocks(count_here, count_next, member, group)
    nb = (mine + 1) // 2
    nc = col_steps(count_next)
    local = x0.shape[1]
    for k, (x_ref, y_ref) in enumerate(((x0, y0), (x1, y1), (x2, y2), (x3, y3))):
        place = pl.ds(aligned(member ^ k, local), local)
        xg_ref[:, place] = x_ref[...]
        yg_ref[:, place] = y_ref[...]
    for k in range(local // LANES):
        block_id = group * k + member
        piece = xg_ref[:, pl.ds(aligned(block_id, LANES), LANES)]
        pot = live_pot(piece, block_id * LANES, count_here) + SHIFT
        write_augmented(xat_ref, k * LANES, piece, pot, True)
        xa_ref[k * LANES : (k + 1) * LANES, :] = jnp.transpose(
            xat_ref[:, k * LANES : (k + 1) * LANES]
        ).astype(BF16)
    sum_ref[...] = jnp.zeros_like(sum_ref)

    def prepare(start, cols):
        feats = yg_ref[:, cols]
        pot = live_pot(feats, start, count_next)
        gb_ref[:, cols] = pot
        write_augmented(ya_ref, start, feats, pot, False)

    in_steps(group * local, prepare)

    def exact():
        top_ref[...] = jnp.full(top_ref.shape, MASKED, F32)
        sum_ref[...] = jnp.zeros_like(sum_ref)

        def row_visit(b, _):
            xa = xa_ref[pl.ds(aligned(b, ROWS), ROWS), :]

            def load(c):
                return [(top_ref[:, lane_tile(c, lt)], sum_ref[:, lane_tile(c, lt)]) for lt in range(LTS)]

            def work(c, z_ref, state):
                after = []
                for lt, (old, total) in enumerate(state):
                    tile = z_ref[:, lt * LANES : (lt + 1) * LANES].reshape(ROWS // 8, 8, LANES)
                    top = jnp.maximum(old, jnp.max(tile, axis=0))
                    total = total * jnp.exp(old - top) + jnp.sum(jnp.exp(tile - top[None]), axis=0)
                    after.append((top, total))
                return after

            def store(c, state):
                for lt, (top, total) in enumerate(state):
                    top_ref[:, lane_tile(c, lt)] = top
                    sum_ref[:, lane_tile(c, lt)] = total

            piped(nc, lambda c: scores(xa, ya_ref, c), work, za_ref, zb_ref, load, store)
            return 0

        lax.fori_loop(0, nb, row_visit, 0)
        tops = top_ref[...]
        top = jnp.max(tops, axis=0, keepdims=True)
        total = jnp.sum(sum_ref[...] * jnp.exp(tops - top), axis=0, keepdims=True)
        log_ref[...] = top + jnp.log(jnp.maximum(total, TINY)) - SHIFT

    thin = 2 * LANES

    def quick_rows(first_block, blocks):
        halves = [xa_ref[pl.ds(aligned(first_block + k, LANES), LANES), :] for k in range(blocks)]

        def tile_sums(c, tiles):
            for t in range(tiles):
                totals = [jnp.zeros((8, LANES), F32) for _ in range(2)]
                for half in halves:
                    z = scores(half, ya_ref, c * tiles + t, thin)
                    for lt in range(2):
                        p = jnp.exp(z[:, lt * LANES : (lt + 1) * LANES])
                        totals[lt] = totals[lt] + jnp.sum(p.reshape(LANES // 8, 8, LANES), axis=0)
                for lt in range(2):
                    sum_ref[:, lane_tile(c * tiles + t, lt, 2)] += totals[lt]

        def pair(i, _):
            tile_sums(i, 4)
            return 0

        lax.fori_loop(0, nc // 2, pair, 0)

        @pl.when(nc % 2 == 1)
        def _():
            tile_sums(nc - 1, 2)

    def quick_visit(b, _):
        quick_rows(2 * b, 2)
        return 0

    lax.fori_loop(0, mine // 2, quick_visit, 0)

    @pl.when(mine % 2 == 1)
    def _():
        quick_rows(mine - 1, 1)

    total = jnp.sum(sum_ref[...], axis=0, keepdims=True)
    log_ref[...] = jnp.where(total > 0.0, jnp.log(jnp.maximum(total, TINY)) - SHIFT, MASKED)
    ids = lax.broadcasted_iota(jnp.int32, total.shape, 1)
    lowest = jnp.min(jnp.where(ids < count_next, total, 1.0))

    @pl.when((lowest < LOWEST) & (nb > 0))
    def _():
        exact()


def column_sums(c, z_ref, _):
    rows, cols = z_ref.shape
    sums = []
    for lt in range(cols // LANES):
        p = jnp.exp(z_ref[:, lt * LANES : (lt + 1) * LANES])
        sums.append(jnp.sum(p.reshape(rows // 8, 8, LANES), axis=0))
    return [sums]


def row_adder(sum_ref, push_ref=None, g_ref=None):
    def first(c, scores_of, kept, count):
        half = LANES
        for start in range(0, count, half):
            scored = scores_of(c, start, half)
            for rg in range(0, half, SUB):
                rows = slice(start + rg, start + rg + SUB)
                total = sum_ref[rows, :]
                push = push_ref[rows, :] if push_ref is not None else None
                for lt in range(LTS):
                    z = piece_of(scored, rg, lt)
                    p = jnp.exp(z)
                    total = total + p
                    kept[0][rows, lane_tile(c, lt)] = p.astype(kept[0].dtype)
                    if push is not None:
                        part = p * (g_ref[:, lane_tile(c, lt)] - z)
                        push = push + part
                        kept[1][rows, lane_tile(c, lt)] = part.astype(kept[1].dtype)
                sum_ref[rows, :] = total
                if push is not None:
                    push_ref[rows, :] = push

    return first


def column_parts(c, plan):
    sums = [[jnp.zeros((8, LANES), F32) for _ in range(LTS)] for _ in plan]
    for rg in range(0, ROWS, 8):
        for k, (kept_ref, weight_ref) in enumerate(plan):
            scale = weight_ref[rg : rg + 8, :]
            for lt in range(LTS):
                sums[k][lt] = sums[k][lt] + scale * kept_ref[rg : rg + 8, lane_tile(c, lt)]
    return sums


def two_stage(mine, nc, first, finish, second, store, matmul_of, kept):
    nb = (mine + 1) // 2
    alone = mine % 2 == 1

    def in_pairs(visit, put):
        put = put or (lambda c, sums: None)

        def pair(i, _):
            one, two = visit(2 * i), visit(2 * i + 1)
            put(2 * i, one)
            put(2 * i + 1, two)
            return 0

        lax.fori_loop(0, nc // 2, pair, 0)

        @pl.when(nc % 2 == 1)
        def _():
            put(nc - 1, visit(nc - 1))

    def stage(start, now, before, rows=ROWS):
        scores_of = matmul_of(start)

        def visit(c):
            first(c, scores_of, now, rows)
            if rows < ROWS:
                for ref in now:
                    ref[rows:, col_tile(c)] = jnp.zeros((ROWS - rows, COLS), ref.dtype)
            return second(c, before) if before else None

        in_pairs(visit, store if before else None)
        finish(start, rows)

    def tail(before):
        in_pairs(lambda c: second(c, before), store)

    even, odd = kept

    @pl.when((nb > 0) & alone)
    def _():
        stage(0, even, None, LANES)

    @pl.when((nb > 0) & jnp.logical_not(alone))
    def _():
        stage(0, even, None)

    def visit(b, _):
        start = pl.multiple_of(b * ROWS - jnp.where(alone, LANES, 0), LANES)

        @pl.when(b % 2 == 1)
        def _():
            stage(start, odd, even)

        @pl.when(b % 2 == 0)
        def _():
            stage(start, even, odd)

        return 0

    lax.fori_loop(1, nb, visit, 0)

    @pl.when((nb > 0) & (nb % 2 == 1))
    def _():
        tail(even)

    @pl.when((nb > 0) & (nb % 2 == 0))
    def _():
        tail(odd)


def col_tile(c):
    return pl.ds(aligned(c, COLS), COLS)


def split2(value):
    high = value.astype(BF16).astype(F32)
    return high, value - high


def turned_weights(columns):
    lane = lax.broadcasted_iota(jnp.int32, (ROWS, LANES), 1)
    packed = jnp.zeros((ROWS, LANES), F32)
    for at, column in columns:
        packed = jnp.where(lane == at, column, packed)
    return jnp.transpose(packed)


def sweep(quick, exact, low_ref, lost=None):
    low_ref[...] = jnp.ones_like(low_ref)
    quick()
    again = jnp.min(low_ref[...]) < LOWEST
    if lost is not None:
        again = again | lost()

    @pl.when(again)
    def _():
        exact()


def row_lse(xa, ya_ref, nc, buffers, top_ref, sum_ref, push_ref=None, g_ref=None):
    top_ref[...] = jnp.full(top_ref.shape, MASKED, F32)
    sum_ref[...] = jnp.zeros_like(sum_ref)
    if push_ref is not None:
        push_ref[...] = jnp.zeros_like(push_ref)

    def work(c, z_ref, _):
        for rg in range(0, ROWS, SUB):
            rows = slice(rg, rg + SUB)
            old = top_ref[rows, :]
            pieces = [piece_of(z_ref, rg, lt) for lt in range(LTS)]
            top = old
            for z in pieces:
                top = jnp.maximum(top, z)
            fade = jnp.exp(old - top)
            total = sum_ref[rows, :] * fade
            push = push_ref[rows, :] * fade if push_ref is not None else None
            for lt, z in enumerate(pieces):
                p = jnp.exp(z - top)
                total = total + p
                if push is not None:
                    push = push + p * (g_ref[:, lane_tile(c, lt)] - z)
            top_ref[rows, :] = top
            sum_ref[rows, :] = total
            if push is not None:
                push_ref[rows, :] = push

    piped(nc, lambda c: scores(xa, ya_ref, c), work, *buffers)
    tops = top_ref[...]
    top = jnp.max(tops, axis=1, keepdims=True)
    fade = jnp.exp(tops - top)
    total = jnp.sum(sum_ref[...] * fade, axis=1, keepdims=True)
    if push_ref is None:
        return top, total
    return top, total, jnp.sum(push_ref[...] * fade, axis=1, keepdims=True)


def row_potential(xa):
    lane = lax.broadcasted_iota(jnp.int32, (ROWS, LANES), 1)
    wide = xa.astype(F32)
    old = jnp.sum(jnp.where((lane >= 32) & (lane < 35), wide, 0.0), axis=1, keepdims=True)
    return lane, wide, old


def with_row_potential(lane, wide, pot):
    high, middle, low = split3(pot)
    new = jnp.where(lane == 32, high, jnp.where(lane == 33, middle, jnp.where(lane == 34, low, wide)))
    return new.astype(BF16)


def kernel_b(counts, xa_ref, yg_ref, gb_ref, l0, l1, l2, l3, g_ref, col_ref, ya_ref, za_ref, zb_ref, p_ref, q_ref, top_ref, sum_ref, weight_ref, low_ref, most_ref, acc_ref):
    _, count_here, count_next, member = around(counts)
    mine = row_blocks(count_here, count_next, member, 4)
    nb = (mine + 1) // 2
    nc = col_steps(count_next)

    def prepare(start, cols):
        logs = [ref[:, cols] for ref in (l0, l1, l2, l3)]
        top = jnp.maximum(jnp.maximum(logs[0], logs[1]), jnp.maximum(logs[2], logs[3]))
        total = sum(jnp.exp(one - top) for one in logs)
        ids = start + lax.broadcasted_iota(jnp.int32, (1, WIDE), 1)
        pot = jnp.where(ids < count_next, -DAMPING * (top + jnp.log(total)), 0.0)
        g_ref[:, cols] = pot
        write_augmented(ya_ref, start, yg_ref[:, cols], pot + gb_ref[:, cols], False)

    in_steps(yg_ref.shape[1], prepare)

    buffers = za_ref, zb_ref

    def quick():
        acc_ref[...] = jnp.zeros_like(acc_ref)

        def matmul_of(first_row):
            sum_ref[...] = jnp.zeros_like(sum_ref)
            return lambda c, start, size: scores(
                xa_ref[pl.ds(pl.multiple_of(first_row + start, size), size), :], ya_ref, c
            )

        def finish(start, rows):
            row = lax.broadcasted_iota(jnp.int32, (ROWS, 1), 0)
            live = live_rows(start, member, count_here) & (row < rows)
            total = jnp.sum(sum_ref[...], axis=1, keepdims=True)
            low_ref[...] = jnp.minimum(low_ref[...], jnp.where(live, total, 1.0))
            pot = -DAMPING * (jnp.log(jnp.maximum(total, TINY)) - SHIFT)
            weight = jnp.where(live, jnp.exp(pot - SHIFT), 0.0)
            weight_ref[...] = jnp.broadcast_to(weight, weight_ref.shape)
            most_ref[...] = jnp.maximum(most_ref[...], weight)

        two_stage(
            mine, nc, row_adder(sum_ref), finish, lambda c, kept: column_parts(c, [(kept[0], weight_ref)]),
            adder([acc_ref]), matmul_of, ((p_ref,), (q_ref,)),
        )

    def exact():
        acc_ref[...] = jnp.zeros_like(acc_ref)

        def row_visit(b, _):
            xa = xa_ref[pl.ds(aligned(b, ROWS), ROWS), :]
            lane, wide, old = row_potential(xa)
            live = old > 0.5 * MASKED
            top, total = row_lse(xa, ya_ref, nc, buffers, top_ref, sum_ref)
            pot = -DAMPING * (top + jnp.log(total) - SHIFT)
            xb = with_row_potential(lane, wide, jnp.where(live, pot + old - SHIFT, MASKED))
            piped(nc, lambda c: scores(xb, ya_ref, c), column_sums, *buffers, store=adder([acc_ref]))
            return 0

        lax.fori_loop(0, nb, row_visit, 0)

    def lost():
        total = jnp.sum(acc_ref[...], axis=0, keepdims=True)
        ids = lax.broadcasted_iota(jnp.int32, total.shape, 1)
        least = jnp.min(jnp.where((ids < count_next) & (nb > 0), total, 1.0))
        return least < jnp.max(most_ref[...]) * 2.0**-91

    most_ref[...] = jnp.zeros_like(most_ref)
    sweep(quick, exact, low_ref, lost)
    col_ref[...] = jnp.sum(acc_ref[...], axis=0, keepdims=True)


def kernel_c(
    counts, xa_ref, yg_ref, gb_ref, g_ref, c0, c1, c2, c3,
    xb_ref, aux_ref, g2_ref, col_ref,
    ya_ref, za_ref, zb_ref, p_ref, w_ref, q_ref, v_ref, top_ref, sum_ref, push_ref, adj_ref, low_ref, cost_ref, weight_ref, acc_ref, acc0_ref, acc1_ref, acc2_ref,
):
    _, count_here, count_next, member = around(counts)
    mine = row_blocks(count_here, count_next, member, 4)
    nb = (mine + 1) // 2
    nc = col_steps(count_next)

    def prepare(start, cols):
        total = (c0[:, cols] + c1[:, cols]) + (c2[:, cols] + c3[:, cols])
        ids = start + lax.broadcasted_iota(jnp.int32, (1, WIDE), 1)
        log = jnp.log(jnp.maximum(total, TINY)) - g_ref[:, cols]
        pot = jnp.where(ids < count_next, -DAMPING * log, 0.0)
        g2_ref[:, cols] = pot
        write_augmented(ya_ref, start, yg_ref[:, cols], pot + gb_ref[:, cols], False)

    in_steps(yg_ref.shape[1], prepare)

    buffers = za_ref, zb_ref
    accs = acc0_ref, acc1_ref, acc2_ref

    ids = lax.broadcasted_iota(jnp.int32, g_ref.shape, 1)
    centre = jnp.sum(jnp.where(ids < count_next, g_ref[...], 0.0), axis=1, keepdims=True)
    centre = centre / (DAMPING * jnp.maximum(count_next, 1).astype(F32)) + 3.0
    cost_ref[...] = g2_ref[...] + (SHIFT - centre)

    def close_rows(start, rows, top, total, push):
        rows_here = pl.ds(pl.multiple_of(start, LANES), ROWS)
        lane, wide, old = row_potential(xa_ref[rows_here, :])
        live = old > 0.5 * MASKED
        if rows < ROWS:
            live = live & (lax.broadcasted_iota(jnp.int32, (ROWS, 1), 0) < rows)
        total = jnp.maximum(total, TINY)
        row_log = top + jnp.log(total) - SHIFT
        pot = jnp.where(live, -DAMPING * row_log, 0.0)
        row_sum = jnp.where(live, jnp.exp(row_log + pot), 0.0)
        adjoint = jnp.where(live, push / total + centre, 0.0)
        inverse = jnp.where(row_sum > 0.0, 1.0 / jnp.maximum(row_sum, TINY), 0.0)
        full = jnp.where(live, pot + old - SHIFT, MASKED)
        xb = with_row_potential(lane, wide, full)
        xb_ref[rows_here, :] = xb
        aux = jnp.where(lane == 0, adjoint, jnp.where(lane == 1, inverse, jnp.where(lane == 2, pot, full)))
        aux_ref[rows_here, :] = aux
        return live, pot, adjoint, xb

    def quick():
        acc_ref[...] = jnp.zeros_like(acc_ref)

        def matmul_of(first_row):
            sum_ref[...] = jnp.zeros_like(sum_ref)
            push_ref[...] = jnp.zeros_like(push_ref)
            return lambda c, start, size: scores(
                xa_ref[pl.ds(pl.multiple_of(first_row + start, size), size), :], ya_ref, c
            )

        def finish(start, rows):
            total = jnp.sum(sum_ref[...], axis=1, keepdims=True)
            push = jnp.sum(push_ref[...], axis=1, keepdims=True)
            live, pot, adjoint, _ = close_rows(start, rows, 0.0, total, push)
            low_ref[...] = jnp.minimum(low_ref[...], jnp.where(live, total, 1.0))
            weight = jnp.where(live, jnp.exp(pot - SHIFT), 0.0)
            pieces = (*split2(weight), *split2(weight * adjoint))
            weight_ref[...] = turned_weights(list(enumerate(pieces)))[0:16, :].astype(BF16)

        def second(c, kept):
            weights = weight_ref[...]
            plan = jnp.dot(weights, kept[0][:, col_tile(c)], preferred_element_type=F32)
            cost = jnp.dot(weights, kept[1][:, col_tile(c)], preferred_element_type=F32)
            return plan, cost

        def store(c, sums):
            acc_ref[0:16, col_tile(c)] += sums[0]
            acc_ref[16:32, col_tile(c)] += sums[1]

        two_stage(
            mine, nc, row_adder(sum_ref, push_ref, cost_ref), finish, second, store, matmul_of,
            ((p_ref, w_ref), (q_ref, v_ref)),
        )
        acc0_ref[0:1, :] = acc_ref[0:1, :] + acc_ref[1:2, :]
        acc1_ref[0:1, :] = acc_ref[16:17, :] + acc_ref[17:18, :]
        acc2_ref[0:1, :] = acc_ref[2:3, :] + acc_ref[3:4, :]
        for ref in accs:
            ref[1:8, :] = jnp.zeros((7, ref.shape[1]), F32)

    def exact():
        for ref in accs:
            ref[...] = jnp.zeros_like(ref)

        def row_visit(b, _):
            xa = xa_ref[pl.ds(aligned(b, ROWS), ROWS), :]
            top, total, push = row_lse(xa, ya_ref, nc, buffers, top_ref, sum_ref, push_ref, cost_ref)
            _, pot, adjoint, xb = close_rows(b * ROWS, ROWS, top, total, push)
            top_ref[...] = jnp.broadcast_to(pot - SHIFT, top_ref.shape)
            adj_ref[...] = jnp.broadcast_to(adjoint, adj_ref.shape)

            def work(c, z_ref, _):
                sums = [[jnp.zeros((8, LANES), F32) for _ in range(LTS)] for _ in range(3)]
                for rg in range(0, ROWS, 8):
                    pot_here = top_ref[rg : rg + 8, :]
                    adj_here = adj_ref[rg : rg + 8, :]
                    for lt in range(LTS):
                        tile = piece_of(z_ref, rg, lt, 8)
                        p = jnp.exp(tile)
                        sums[0][lt] = sums[0][lt] + p
                        sums[1][lt] = sums[1][lt] + p * (cost_ref[:, lane_tile(c, lt)] + (pot_here - tile))
                        sums[2][lt] = sums[2][lt] + p * adj_here
                return sums

            piped(nc, lambda c: scores(xb, ya_ref, c), work, *buffers, store=adder(accs))
            return 0

        lax.fori_loop(0, nb, row_visit, 0)

    sweep(quick, exact, low_ref)
    mass = jnp.sum(acc0_ref[...], axis=0, keepdims=True)
    slots = mass.shape[1]
    col_ref[:, 0:slots] = mass
    push = jnp.sum(acc1_ref[...], axis=0, keepdims=True)
    col_ref[:, slots : 2 * slots] = push + centre * mass
    col_ref[:, 2 * slots :] = jnp.sum(acc2_ref[...], axis=0, keepdims=True)


def kernel_d(
    counts, xb_ref, aux_ref, yg_ref, gb_ref, g2_ref, s0, s1, s2, s3,
    stat_ref, send_ref,
    ya_ref, p_ref, q_ref, first_ref, second_ref, weight_ref, acc_ref,
):
    _, count_here, count_next, member = around(counts)
    mine = row_blocks(count_here, count_next, member, 4)
    nb = (mine + 1) // 2
    nc = col_steps(count_next)
    slots = yg_ref.shape[1]
    local = xb_ref.shape[0]
    acc_ref[...] = jnp.zeros_like(acc_ref)

    def prepare(start, cols):
        mass, push, pulled = (
            (s0[:, part] + s1[:, part]) + (s2[:, part] + s3[:, part])
            for part in (pl.ds(start + k * slots, WIDE) for k in range(3))
        )
        inverse = jnp.where(mass > 0.0, 1.0 / jnp.maximum(mass, TINY), 0.0)
        pot = g2_ref[:, cols]
        stat_ref[0:1, cols] = pot + gb_ref[:, cols]
        stat_ref[1:2, cols] = push * inverse
        stat_ref[2:3, cols] = (push - DAMPING * pulled) * inverse
        stat_ref[3:4, cols] = inverse
        stat_ref[4:5, cols] = pot
        stat_ref[5:8, cols] = jnp.zeros((3, WIDE), F32)
        write_augmented(ya_ref, start, yg_ref[:, cols], pot + gb_ref[:, cols], False)

    in_steps(slots, prepare)
    send_ref[:, slots : slots + local] = jnp.full((1, local), MASKED, F32)
    send_ref[:, slots + local :] = jnp.zeros((1, local), F32)

    def matmul_of(first_row):
        first_ref[...] = jnp.zeros_like(first_ref)
        second_ref[...] = jnp.zeros_like(second_ref)
        return lambda c, start, size: scores(
            xb_ref[pl.ds(pl.multiple_of(first_row + start, size), size), :], ya_ref, c
        )

    def sums(c, scores_of, kept, count):
        half = LANES
        for start in range(0, count, half):
            scored = scores_of(c, start, half)
            for rg in range(0, half, SUB):
                rows = slice(start + rg, start + rg + SUB)
                first = first_ref[rows, :]
                second = second_ref[rows, :]
                for lt in range(LTS):
                    p = jnp.exp(piece_of(scored, rg, lt))
                    kept[0][rows, lane_tile(c, lt)] = p
                    first = first + p * stat_ref[1:2, lane_tile(c, lt)]
                    second = second + p * stat_ref[2:3, lane_tile(c, lt)]
                first_ref[rows, :] = first
                second_ref[rows, :] = second

    def finish(start, rows):
        first = jnp.sum(first_ref[...], axis=1, keepdims=True)
        second = jnp.sum(second_ref[...], axis=1, keepdims=True)
        aux = aux_ref[pl.ds(pl.multiple_of(start, LANES), ROWS), :]
        start_adj, inverse, pot, full = aux[:, 0:1], aux[:, 1:2], aux[:, 2:3], aux[:, 3:4]
        middle_adj = start_adj - DAMPING * first * inverse
        last_adj = start_adj - DAMPING * second * inverse
        weight_ref[...] = jnp.broadcast_to(middle_adj, weight_ref.shape)
        alpha = 1.0 + DAMPING * last_adj - pot
        lane = lax.broadcasted_iota(jnp.int32, (ROWS, LANES), 1)
        packed = jnp.transpose(jnp.where(lane == 0, full, alpha))
        send_ref[:, pl.ds(pl.multiple_of(slots + start, LANES), ROWS)] = packed[0:1, :]
        send_ref[:, pl.ds(pl.multiple_of(slots + local + start, LANES), ROWS)] = packed[1:2, :]

    two_stage(
        mine, nc, sums, finish, lambda c, kept: column_parts(c, [(kept[0], weight_ref)]), adder([acc_ref]), matmul_of,
        ((p_ref,), (q_ref,)),
    )
    send_ref[:, 0:slots] = jnp.sum(acc_ref[...], axis=0, keepdims=True)


def kernel_f(counts, p0, p1, p2, p3, stat_ref, col_ref, mine_ref, early_ref, parts_ref):
    member = lax.axis_index("cell")
    slots, local = stat_ref.shape[1], mine_ref.shape[1]
    for k, ref in enumerate((p0, p1, p2, p3)):
        parts_ref[member ^ k] = ref[...]
    total = (p0[:, 0:slots] + p1[:, 0:slots]) + (p2[:, 0:slots] + p3[:, 0:slots])
    last = stat_ref[1:2, :] - DAMPING * total * stat_ref[3:4, :]
    col_ref[0:1, :] = stat_ref[0:1, :]
    col_ref[1:2, :] = DAMPING * last - stat_ref[4:5, :]
    for block in range(slots // LANES):
        owner, place = block % 4, block // 4
        lanes = slice(block * LANES, (block + 1) * LANES)
        for k in range(2):
            at = slots + k * local + place * LANES
            early_ref[k : k + 1, lanes] = parts_ref[owner, :, at : at + LANES]
    here = pl.ds(aligned(member, local), local)
    mine_ref[...] = early_ref[:, here]
    early_ref[:, slots:] = col_ref[:, here]


def kernel_e(
    counts, *refs, earlier,
):
    own_ref, rowpot_ref, other_ref, colpot_ref = refs[:4]
    base_ref = refs[4] if earlier else None
    out_ref, xw_ref, tile_ref, ys_ref, beta_ref, za_ref, zb_ref, pull_ref, sum_ref = refs[5 if earlier else 4 :]
    local, slots = own_ref.shape[1], other_ref.shape[1]
    before, here, after, member = around(counts)
    count_rows = jnp.clip(here - member * local, 0, local)
    count_cols = before if earlier else after
    if earlier:
        own_at = slots
    else:
        own_at = 0
    nc = col_steps(count_cols)
    nb = jnp.where(count_cols > 0, (count_rows + ROWS - 1) // ROWS, 0)
    out_ref[...] = base_ref[...] if earlier else jnp.zeros_like(out_ref)

    def prepare(c, _):
        cols = pl.ds(aligned(c, COLS), COLS)
        write_augmented(tile_ref, 0, other_ref[:, cols], colpot_ref[0:1, cols], False)
        ys_ref[cols, :] = jnp.transpose(tile_ref[...]).astype(BF16)
        beta_ref[cols, :] = jnp.transpose(jnp.broadcast_to(colpot_ref[1:2, cols], (LANES, COLS)))
        return 0

    @pl.when(nb > 0)
    def _():
        lax.fori_loop(0, nc, prepare, 0)

    def row_visit(b, _):
        rows_here = pl.ds(aligned(b, ROWS), ROWS)
        own = own_ref[:, rows_here]
        own_pots = pl.ds(aligned(b + own_at // ROWS, ROWS), ROWS)
        write_augmented(xw_ref, 0, own, rowpot_ref[0:1, own_pots], True)
        xw = xw_ref[...]
        alpha = rowpot_ref[1:2, own_pots]
        sum_ref[...] = jnp.zeros_like(sum_ref)
        pull_ref[...] = jnp.zeros_like(pull_ref)

        def matmul(c):
            return jnp.dot(ys_ref[pl.ds(aligned(c, COLS), COLS), :], xw, preferred_element_type=F32)

        def work(c, z_ref, _):
            rounded = []
            sums = [jnp.zeros((8, LANES), F32) for _ in range(ROWS // LANES)]
            for jg in range(0, COLS, 16):
                beta = beta_ref[pl.ds(pl.multiple_of(c * COLS + jg, 16), 16), :]
                line = []
                for lt in range(ROWS // LANES):
                    tile = piece_of(z_ref, jg, lt, 16)
                    grad = jnp.exp(tile) * (tile + (alpha[:, lt * LANES : (lt + 1) * LANES] + beta))
                    sums[lt] = sums[lt] + (grad[0:8] + grad[8:16])
                    line.append(grad.astype(BF16))
                rounded.append(jnp.concatenate(line, axis=1))
            for lt in range(ROWS // LANES):
                sum_ref[:, lt * LANES : (lt + 1) * LANES] += sums[lt]
            feats = other_ref[:, pl.ds(aligned(c, COLS), COLS)]
            pull_ref[...] += jnp.dot(feats, jnp.concatenate(rounded, axis=0), preferred_element_type=F32)

        piped(nc, matmul, work, za_ref, zb_ref)
        total = jnp.sum(sum_ref[...], axis=0, keepdims=True)
        out_ref[:, rows_here] += 2.0 * (own.astype(F32) * total - pull_ref[...])
        return 0

    lax.fori_loop(0, nb, row_visit, 0)


def run(body, name, outs, scratch, limit, counts, *operands, flops=0):
    vmem = pl.BlockSpec(memory_space=pltpu.VMEM)
    return pl.pallas_call(
        body,
        name=name,
        out_shape=outs,
        in_specs=[pl.BlockSpec(memory_space=pltpu.SMEM)] + [vmem] * len(operands),
        out_specs=jax.tree.map(lambda _: vmem, outs),
        scratch_shapes=scratch,
        compiler_params=pltpu.CompilerParams(vmem_limit_bytes=limit * 1024 * 1024),
        cost_estimate=pl.CostEstimate(flops=flops, bytes_accessed=4_000_000, transcendentals=9_000_000),
    )(counts, *operands)


def shape(*dims, dtype=F32):
    return jax.ShapeDtypeStruct(dims, dtype)


def shifted(block, distance):
    size = lax.axis_size("tm")
    route = [(i - distance, i) for i in range(size) if 0 <= i - distance < size]
    return lax.ppermute(block, "tm", route)


def from_later(block, k):
    times, size = lax.axis_size("tm"), lax.axis_size("cell")
    route = [((t + 1) * size + (i ^ k), t * size + i) for t in range(times - 1) for i in range(size)]
    return lax.ppermute(block, ("tm", "cell"), route)


def swapped(block, k):
    return lax.ppermute(block, "cell", [(i, i ^ k) for i in range(lax.axis_size("cell"))])


def exchanged(block):
    near = swapped(block, 1)
    far = swapped(block, 2)
    return [block, near, far, swapped(far, 1)]


def per_device(embedding, counts):
    feat_dim, local = embedding.shape
    group = lax.axis_size("cell")
    slots = local * group

    ahead, ahead_far = from_later(embedding, 0), from_later(embedding, 2)
    source_parts = exchanged(embedding)
    target_parts = [ahead, swapped(ahead, 1), ahead_far, swapped(ahead_far, 1)]

    flops = 2 * local * slots * DEPTH
    aug = pltpu.VMEM((DEPTH, slots), BF16)
    narrow = pltpu.VMEM((ROWS, LANES), F32)
    wide = pltpu.VMEM((ROWS, slots), F32)
    half = pltpu.VMEM((ROWS, slots), BF16)
    turned_rows = pltpu.VMEM((16, ROWS), BF16)
    buffers = [pltpu.VMEM((ROWS, COLS), F32)] * 2
    long = pltpu.VMEM((8, slots), F32)
    grouped, targets, xa, gb, log = run(
        kernel_a, "column_log",
        (
            shape(feat_dim, slots, dtype=BF16), shape(feat_dim, slots, dtype=BF16),
            shape(local, DEPTH, dtype=BF16), shape(1, slots), shape(1, slots),
        ),
        [aug, pltpu.VMEM((DEPTH, local), F32), *buffers, long, long],
        16, counts, *source_parts, *target_parts, flops=flops,
    )
    logs = exchanged(log)
    g1, col1 = run(
        kernel_b, "first_sweep",
        (shape(1, slots), shape(1, slots)),
        [aug, *buffers, wide, wide, narrow, narrow, narrow, narrow, narrow, long],
        24, counts, xa, targets, gb, *logs, flops=2 * flops,
    )
    grouped, col1 = lax.optimization_barrier((grouped, col1))
    earlier = shifted(grouped, 1)
    xb, aux, g2, stats = run(
        kernel_c, "second_sweep",
        (shape(local, DEPTH, dtype=BF16), shape(local, LANES), shape(1, slots), shape(1, 3 * slots)),
        [
            aug, *buffers, half, half, half, half, narrow, narrow, narrow, narrow, narrow,
            pltpu.VMEM((1, slots), F32), turned_rows, pltpu.VMEM((32, slots), F32), long, long, long,
        ],
        28, counts, xa, targets, gb, g1, *exchanged(col1), flops=2 * flops,
    )
    xb, earlier = lax.optimization_barrier((xb, earlier))
    stat, send = run(
        kernel_d, "adjoint",
        (shape(8, slots), shape(1, slots + 2 * local)),
        [aug, wide, wide, narrow, narrow, narrow, long],
        24, counts, xb, aux, targets, gb, g2, *exchanged(stats), flops=2 * flops,
    )
    col_pair, rows_mine, early = run(
        kernel_f, "assemble",
        (shape(2, slots), shape(2, local), shape(2, slots + local)),
        [pltpu.VMEM((group, 1, slots + 2 * local), F32)],
        8, counts, *exchanged(send), stat,
    )
    early = shifted(early, 1)

    turned = [pltpu.VMEM((COLS, ROWS), F32)] * 2
    scratch_e = [
        pltpu.VMEM((DEPTH, ROWS), BF16), pltpu.VMEM((DEPTH, COLS), F32), pltpu.VMEM((slots, DEPTH), BF16),
        pltpu.VMEM((slots, LANES), F32), *turned, pltpu.VMEM((feat_dim, ROWS), F32), pltpu.VMEM((8, ROWS), F32),
    ]
    source_grad = run(
        functools.partial(kernel_e, earlier=False), "source_gradient", shape(feat_dim, local), scratch_e,
        16, counts, embedding, rows_mine, targets, col_pair, flops=2 * flops,
    )
    return run(
        functools.partial(kernel_e, earlier=True), "target_gradient", shape(feat_dim, local), scratch_e,
        16, counts, embedding, early, earlier, early, source_grad, flops=2 * flops,
    )


def solution(mesh):
    in_specs = (P(None, ("tm", "cell")), P())
    out_specs = P(None, ("tm", "cell"))
    return jax.shard_map(
        per_device, mesh=mesh, in_specs=in_specs, out_specs=out_specs, check_vma=False
    )
```

```python
import functools

import jax
import jax.numpy as jnp
from jax import lax
from jax.experimental import pallas as pl
from jax.experimental.pallas import tpu as pltpu
from jax.sharding import PartitionSpec as P

ENTROPY = 0.25
PENALTY = 5.0
DAMPING = PENALTY / (PENALTY + ENTROPY)
MASKED = -1e30
SQ_SCALE = 1.0 / ENTROPY
DOT_SCALE = 2.0 / ENTROPY
TINY = 1e-37
SHIFT = 44.0
LOWEST = 1e-24

ROWS = 256
COLS = 512
LANES = 128
DEPTH = 128
F32 = jnp.float32
BF16 = jnp.bfloat16


def split3(value):
    high = value.astype(BF16).astype(F32)
    rest = value - high
    middle = rest.astype(BF16).astype(F32)
    return high, middle, rest - middle


def write_augmented(out_ref, start, feats, pot, is_row):
    n = feats.shape[1]
    cols = pl.ds(start, n)
    scaled = feats.astype(F32) * DOT_SCALE if is_row else feats
    out_ref[0:32, cols] = scaled.astype(out_ref.dtype)
    first = 0 if is_row else 3
    ones_from = 3 if is_row else 0
    row = lax.broadcasted_iota(jnp.int32, (16, n), 0)
    tail = jnp.where((row >= ones_from) & (row < ones_from + 3), 1.0, 0.0)
    for k, piece in enumerate(split3(pot)):
        tail = jnp.where(row == first + k, piece, tail)
    out_ref[32:48, cols] = tail.astype(out_ref.dtype)
    out_ref[48:128, cols] = jnp.zeros((80, n), out_ref.dtype)


def square_sum(feats):
    wide = feats.astype(F32)
    return jnp.sum(wide * wide, axis=0, keepdims=True)


def live_pot(feats, start, count):
    ids = start + lax.broadcasted_iota(jnp.int32, (1, feats.shape[1]), 1)
    return jnp.where(ids < count, -SQ_SCALE * square_sum(feats), MASKED)


def aligned(index, size):
    return pl.multiple_of(index * size, size)


def around(counts):
    size = counts.shape[0]
    time, member = lax.axis_index("tm"), lax.axis_index("cell")
    before = jnp.where(time > 0, counts[jnp.maximum(time - 1, 0)], 0)
    after = jnp.where(time + 1 < size, counts[jnp.minimum(time + 1, size - 1)], 0)
    return before, counts[time], after, member


def row_blocks(count_here, count_next, member, group):
    blocks = pl.cdiv(count_here, LANES)
    mine = jnp.maximum((blocks - member + group - 1) // group, 0)
    return jnp.where(count_next > 0, mine, 0)


def live_rows(start, member, count, group=4):
    row = lax.broadcasted_iota(jnp.int32, (ROWS, 1), 0)
    slot = (group * (start // LANES) + member) * LANES + row
    return slot + jnp.where(row >= LANES, (group - 1) * LANES, 0) < count


def col_steps(count):
    return (count + COLS - 1) // COLS


LTS = COLS // LANES
SUB = 32
WIDE = 1536


def scores(xa, ya_ref, c, cols=COLS):
    return jnp.dot(xa, ya_ref[:, pl.ds(aligned(c, cols), cols)], preferred_element_type=F32)


def piped(count, matmul, work, first_ref, second_ref, load=None, store=None):
    load = load or (lambda c: None)
    store = store or (lambda c, state: None)
    first_ref[...] = matmul(0)

    def pair(i, _):
        here, there = 2 * i, 2 * i + 1
        states = load(here), load(there)
        second_ref[...] = matmul(there)
        one = work(here, first_ref, states[0])
        first_ref[...] = matmul(jnp.minimum(there + 1, count - 1))
        two = work(there, second_ref, states[1])
        store(here, one)
        store(there, two)
        return 0

    lax.fori_loop(0, count // 2, pair, 0)

    @pl.when(count % 2 == 1)
    def _():
        store(count - 1, work(count - 1, first_ref, load(count - 1)))


def adder(acc_refs):
    def store(c, sums):
        for k, acc_ref in enumerate(acc_refs):
            lts = len(sums[k])
            for lt in range(lts):
                acc_ref[:, lane_tile(c, lt, lts)] += sums[k][lt]

    return store


def lane_tile(c, lt, lts=LTS):
    return pl.ds(aligned(c * lts + lt, LANES), LANES)


def piece_of(z_ref, rg, lt, size=SUB):
    return z_ref[rg : rg + size, lt * LANES : (lt + 1) * LANES]


def in_steps(total, visit):
    for start in range(0, total, WIDE):
        visit(start, slice(start, start + WIDE))


def kernel_a(
    counts, x0, x1, x2, x3, y0, y1, y2, y3,
    xg_ref, yg_ref, xt_ref, xa_ref, gb_ref, log_ref,
    ya_ref, xat_ref, za_ref, zb_ref, top_ref, sum_ref,
):
    _, count_here, count_next, member = around(counts)
    group = 4
    mine = row_blocks(count_here, count_next, member, group)
    nb = (mine + 1) // 2
    nc = col_steps(count_next)
    local = x0.shape[1]
    for k, (x_ref, y_ref) in enumerate(((x0, y0), (x1, y1), (x2, y2), (x3, y3))):
        place = pl.ds(aligned(member ^ k, local), local)
        xg_ref[:, place] = x_ref[...]
        yg_ref[:, place] = y_ref[...]
    for k in range(local // LANES):
        block_id = group * k + member
        piece = xg_ref[:, pl.ds(aligned(block_id, LANES), LANES)]
        xt_ref[:, k * LANES : (k + 1) * LANES] = piece
        pot = live_pot(piece, block_id * LANES, count_here) + SHIFT
        write_augmented(xat_ref, k * LANES, piece, pot, True)
        xa_ref[k * LANES : (k + 1) * LANES, :] = jnp.transpose(
            xat_ref[:, k * LANES : (k + 1) * LANES]
        ).astype(BF16)
    sum_ref[...] = jnp.zeros_like(sum_ref)

    def prepare(start, cols):
        feats = yg_ref[:, cols]
        pot = live_pot(feats, start, count_next)
        gb_ref[:, cols] = pot
        write_augmented(ya_ref, start, feats, pot, False)

    in_steps(group * local, prepare)

    def exact():
        top_ref[...] = jnp.full(top_ref.shape, MASKED, F32)
        sum_ref[...] = jnp.zeros_like(sum_ref)

        def row_visit(b, _):
            xa = xa_ref[pl.ds(aligned(b, ROWS), ROWS), :]

            def load(c):
                return [(top_ref[:, lane_tile(c, lt)], sum_ref[:, lane_tile(c, lt)]) for lt in range(LTS)]

            def work(c, z_ref, state):
                after = []
                for lt, (old, total) in enumerate(state):
                    tile = z_ref[:, lt * LANES : (lt + 1) * LANES].reshape(ROWS // 8, 8, LANES)
                    top = jnp.maximum(old, jnp.max(tile, axis=0))
                    total = total * jnp.exp(old - top) + jnp.sum(jnp.exp(tile - top[None]), axis=0)
                    after.append((top, total))
                return after

            def store(c, state):
                for lt, (top, total) in enumerate(state):
                    top_ref[:, lane_tile(c, lt)] = top
                    sum_ref[:, lane_tile(c, lt)] = total

            piped(nc, lambda c: scores(xa, ya_ref, c), work, za_ref, zb_ref, load, store)
            return 0

        lax.fori_loop(0, nb, row_visit, 0)
        tops = top_ref[...]
        top = jnp.max(tops, axis=0, keepdims=True)
        total = jnp.sum(sum_ref[...] * jnp.exp(tops - top), axis=0, keepdims=True)
        log_ref[...] = top + jnp.log(jnp.maximum(total, TINY)) - SHIFT

    thin = 2 * LANES

    def quick_rows(first_block, blocks):
        halves = [xa_ref[pl.ds(aligned(first_block + k, LANES), LANES), :] for k in range(blocks)]

        def tile_sums(c, tiles):
            for t in range(tiles):
                totals = [jnp.zeros((8, LANES), F32) for _ in range(2)]
                for half in halves:
                    z = scores(half, ya_ref, c * tiles + t, thin)
                    for lt in range(2):
                        p = jnp.exp(z[:, lt * LANES : (lt + 1) * LANES])
                        totals[lt] = totals[lt] + jnp.sum(p.reshape(LANES // 8, 8, LANES), axis=0)
                for lt in range(2):
                    sum_ref[:, lane_tile(c * tiles + t, lt, 2)] += totals[lt]

        def pair(i, _):
            tile_sums(i, 4)
            return 0

        lax.fori_loop(0, nc // 2, pair, 0)

        @pl.when(nc % 2 == 1)
        def _():
            tile_sums(nc - 1, 2)

    def quick_visit(b, _):
        quick_rows(2 * b, 2)
        return 0

    lax.fori_loop(0, mine // 2, quick_visit, 0)

    @pl.when(mine % 2 == 1)
    def _():
        quick_rows(mine - 1, 1)

    total = jnp.sum(sum_ref[...], axis=0, keepdims=True)
    log_ref[...] = jnp.where(total > 0.0, jnp.log(jnp.maximum(total, TINY)) - SHIFT, MASKED)
    ids = lax.broadcasted_iota(jnp.int32, total.shape, 1)
    lowest = jnp.min(jnp.where(ids < count_next, total, 1.0))

    @pl.when((lowest < LOWEST) & (nb > 0))
    def _():
        exact()


def column_sums(c, z_ref, _):
    rows, cols = z_ref.shape
    sums = []
    for lt in range(cols // LANES):
        p = jnp.exp(z_ref[:, lt * LANES : (lt + 1) * LANES])
        sums.append(jnp.sum(p.reshape(rows // 8, 8, LANES), axis=0))
    return [sums]


def row_adder(sum_ref, push_ref=None, g_ref=None):
    def first(c, scores_of, kept, count):
        half = LANES
        for start in range(0, count, half):
            scored = scores_of(c, start, half)
            for rg in range(0, half, SUB):
                rows = slice(start + rg, start + rg + SUB)
                total = sum_ref[rows, :]
                push = push_ref[rows, :] if push_ref is not None else None
                for lt in range(LTS):
                    z = piece_of(scored, rg, lt)
                    p = jnp.exp(z)
                    total = total + p
                    kept[0][rows, lane_tile(c, lt)] = p.astype(kept[0].dtype)
                    if push is not None:
                        part = p * (g_ref[:, lane_tile(c, lt)] - z)
                        push = push + part
                        kept[1][rows, lane_tile(c, lt)] = part.astype(kept[1].dtype)
                sum_ref[rows, :] = total
                if push is not None:
                    push_ref[rows, :] = push

    return first


def column_parts(c, plan):
    sums = [[jnp.zeros((8, LANES), F32) for _ in range(LTS)] for _ in plan]
    for rg in range(0, ROWS, 8):
        for k, (kept_ref, weight_ref) in enumerate(plan):
            scale = weight_ref[rg : rg + 8, :]
            for lt in range(LTS):
                sums[k][lt] = sums[k][lt] + scale * kept_ref[rg : rg + 8, lane_tile(c, lt)]
    return sums


def two_stage(mine, nc, first, finish, second, store, matmul_of, kept):
    nb = (mine + 1) // 2
    alone = mine % 2 == 1

    def in_pairs(visit, put):
        put = put or (lambda c, sums: None)

        def pair(i, _):
            one, two = visit(2 * i), visit(2 * i + 1)
            put(2 * i, one)
            put(2 * i + 1, two)
            return 0

        lax.fori_loop(0, nc // 2, pair, 0)

        @pl.when(nc % 2 == 1)
        def _():
            put(nc - 1, visit(nc - 1))

    def stage(start, now, before, rows=ROWS):
        scores_of = matmul_of(start)

        def visit(c):
            first(c, scores_of, now, rows)
            if rows < ROWS:
                for ref in now:
                    ref[rows:, col_tile(c)] = jnp.zeros((ROWS - rows, COLS), ref.dtype)
            return second(c, before) if before else None

        in_pairs(visit, store if before else None)
        finish(start, rows)

    def tail(before):
        in_pairs(lambda c: second(c, before), store)

    even, odd = kept

    @pl.when((nb > 0) & alone)
    def _():
        stage(0, even, None, LANES)

    @pl.when((nb > 0) & jnp.logical_not(alone))
    def _():
        stage(0, even, None)

    def visit(b, _):
        start = pl.multiple_of(b * ROWS - jnp.where(alone, LANES, 0), LANES)

        @pl.when(b % 2 == 1)
        def _():
            stage(start, odd, even)

        @pl.when(b % 2 == 0)
        def _():
            stage(start, even, odd)

        return 0

    lax.fori_loop(1, nb, visit, 0)

    @pl.when((nb > 0) & (nb % 2 == 1))
    def _():
        tail(even)

    @pl.when((nb > 0) & (nb % 2 == 0))
    def _():
        tail(odd)


def col_tile(c):
    return pl.ds(aligned(c, COLS), COLS)


def split2(value):
    high = value.astype(BF16).astype(F32)
    return high, value - high


def turned_weights(columns):
    lane = lax.broadcasted_iota(jnp.int32, (ROWS, LANES), 1)
    packed = jnp.zeros((ROWS, LANES), F32)
    for at, column in columns:
        packed = jnp.where(lane == at, column, packed)
    return jnp.transpose(packed)


def sweep(quick, exact, low_ref, lost=None):
    low_ref[...] = jnp.ones_like(low_ref)
    quick()
    again = jnp.min(low_ref[...]) < LOWEST
    if lost is not None:
        again = again | lost()

    @pl.when(again)
    def _():
        exact()


def row_lse(xa, ya_ref, nc, buffers, top_ref, sum_ref, push_ref=None, g_ref=None):
    top_ref[...] = jnp.full(top_ref.shape, MASKED, F32)
    sum_ref[...] = jnp.zeros_like(sum_ref)
    if push_ref is not None:
        push_ref[...] = jnp.zeros_like(push_ref)

    def work(c, z_ref, _):
        for rg in range(0, ROWS, SUB):
            rows = slice(rg, rg + SUB)
            old = top_ref[rows, :]
            pieces = [piece_of(z_ref, rg, lt) for lt in range(LTS)]
            top = old
            for z in pieces:
                top = jnp.maximum(top, z)
            fade = jnp.exp(old - top)
            total = sum_ref[rows, :] * fade
            push = push_ref[rows, :] * fade if push_ref is not None else None
            for lt, z in enumerate(pieces):
                p = jnp.exp(z - top)
                total = total + p
                if push is not None:
                    push = push + p * (g_ref[:, lane_tile(c, lt)] - z)
            top_ref[rows, :] = top
            sum_ref[rows, :] = total
            if push is not None:
                push_ref[rows, :] = push

    piped(nc, lambda c: scores(xa, ya_ref, c), work, *buffers)
    tops = top_ref[...]
    top = jnp.max(tops, axis=1, keepdims=True)
    fade = jnp.exp(tops - top)
    total = jnp.sum(sum_ref[...] * fade, axis=1, keepdims=True)
    if push_ref is None:
        return top, total
    return top, total, jnp.sum(push_ref[...] * fade, axis=1, keepdims=True)


def row_potential(xa):
    lane = lax.broadcasted_iota(jnp.int32, (ROWS, LANES), 1)
    wide = xa.astype(F32)
    old = jnp.sum(jnp.where((lane >= 32) & (lane < 35), wide, 0.0), axis=1, keepdims=True)
    return lane, wide, old


def with_row_potential(lane, wide, pot):
    high, middle, low = split3(pot)
    new = jnp.where(lane == 32, high, jnp.where(lane == 33, middle, jnp.where(lane == 34, low, wide)))
    return new.astype(BF16)


def kernel_b(counts, xa_ref, yg_ref, gb_ref, l0, l1, l2, l3, g_ref, col_ref, ya_ref, za_ref, zb_ref, p_ref, q_ref, top_ref, sum_ref, weight_ref, low_ref, most_ref, acc_ref):
    _, count_here, count_next, member = around(counts)
    mine = row_blocks(count_here, count_next, member, 4)
    nb = (mine + 1) // 2
    nc = col_steps(count_next)

    def prepare(start, cols):
        logs = [ref[:, cols] for ref in (l0, l1, l2, l3)]
        top = jnp.maximum(jnp.maximum(logs[0], logs[1]), jnp.maximum(logs[2], logs[3]))
        total = sum(jnp.exp(one - top) for one in logs)
        ids = start + lax.broadcasted_iota(jnp.int32, (1, WIDE), 1)
        pot = jnp.where(ids < count_next, -DAMPING * (top + jnp.log(total)), 0.0)
        g_ref[:, cols] = pot
        write_augmented(ya_ref, start, yg_ref[:, cols], pot + gb_ref[:, cols], False)

    in_steps(yg_ref.shape[1], prepare)

    buffers = za_ref, zb_ref

    def quick():
        acc_ref[...] = jnp.zeros_like(acc_ref)

        def matmul_of(first_row):
            sum_ref[...] = jnp.zeros_like(sum_ref)
            return lambda c, start, size: scores(
                xa_ref[pl.ds(pl.multiple_of(first_row + start, size), size), :], ya_ref, c
            )

        def finish(start, rows):
            row = lax.broadcasted_iota(jnp.int32, (ROWS, 1), 0)
            live = live_rows(start, member, count_here) & (row < rows)
            total = jnp.sum(sum_ref[...], axis=1, keepdims=True)
            low_ref[...] = jnp.minimum(low_ref[...], jnp.where(live, total, 1.0))
            pot = -DAMPING * (jnp.log(jnp.maximum(total, TINY)) - SHIFT)
            weight = jnp.where(live, jnp.exp(pot - SHIFT), 0.0)
            weight_ref[...] = jnp.broadcast_to(weight, weight_ref.shape)
            most_ref[...] = jnp.maximum(most_ref[...], weight)

        two_stage(
            mine, nc, row_adder(sum_ref), finish, lambda c, kept: column_parts(c, [(kept[0], weight_ref)]),
            adder([acc_ref]), matmul_of, ((p_ref,), (q_ref,)),
        )

    def exact():
        acc_ref[...] = jnp.zeros_like(acc_ref)

        def row_visit(b, _):
            xa = xa_ref[pl.ds(aligned(b, ROWS), ROWS), :]
            lane, wide, old = row_potential(xa)
            live = old > 0.5 * MASKED
            top, total = row_lse(xa, ya_ref, nc, buffers, top_ref, sum_ref)
            pot = -DAMPING * (top + jnp.log(total) - SHIFT)
            xb = with_row_potential(lane, wide, jnp.where(live, pot + old - SHIFT, MASKED))
            piped(nc, lambda c: scores(xb, ya_ref, c), column_sums, *buffers, store=adder([acc_ref]))
            return 0

        lax.fori_loop(0, nb, row_visit, 0)

    def lost():
        total = jnp.sum(acc_ref[...], axis=0, keepdims=True)
        ids = lax.broadcasted_iota(jnp.int32, total.shape, 1)
        least = jnp.min(jnp.where((ids < count_next) & (nb > 0), total, 1.0))
        return least < jnp.max(most_ref[...]) * 2.0**-91

    most_ref[...] = jnp.zeros_like(most_ref)
    sweep(quick, exact, low_ref, lost)
    col_ref[...] = jnp.sum(acc_ref[...], axis=0, keepdims=True)


def kernel_c(
    counts, xa_ref, yg_ref, gb_ref, g_ref, c0, c1, c2, c3,
    xb_ref, aux_ref, g2_ref, col_ref,
    ya_ref, za_ref, zb_ref, p_ref, w_ref, q_ref, v_ref, top_ref, sum_ref, push_ref, adj_ref, low_ref, cost_ref, weight_ref, acc_ref, acc0_ref, acc1_ref, acc2_ref,
):
    _, count_here, count_next, member = around(counts)
    mine = row_blocks(count_here, count_next, member, 4)
    nb = (mine + 1) // 2
    nc = col_steps(count_next)

    def prepare(start, cols):
        total = (c0[:, cols] + c1[:, cols]) + (c2[:, cols] + c3[:, cols])
        ids = start + lax.broadcasted_iota(jnp.int32, (1, WIDE), 1)
        log = jnp.log(jnp.maximum(total, TINY)) - g_ref[:, cols]
        pot = jnp.where(ids < count_next, -DAMPING * log, 0.0)
        g2_ref[:, cols] = pot
        write_augmented(ya_ref, start, yg_ref[:, cols], pot + gb_ref[:, cols], False)

    in_steps(yg_ref.shape[1], prepare)

    buffers = za_ref, zb_ref
    accs = acc0_ref, acc1_ref, acc2_ref

    ids = lax.broadcasted_iota(jnp.int32, g_ref.shape, 1)
    centre = jnp.sum(jnp.where(ids < count_next, g_ref[...], 0.0), axis=1, keepdims=True)
    centre = centre / (DAMPING * jnp.maximum(count_next, 1).astype(F32)) + 3.0
    cost_ref[...] = g2_ref[...] + (SHIFT - centre)

    def close_rows(start, rows, top, total, push):
        rows_here = pl.ds(pl.multiple_of(start, LANES), ROWS)
        lane, wide, old = row_potential(xa_ref[rows_here, :])
        live = old > 0.5 * MASKED
        if rows < ROWS:
            live = live & (lax.broadcasted_iota(jnp.int32, (ROWS, 1), 0) < rows)
        total = jnp.maximum(total, TINY)
        row_log = top + jnp.log(total) - SHIFT
        pot = jnp.where(live, -DAMPING * row_log, 0.0)
        row_sum = jnp.where(live, jnp.exp(row_log + pot), 0.0)
        adjoint = jnp.where(live, push / total + centre, 0.0)
        inverse = jnp.where(row_sum > 0.0, 1.0 / jnp.maximum(row_sum, TINY), 0.0)
        full = jnp.where(live, pot + old - SHIFT, MASKED)
        xb = with_row_potential(lane, wide, full)
        xb_ref[rows_here, :] = xb
        aux = jnp.where(lane == 0, adjoint, jnp.where(lane == 1, inverse, jnp.where(lane == 2, pot, full)))
        aux_ref[rows_here, :] = aux
        return live, pot, adjoint, xb

    def quick():
        acc_ref[...] = jnp.zeros_like(acc_ref)

        def matmul_of(first_row):
            sum_ref[...] = jnp.zeros_like(sum_ref)
            push_ref[...] = jnp.zeros_like(push_ref)
            return lambda c, start, size: scores(
                xa_ref[pl.ds(pl.multiple_of(first_row + start, size), size), :], ya_ref, c
            )

        def finish(start, rows):
            total = jnp.sum(sum_ref[...], axis=1, keepdims=True)
            push = jnp.sum(push_ref[...], axis=1, keepdims=True)
            live, pot, adjoint, _ = close_rows(start, rows, 0.0, total, push)
            low_ref[...] = jnp.minimum(low_ref[...], jnp.where(live, total, 1.0))
            weight = jnp.where(live, jnp.exp(pot - SHIFT), 0.0)
            pieces = (*split2(weight), *split2(weight * adjoint))
            weight_ref[...] = turned_weights(list(enumerate(pieces)))[0:16, :].astype(BF16)

        def second(c, kept):
            weights = weight_ref[...]
            plan = jnp.dot(weights, kept[0][:, col_tile(c)], preferred_element_type=F32)
            cost = jnp.dot(weights, kept[1][:, col_tile(c)], preferred_element_type=F32)
            return plan, cost

        def store(c, sums):
            acc_ref[0:16, col_tile(c)] += sums[0]
            acc_ref[16:32, col_tile(c)] += sums[1]

        two_stage(
            mine, nc, row_adder(sum_ref, push_ref, cost_ref), finish, second, store, matmul_of,
            ((p_ref, w_ref), (q_ref, v_ref)),
        )
        acc0_ref[0:1, :] = acc_ref[0:1, :] + acc_ref[1:2, :]
        acc1_ref[0:1, :] = acc_ref[16:17, :] + acc_ref[17:18, :]
        acc2_ref[0:1, :] = acc_ref[2:3, :] + acc_ref[3:4, :]
        for ref in accs:
            ref[1:8, :] = jnp.zeros((7, ref.shape[1]), F32)

    def exact():
        for ref in accs:
            ref[...] = jnp.zeros_like(ref)

        def row_visit(b, _):
            xa = xa_ref[pl.ds(aligned(b, ROWS), ROWS), :]
            top, total, push = row_lse(xa, ya_ref, nc, buffers, top_ref, sum_ref, push_ref, cost_ref)
            _, pot, adjoint, xb = close_rows(b * ROWS, ROWS, top, total, push)
            top_ref[...] = jnp.broadcast_to(pot - SHIFT, top_ref.shape)
            adj_ref[...] = jnp.broadcast_to(adjoint, adj_ref.shape)

            def work(c, z_ref, _):
                sums = [[jnp.zeros((8, LANES), F32) for _ in range(LTS)] for _ in range(3)]
                for rg in range(0, ROWS, 8):
                    pot_here = top_ref[rg : rg + 8, :]
                    adj_here = adj_ref[rg : rg + 8, :]
                    for lt in range(LTS):
                        tile = piece_of(z_ref, rg, lt, 8)
                        p = jnp.exp(tile)
                        sums[0][lt] = sums[0][lt] + p
                        sums[1][lt] = sums[1][lt] + p * (cost_ref[:, lane_tile(c, lt)] + (pot_here - tile))
                        sums[2][lt] = sums[2][lt] + p * adj_here
                return sums

            piped(nc, lambda c: scores(xb, ya_ref, c), work, *buffers, store=adder(accs))
            return 0

        lax.fori_loop(0, nb, row_visit, 0)

    sweep(quick, exact, low_ref)
    mass = jnp.sum(acc0_ref[...], axis=0, keepdims=True)
    slots = mass.shape[1]
    col_ref[:, 0:slots] = mass
    push = jnp.sum(acc1_ref[...], axis=0, keepdims=True)
    col_ref[:, slots : 2 * slots] = push + centre * mass
    col_ref[:, 2 * slots :] = jnp.sum(acc2_ref[...], axis=0, keepdims=True)


def kernel_d(
    counts, xb_ref, aux_ref, yg_ref, gb_ref, g2_ref, s0, s1, s2, s3,
    stat_ref, send_ref,
    ya_ref, p_ref, q_ref, first_ref, second_ref, weight_ref, acc_ref,
):
    _, count_here, count_next, member = around(counts)
    mine = row_blocks(count_here, count_next, member, 4)
    nb = (mine + 1) // 2
    nc = col_steps(count_next)
    slots = yg_ref.shape[1]
    local = xb_ref.shape[0]
    acc_ref[...] = jnp.zeros_like(acc_ref)

    def prepare(start, cols):
        mass, push, pulled = (
            (s0[:, part] + s1[:, part]) + (s2[:, part] + s3[:, part])
            for part in (pl.ds(start + k * slots, WIDE) for k in range(3))
        )
        inverse = jnp.where(mass > 0.0, 1.0 / jnp.maximum(mass, TINY), 0.0)
        pot = g2_ref[:, cols]
        stat_ref[0:1, cols] = pot + gb_ref[:, cols]
        stat_ref[1:2, cols] = push * inverse
        stat_ref[2:3, cols] = (push - DAMPING * pulled) * inverse
        stat_ref[3:4, cols] = inverse
        stat_ref[4:5, cols] = pot
        stat_ref[5:8, cols] = jnp.zeros((3, WIDE), F32)
        write_augmented(ya_ref, start, yg_ref[:, cols], pot + gb_ref[:, cols], False)

    in_steps(slots, prepare)
    send_ref[:, slots : slots + local] = jnp.full((1, local), MASKED, F32)
    send_ref[:, slots + local :] = jnp.zeros((1, local), F32)

    def matmul_of(first_row):
        first_ref[...] = jnp.zeros_like(first_ref)
        second_ref[...] = jnp.zeros_like(second_ref)
        return lambda c, start, size: scores(
            xb_ref[pl.ds(pl.multiple_of(first_row + start, size), size), :], ya_ref, c
        )

    def sums(c, scores_of, kept, count):
        half = LANES
        for start in range(0, count, half):
            scored = scores_of(c, start, half)
            for rg in range(0, half, SUB):
                rows = slice(start + rg, start + rg + SUB)
                first = first_ref[rows, :]
                second = second_ref[rows, :]
                for lt in range(LTS):
                    p = jnp.exp(piece_of(scored, rg, lt))
                    kept[0][rows, lane_tile(c, lt)] = p
                    first = first + p * stat_ref[1:2, lane_tile(c, lt)]
                    second = second + p * stat_ref[2:3, lane_tile(c, lt)]
                first_ref[rows, :] = first
                second_ref[rows, :] = second

    def finish(start, rows):
        first = jnp.sum(first_ref[...], axis=1, keepdims=True)
        second = jnp.sum(second_ref[...], axis=1, keepdims=True)
        aux = aux_ref[pl.ds(pl.multiple_of(start, LANES), ROWS), :]
        start_adj, inverse, pot, full = aux[:, 0:1], aux[:, 1:2], aux[:, 2:3], aux[:, 3:4]
        middle_adj = start_adj - DAMPING * first * inverse
        last_adj = start_adj - DAMPING * second * inverse
        weight_ref[...] = jnp.broadcast_to(middle_adj, weight_ref.shape)
        alpha = 1.0 + DAMPING * last_adj - pot
        lane = lax.broadcasted_iota(jnp.int32, (ROWS, LANES), 1)
        packed = jnp.transpose(jnp.where(lane == 0, full, alpha))
        send_ref[:, pl.ds(pl.multiple_of(slots + start, LANES), ROWS)] = packed[0:1, :]
        send_ref[:, pl.ds(pl.multiple_of(slots + local + start, LANES), ROWS)] = packed[1:2, :]

    two_stage(
        mine, nc, sums, finish, lambda c, kept: column_parts(c, [(kept[0], weight_ref)]), adder([acc_ref]), matmul_of,
        ((p_ref,), (q_ref,)),
    )
    send_ref[:, 0:slots] = jnp.sum(acc_ref[...], axis=0, keepdims=True)


def kernel_f(counts, p0, p1, p2, p3, stat_ref, col_ref, early_ref, parts_ref):
    member = lax.axis_index("cell")
    slots = stat_ref.shape[1]
    local = early_ref.shape[1] - slots
    for k, ref in enumerate((p0, p1, p2, p3)):
        parts_ref[member ^ k] = ref[...]
    total = (p0[:, 0:slots] + p1[:, 0:slots]) + (p2[:, 0:slots] + p3[:, 0:slots])
    last = stat_ref[1:2, :] - DAMPING * total * stat_ref[3:4, :]
    col_ref[0:1, :] = stat_ref[0:1, :]
    col_ref[1:2, :] = DAMPING * last - stat_ref[4:5, :]
    for block in range(slots // LANES):
        owner, place = block % 4, block // 4
        lanes = slice(block * LANES, (block + 1) * LANES)
        for k in range(2):
            at = slots + k * local + place * LANES
            early_ref[k : k + 1, lanes] = parts_ref[owner, :, at : at + LANES]
    here = pl.ds(aligned(member, local), local)
    early_ref[:, slots:] = col_ref[:, here]


def kernel_e(
    counts, *refs, earlier,
):
    own_ref, rowpot_ref, other_ref, colpot_ref = refs[:4]
    local, slots = own_ref.shape[1], other_ref.shape[1]
    before, here, after, member = around(counts)
    if earlier:
        out_ref, xw_ref, tile_ref, ys_ref, beta_ref, za_ref, zb_ref, pull_ref, sum_ref = refs[4:]
        count_cols = before
        count_rows = jnp.clip(here - member * local, 0, local)
        nb = jnp.where(count_cols > 0, (count_rows + ROWS - 1) // ROWS, 0)
        pot_at = slots
    else:
        out_refs = refs[4:8]
        xw_ref, tile_ref, ys_ref, beta_ref, za_ref, zb_ref, pull_ref, sum_ref, out_ref = refs[8:]
        count_cols = after
        nb = (row_blocks(here, after, member, 4) + 1) // 2
        pot_at = slots
    nc = col_steps(count_cols)
    out_ref[...] = jnp.zeros_like(out_ref)

    def prepare(c, _):
        cols = pl.ds(aligned(c, COLS), COLS)
        write_augmented(tile_ref, 0, other_ref[:, cols], colpot_ref[0:1, cols], False)
        ys_ref[cols, :] = jnp.transpose(tile_ref[...]).astype(BF16)
        beta_ref[cols, :] = jnp.transpose(jnp.broadcast_to(colpot_ref[1:2, cols], (LANES, COLS)))
        return 0

    @pl.when(nb > 0)
    def _():
        lax.fori_loop(0, nc, prepare, 0)

    def row_visit(b, _):
        rows_here = pl.ds(aligned(b, ROWS), ROWS)
        own = own_ref[:, rows_here]
        pots = rowpot_ref[0:1, pl.ds(aligned(b + pot_at // ROWS, ROWS), ROWS)]
        write_augmented(xw_ref, 0, own, pots, True)
        xw = xw_ref[...]
        if earlier:
            alpha = rowpot_ref[1:2, pl.ds(aligned(b + pot_at // ROWS, ROWS), ROWS)]
        else:
            alpha = rowpot_ref[0:1, pl.ds(aligned(b + (pot_at + local) // ROWS, ROWS), ROWS)]
        sum_ref[...] = jnp.zeros_like(sum_ref)
        pull_ref[...] = jnp.zeros_like(pull_ref)

        def matmul(c):
            return jnp.dot(ys_ref[pl.ds(aligned(c, COLS), COLS), :], xw, preferred_element_type=F32)

        def work(c, z_ref, _):
            rounded = []
            sums = [jnp.zeros((8, LANES), F32) for _ in range(ROWS // LANES)]
            for jg in range(0, COLS, 16):
                beta = beta_ref[pl.ds(pl.multiple_of(c * COLS + jg, 16), 16), :]
                line = []
                for lt in range(ROWS // LANES):
                    tile = piece_of(z_ref, jg, lt, 16)
                    grad = jnp.exp(tile) * (tile + (alpha[:, lt * LANES : (lt + 1) * LANES] + beta))
                    sums[lt] = sums[lt] + (grad[0:8] + grad[8:16])
                    line.append(grad.astype(BF16))
                rounded.append(jnp.concatenate(line, axis=1))
            for lt in range(ROWS // LANES):
                sum_ref[:, lt * LANES : (lt + 1) * LANES] += sums[lt]
            feats = other_ref[:, pl.ds(aligned(c, COLS), COLS)]
            pull_ref[...] += jnp.dot(feats, jnp.concatenate(rounded, axis=0), preferred_element_type=F32)

        piped(nc, matmul, work, za_ref, zb_ref)
        total = jnp.sum(sum_ref[...], axis=0, keepdims=True)
        out_ref[:, rows_here] = 2.0 * (own.astype(F32) * total - pull_ref[...])
        return 0

    lax.fori_loop(0, nb, row_visit, 0)
    if not earlier:
        width = local // 4
        for k, ref in enumerate(out_refs):
            ref[...] = out_ref[:, pl.ds(pl.multiple_of((member ^ k) * width, LANES), width)]


def kernel_g(counts, target_ref, p0, p1, p2, p3, out_ref):
    member = lax.axis_index("cell")
    for k, ref in enumerate((p0, p1, p2, p3)):
        for i in range(ref.shape[1] // LANES):
            lanes = pl.ds(aligned(4 * i + (member ^ k), LANES), LANES)
            out_ref[:, lanes] = target_ref[:, lanes] + ref[:, i * LANES : (i + 1) * LANES]


def run(body, name, outs, scratch, limit, counts, *operands, flops=0):
    vmem = pl.BlockSpec(memory_space=pltpu.VMEM)
    return pl.pallas_call(
        body,
        name=name,
        out_shape=outs,
        in_specs=[pl.BlockSpec(memory_space=pltpu.SMEM)] + [vmem] * len(operands),
        out_specs=jax.tree.map(lambda _: vmem, outs),
        scratch_shapes=scratch,
        compiler_params=pltpu.CompilerParams(vmem_limit_bytes=limit * 1024 * 1024),
        cost_estimate=pl.CostEstimate(flops=flops, bytes_accessed=4_000_000, transcendentals=9_000_000),
    )(counts, *operands)


def shape(*dims, dtype=F32):
    return jax.ShapeDtypeStruct(dims, dtype)


def shifted(block, distance):
    size = lax.axis_size("tm")
    route = [(i - distance, i) for i in range(size) if 0 <= i - distance < size]
    return lax.ppermute(block, "tm", route)


def from_later(block, k):
    times, size = lax.axis_size("tm"), lax.axis_size("cell")
    route = [((t + 1) * size + (i ^ k), t * size + i) for t in range(times - 1) for i in range(size)]
    return lax.ppermute(block, ("tm", "cell"), route)


def swapped(block, k):
    return lax.ppermute(block, "cell", [(i, i ^ k) for i in range(lax.axis_size("cell"))])


def exchanged(block):
    near = swapped(block, 1)
    far = swapped(block, 2)
    return [block, near, far, swapped(far, 1)]


def per_device(embedding, counts):
    feat_dim, local = embedding.shape
    group = lax.axis_size("cell")
    slots = local * group

    ahead, ahead_far = from_later(embedding, 0), from_later(embedding, 2)
    source_parts = exchanged(embedding)
    target_parts = [ahead, swapped(ahead, 1), ahead_far, swapped(ahead_far, 1)]

    flops = 2 * local * slots * DEPTH
    aug = pltpu.VMEM((DEPTH, slots), BF16)
    narrow = pltpu.VMEM((ROWS, LANES), F32)
    wide = pltpu.VMEM((ROWS, slots), F32)
    half = pltpu.VMEM((ROWS, slots), BF16)
    turned_rows = pltpu.VMEM((16, ROWS), BF16)
    buffers = [pltpu.VMEM((ROWS, COLS), F32)] * 2
    long = pltpu.VMEM((8, slots), F32)
    grouped, targets, dealt, xa, gb, log = run(
        kernel_a, "column_log",
        (
            shape(feat_dim, slots, dtype=BF16), shape(feat_dim, slots, dtype=BF16), shape(feat_dim, local, dtype=BF16),
            shape(local, DEPTH, dtype=BF16), shape(1, slots), shape(1, slots),
        ),
        [aug, pltpu.VMEM((DEPTH, local), F32), *buffers, long, long],
        16, counts, *source_parts, *target_parts, flops=flops,
    )
    logs = exchanged(log)
    g1, col1 = run(
        kernel_b, "first_sweep",
        (shape(1, slots), shape(1, slots)),
        [aug, *buffers, wide, wide, narrow, narrow, narrow, narrow, narrow, long],
        24, counts, xa, targets, gb, *logs, flops=2 * flops,
    )
    grouped, col1 = lax.optimization_barrier((grouped, col1))
    earlier = shifted(grouped, 1)
    xb, aux, g2, stats = run(
        kernel_c, "second_sweep",
        (shape(local, DEPTH, dtype=BF16), shape(local, LANES), shape(1, slots), shape(1, 3 * slots)),
        [
            aug, *buffers, half, half, half, half, narrow, narrow, narrow, narrow, narrow,
            pltpu.VMEM((1, slots), F32), turned_rows, pltpu.VMEM((32, slots), F32), long, long, long,
        ],
        28, counts, xa, targets, gb, g1, *exchanged(col1), flops=2 * flops,
    )
    xb, earlier = lax.optimization_barrier((xb, earlier))
    stat, send = run(
        kernel_d, "adjoint",
        (shape(8, slots), shape(1, slots + 2 * local)),
        [aug, wide, wide, narrow, narrow, narrow, long],
        24, counts, xb, aux, targets, gb, g2, *exchanged(stats), flops=2 * flops,
    )
    col_pair, early = run(
        kernel_f, "assemble",
        (shape(2, slots), shape(2, slots + local)),
        [pltpu.VMEM((group, 1, slots + 2 * local), F32)],
        8, counts, *exchanged(send), stat,
    )
    early = shifted(early, 1)

    turned = [pltpu.VMEM((COLS, ROWS), F32)] * 2
    scratch_e = [
        pltpu.VMEM((DEPTH, ROWS), BF16), pltpu.VMEM((DEPTH, COLS), F32), pltpu.VMEM((slots, DEPTH), BF16),
        pltpu.VMEM((slots, LANES), F32), *turned, pltpu.VMEM((feat_dim, ROWS), F32), pltpu.VMEM((8, ROWS), F32),
    ]
    parts = run(
        functools.partial(kernel_e, earlier=False), "source_gradient", (shape(feat_dim, local // group),) * group,
        scratch_e + [pltpu.VMEM((feat_dim, local), F32)],
        16, counts, dealt, send, targets, col_pair, flops=2 * flops,
    )
    parts = [parts[0]] + [swapped(parts[k], k) for k in range(1, group)]
    target_grad = run(
        functools.partial(kernel_e, earlier=True), "target_gradient", shape(feat_dim, local), scratch_e,
        16, counts, embedding, early, earlier, early, flops=2 * flops,
    )
    return run(kernel_g, "total", shape(feat_dim, local), [], 8, counts, target_grad, *parts)


def solution(mesh):
    in_specs = (P(None, ("tm", "cell")), P())
    out_specs = P(None, ("tm", "cell"))
    return jax.shard_map(
        per_device, mesh=mesh, in_specs=in_specs, out_specs=out_specs, check_vma=False
    )
```

```python
import functools

import jax
import jax.numpy as jnp
from jax import lax
from jax.experimental import pallas as pl
from jax.experimental.pallas import tpu as pltpu
from jax.sharding import PartitionSpec as P

ENTROPY = 0.25
PENALTY = 5.0
DAMPING = PENALTY / (PENALTY + ENTROPY)
MASKED = -1e30
SQ_SCALE = 1.0 / ENTROPY
DOT_SCALE = 2.0 / ENTROPY
TINY = 1e-37
SHIFT = 44.0
LOWEST = 1e-24

ROWS = 256
COLS = 512
LANES = 128
DEPTH = 128
F32 = jnp.float32
HBM = pltpu.HBM
BF16 = jnp.bfloat16


def split3(value):
    high = value.astype(BF16).astype(F32)
    rest = value - high
    middle = rest.astype(BF16).astype(F32)
    return high, middle, rest - middle


def write_augmented(out_ref, start, feats, pot, is_row):
    n = feats.shape[1]
    cols = pl.ds(start, n)
    scaled = feats.astype(F32) * DOT_SCALE if is_row else feats
    out_ref[0:32, cols] = scaled.astype(out_ref.dtype)
    first = 0 if is_row else 3
    ones_from = 3 if is_row else 0
    row = lax.broadcasted_iota(jnp.int32, (16, n), 0)
    tail = jnp.where((row >= ones_from) & (row < ones_from + 3), 1.0, 0.0)
    for k, piece in enumerate(split3(pot)):
        tail = jnp.where(row == first + k, piece, tail)
    out_ref[32:48, cols] = tail.astype(out_ref.dtype)
    out_ref[48:128, cols] = jnp.zeros((80, n), out_ref.dtype)


def square_sum(feats):
    wide = feats.astype(F32)
    return jnp.sum(wide * wide, axis=0, keepdims=True)


def live_pot(feats, start, count):
    ids = start + lax.broadcasted_iota(jnp.int32, (1, feats.shape[1]), 1)
    return jnp.where(ids < count, -SQ_SCALE * square_sum(feats), MASKED)


def aligned(index, size):
    return pl.multiple_of(index * size, size)


def around(counts):
    size = counts.shape[0]
    time, member = lax.axis_index("tm"), lax.axis_index("cell")
    before = jnp.where(time > 0, counts[jnp.maximum(time - 1, 0)], 0)
    after = jnp.where(time + 1 < size, counts[jnp.minimum(time + 1, size - 1)], 0)
    return before, counts[time], after, member


def row_blocks(count_here, count_next, member, group):
    blocks = pl.cdiv(count_here, LANES)
    mine = jnp.maximum((blocks - member + group - 1) // group, 0)
    return jnp.where(count_next > 0, mine, 0)


def live_rows(start, member, count, group=4):
    row = lax.broadcasted_iota(jnp.int32, (1, ROWS), 1)
    slot = (group * (start // LANES) + member) * LANES + row
    return slot + jnp.where(row >= LANES, (group - 1) * LANES, 0) < count


def col_steps(count):
    return (count + COLS - 1) // COLS


LTS = COLS // LANES
SUB = 32
WIDE = 1536


def scores(xa, ya_ref, c, cols=COLS):
    return jnp.dot(xa, ya_ref[:, pl.ds(aligned(c, cols), cols)], preferred_element_type=F32)


def piped(count, matmul, work, first_ref, second_ref, load=None, store=None):
    load = load or (lambda c: None)
    store = store or (lambda c, state: None)
    first_ref[...] = matmul(0)

    def pair(i, _):
        here, there = 2 * i, 2 * i + 1
        states = load(here), load(there)
        second_ref[...] = matmul(there)
        one = work(here, first_ref, states[0])
        first_ref[...] = matmul(jnp.minimum(there + 1, count - 1))
        two = work(there, second_ref, states[1])
        store(here, one)
        store(there, two)
        return 0

    lax.fori_loop(0, count // 2, pair, 0)

    @pl.when(count % 2 == 1)
    def _():
        store(count - 1, work(count - 1, first_ref, load(count - 1)))


def adder(acc_refs):
    def store(c, sums):
        for k, acc_ref in enumerate(acc_refs):
            lts = len(sums[k])
            for lt in range(lts):
                acc_ref[:, lane_tile(c, lt, lts)] += sums[k][lt]

    return store


def lane_tile(c, lt, lts=LTS):
    return pl.ds(aligned(c * lts + lt, LANES), LANES)


def piece_of(z_ref, rg, lt, size=SUB):
    return z_ref[rg : rg + size, lt * LANES : (lt + 1) * LANES]


def in_steps(total, visit):
    for start in range(0, total, WIDE):
        visit(start, slice(start, start + WIDE))


def kernel_a(
    counts, x0, x1, x2, x3, y0, y1, y2, y3,
    counts_ref, xg_ref, yg_ref, xt_ref, xa_ref, base_ref, gb_ref, log_ref,
    copied, ya_ref, xat_ref, za_ref, zb_ref, top_ref, sum_ref,
):
    _, count_here, count_next, member = around(counts)
    group = 4
    mine = row_blocks(count_here, count_next, member, group)
    nb = (mine + 1) // 2
    nc = col_steps(count_next)
    local = x0.shape[1]
    own = pltpu.make_async_copy(x0, xg_ref.at[:, pl.ds(aligned(member, local), local)], copied)
    own.start()
    for i in range(counts.shape[0]):
        counts_ref[i] = counts[i]
    for k, y_ref in enumerate((y0, y1, y2, y3)):
        yg_ref[:, pl.ds(aligned(member ^ k, local), local)] = y_ref[...]
    for k, x_ref in enumerate((x1, x2, x3)):
        xg_ref[:, pl.ds(aligned(member ^ (k + 1), local), local)] = x_ref[...]
    sum_ref[...] = jnp.zeros_like(sum_ref)

    def prepare(start, cols):
        feats = yg_ref[:, cols]
        pot = live_pot(feats, start, count_next)
        gb_ref[:, cols] = pot
        write_augmented(ya_ref, start, feats, pot, False)

    in_steps(group * local, prepare)
    own.wait()
    for k in range(local // LANES):
        lanes = slice(k * LANES, (k + 1) * LANES)
        block_id = group * k + member
        piece = xg_ref[:, pl.ds(aligned(block_id, LANES), LANES)]
        xt_ref[:, lanes] = piece
        pot = live_pot(piece, block_id * LANES, count_here) + SHIFT
        base_ref[:, lanes] = pot
        write_augmented(xat_ref, k * LANES, piece, pot, True)
        xa_ref[lanes, :] = jnp.transpose(xat_ref[:, lanes]).astype(BF16)

    def exact():
        top_ref[...] = jnp.full(top_ref.shape, MASKED, F32)
        sum_ref[...] = jnp.zeros_like(sum_ref)

        def row_visit(b, _):
            xa = xa_ref[pl.ds(aligned(b, ROWS), ROWS), :]

            def load(c):
                return [(top_ref[:, lane_tile(c, lt)], sum_ref[:, lane_tile(c, lt)]) for lt in range(LTS)]

            def work(c, z_ref, state):
                after = []
                for lt, (old, total) in enumerate(state):
                    tile = z_ref[:, lt * LANES : (lt + 1) * LANES].reshape(ROWS // 8, 8, LANES)
                    top = jnp.maximum(old, jnp.max(tile, axis=0))
                    total = total * jnp.exp(old - top) + jnp.sum(jnp.exp(tile - top[None]), axis=0)
                    after.append((top, total))
                return after

            def store(c, state):
                for lt, (top, total) in enumerate(state):
                    top_ref[:, lane_tile(c, lt)] = top
                    sum_ref[:, lane_tile(c, lt)] = total

            piped(nc, lambda c: scores(xa, ya_ref, c), work, za_ref, zb_ref, load, store)
            return 0

        lax.fori_loop(0, nb, row_visit, 0)
        tops = top_ref[...]
        top = jnp.max(tops, axis=0, keepdims=True)
        total = jnp.sum(sum_ref[...] * jnp.exp(tops - top), axis=0, keepdims=True)
        log_ref[...] = top + jnp.log(jnp.maximum(total, TINY)) - SHIFT

    thin = 2 * LANES

    def quick_rows(first_block, blocks):
        halves = [xa_ref[pl.ds(aligned(first_block + k, LANES), LANES), :] for k in range(blocks)]

        def tile_sums(c, tiles):
            for t in range(tiles):
                totals = [jnp.zeros((8, LANES), F32) for _ in range(2)]
                for half in halves:
                    z = scores(half, ya_ref, c * tiles + t, thin)
                    for lt in range(2):
                        p = jnp.exp(z[:, lt * LANES : (lt + 1) * LANES])
                        totals[lt] = totals[lt] + jnp.sum(p.reshape(LANES // 8, 8, LANES), axis=0)
                for lt in range(2):
                    sum_ref[:, lane_tile(c * tiles + t, lt, 2)] += totals[lt]

        def pair(i, _):
            tile_sums(i, 4)
            return 0

        lax.fori_loop(0, nc // 2, pair, 0)

        @pl.when(nc % 2 == 1)
        def _():
            tile_sums(nc - 1, 2)

    def quick_visit(b, _):
        quick_rows(2 * b, 2)
        return 0

    lax.fori_loop(0, mine // 2, quick_visit, 0)

    @pl.when(mine % 2 == 1)
    def _():
        quick_rows(mine - 1, 1)

    total = jnp.sum(sum_ref[...], axis=0, keepdims=True)
    log_ref[...] = jnp.where(total > 0.0, jnp.log(jnp.maximum(total, TINY)) - SHIFT, MASKED)
    ids = lax.broadcasted_iota(jnp.int32, total.shape, 1)
    lowest = jnp.min(jnp.where(ids < count_next, total, 1.0))

    @pl.when((lowest < LOWEST) & (nb > 0))
    def _():
        exact()


def column_sums(c, z_ref, _):
    rows, cols = z_ref.shape
    sums = []
    for lt in range(cols // LANES):
        p = jnp.exp(z_ref[:, lt * LANES : (lt + 1) * LANES])
        sums.append(jnp.sum(p.reshape(rows // 8, 8, LANES), axis=0))
    return [sums]


def row_adder(sum_ref, push_ref=None, g_ref=None):
    def first(c, scores_of, kept, count):
        half = LANES
        for start in range(0, count, half):
            scored = scores_of(c, start, half)
            for rg in range(0, half, SUB):
                rows = slice(start + rg, start + rg + SUB)
                total = sum_ref[rows, :]
                push = push_ref[rows, :] if push_ref is not None else None
                for lt in range(LTS):
                    z = piece_of(scored, rg, lt)
                    p = jnp.exp(z)
                    total = total + p
                    kept[0][rows, lane_tile(c, lt)] = p.astype(kept[0].dtype)
                    if push is not None:
                        part = p * (g_ref[:, lane_tile(c, lt)] - z)
                        push = push + part
                        kept[1][rows, lane_tile(c, lt)] = part.astype(kept[1].dtype)
                sum_ref[rows, :] = total
                if push is not None:
                    push_ref[rows, :] = push

    return first


def column_parts(c, plan):
    sums = [[jnp.zeros((8, LANES), F32) for _ in range(LTS)] for _ in plan]
    for rg in range(0, ROWS, 8):
        for k, (kept_ref, weight_ref) in enumerate(plan):
            scale = weight_ref[rg : rg + 8, :]
            for lt in range(LTS):
                sums[k][lt] = sums[k][lt] + scale * kept_ref[rg : rg + 8, lane_tile(c, lt)]
    return sums


def two_stage(mine, nc, first, finish, second, store, matmul_of, kept):
    nb = (mine + 1) // 2
    alone = mine % 2 == 1

    def in_pairs(visit, put):
        put = put or (lambda c, sums: None)

        def pair(i, _):
            one, two = visit(2 * i), visit(2 * i + 1)
            put(2 * i, one)
            put(2 * i + 1, two)
            return 0

        lax.fori_loop(0, nc // 2, pair, 0)

        @pl.when(nc % 2 == 1)
        def _():
            put(nc - 1, visit(nc - 1))

    def stage(start, now, before, rows=ROWS):
        scores_of = matmul_of(start)

        def visit(c):
            first(c, scores_of, now, rows)
            if rows < ROWS:
                for ref in now:
                    ref[rows:, col_tile(c)] = jnp.zeros((ROWS - rows, COLS), ref.dtype)
            return second(c, before) if before else None

        in_pairs(visit, store if before else None)
        finish(start, rows)

    def tail(before):
        in_pairs(lambda c: second(c, before), store)

    even, odd = kept

    @pl.when((nb > 0) & alone)
    def _():
        stage(0, even, None, LANES)

    @pl.when((nb > 0) & jnp.logical_not(alone))
    def _():
        stage(0, even, None)

    def visit(b, _):
        start = pl.multiple_of(b * ROWS - jnp.where(alone, LANES, 0), LANES)

        @pl.when(b % 2 == 1)
        def _():
            stage(start, odd, even)

        @pl.when(b % 2 == 0)
        def _():
            stage(start, even, odd)

        return 0

    lax.fori_loop(1, nb, visit, 0)

    @pl.when((nb > 0) & (nb % 2 == 1))
    def _():
        tail(even)

    @pl.when((nb > 0) & (nb % 2 == 0))
    def _():
        tail(odd)


def col_tile(c):
    return pl.ds(aligned(c, COLS), COLS)


def split2(value):
    high = value.astype(BF16).astype(F32)
    return high, value - high


def row_totals(ref):
    return jnp.sum(jnp.transpose(ref[...]), axis=0, keepdims=True)


def spread(row):
    return jnp.transpose(jnp.broadcast_to(row, (LANES, ROWS)))


def laid(column):
    return jnp.transpose(jnp.broadcast_to(column, (ROWS, LANES)))[0:1, :]


def sweep(quick, exact, low_ref, lost=None):
    low_ref[...] = jnp.ones_like(low_ref)
    quick()
    again = jnp.min(low_ref[...]) < LOWEST
    if lost is not None:
        again = again | lost()

    @pl.when(again)
    def _():
        exact()


def row_lse(xa, ya_ref, nc, buffers, top_ref, sum_ref, push_ref=None, g_ref=None):
    top_ref[...] = jnp.full(top_ref.shape, MASKED, F32)
    sum_ref[...] = jnp.zeros_like(sum_ref)
    if push_ref is not None:
        push_ref[...] = jnp.zeros_like(push_ref)

    def work(c, z_ref, _):
        for rg in range(0, ROWS, SUB):
            rows = slice(rg, rg + SUB)
            old = top_ref[rows, :]
            pieces = [piece_of(z_ref, rg, lt) for lt in range(LTS)]
            top = old
            for z in pieces:
                top = jnp.maximum(top, z)
            fade = jnp.exp(old - top)
            total = sum_ref[rows, :] * fade
            push = push_ref[rows, :] * fade if push_ref is not None else None
            for lt, z in enumerate(pieces):
                p = jnp.exp(z - top)
                total = total + p
                if push is not None:
                    push = push + p * (g_ref[:, lane_tile(c, lt)] - z)
            top_ref[rows, :] = top
            sum_ref[rows, :] = total
            if push is not None:
                push_ref[rows, :] = push

    piped(nc, lambda c: scores(xa, ya_ref, c), work, *buffers)
    tops = top_ref[...]
    top = jnp.max(tops, axis=1, keepdims=True)
    fade = jnp.exp(tops - top)
    total = jnp.sum(sum_ref[...] * fade, axis=1, keepdims=True)
    if push_ref is None:
        return top, total
    return top, total, jnp.sum(push_ref[...] * fade, axis=1, keepdims=True)


def row_potential(xa):
    lane = lax.broadcasted_iota(jnp.int32, (ROWS, LANES), 1)
    wide = xa.astype(F32)
    old = jnp.sum(jnp.where((lane >= 32) & (lane < 35), wide, 0.0), axis=1, keepdims=True)
    return lane, wide, old


def with_row_potential(lane, wide, pot):
    high, middle, low = split3(pot)
    new = jnp.where(lane == 32, high, jnp.where(lane == 33, middle, jnp.where(lane == 34, low, wide)))
    return new.astype(BF16)


def kernel_b(counts, xa_ref, yg_ref, gb_ref, l0, l1, l2, l3, g_ref, col_ref, ya_ref, za_ref, zb_ref, p_ref, q_ref, top_ref, sum_ref, weight_ref, low_ref, most_ref, acc_ref):
    _, count_here, count_next, member = around(counts)
    mine = row_blocks(count_here, count_next, member, 4)
    nb = (mine + 1) // 2
    nc = col_steps(count_next)

    def prepare(start, cols):
        logs = [ref[:, cols] for ref in (l0, l1, l2, l3)]
        top = jnp.maximum(jnp.maximum(logs[0], logs[1]), jnp.maximum(logs[2], logs[3]))
        total = sum(jnp.exp(one - top) for one in logs)
        ids = start + lax.broadcasted_iota(jnp.int32, (1, WIDE), 1)
        pot = jnp.where(ids < count_next, -DAMPING * (top + jnp.log(total)), 0.0)
        g_ref[:, cols] = pot
        write_augmented(ya_ref, start, yg_ref[:, cols], pot + gb_ref[:, cols], False)

    in_steps(yg_ref.shape[1], prepare)

    buffers = za_ref, zb_ref

    def quick():
        acc_ref[...] = jnp.zeros_like(acc_ref)

        def matmul_of(first_row):
            sum_ref[...] = jnp.zeros_like(sum_ref)
            return lambda c, start, size: scores(
                xa_ref[pl.ds(pl.multiple_of(first_row + start, size), size), :], ya_ref, c
            )

        def finish(start, rows):
            row = lax.broadcasted_iota(jnp.int32, (1, ROWS), 1)
            live = live_rows(start, member, count_here) & (row < rows)
            total = row_totals(sum_ref)
            low_ref[...] = jnp.minimum(low_ref[...], jnp.where(live, total, 1.0))
            pot = -DAMPING * (jnp.log(jnp.maximum(total, TINY)) - SHIFT)
            weight = jnp.where(live, jnp.exp(pot - SHIFT), 0.0)
            weight_ref[...] = spread(weight)
            most_ref[...] = jnp.maximum(most_ref[...], weight)

        two_stage(
            mine, nc, row_adder(sum_ref), finish, lambda c, kept: column_parts(c, [(kept[0], weight_ref)]),
            adder([acc_ref]), matmul_of, ((p_ref,), (q_ref,)),
        )

    def exact():
        acc_ref[...] = jnp.zeros_like(acc_ref)

        def row_visit(b, _):
            xa = xa_ref[pl.ds(aligned(b, ROWS), ROWS), :]
            lane, wide, old = row_potential(xa)
            live = old > 0.5 * MASKED
            top, total = row_lse(xa, ya_ref, nc, buffers, top_ref, sum_ref)
            pot = -DAMPING * (top + jnp.log(total) - SHIFT)
            xb = with_row_potential(lane, wide, jnp.where(live, pot + old - SHIFT, MASKED))
            piped(nc, lambda c: scores(xb, ya_ref, c), column_sums, *buffers, store=adder([acc_ref]))
            return 0

        lax.fori_loop(0, nb, row_visit, 0)

    def lost():
        total = jnp.sum(acc_ref[...], axis=0, keepdims=True)
        ids = lax.broadcasted_iota(jnp.int32, total.shape, 1)
        least = jnp.min(jnp.where((ids < count_next) & (nb > 0), total, 1.0))
        return least < jnp.max(most_ref[...]) * 2.0**-91

    most_ref[...] = jnp.zeros_like(most_ref)
    sweep(quick, exact, low_ref, lost)
    col_ref[...] = jnp.sum(acc_ref[...], axis=0, keepdims=True)


def kernel_c(
    counts, xa_ref, xt_ref, base_ref, yg_ref, gb_ref, g_ref, c0, c1, c2, c3,
    rows_ref, g2_ref, col_ref,
    ya_ref, za_ref, zb_ref, p_ref, w_ref, q_ref, v_ref, top_ref, sum_ref, push_ref, adj_ref, low_ref, cost_ref, weight_ref, xat_ref, acc_ref, acc0_ref, acc1_ref, acc2_ref,
):
    _, count_here, count_next, member = around(counts)
    mine = row_blocks(count_here, count_next, member, 4)
    nb = (mine + 1) // 2
    nc = col_steps(count_next)

    def prepare(start, cols):
        total = (c0[:, cols] + c1[:, cols]) + (c2[:, cols] + c3[:, cols])
        ids = start + lax.broadcasted_iota(jnp.int32, (1, WIDE), 1)
        log = jnp.log(jnp.maximum(total, TINY)) - g_ref[:, cols]
        pot = jnp.where(ids < count_next, -DAMPING * log, 0.0)
        g2_ref[:, cols] = pot
        write_augmented(ya_ref, start, yg_ref[:, cols], pot + gb_ref[:, cols], False)

    in_steps(yg_ref.shape[1], prepare)

    buffers = za_ref, zb_ref
    accs = acc0_ref, acc1_ref, acc2_ref

    ids = lax.broadcasted_iota(jnp.int32, g_ref.shape, 1)
    centre = jnp.sum(jnp.where(ids < count_next, g_ref[...], 0.0), axis=1, keepdims=True)
    centre = centre / (DAMPING * jnp.maximum(count_next, 1).astype(F32)) + 3.0
    cost_ref[...] = g2_ref[...] + (SHIFT - centre)

    line = lax.broadcasted_iota(jnp.int32, rows_ref.shape, 0)
    rows_ref[...] = jnp.where(line == 3, MASKED, 0.0)

    def close_rows(start, rows, row_log, mean_cost):
        rows_here = pl.ds(pl.multiple_of(start, LANES), ROWS)
        live = live_rows(start, member, count_here) & (lax.broadcasted_iota(jnp.int32, (1, ROWS), 1) < rows)
        pot = jnp.where(live, -DAMPING * row_log, 0.0)
        row_sum = jnp.where(live, jnp.exp(row_log + pot), 0.0)
        adjoint = jnp.where(live, mean_cost + centre, 0.0)
        full = jnp.where(live, pot + base_ref[:, rows_here] - SHIFT, MASKED)
        rows_ref[0:1, rows_here] = adjoint
        rows_ref[1:2, rows_here] = jnp.where(row_sum > 0.0, 1.0 / jnp.maximum(row_sum, TINY), 0.0)
        rows_ref[2:3, rows_here] = pot
        rows_ref[3:4, rows_here] = full
        return live, pot, adjoint, full

    def quick():
        acc_ref[...] = jnp.zeros_like(acc_ref)

        def matmul_of(first_row):
            sum_ref[...] = jnp.zeros_like(sum_ref)
            push_ref[...] = jnp.zeros_like(push_ref)
            return lambda c, start, size: scores(
                xa_ref[pl.ds(pl.multiple_of(first_row + start, size), size), :], ya_ref, c
            )

        def finish(start, rows):
            total = row_totals(sum_ref)
            safe = jnp.maximum(total, TINY)
            live, pot, adjoint, _ = close_rows(start, rows, jnp.log(safe) - SHIFT, row_totals(push_ref) / safe)
            low_ref[...] = jnp.minimum(low_ref[...], jnp.where(live, total, 1.0))
            weight = jnp.where(live, jnp.exp(pot - SHIFT), 0.0)
            row = lax.broadcasted_iota(jnp.int32, (16, ROWS), 0)
            packed = jnp.zeros((16, ROWS), F32)
            for k, piece in enumerate((*split2(weight), *split2(weight * adjoint))):
                packed = jnp.where(row == k, piece, packed)
            weight_ref[...] = packed.astype(BF16)

        def second(c, kept):
            weights = weight_ref[...]
            plan = jnp.dot(weights, kept[0][:, col_tile(c)], preferred_element_type=F32)
            cost = jnp.dot(weights, kept[1][:, col_tile(c)], preferred_element_type=F32)
            return plan, cost

        def store(c, sums):
            acc_ref[0:16, col_tile(c)] += sums[0]
            acc_ref[16:32, col_tile(c)] += sums[1]

        two_stage(
            mine, nc, row_adder(sum_ref, push_ref, cost_ref), finish, second, store, matmul_of,
            ((p_ref, w_ref), (q_ref, v_ref)),
        )
        acc0_ref[0:1, :] = acc_ref[0:1, :] + acc_ref[1:2, :]
        acc1_ref[0:1, :] = acc_ref[16:17, :] + acc_ref[17:18, :]
        acc2_ref[0:1, :] = acc_ref[2:3, :] + acc_ref[3:4, :]
        for ref in accs:
            ref[1:8, :] = jnp.zeros((7, ref.shape[1]), F32)

    def exact():
        for ref in accs:
            ref[...] = jnp.zeros_like(ref)

        def row_visit(b, _):
            xa = xa_ref[pl.ds(aligned(b, ROWS), ROWS), :]
            top, total, push = row_lse(xa, ya_ref, nc, buffers, top_ref, sum_ref, push_ref, cost_ref)
            _, pot, adjoint, full = close_rows(
                b * ROWS, ROWS, laid(top + jnp.log(total) - SHIFT), laid(push / total)
            )
            top_ref[...] = spread(pot - SHIFT)
            adj_ref[...] = spread(adjoint)
            write_augmented(xat_ref, 0, xt_ref[:, pl.ds(aligned(b, ROWS), ROWS)], full, True)
            xb = jnp.transpose(xat_ref[...]).astype(BF16)

            def work(c, z_ref, _):
                sums = [[jnp.zeros((8, LANES), F32) for _ in range(LTS)] for _ in range(3)]
                for rg in range(0, ROWS, 8):
                    pot_here = top_ref[rg : rg + 8, :]
                    adj_here = adj_ref[rg : rg + 8, :]
                    for lt in range(LTS):
                        tile = piece_of(z_ref, rg, lt, 8)
                        p = jnp.exp(tile)
                        sums[0][lt] = sums[0][lt] + p
                        sums[1][lt] = sums[1][lt] + p * (cost_ref[:, lane_tile(c, lt)] + (pot_here - tile))
                        sums[2][lt] = sums[2][lt] + p * adj_here
                return sums

            piped(nc, lambda c: scores(xb, ya_ref, c), work, *buffers, store=adder(accs))
            return 0

        lax.fori_loop(0, nb, row_visit, 0)

    sweep(quick, exact, low_ref)
    mass = jnp.sum(acc0_ref[...], axis=0, keepdims=True)
    slots = mass.shape[1]
    col_ref[:, 0:slots] = mass
    push = jnp.sum(acc1_ref[...], axis=0, keepdims=True)
    col_ref[:, slots : 2 * slots] = push + centre * mass
    col_ref[:, 2 * slots :] = jnp.sum(acc2_ref[...], axis=0, keepdims=True)


def kernel_d(
    counts, xt_ref, rows_ref, yg_ref, gb_ref, g2_ref, s0, s1, s2, s3,
    stat_ref, send_ref,
    ya_ref, xat_ref, xb_ref, p_ref, q_ref, first_ref, second_ref, weight_ref, acc_ref,
):
    _, count_here, count_next, member = around(counts)
    mine = row_blocks(count_here, count_next, member, 4)
    nb = (mine + 1) // 2
    nc = col_steps(count_next)
    slots = yg_ref.shape[1]
    local = xt_ref.shape[1]
    acc_ref[...] = jnp.zeros_like(acc_ref)

    def prepare(start, cols):
        mass, push, pulled = (
            (s0[:, part] + s1[:, part]) + (s2[:, part] + s3[:, part])
            for part in (pl.ds(start + k * slots, WIDE) for k in range(3))
        )
        inverse = jnp.where(mass > 0.0, 1.0 / jnp.maximum(mass, TINY), 0.0)
        pot = g2_ref[:, cols]
        stat_ref[0:1, cols] = pot + gb_ref[:, cols]
        stat_ref[1:2, cols] = push * inverse
        stat_ref[2:3, cols] = (push - DAMPING * pulled) * inverse
        stat_ref[3:4, cols] = inverse
        stat_ref[4:5, cols] = pot
        stat_ref[5:8, cols] = jnp.zeros((3, WIDE), F32)
        write_augmented(ya_ref, start, yg_ref[:, cols], pot + gb_ref[:, cols], False)

    in_steps(slots, prepare)
    for block in range(local // ROWS):
        @pl.when(2 * block < mine)
        def _():
            rows = slice(block * ROWS, (block + 1) * ROWS)
            write_augmented(xat_ref, 0, xt_ref[:, rows], rows_ref[3:4, rows], True)
            xb_ref[rows, :] = jnp.transpose(xat_ref[...]).astype(BF16)

    send_ref[:, slots : slots + local] = jnp.full((1, local), MASKED, F32)
    send_ref[:, slots + local :] = jnp.zeros((1, local), F32)

    def matmul_of(first_row):
        first_ref[...] = jnp.zeros_like(first_ref)
        second_ref[...] = jnp.zeros_like(second_ref)
        return lambda c, start, size: scores(
            xb_ref[pl.ds(pl.multiple_of(first_row + start, size), size), :], ya_ref, c
        )

    def sums(c, scores_of, kept, count):
        half = LANES
        for start in range(0, count, half):
            scored = scores_of(c, start, half)
            for rg in range(0, half, SUB):
                rows = slice(start + rg, start + rg + SUB)
                first = first_ref[rows, :]
                second = second_ref[rows, :]
                for lt in range(LTS):
                    p = jnp.exp(piece_of(scored, rg, lt))
                    kept[0][rows, lane_tile(c, lt)] = p
                    first = first + p * stat_ref[1:2, lane_tile(c, lt)]
                    second = second + p * stat_ref[2:3, lane_tile(c, lt)]
                first_ref[rows, :] = first
                second_ref[rows, :] = second

    def finish(start, rows):
        first, second = row_totals(first_ref), row_totals(second_ref)
        rows_here = pl.ds(pl.multiple_of(start, LANES), ROWS)
        start_adj, inverse, pot, full = (rows_ref[k : k + 1, rows_here] for k in range(4))
        middle_adj = start_adj - DAMPING * first * inverse
        last_adj = start_adj - DAMPING * second * inverse
        weight_ref[...] = spread(middle_adj)
        send_ref[:, pl.ds(pl.multiple_of(slots + start, LANES), ROWS)] = full
        send_ref[:, pl.ds(pl.multiple_of(slots + local + start, LANES), ROWS)] = 1.0 + DAMPING * last_adj - pot

    two_stage(
        mine, nc, sums, finish, lambda c, kept: column_parts(c, [(kept[0], weight_ref)]), adder([acc_ref]), matmul_of,
        ((p_ref,), (q_ref,)),
    )
    send_ref[:, 0:slots] = jnp.sum(acc_ref[...], axis=0, keepdims=True)


def kernel_f(counts, p0, p1, p2, p3, stat_ref, col_ref, early_ref, parts_ref):
    member = lax.axis_index("cell")
    slots = stat_ref.shape[1]
    local = early_ref.shape[1] - slots
    for k, ref in enumerate((p0, p1, p2, p3)):
        parts_ref[member ^ k] = ref[...]
    total = (p0[:, 0:slots] + p1[:, 0:slots]) + (p2[:, 0:slots] + p3[:, 0:slots])
    last = stat_ref[1:2, :] - DAMPING * total * stat_ref[3:4, :]
    col_ref[0:1, :] = stat_ref[0:1, :]
    col_ref[1:2, :] = DAMPING * last - stat_ref[4:5, :]
    for block in range(slots // LANES):
        owner, place = block % 4, block // 4
        lanes = slice(block * LANES, (block + 1) * LANES)
        for k in range(2):
            at = slots + k * local + place * LANES
            early_ref[k : k + 1, lanes] = parts_ref[owner, :, at : at + LANES]
    here = pl.ds(aligned(member, local), local)
    early_ref[:, slots:] = col_ref[:, here]


def kernel_e(
    counts, *refs, earlier,
):
    own_ref, rowpot_ref, other_ref, colpot_ref = refs[:4]
    local, slots = own_ref.shape[1], other_ref.shape[1]
    before, here, after, member = around(counts)
    if earlier:
        out_ref, xw_ref, tile_ref, ys_ref, beta_ref, za_ref, zb_ref, pull_ref, sum_ref = refs[4:]
        count_cols = before
        count_rows = jnp.clip(here - member * local, 0, local)
        nb = jnp.where(count_cols > 0, (count_rows + ROWS - 1) // ROWS, 0)
        pot_at = slots
    else:
        out_refs = refs[4:8]
        xw_ref, tile_ref, ys_ref, beta_ref, za_ref, zb_ref, pull_ref, sum_ref, out_ref = refs[8:]
        count_cols = after
        nb = (row_blocks(here, after, member, 4) + 1) // 2
        pot_at = slots
    nc = col_steps(count_cols)
    out_ref[...] = jnp.zeros_like(out_ref)

    def prepare(c, _):
        cols = pl.ds(aligned(c, COLS), COLS)
        write_augmented(tile_ref, 0, other_ref[:, cols], colpot_ref[0:1, cols], False)
        ys_ref[cols, :] = jnp.transpose(tile_ref[...]).astype(BF16)
        beta_ref[cols, :] = jnp.transpose(jnp.broadcast_to(colpot_ref[1:2, cols], (LANES, COLS)))
        return 0

    @pl.when(nb > 0)
    def _():
        lax.fori_loop(0, nc, prepare, 0)

    def row_visit(b, _):
        rows_here = pl.ds(aligned(b, ROWS), ROWS)
        own = own_ref[:, rows_here]
        pots = rowpot_ref[0:1, pl.ds(aligned(b + pot_at // ROWS, ROWS), ROWS)]
        write_augmented(xw_ref, 0, own, pots, True)
        xw = xw_ref[...]
        if earlier:
            alpha = rowpot_ref[1:2, pl.ds(aligned(b + pot_at // ROWS, ROWS), ROWS)]
        else:
            alpha = rowpot_ref[0:1, pl.ds(aligned(b + (pot_at + local) // ROWS, ROWS), ROWS)]
        sum_ref[...] = jnp.zeros_like(sum_ref)
        pull_ref[...] = jnp.zeros_like(pull_ref)

        def matmul(c):
            return jnp.dot(ys_ref[pl.ds(aligned(c, COLS), COLS), :], xw, preferred_element_type=F32)

        def work(c, z_ref, _):
            rounded = []
            sums = [jnp.zeros((8, LANES), F32) for _ in range(ROWS // LANES)]
            for jg in range(0, COLS, 16):
                beta = beta_ref[pl.ds(pl.multiple_of(c * COLS + jg, 16), 16), :]
                line = []
                for lt in range(ROWS // LANES):
                    tile = piece_of(z_ref, jg, lt, 16)
                    grad = jnp.exp(tile) * (tile + (alpha[:, lt * LANES : (lt + 1) * LANES] + beta))
                    sums[lt] = sums[lt] + (grad[0:8] + grad[8:16])
                    line.append(grad.astype(BF16))
                rounded.append(jnp.concatenate(line, axis=1))
            for lt in range(ROWS // LANES):
                sum_ref[:, lt * LANES : (lt + 1) * LANES] += sums[lt]
            feats = other_ref[:, pl.ds(aligned(c, COLS), COLS)]
            pull_ref[...] += jnp.dot(feats, jnp.concatenate(rounded, axis=0), preferred_element_type=F32)

        piped(nc, matmul, work, za_ref, zb_ref)
        total = jnp.sum(sum_ref[...], axis=0, keepdims=True)
        out_ref[:, rows_here] = 2.0 * (own.astype(F32) * total - pull_ref[...])
        return 0

    lax.fori_loop(0, nb, row_visit, 0)
    if not earlier:
        width = local // 4
        for k, ref in enumerate(out_refs):
            ref[...] = out_ref[:, pl.ds(pl.multiple_of((member ^ k) * width, LANES), width)]


def kernel_g(counts, target_ref, p0, p1, p2, p3, out_ref):
    member = lax.axis_index("cell")
    for k, ref in enumerate((p0, p1, p2, p3)):
        for i in range(ref.shape[1] // LANES):
            lanes = pl.ds(aligned(4 * i + (member ^ k), LANES), LANES)
            out_ref[:, lanes] = target_ref[:, lanes] + ref[:, i * LANES : (i + 1) * LANES]


def run(body, name, outs, scratch, limit, counts, *operands, flops=0, first=pltpu.VMEM, counts_out=False):
    vmem = pl.BlockSpec(memory_space=pltpu.VMEM)
    smem = pl.BlockSpec(memory_space=pltpu.SMEM)
    out_specs = jax.tree.map(lambda _: vmem, outs)
    if counts_out:
        out_specs = (smem, *out_specs[1:])
    return pl.pallas_call(
        body,
        name=name,
        out_shape=outs,
        in_specs=[smem, pl.BlockSpec(memory_space=first)] + [vmem] * (len(operands) - 1),
        out_specs=out_specs,
        scratch_shapes=scratch,
        compiler_params=pltpu.CompilerParams(vmem_limit_bytes=limit * 1024 * 1024),
        cost_estimate=pl.CostEstimate(flops=flops, bytes_accessed=4_000_000, transcendentals=9_000_000),
    )(counts, *operands)


def shape(*dims, dtype=F32):
    return jax.ShapeDtypeStruct(dims, dtype)


def shifted(block, distance):
    size = lax.axis_size("tm")
    route = [(i - distance, i) for i in range(size) if 0 <= i - distance < size]
    return lax.ppermute(block, "tm", route)


def from_later(block, k):
    times, size = lax.axis_size("tm"), lax.axis_size("cell")
    route = [((t + 1) * size + (i ^ k), t * size + i) for t in range(times - 1) for i in range(size)]
    return lax.ppermute(block, ("tm", "cell"), route)


def swapped(block, k):
    return lax.ppermute(block, "cell", [(i, i ^ k) for i in range(lax.axis_size("cell"))])


def exchanged(block):
    near = swapped(block, 1)
    far = swapped(block, 2)
    return [block, near, far, swapped(far, 1)]


def per_device(embedding, counts):
    feat_dim, local = embedding.shape
    group = lax.axis_size("cell")
    slots = local * group

    ahead, ahead_far = from_later(embedding, 0), from_later(embedding, 2)
    source_parts = exchanged(embedding)
    target_parts = [ahead, swapped(ahead, 1), ahead_far, swapped(ahead_far, 1)]

    flops = 2 * local * slots * DEPTH
    aug = pltpu.VMEM((DEPTH, slots), BF16)
    narrow = pltpu.VMEM((ROWS, LANES), F32)
    flat = pltpu.VMEM((1, ROWS), F32)
    tile = pltpu.VMEM((DEPTH, ROWS), F32)
    wide = pltpu.VMEM((ROWS, slots), F32)
    half = pltpu.VMEM((ROWS, slots), BF16)
    turned_rows = pltpu.VMEM((16, ROWS), BF16)
    buffers = [pltpu.VMEM((ROWS, COLS), F32)] * 2
    long = pltpu.VMEM((8, slots), F32)
    counts, grouped, targets, dealt, xa, base, gb, log = run(
        kernel_a, "column_log",
        (
            shape(*counts.shape, dtype=jnp.int32),
            shape(feat_dim, slots, dtype=BF16), shape(feat_dim, slots, dtype=BF16), shape(feat_dim, local, dtype=BF16),
            shape(local, DEPTH, dtype=BF16), shape(1, local), shape(1, slots), shape(1, slots),
        ),
        [pltpu.SemaphoreType.DMA, aug, pltpu.VMEM((DEPTH, local), F32), *buffers, long, long],
        16, counts, *source_parts, *target_parts, flops=flops, first=HBM, counts_out=True,
    )
    logs = exchanged(log)
    g1, col1 = run(
        kernel_b, "first_sweep",
        (shape(1, slots), shape(1, slots)),
        [aug, *buffers, wide, wide, narrow, narrow, narrow, flat, flat, long],
        24, counts, xa, targets, gb, *logs, flops=2 * flops,
    )
    grouped, col1 = lax.optimization_barrier((grouped, col1))
    earlier = shifted(grouped, 1)
    rows, g2, stats = run(
        kernel_c, "second_sweep",
        (shape(8, local), shape(1, slots), shape(1, 3 * slots)),
        [
            aug, *buffers, half, half, half, half, narrow, narrow, narrow, narrow, flat,
            pltpu.VMEM((1, slots), F32), turned_rows, tile, pltpu.VMEM((32, slots), F32), long, long, long,
        ],
        28, counts, xa, dealt, base, targets, gb, g1, *exchanged(col1), flops=2 * flops,
    )
    rows, earlier = lax.optimization_barrier((rows, earlier))
    stat, send = run(
        kernel_d, "adjoint",
        (shape(8, slots), shape(1, slots + 2 * local)),
        [aug, tile, pltpu.VMEM((local, DEPTH), BF16), wide, wide, narrow, narrow, narrow, long],
        24, counts, dealt, rows, targets, gb, g2, *exchanged(stats), flops=2 * flops,
    )
    col_pair, early = run(
        kernel_f, "assemble",
        (shape(2, slots), shape(2, slots + local)),
        [pltpu.VMEM((group, 1, slots + 2 * local), F32)],
        8, counts, *exchanged(send), stat,
    )
    early = shifted(early, 1)

    turned = [pltpu.VMEM((COLS, ROWS), F32)] * 2
    scratch_e = [
        pltpu.VMEM((DEPTH, ROWS), BF16), pltpu.VMEM((DEPTH, COLS), F32), pltpu.VMEM((slots, DEPTH), BF16),
        pltpu.VMEM((slots, LANES), F32), *turned, pltpu.VMEM((feat_dim, ROWS), F32), pltpu.VMEM((8, ROWS), F32),
    ]
    parts = run(
        functools.partial(kernel_e, earlier=False), "source_gradient", (shape(feat_dim, local // group),) * group,
        scratch_e + [pltpu.VMEM((feat_dim, local), F32)],
        16, counts, dealt, send, targets, col_pair, flops=2 * flops,
    )
    parts = [parts[0]] + [swapped(parts[k], k) for k in range(1, group)]
    target_grad = run(
        functools.partial(kernel_e, earlier=True), "target_gradient", shape(feat_dim, local), scratch_e,
        16, counts, embedding, early, earlier, early, flops=2 * flops,
    )
    return run(kernel_g, "total", shape(feat_dim, local), [], 8, counts, target_grad, *parts)


def solution(mesh):
    in_specs = (P(None, ("tm", "cell")), P())
    out_specs = P(None, ("tm", "cell"))
    return jax.shard_map(
        per_device, mesh=mesh, in_specs=in_specs, out_specs=out_specs, check_vma=False
    )
```

```python
import functools

import jax
import jax.numpy as jnp
from jax import lax
from jax.experimental import pallas as pl
from jax.experimental.pallas import tpu as pltpu
from jax.sharding import PartitionSpec as P

ENTROPY = 0.25
PENALTY = 5.0
DAMPING = PENALTY / (PENALTY + ENTROPY)
MASKED = -1e30
SQ_SCALE = 1.0 / ENTROPY
DOT_SCALE = 2.0 / ENTROPY
TINY = 1e-37
SHIFT = 44.0
LOWEST = 1e-24

ROWS = 256
COLS = 512
LANES = 128
DEPTH = 128
F32 = jnp.float32
BF16 = jnp.bfloat16


def split3(value):
    high = value.astype(BF16).astype(F32)
    rest = value - high
    middle = rest.astype(BF16).astype(F32)
    return high, middle, rest - middle


def write_augmented(out_ref, start, feats, pot, is_row):
    n = feats.shape[1]
    cols = pl.ds(start, n)
    scaled = feats.astype(F32) * DOT_SCALE if is_row else feats
    out_ref[0:32, cols] = scaled.astype(out_ref.dtype)
    first = 0 if is_row else 3
    ones_from = 3 if is_row else 0
    row = lax.broadcasted_iota(jnp.int32, (16, n), 0)
    tail = jnp.where((row >= ones_from) & (row < ones_from + 3), 1.0, 0.0)
    for k, piece in enumerate(split3(pot)):
        tail = jnp.where(row == first + k, piece, tail)
    out_ref[32:48, cols] = tail.astype(out_ref.dtype)
    out_ref[48:128, cols] = jnp.zeros((80, n), out_ref.dtype)


def square_sum(feats):
    wide = feats.astype(F32)
    return jnp.sum(wide * wide, axis=0, keepdims=True)


def live_pot(feats, start, count):
    ids = start + lax.broadcasted_iota(jnp.int32, (1, feats.shape[1]), 1)
    return jnp.where(ids < count, -SQ_SCALE * square_sum(feats), MASKED)


def aligned(index, size):
    return pl.multiple_of(index * size, size)


def around(counts):
    size = counts.shape[0]
    time, member = lax.axis_index("tm"), lax.axis_index("cell")
    before = jnp.where(time > 0, counts[jnp.maximum(time - 1, 0)], 0)
    after = jnp.where(time + 1 < size, counts[jnp.minimum(time + 1, size - 1)], 0)
    return before, counts[time], after, member


def row_blocks(count_here, count_next, member, group):
    blocks = pl.cdiv(count_here, LANES)
    mine = jnp.maximum((blocks - member + group - 1) // group, 0)
    return jnp.where(count_next > 0, mine, 0)


def live_rows(start, member, count, group=4):
    row = lax.broadcasted_iota(jnp.int32, (1, ROWS), 1)
    slot = (group * (start // LANES) + member) * LANES + row
    return slot + jnp.where(row >= LANES, (group - 1) * LANES, 0) < count


def col_steps(count):
    return (count + COLS - 1) // COLS


LTS = COLS // LANES
SUB = 32
WIDE = 1536


def scores(xa, ya_ref, c, cols=COLS):
    return jnp.dot(xa, ya_ref[:, pl.ds(aligned(c, cols), cols)], preferred_element_type=F32)


def piped(count, matmul, work, first_ref, second_ref, load=None, store=None):
    load = load or (lambda c: None)
    store = store or (lambda c, state: None)
    first_ref[...] = matmul(0)

    def pair(i, _):
        here, there = 2 * i, 2 * i + 1
        states = load(here), load(there)
        second_ref[...] = matmul(there)
        one = work(here, first_ref, states[0])
        first_ref[...] = matmul(jnp.minimum(there + 1, count - 1))
        two = work(there, second_ref, states[1])
        store(here, one)
        store(there, two)
        return 0

    lax.fori_loop(0, count // 2, pair, 0)

    @pl.when(count % 2 == 1)
    def _():
        store(count - 1, work(count - 1, first_ref, load(count - 1)))


def adder(acc_refs):
    def store(c, sums):
        for k, acc_ref in enumerate(acc_refs):
            lts = len(sums[k])
            for lt in range(lts):
                acc_ref[:, lane_tile(c, lt, lts)] += sums[k][lt]

    return store


def lane_tile(c, lt, lts=LTS):
    return pl.ds(aligned(c * lts + lt, LANES), LANES)


def piece_of(z_ref, rg, lt, size=SUB):
    return z_ref[rg : rg + size, lt * LANES : (lt + 1) * LANES]


def in_steps(total, visit):
    for start in range(0, total, WIDE):
        visit(start, slice(start, start + WIDE))


def kernel_a(
    counts, x0, x1, x2, x3, y0, y1, y2, y3,
    counts_ref, xg_ref, yg_ref, xt_ref, xa_ref, base_ref, gb_ref, log_ref,
    ya_ref, xat_ref, za_ref, zb_ref, top_ref, sum_ref,
):
    _, count_here, count_next, member = around(counts)
    group = 4
    mine = row_blocks(count_here, count_next, member, group)
    nb = (mine + 1) // 2
    nc = col_steps(count_next)
    local = x0.shape[1]
    for i in range(counts.shape[0]):
        counts_ref[i] = counts[i]
    for k, y_ref in enumerate((y0, y1, y2, y3)):
        yg_ref[:, pl.ds(aligned(member ^ k, local), local)] = y_ref[...]
    for k, x_ref in enumerate((x0, x1, x2, x3)):
        xg_ref[:, pl.ds(aligned(member ^ k, local), local)] = x_ref[...]
    sum_ref[...] = jnp.zeros_like(sum_ref)

    def prepare(start, cols):
        feats = yg_ref[:, cols]
        pot = live_pot(feats, start, count_next)
        gb_ref[:, cols] = pot
        write_augmented(ya_ref, start, feats, pot, False)

    in_steps(group * local, prepare)
    for k in range(local // LANES):
        lanes = slice(k * LANES, (k + 1) * LANES)
        block_id = group * k + member
        piece = xg_ref[:, pl.ds(aligned(block_id, LANES), LANES)]
        xt_ref[:, lanes] = piece
        pot = live_pot(piece, block_id * LANES, count_here) + SHIFT
        base_ref[:, lanes] = pot
        write_augmented(xat_ref, k * LANES, piece, pot, True)
        xa_ref[lanes, :] = jnp.transpose(xat_ref[:, lanes]).astype(BF16)

    def exact():
        top_ref[...] = jnp.full(top_ref.shape, MASKED, F32)
        sum_ref[...] = jnp.zeros_like(sum_ref)

        def row_visit(b, _):
            xa = xa_ref[pl.ds(aligned(b, ROWS), ROWS), :]

            def load(c):
                return [(top_ref[:, lane_tile(c, lt)], sum_ref[:, lane_tile(c, lt)]) for lt in range(LTS)]

            def work(c, z_ref, state):
                after = []
                for lt, (old, total) in enumerate(state):
                    tile = z_ref[:, lt * LANES : (lt + 1) * LANES].reshape(ROWS // 8, 8, LANES)
                    top = jnp.maximum(old, jnp.max(tile, axis=0))
                    total = total * jnp.exp(old - top) + jnp.sum(jnp.exp(tile - top[None]), axis=0)
                    after.append((top, total))
                return after

            def store(c, state):
                for lt, (top, total) in enumerate(state):
                    top_ref[:, lane_tile(c, lt)] = top
                    sum_ref[:, lane_tile(c, lt)] = total

            piped(nc, lambda c: scores(xa, ya_ref, c), work, za_ref, zb_ref, load, store)
            return 0

        lax.fori_loop(0, nb, row_visit, 0)
        tops = top_ref[...]
        top = jnp.max(tops, axis=0, keepdims=True)
        total = jnp.sum(sum_ref[...] * jnp.exp(tops - top), axis=0, keepdims=True)
        log_ref[...] = top + jnp.log(jnp.maximum(total, TINY)) - SHIFT

    thin = 2 * LANES

    def quick_rows(first_block, blocks):
        halves = [xa_ref[pl.ds(aligned(first_block + k, LANES), LANES), :] for k in range(blocks)]

        def tile_sums(c, tiles):
            for t in range(tiles):
                totals = [jnp.zeros((8, LANES), F32) for _ in range(2)]
                for half in halves:
                    z = scores(half, ya_ref, c * tiles + t, thin)
                    for lt in range(2):
                        p = jnp.exp(z[:, lt * LANES : (lt + 1) * LANES])
                        totals[lt] = totals[lt] + jnp.sum(p.reshape(LANES // 8, 8, LANES), axis=0)
                for lt in range(2):
                    sum_ref[:, lane_tile(c * tiles + t, lt, 2)] += totals[lt]

        def pair(i, _):
            tile_sums(i, 4)
            return 0

        lax.fori_loop(0, nc // 2, pair, 0)

        @pl.when(nc % 2 == 1)
        def _():
            tile_sums(nc - 1, 2)

    def quick_visit(b, _):
        quick_rows(2 * b, 2)
        return 0

    lax.fori_loop(0, mine // 2, quick_visit, 0)

    @pl.when(mine % 2 == 1)
    def _():
        quick_rows(mine - 1, 1)

    total = jnp.sum(sum_ref[...], axis=0, keepdims=True)
    log_ref[...] = jnp.where(total > 0.0, jnp.log(jnp.maximum(total, TINY)) - SHIFT, MASKED)
    ids = lax.broadcasted_iota(jnp.int32, total.shape, 1)
    lowest = jnp.min(jnp.where(ids < count_next, total, 1.0))

    @pl.when((lowest < LOWEST) & (nb > 0))
    def _():
        exact()


def column_sums(c, z_ref, _):
    rows, cols = z_ref.shape
    sums = []
    for lt in range(cols // LANES):
        p = jnp.exp(z_ref[:, lt * LANES : (lt + 1) * LANES])
        sums.append(jnp.sum(p.reshape(rows // 8, 8, LANES), axis=0))
    return [sums]


def row_adder(sum_ref, push_ref=None, g_ref=None):
    def first(c, scores_of, kept, count):
        half = LANES
        for start in range(0, count, half):
            scored = scores_of(c, start, half)
            for rg in range(0, half, SUB):
                rows = slice(start + rg, start + rg + SUB)
                total = sum_ref[rows, :]
                push = push_ref[rows, :] if push_ref is not None else None
                for lt in range(LTS):
                    z = piece_of(scored, rg, lt)
                    p = jnp.exp(z)
                    total = total + p
                    kept[0][rows, lane_tile(c, lt)] = p.astype(kept[0].dtype)
                    if push is not None:
                        part = p * (g_ref[:, lane_tile(c, lt)] - z)
                        push = push + part
                        kept[1][rows, lane_tile(c, lt)] = part.astype(kept[1].dtype)
                sum_ref[rows, :] = total
                if push is not None:
                    push_ref[rows, :] = push

    return first


def column_parts(c, plan):
    sums = [[jnp.zeros((8, LANES), F32) for _ in range(LTS)] for _ in plan]
    for rg in range(0, ROWS, 8):
        for k, (kept_ref, weight_ref) in enumerate(plan):
            scale = weight_ref[rg : rg + 8, :]
            for lt in range(LTS):
                sums[k][lt] = sums[k][lt] + scale * kept_ref[rg : rg + 8, lane_tile(c, lt)]
    return sums


def two_stage(mine, nc, first, finish, second, store, matmul_of, kept):
    nb = (mine + 1) // 2
    alone = mine % 2 == 1

    def in_pairs(visit, put):
        put = put or (lambda c, sums: None)

        def pair(i, _):
            one, two = visit(2 * i), visit(2 * i + 1)
            put(2 * i, one)
            put(2 * i + 1, two)
            return 0

        lax.fori_loop(0, nc // 2, pair, 0)

        @pl.when(nc % 2 == 1)
        def _():
            put(nc - 1, visit(nc - 1))

    def stage(start, now, before, rows=ROWS):
        scores_of = matmul_of(start)

        def visit(c):
            first(c, scores_of, now, rows)
            if rows < ROWS:
                for ref in now:
                    ref[rows:, col_tile(c)] = jnp.zeros((ROWS - rows, COLS), ref.dtype)
            return second(c, before) if before else None

        in_pairs(visit, store if before else None)
        finish(start, rows)

    def tail(before):
        in_pairs(lambda c: second(c, before), store)

    even, odd = kept

    @pl.when((nb > 0) & alone)
    def _():
        stage(0, even, None, LANES)

    @pl.when((nb > 0) & jnp.logical_not(alone))
    def _():
        stage(0, even, None)

    def visit(b, _):
        start = pl.multiple_of(b * ROWS - jnp.where(alone, LANES, 0), LANES)

        @pl.when(b % 2 == 1)
        def _():
            stage(start, odd, even)

        @pl.when(b % 2 == 0)
        def _():
            stage(start, even, odd)

        return 0

    lax.fori_loop(1, nb, visit, 0)

    @pl.when((nb > 0) & (nb % 2 == 1))
    def _():
        tail(even)

    @pl.when((nb > 0) & (nb % 2 == 0))
    def _():
        tail(odd)


def col_tile(c):
    return pl.ds(aligned(c, COLS), COLS)


def split2(value):
    high = value.astype(BF16).astype(F32)
    return high, value - high


def row_totals(ref):
    return jnp.sum(jnp.transpose(ref[...]), axis=0, keepdims=True)


def spread(row):
    return jnp.transpose(jnp.broadcast_to(row, (LANES, ROWS)))


def laid(column):
    return jnp.transpose(jnp.broadcast_to(column, (ROWS, LANES)))[0:1, :]


def sweep(quick, exact, low_ref, lost=None):
    low_ref[...] = jnp.ones_like(low_ref)
    quick()
    again = jnp.min(low_ref[...]) < LOWEST
    if lost is not None:
        again = again | lost()

    @pl.when(again)
    def _():
        exact()


def row_lse(xa, ya_ref, nc, buffers, top_ref, sum_ref, push_ref=None, g_ref=None):
    top_ref[...] = jnp.full(top_ref.shape, MASKED, F32)
    sum_ref[...] = jnp.zeros_like(sum_ref)
    if push_ref is not None:
        push_ref[...] = jnp.zeros_like(push_ref)

    def work(c, z_ref, _):
        for rg in range(0, ROWS, SUB):
            rows = slice(rg, rg + SUB)
            old = top_ref[rows, :]
            pieces = [piece_of(z_ref, rg, lt) for lt in range(LTS)]
            top = old
            for z in pieces:
                top = jnp.maximum(top, z)
            fade = jnp.exp(old - top)
            total = sum_ref[rows, :] * fade
            push = push_ref[rows, :] * fade if push_ref is not None else None
            for lt, z in enumerate(pieces):
                p = jnp.exp(z - top)
                total = total + p
                if push is not None:
                    push = push + p * (g_ref[:, lane_tile(c, lt)] - z)
            top_ref[rows, :] = top
            sum_ref[rows, :] = total
            if push is not None:
                push_ref[rows, :] = push

    piped(nc, lambda c: scores(xa, ya_ref, c), work, *buffers)
    tops = top_ref[...]
    top = jnp.max(tops, axis=1, keepdims=True)
    fade = jnp.exp(tops - top)
    total = jnp.sum(sum_ref[...] * fade, axis=1, keepdims=True)
    if push_ref is None:
        return top, total
    return top, total, jnp.sum(push_ref[...] * fade, axis=1, keepdims=True)


def row_potential(xa):
    lane = lax.broadcasted_iota(jnp.int32, (ROWS, LANES), 1)
    wide = xa.astype(F32)
    old = jnp.sum(jnp.where((lane >= 32) & (lane < 35), wide, 0.0), axis=1, keepdims=True)
    return lane, wide, old


def with_row_potential(lane, wide, pot):
    high, middle, low = split3(pot)
    new = jnp.where(lane == 32, high, jnp.where(lane == 33, middle, jnp.where(lane == 34, low, wide)))
    return new.astype(BF16)


def kernel_b(counts, xa_ref, yg_ref, gb_ref, l0, l1, l2, l3, g_ref, col_ref, ya_ref, za_ref, zb_ref, p_ref, q_ref, top_ref, sum_ref, weight_ref, low_ref, most_ref, acc_ref):
    _, count_here, count_next, member = around(counts)
    mine = row_blocks(count_here, count_next, member, 4)
    nb = (mine + 1) // 2
    nc = col_steps(count_next)

    def prepare(start, cols):
        logs = [ref[:, cols] for ref in (l0, l1, l2, l3)]
        top = jnp.maximum(jnp.maximum(logs[0], logs[1]), jnp.maximum(logs[2], logs[3]))
        total = sum(jnp.exp(one - top) for one in logs)
        ids = start + lax.broadcasted_iota(jnp.int32, (1, WIDE), 1)
        pot = jnp.where(ids < count_next, -DAMPING * (top + jnp.log(total)), 0.0)
        g_ref[:, cols] = pot
        write_augmented(ya_ref, start, yg_ref[:, cols], pot + gb_ref[:, cols], False)

    in_steps(yg_ref.shape[1], prepare)

    buffers = za_ref, zb_ref

    def quick():
        acc_ref[...] = jnp.zeros_like(acc_ref)

        def matmul_of(first_row):
            sum_ref[...] = jnp.zeros_like(sum_ref)
            return lambda c, start, size: scores(
                xa_ref[pl.ds(pl.multiple_of(first_row + start, size), size), :], ya_ref, c
            )

        def finish(start, rows):
            row = lax.broadcasted_iota(jnp.int32, (1, ROWS), 1)
            live = live_rows(start, member, count_here) & (row < rows)
            total = row_totals(sum_ref)
            low_ref[...] = jnp.minimum(low_ref[...], jnp.where(live, total, 1.0))
            pot = -DAMPING * (jnp.log(jnp.maximum(total, TINY)) - SHIFT)
            weight = jnp.where(live, jnp.exp(pot - SHIFT), 0.0)
            weight_ref[...] = spread(weight)
            most_ref[...] = jnp.maximum(most_ref[...], weight)

        two_stage(
            mine, nc, row_adder(sum_ref), finish, lambda c, kept: column_parts(c, [(kept[0], weight_ref)]),
            adder([acc_ref]), matmul_of, ((p_ref,), (q_ref,)),
        )

    def exact():
        acc_ref[...] = jnp.zeros_like(acc_ref)

        def row_visit(b, _):
            xa = xa_ref[pl.ds(aligned(b, ROWS), ROWS), :]
            lane, wide, old = row_potential(xa)
            live = old > 0.5 * MASKED
            top, total = row_lse(xa, ya_ref, nc, buffers, top_ref, sum_ref)
            pot = -DAMPING * (top + jnp.log(total) - SHIFT)
            xb = with_row_potential(lane, wide, jnp.where(live, pot + old - SHIFT, MASKED))
            piped(nc, lambda c: scores(xb, ya_ref, c), column_sums, *buffers, store=adder([acc_ref]))
            return 0

        lax.fori_loop(0, nb, row_visit, 0)

    def lost():
        total = jnp.sum(acc_ref[...], axis=0, keepdims=True)
        ids = lax.broadcasted_iota(jnp.int32, total.shape, 1)
        least = jnp.min(jnp.where((ids < count_next) & (nb > 0), total, 1.0))
        return least < jnp.max(most_ref[...]) * 2.0**-91

    most_ref[...] = jnp.zeros_like(most_ref)
    sweep(quick, exact, low_ref, lost)
    col_ref[...] = jnp.sum(acc_ref[...], axis=0, keepdims=True)


def kernel_c(
    counts, xa_ref, xt_ref, base_ref, yg_ref, gb_ref, g_ref, c0, c1, c2, c3,
    rows_ref, g2_ref, col_ref,
    ya_ref, za_ref, zb_ref, p_ref, w_ref, q_ref, v_ref, top_ref, sum_ref, push_ref, adj_ref, low_ref, cost_ref, weight_ref, xat_ref, acc_ref, acc0_ref, acc1_ref, acc2_ref,
):
    _, count_here, count_next, member = around(counts)
    mine = row_blocks(count_here, count_next, member, 4)
    nb = (mine + 1) // 2
    nc = col_steps(count_next)

    def prepare(start, cols):
        total = (c0[:, cols] + c1[:, cols]) + (c2[:, cols] + c3[:, cols])
        ids = start + lax.broadcasted_iota(jnp.int32, (1, WIDE), 1)
        log = jnp.log(jnp.maximum(total, TINY)) - g_ref[:, cols]
        pot = jnp.where(ids < count_next, -DAMPING * log, 0.0)
        g2_ref[:, cols] = pot
        write_augmented(ya_ref, start, yg_ref[:, cols], pot + gb_ref[:, cols], False)

    in_steps(yg_ref.shape[1], prepare)

    buffers = za_ref, zb_ref
    accs = acc0_ref, acc1_ref, acc2_ref

    ids = lax.broadcasted_iota(jnp.int32, g_ref.shape, 1)
    centre = jnp.sum(jnp.where(ids < count_next, g_ref[...], 0.0), axis=1, keepdims=True)
    centre = centre / (DAMPING * jnp.maximum(count_next, 1).astype(F32)) + 3.0
    cost_ref[...] = g2_ref[...] + (SHIFT - centre)

    line = lax.broadcasted_iota(jnp.int32, rows_ref.shape, 0)
    rows_ref[...] = jnp.where(line == 3, MASKED, 0.0)

    def close_rows(start, rows, row_log, mean_cost):
        rows_here = pl.ds(pl.multiple_of(start, LANES), ROWS)
        live = live_rows(start, member, count_here) & (lax.broadcasted_iota(jnp.int32, (1, ROWS), 1) < rows)
        pot = jnp.where(live, -DAMPING * row_log, 0.0)
        row_sum = jnp.where(live, jnp.exp(row_log + pot), 0.0)
        adjoint = jnp.where(live, mean_cost + centre, 0.0)
        full = jnp.where(live, pot + base_ref[:, rows_here] - SHIFT, MASKED)
        rows_ref[0:1, rows_here] = adjoint
        rows_ref[1:2, rows_here] = jnp.where(row_sum > 0.0, 1.0 / jnp.maximum(row_sum, TINY), 0.0)
        rows_ref[2:3, rows_here] = pot
        rows_ref[3:4, rows_here] = full
        return live, pot, adjoint, full

    def quick():
        acc_ref[...] = jnp.zeros_like(acc_ref)

        def matmul_of(first_row):
            sum_ref[...] = jnp.zeros_like(sum_ref)
            push_ref[...] = jnp.zeros_like(push_ref)
            return lambda c, start, size: scores(
                xa_ref[pl.ds(pl.multiple_of(first_row + start, size), size), :], ya_ref, c
            )

        def finish(start, rows):
            total = row_totals(sum_ref)
            safe = jnp.maximum(total, TINY)
            live, pot, adjoint, _ = close_rows(start, rows, jnp.log(safe) - SHIFT, row_totals(push_ref) / safe)
            low_ref[...] = jnp.minimum(low_ref[...], jnp.where(live, total, 1.0))
            weight = jnp.where(live, jnp.exp(pot - SHIFT), 0.0)
            row = lax.broadcasted_iota(jnp.int32, (16, ROWS), 0)
            packed = jnp.zeros((16, ROWS), F32)
            for k, piece in enumerate((*split2(weight), *split2(weight * adjoint))):
                packed = jnp.where(row == k, piece, packed)
            weight_ref[...] = packed.astype(BF16)

        def second(c, kept):
            weights = weight_ref[...]
            plan = jnp.dot(weights, kept[0][:, col_tile(c)], preferred_element_type=F32)
            cost = jnp.dot(weights, kept[1][:, col_tile(c)], preferred_element_type=F32)
            return plan, cost

        def store(c, sums):
            acc_ref[0:16, col_tile(c)] += sums[0]
            acc_ref[16:32, col_tile(c)] += sums[1]

        two_stage(
            mine, nc, row_adder(sum_ref, push_ref, cost_ref), finish, second, store, matmul_of,
            ((p_ref, w_ref), (q_ref, v_ref)),
        )
        acc0_ref[0:1, :] = acc_ref[0:1, :] + acc_ref[1:2, :]
        acc1_ref[0:1, :] = acc_ref[16:17, :] + acc_ref[17:18, :]
        acc2_ref[0:1, :] = acc_ref[2:3, :] + acc_ref[3:4, :]
        for ref in accs:
            ref[1:8, :] = jnp.zeros((7, ref.shape[1]), F32)

    def exact():
        for ref in accs:
            ref[...] = jnp.zeros_like(ref)

        def row_visit(b, _):
            xa = xa_ref[pl.ds(aligned(b, ROWS), ROWS), :]
            top, total, push = row_lse(xa, ya_ref, nc, buffers, top_ref, sum_ref, push_ref, cost_ref)
            _, pot, adjoint, full = close_rows(
                b * ROWS, ROWS, laid(top + jnp.log(total) - SHIFT), laid(push / total)
            )
            top_ref[...] = spread(pot - SHIFT)
            adj_ref[...] = spread(adjoint)
            write_augmented(xat_ref, 0, xt_ref[:, pl.ds(aligned(b, ROWS), ROWS)], full, True)
            xb = jnp.transpose(xat_ref[...]).astype(BF16)

            def work(c, z_ref, _):
                sums = [[jnp.zeros((8, LANES), F32) for _ in range(LTS)] for _ in range(3)]
                for rg in range(0, ROWS, 8):
                    pot_here = top_ref[rg : rg + 8, :]
                    adj_here = adj_ref[rg : rg + 8, :]
                    for lt in range(LTS):
                        tile = piece_of(z_ref, rg, lt, 8)
                        p = jnp.exp(tile)
                        sums[0][lt] = sums[0][lt] + p
                        sums[1][lt] = sums[1][lt] + p * (cost_ref[:, lane_tile(c, lt)] + (pot_here - tile))
                        sums[2][lt] = sums[2][lt] + p * adj_here
                return sums

            piped(nc, lambda c: scores(xb, ya_ref, c), work, *buffers, store=adder(accs))
            return 0

        lax.fori_loop(0, nb, row_visit, 0)

    sweep(quick, exact, low_ref)
    mass = jnp.sum(acc0_ref[...], axis=0, keepdims=True)
    slots = mass.shape[1]
    col_ref[:, 0:slots] = mass
    push = jnp.sum(acc1_ref[...], axis=0, keepdims=True)
    col_ref[:, slots : 2 * slots] = push + centre * mass
    col_ref[:, 2 * slots :] = jnp.sum(acc2_ref[...], axis=0, keepdims=True)


def kernel_d(
    counts, xt_ref, rows_ref, yg_ref, gb_ref, g2_ref, s0, s1, s2, s3,
    stat_ref, send_ref,
    ya_ref, xat_ref, xb_ref, p_ref, q_ref, first_ref, second_ref, weight_ref, acc_ref,
):
    _, count_here, count_next, member = around(counts)
    mine = row_blocks(count_here, count_next, member, 4)
    nb = (mine + 1) // 2
    nc = col_steps(count_next)
    slots = yg_ref.shape[1]
    local = xt_ref.shape[1]
    acc_ref[...] = jnp.zeros_like(acc_ref)

    def prepare(start, cols):
        mass, push, pulled = (
            (s0[:, part] + s1[:, part]) + (s2[:, part] + s3[:, part])
            for part in (pl.ds(start + k * slots, WIDE) for k in range(3))
        )
        inverse = jnp.where(mass > 0.0, 1.0 / jnp.maximum(mass, TINY), 0.0)
        pot = g2_ref[:, cols]
        stat_ref[0:1, cols] = pot + gb_ref[:, cols]
        stat_ref[1:2, cols] = push * inverse
        stat_ref[2:3, cols] = (push - DAMPING * pulled) * inverse
        stat_ref[3:4, cols] = inverse
        stat_ref[4:5, cols] = pot
        stat_ref[5:8, cols] = jnp.zeros((3, WIDE), F32)
        write_augmented(ya_ref, start, yg_ref[:, cols], pot + gb_ref[:, cols], False)

    in_steps(slots, prepare)
    for block in range(local // ROWS):
        @pl.when(2 * block < mine)
        def _():
            rows = slice(block * ROWS, (block + 1) * ROWS)
            write_augmented(xat_ref, 0, xt_ref[:, rows], rows_ref[3:4, rows], True)
            xb_ref[rows, :] = jnp.transpose(xat_ref[...]).astype(BF16)

    send_ref[:, slots : slots + local] = jnp.full((1, local), MASKED, F32)
    send_ref[:, slots + local :] = jnp.zeros((1, local), F32)

    def matmul_of(first_row):
        first_ref[...] = jnp.zeros_like(first_ref)
        second_ref[...] = jnp.zeros_like(second_ref)
        return lambda c, start, size: scores(
            xb_ref[pl.ds(pl.multiple_of(first_row + start, size), size), :], ya_ref, c
        )

    def sums(c, scores_of, kept, count):
        half = LANES
        for start in range(0, count, half):
            scored = scores_of(c, start, half)
            for rg in range(0, half, SUB):
                rows = slice(start + rg, start + rg + SUB)
                first = first_ref[rows, :]
                second = second_ref[rows, :]
                for lt in range(LTS):
                    p = jnp.exp(piece_of(scored, rg, lt))
                    kept[0][rows, lane_tile(c, lt)] = p
                    first = first + p * stat_ref[1:2, lane_tile(c, lt)]
                    second = second + p * stat_ref[2:3, lane_tile(c, lt)]
                first_ref[rows, :] = first
                second_ref[rows, :] = second

    def finish(start, rows):
        first, second = row_totals(first_ref), row_totals(second_ref)
        rows_here = pl.ds(pl.multiple_of(start, LANES), ROWS)
        start_adj, inverse, pot, full = (rows_ref[k : k + 1, rows_here] for k in range(4))
        middle_adj = start_adj - DAMPING * first * inverse
        last_adj = start_adj - DAMPING * second * inverse
        weight_ref[...] = spread(middle_adj)
        send_ref[:, pl.ds(pl.multiple_of(slots + start, LANES), ROWS)] = full
        send_ref[:, pl.ds(pl.multiple_of(slots + local + start, LANES), ROWS)] = 1.0 + DAMPING * last_adj - pot

    two_stage(
        mine, nc, sums, finish, lambda c, kept: column_parts(c, [(kept[0], weight_ref)]), adder([acc_ref]), matmul_of,
        ((p_ref,), (q_ref,)),
    )
    send_ref[:, 0:slots] = jnp.sum(acc_ref[...], axis=0, keepdims=True)


def kernel_f(counts, p0, p1, p2, p3, stat_ref, col_ref, early_ref, parts_ref):
    member = lax.axis_index("cell")
    slots = stat_ref.shape[1]
    local = early_ref.shape[1] - slots
    for k, ref in enumerate((p0, p1, p2, p3)):
        parts_ref[member ^ k] = ref[...]
    total = (p0[:, 0:slots] + p1[:, 0:slots]) + (p2[:, 0:slots] + p3[:, 0:slots])
    last = stat_ref[1:2, :] - DAMPING * total * stat_ref[3:4, :]
    col_ref[0:1, :] = stat_ref[0:1, :]
    col_ref[1:2, :] = DAMPING * last - stat_ref[4:5, :]
    for block in range(slots // LANES):
        owner, place = block % 4, block // 4
        lanes = slice(block * LANES, (block + 1) * LANES)
        for k in range(2):
            at = slots + k * local + place * LANES
            early_ref[k : k + 1, lanes] = parts_ref[owner, :, at : at + LANES]
    here = pl.ds(aligned(member, local), local)
    early_ref[:, slots:] = col_ref[:, here]


def kernel_e(counts, *refs, earlier):
    own_ref, rowpot_ref, other_ref, colpot_ref = refs[:4]
    local, slots = own_ref.shape[1], other_ref.shape[1]
    before, here, after, member = around(counts)
    if earlier:
        out_ref, tile_ref, xa_ref, ya_ref, alpha_ref, sum_ref, pull_ref = refs[4:]
        count_cols = before
        count_rows = jnp.clip(here - member * local, 0, local)
        nb = jnp.where(count_cols > 0, (count_rows + ROWS - 1) // ROWS, 0)
    else:
        out_refs = refs[4:8]
        tile_ref, xa_ref, ya_ref, alpha_ref, sum_ref, pull_ref, out_ref = refs[8:]
        count_cols = after
        nb = (row_blocks(here, after, member, 4) + 1) // 2
    nc = col_steps(count_cols)
    out_ref[...] = jnp.zeros_like(out_ref)

    def prepare(start, cols):
        @pl.when((nb > 0) & (start < count_cols))
        def _():
            write_augmented(ya_ref, start, other_ref[:, cols], colpot_ref[0:1, cols], False)

    in_steps(slots, prepare)

    def row_visit(b, _):
        rows_here = pl.ds(aligned(b, ROWS), ROWS)
        own = own_ref[:, rows_here]
        write_augmented(tile_ref, 0, own, rowpot_ref[0:1, pl.ds(aligned(b + slots // ROWS, ROWS), ROWS)], True)
        xa_ref[...] = jnp.transpose(tile_ref[...]).astype(BF16)
        if earlier:
            alpha = rowpot_ref[1:2, pl.ds(aligned(b + slots // ROWS, ROWS), ROWS)]
        else:
            alpha = rowpot_ref[0:1, pl.ds(aligned(b + (slots + local) // ROWS, ROWS), ROWS)]
        alpha_ref[...] = spread(alpha)
        sum_ref[...] = jnp.zeros_like(sum_ref)
        pull_ref[...] = jnp.zeros_like(pull_ref)

        def visit(c):
            rounded = []
            for start in range(0, ROWS, LANES):
                scored = scores(xa_ref[start : start + LANES, :], ya_ref, c)
                for rg in range(0, LANES, SUB):
                    rows = slice(start + rg, start + rg + SUB)
                    alpha = alpha_ref[rows, :]
                    total = sum_ref[rows, :]
                    line = []
                    for lt in range(LTS):
                        z = piece_of(scored, rg, lt)
                        grad = jnp.exp(z) * (z + (alpha + colpot_ref[1:2, lane_tile(c, lt)]))
                        total = total + grad
                        line.append(grad.astype(BF16))
                    sum_ref[rows, :] = total
                    rounded.append(jnp.concatenate(line, axis=1))
            return lax.dot_general(
                jnp.concatenate(rounded, axis=0), other_ref[:, col_tile(c)], (((1,), (1,)), ((), ())),
                preferred_element_type=F32,
            )

        def pair(i, _):
            pull_ref[...] += visit(2 * i) + visit(2 * i + 1)
            return 0

        lax.fori_loop(0, nc // 2, pair, 0)

        @pl.when(nc % 2 == 1)
        def _():
            pull_ref[...] += visit(nc - 1)

        pulled = jnp.concatenate([pull_ref[...], jnp.zeros((ROWS, LANES - 32), F32)], axis=1)
        out_ref[:, rows_here] = 2.0 * (own.astype(F32) * row_totals(sum_ref) - jnp.transpose(pulled)[0:32, :])
        return 0

    lax.fori_loop(0, nb, row_visit, 0)
    if not earlier:
        width = local // 4
        for k, ref in enumerate(out_refs):
            ref[...] = out_ref[:, pl.ds(pl.multiple_of((member ^ k) * width, LANES), width)]


def kernel_g(counts, target_ref, p0, p1, p2, p3, out_ref):
    member = lax.axis_index("cell")
    for k, ref in enumerate((p0, p1, p2, p3)):
        for i in range(ref.shape[1] // LANES):
            lanes = pl.ds(aligned(4 * i + (member ^ k), LANES), LANES)
            out_ref[:, lanes] = target_ref[:, lanes] + ref[:, i * LANES : (i + 1) * LANES]


def run(body, name, outs, scratch, limit, counts, *operands, flops=0, counts_out=False):
    vmem = pl.BlockSpec(memory_space=pltpu.VMEM)
    smem = pl.BlockSpec(memory_space=pltpu.SMEM)
    out_specs = jax.tree.map(lambda _: vmem, outs)
    if counts_out:
        out_specs = (smem, *out_specs[1:])
    return pl.pallas_call(
        body,
        name=name,
        out_shape=outs,
        in_specs=[smem] + [vmem] * len(operands),
        out_specs=out_specs,
        scratch_shapes=scratch,
        compiler_params=pltpu.CompilerParams(vmem_limit_bytes=limit * 1024 * 1024),
        cost_estimate=pl.CostEstimate(flops=flops, bytes_accessed=4_000_000, transcendentals=9_000_000),
    )(counts, *operands)


def shape(*dims, dtype=F32):
    return jax.ShapeDtypeStruct(dims, dtype)


def shifted(block, distance):
    size = lax.axis_size("tm")
    route = [(i - distance, i) for i in range(size) if 0 <= i - distance < size]
    return lax.ppermute(block, "tm", route)


def from_later(block, k):
    times, size = lax.axis_size("tm"), lax.axis_size("cell")
    route = [((t + 1) * size + (i ^ k), t * size + i) for t in range(times - 1) for i in range(size)]
    return lax.ppermute(block, ("tm", "cell"), route)


def swapped(block, k):
    return lax.ppermute(block, "cell", [(i, i ^ k) for i in range(lax.axis_size("cell"))])


def exchanged(block):
    near = swapped(block, 1)
    far = swapped(block, 2)
    return [block, near, far, swapped(far, 1)]


def per_device(embedding, counts):
    feat_dim, local = embedding.shape
    group = lax.axis_size("cell")
    slots = local * group

    ahead, ahead_far = from_later(embedding, 0), from_later(embedding, 2)
    source_parts = exchanged(embedding)
    target_parts = [ahead, swapped(ahead, 1), ahead_far, swapped(ahead_far, 1)]

    flops = 2 * local * slots * DEPTH
    aug = pltpu.VMEM((DEPTH, slots), BF16)
    narrow = pltpu.VMEM((ROWS, LANES), F32)
    flat = pltpu.VMEM((1, ROWS), F32)
    tile = pltpu.VMEM((DEPTH, ROWS), F32)
    wide = pltpu.VMEM((ROWS, slots), F32)
    half = pltpu.VMEM((ROWS, slots), BF16)
    turned_rows = pltpu.VMEM((16, ROWS), BF16)
    buffers = [pltpu.VMEM((ROWS, COLS), F32)] * 2
    long = pltpu.VMEM((8, slots), F32)
    counts, grouped, targets, dealt, xa, base, gb, log = run(
        kernel_a, "column_log",
        (
            shape(*counts.shape, dtype=jnp.int32),
            shape(feat_dim, slots, dtype=BF16), shape(feat_dim, slots, dtype=BF16), shape(feat_dim, local, dtype=BF16),
            shape(local, DEPTH, dtype=BF16), shape(1, local), shape(1, slots), shape(1, slots),
        ),
        [aug, pltpu.VMEM((DEPTH, local), F32), *buffers, long, long],
        16, counts, *source_parts, *target_parts, flops=flops, counts_out=True,
    )
    logs = exchanged(log)
    g1, col1 = run(
        kernel_b, "first_sweep",
        (shape(1, slots), shape(1, slots)),
        [aug, *buffers, wide, wide, narrow, narrow, narrow, flat, flat, long],
        24, counts, xa, targets, gb, *logs, flops=2 * flops,
    )
    grouped, col1 = lax.optimization_barrier((grouped, col1))
    earlier = shifted(grouped, 1)
    rows, g2, stats = run(
        kernel_c, "second_sweep",
        (shape(8, local), shape(1, slots), shape(1, 3 * slots)),
        [
            aug, *buffers, half, half, half, half, narrow, narrow, narrow, narrow, flat,
            pltpu.VMEM((1, slots), F32), turned_rows, tile, pltpu.VMEM((32, slots), F32), long, long, long,
        ],
        28, counts, xa, dealt, base, targets, gb, g1, *exchanged(col1), flops=2 * flops,
    )
    rows, earlier = lax.optimization_barrier((rows, earlier))
    stat, send = run(
        kernel_d, "adjoint",
        (shape(8, slots), shape(1, slots + 2 * local)),
        [aug, tile, pltpu.VMEM((local, DEPTH), BF16), wide, wide, narrow, narrow, narrow, long],
        24, counts, dealt, rows, targets, gb, g2, *exchanged(stats), flops=2 * flops,
    )
    col_pair, early = run(
        kernel_f, "assemble",
        (shape(2, slots), shape(2, slots + local)),
        [pltpu.VMEM((group, 1, slots + 2 * local), F32)],
        8, counts, *exchanged(send), stat,
    )
    early = shifted(early, 1)

    scratch_e = [
        tile, pltpu.VMEM((ROWS, DEPTH), BF16), aug, narrow, narrow, pltpu.VMEM((ROWS, feat_dim), F32),
    ]
    parts = run(
        functools.partial(kernel_e, earlier=False), "source_gradient", (shape(feat_dim, local // group),) * group,
        scratch_e + [pltpu.VMEM((feat_dim, local), F32)],
        16, counts, dealt, send, targets, col_pair, flops=2 * flops,
    )
    parts = [parts[0]] + [swapped(parts[k], k) for k in range(1, group)]
    target_grad = run(
        functools.partial(kernel_e, earlier=True), "target_gradient", shape(feat_dim, local), scratch_e,
        16, counts, embedding, early, earlier, early, flops=2 * flops,
    )
    return run(kernel_g, "total", shape(feat_dim, local), [], 8, counts, target_grad, *parts)


def solution(mesh):
    in_specs = (P(None, ("tm", "cell")), P())
    out_specs = P(None, ("tm", "cell"))
    return jax.shard_map(
        per_device, mesh=mesh, in_specs=in_specs, out_specs=out_specs, check_vma=False
    )
```

```python
import functools

import jax
import jax.numpy as jnp
from jax import lax
from jax.experimental import pallas as pl
from jax.experimental.pallas import tpu as pltpu
from jax.sharding import PartitionSpec as P

ENTROPY = 0.25
PENALTY = 5.0
DAMPING = PENALTY / (PENALTY + ENTROPY)
MASKED = -1e30
SQ_SCALE = 1.0 / ENTROPY
DOT_SCALE = 2.0 / ENTROPY
TINY = 1e-37
SHIFT = 44.0
LOWEST = 1e-24

ROWS = 256
COLS = 512
LANES = 128
DEPTH = 128
F32 = jnp.float32
BF16 = jnp.bfloat16


def split3(value):
    high = value.astype(BF16).astype(F32)
    rest = value - high
    middle = rest.astype(BF16).astype(F32)
    return high, middle, rest - middle


def write_augmented(out_ref, start, feats, pot, is_row):
    n = feats.shape[1]
    cols = pl.ds(start, n)
    scaled = feats.astype(F32) * DOT_SCALE if is_row else feats
    out_ref[0:32, cols] = scaled.astype(out_ref.dtype)
    first = 0 if is_row else 3
    ones_from = 3 if is_row else 0
    row = lax.broadcasted_iota(jnp.int32, (16, n), 0)
    tail = jnp.where((row >= ones_from) & (row < ones_from + 3), 1.0, 0.0)
    for k, piece in enumerate(split3(pot)):
        tail = jnp.where(row == first + k, piece, tail)
    out_ref[32:48, cols] = tail.astype(out_ref.dtype)
    out_ref[48:128, cols] = jnp.zeros((80, n), out_ref.dtype)


def square_sum(feats):
    wide = feats.astype(F32)
    return jnp.sum(wide * wide, axis=0, keepdims=True)


def live_pot(feats, start, count):
    ids = start + lax.broadcasted_iota(jnp.int32, (1, feats.shape[1]), 1)
    return jnp.where(ids < count, -SQ_SCALE * square_sum(feats), MASKED)


def aligned(index, size):
    return pl.multiple_of(index * size, size)


def around(counts):
    size = counts.shape[0]
    time, member = lax.axis_index("tm"), lax.axis_index("cell")
    before = jnp.where(time > 0, counts[jnp.maximum(time - 1, 0)], 0)
    after = jnp.where(time + 1 < size, counts[jnp.minimum(time + 1, size - 1)], 0)
    return before, counts[time], after, member


def row_blocks(count_here, count_next, member, group):
    blocks = pl.cdiv(count_here, LANES)
    mine = jnp.maximum((blocks - member + group - 1) // group, 0)
    return jnp.where(count_next > 0, mine, 0)


def live_rows(start, member, count, group=4):
    row = lax.broadcasted_iota(jnp.int32, (1, ROWS), 1)
    slot = (group * (start // LANES) + member) * LANES + row
    return slot + jnp.where(row >= LANES, (group - 1) * LANES, 0) < count


def col_steps(count):
    return (count + COLS - 1) // COLS


LTS = COLS // LANES
SUB = 32
WIDE = 1536


def scores(xa, ya_ref, c, cols=COLS):
    return jnp.dot(xa, ya_ref[:, pl.ds(aligned(c, cols), cols)], preferred_element_type=F32)


def piped(count, matmul, work, first_ref, second_ref, load=None, store=None):
    load = load or (lambda c: None)
    store = store or (lambda c, state: None)
    first_ref[...] = matmul(0)

    def pair(i, _):
        here, there = 2 * i, 2 * i + 1
        states = load(here), load(there)
        second_ref[...] = matmul(there)
        one = work(here, first_ref, states[0])
        first_ref[...] = matmul(jnp.minimum(there + 1, count - 1))
        two = work(there, second_ref, states[1])
        store(here, one)
        store(there, two)
        return 0

    lax.fori_loop(0, count // 2, pair, 0)

    @pl.when(count % 2 == 1)
    def _():
        store(count - 1, work(count - 1, first_ref, load(count - 1)))


def adder(acc_refs):
    def store(c, sums):
        for k, acc_ref in enumerate(acc_refs):
            lts = len(sums[k])
            for lt in range(lts):
                acc_ref[:, lane_tile(c, lt, lts)] += sums[k][lt]

    return store


def lane_tile(c, lt, lts=LTS):
    return pl.ds(aligned(c * lts + lt, LANES), LANES)


def piece_of(z_ref, rg, lt, size=SUB):
    return z_ref[rg : rg + size, lt * LANES : (lt + 1) * LANES]


def in_steps(total, visit):
    for start in range(0, total, WIDE):
        visit(start, slice(start, start + WIDE))


def kernel_a(
    counts, x0, x1, x2, x3, y0, y1, y2, y3,
    counts_ref, xg_ref, yg_ref, xt_ref, xa_ref, base_ref, gb_ref, log_ref,
    ya_ref, xat_ref, za_ref, zb_ref, top_ref, sum_ref,
):
    _, count_here, count_next, member = around(counts)
    group = 4
    mine = row_blocks(count_here, count_next, member, group)
    nb = (mine + 1) // 2
    nc = col_steps(count_next)
    local = x0.shape[1]
    for i in range(counts.shape[0]):
        counts_ref[i] = counts[i]
    for k, y_ref in enumerate((y0, y1, y2, y3)):
        yg_ref[:, pl.ds(aligned(member ^ k, local), local)] = y_ref[...]
    for k, x_ref in enumerate((x0, x1, x2, x3)):
        xg_ref[:, pl.ds(aligned(member ^ k, local), local)] = x_ref[...]
    sum_ref[...] = jnp.zeros_like(sum_ref)

    def prepare(start, cols):
        feats = yg_ref[:, cols]
        pot = live_pot(feats, start, count_next)
        gb_ref[:, cols] = pot
        write_augmented(ya_ref, start, feats, pot, False)

    in_steps(group * local, prepare)
    for k in range(local // LANES):
        lanes = slice(k * LANES, (k + 1) * LANES)
        block_id = group * k + member
        piece = xg_ref[:, pl.ds(aligned(block_id, LANES), LANES)]
        xt_ref[:, lanes] = piece
        pot = live_pot(piece, block_id * LANES, count_here) + SHIFT
        base_ref[:, lanes] = pot
        write_augmented(xat_ref, k * LANES, piece, pot, True)
        xa_ref[lanes, :] = jnp.transpose(xat_ref[:, lanes]).astype(BF16)

    def exact():
        top_ref[...] = jnp.full(top_ref.shape, MASKED, F32)
        sum_ref[...] = jnp.zeros_like(sum_ref)

        def row_visit(b, _):
            xa = xa_ref[pl.ds(aligned(b, ROWS), ROWS), :]

            def load(c):
                return [(top_ref[:, lane_tile(c, lt)], sum_ref[:, lane_tile(c, lt)]) for lt in range(LTS)]

            def work(c, z_ref, state):
                after = []
                for lt, (old, total) in enumerate(state):
                    tile = z_ref[:, lt * LANES : (lt + 1) * LANES].reshape(ROWS // 8, 8, LANES)
                    top = jnp.maximum(old, jnp.max(tile, axis=0))
                    total = total * jnp.exp(old - top) + jnp.sum(jnp.exp(tile - top[None]), axis=0)
                    after.append((top, total))
                return after

            def store(c, state):
                for lt, (top, total) in enumerate(state):
                    top_ref[:, lane_tile(c, lt)] = top
                    sum_ref[:, lane_tile(c, lt)] = total

            piped(nc, lambda c: scores(xa, ya_ref, c), work, za_ref, zb_ref, load, store)
            return 0

        lax.fori_loop(0, nb, row_visit, 0)
        tops = top_ref[...]
        top = jnp.max(tops, axis=0, keepdims=True)
        total = jnp.sum(sum_ref[...] * jnp.exp(tops - top), axis=0, keepdims=True)
        log_ref[...] = top + jnp.log(jnp.maximum(total, TINY)) - SHIFT

    def quick_rows(first_block, blocks):
        def tile_sums(c):
            totals = [jnp.zeros((8, LANES), F32) for _ in range(LTS)]
            for k in range(blocks):
                z = scores(xa_ref[pl.ds(aligned(first_block + k, LANES), LANES), :], ya_ref, c)
                for lt in range(LTS):
                    p = jnp.exp(z[:, lt * LANES : (lt + 1) * LANES])
                    totals[lt] = totals[lt] + jnp.sum(p.reshape(LANES // 8, 8, LANES), axis=0)
            return [totals]

        store = adder([sum_ref])

        def pair(i, _):
            one, two = tile_sums(2 * i), tile_sums(2 * i + 1)
            store(2 * i, one)
            store(2 * i + 1, two)
            return 0

        lax.fori_loop(0, nc // 2, pair, 0)

        @pl.when(nc % 2 == 1)
        def _():
            store(nc - 1, tile_sums(nc - 1))

    def quick_visit(b, _):
        quick_rows(2 * b, 2)
        return 0

    lax.fori_loop(0, mine // 2, quick_visit, 0)

    @pl.when(mine % 2 == 1)
    def _():
        quick_rows(mine - 1, 1)

    total = jnp.sum(sum_ref[...], axis=0, keepdims=True)
    log_ref[...] = jnp.where(total > 0.0, jnp.log(jnp.maximum(total, TINY)) - SHIFT, MASKED)
    ids = lax.broadcasted_iota(jnp.int32, total.shape, 1)
    lowest = jnp.min(jnp.where(ids < count_next, total, 1.0))

    @pl.when((lowest < LOWEST) & (nb > 0))
    def _():
        exact()


def column_sums(c, z_ref, _):
    rows, cols = z_ref.shape
    sums = []
    for lt in range(cols // LANES):
        p = jnp.exp(z_ref[:, lt * LANES : (lt + 1) * LANES])
        sums.append(jnp.sum(p.reshape(rows // 8, 8, LANES), axis=0))
    return [sums]


def row_adder(sum_ref, push_ref=None, g_ref=None):
    def first(c, scores_of, kept, count):
        half = LANES
        for start in range(0, count, half):
            scored = scores_of(c, start, half)
            for rg in range(0, half, SUB):
                rows = slice(start + rg, start + rg + SUB)
                total = sum_ref[rows, :]
                push = push_ref[rows, :] if push_ref is not None else None
                for lt in range(LTS):
                    z = piece_of(scored, rg, lt)
                    p = jnp.exp(z)
                    total = total + p
                    kept[0][rows, lane_tile(c, lt)] = p.astype(kept[0].dtype)
                    if push is not None:
                        part = p * (g_ref[:, lane_tile(c, lt)] - z)
                        push = push + part
                        kept[1][rows, lane_tile(c, lt)] = part.astype(kept[1].dtype)
                sum_ref[rows, :] = total
                if push is not None:
                    push_ref[rows, :] = push

    return first


def column_parts(c, plan):
    sums = [[jnp.zeros((8, LANES), F32) for _ in range(LTS)] for _ in plan]
    for rg in range(0, ROWS, 8):
        for k, (kept_ref, weight_ref) in enumerate(plan):
            scale = weight_ref[rg : rg + 8, :]
            for lt in range(LTS):
                sums[k][lt] = sums[k][lt] + scale * kept_ref[rg : rg + 8, lane_tile(c, lt)]
    return sums


def two_stage(mine, nc, first, finish, second, store, matmul_of, kept):
    nb = (mine + 1) // 2
    alone = mine % 2 == 1

    def in_pairs(visit, put):
        put = put or (lambda c, sums: None)

        def pair(i, _):
            one, two = visit(2 * i), visit(2 * i + 1)
            put(2 * i, one)
            put(2 * i + 1, two)
            return 0

        lax.fori_loop(0, nc // 2, pair, 0)

        @pl.when(nc % 2 == 1)
        def _():
            put(nc - 1, visit(nc - 1))

    def stage(start, now, before, rows=ROWS):
        scores_of = matmul_of(start)

        def visit(c):
            first(c, scores_of, now, rows)
            if rows < ROWS:
                for ref in now:
                    ref[rows:, col_tile(c)] = jnp.zeros((ROWS - rows, COLS), ref.dtype)
            return second(c, before) if before else None

        in_pairs(visit, store if before else None)
        finish(start, rows)

    def tail(before):
        in_pairs(lambda c: second(c, before), store)

    even, odd = kept

    @pl.when((nb > 0) & alone)
    def _():
        stage(0, even, None, LANES)

    @pl.when((nb > 0) & jnp.logical_not(alone))
    def _():
        stage(0, even, None)

    def visit(b, _):
        start = pl.multiple_of(b * ROWS - jnp.where(alone, LANES, 0), LANES)

        @pl.when(b % 2 == 1)
        def _():
            stage(start, odd, even)

        @pl.when(b % 2 == 0)
        def _():
            stage(start, even, odd)

        return 0

    lax.fori_loop(1, nb, visit, 0)

    @pl.when((nb > 0) & (nb % 2 == 1))
    def _():
        tail(even)

    @pl.when((nb > 0) & (nb % 2 == 0))
    def _():
        tail(odd)


def col_tile(c):
    return pl.ds(aligned(c, COLS), COLS)


def split2(value):
    high = value.astype(BF16).astype(F32)
    return high, value - high


def row_totals(ref):
    return jnp.sum(jnp.transpose(ref[...]), axis=0, keepdims=True)


def spread(row):
    return jnp.transpose(jnp.broadcast_to(row, (LANES, ROWS)))


def laid(column):
    return jnp.transpose(jnp.broadcast_to(column, (ROWS, LANES)))[0:1, :]


def sweep(quick, exact, low_ref, lost=None):
    low_ref[...] = jnp.ones_like(low_ref)
    quick()
    again = jnp.min(low_ref[...]) < LOWEST
    if lost is not None:
        again = again | lost()

    @pl.when(again)
    def _():
        exact()


def row_lse(xa, ya_ref, nc, buffers, top_ref, sum_ref, push_ref=None, g_ref=None):
    top_ref[...] = jnp.full(top_ref.shape, MASKED, F32)
    sum_ref[...] = jnp.zeros_like(sum_ref)
    if push_ref is not None:
        push_ref[...] = jnp.zeros_like(push_ref)

    def work(c, z_ref, _):
        for rg in range(0, ROWS, SUB):
            rows = slice(rg, rg + SUB)
            old = top_ref[rows, :]
            pieces = [piece_of(z_ref, rg, lt) for lt in range(LTS)]
            top = old
            for z in pieces:
                top = jnp.maximum(top, z)
            fade = jnp.exp(old - top)
            total = sum_ref[rows, :] * fade
            push = push_ref[rows, :] * fade if push_ref is not None else None
            for lt, z in enumerate(pieces):
                p = jnp.exp(z - top)
                total = total + p
                if push is not None:
                    push = push + p * (g_ref[:, lane_tile(c, lt)] - z)
            top_ref[rows, :] = top
            sum_ref[rows, :] = total
            if push is not None:
                push_ref[rows, :] = push

    piped(nc, lambda c: scores(xa, ya_ref, c), work, *buffers)
    tops = top_ref[...]
    top = jnp.max(tops, axis=1, keepdims=True)
    fade = jnp.exp(tops - top)
    total = jnp.sum(sum_ref[...] * fade, axis=1, keepdims=True)
    if push_ref is None:
        return top, total
    return top, total, jnp.sum(push_ref[...] * fade, axis=1, keepdims=True)


def row_potential(xa):
    lane = lax.broadcasted_iota(jnp.int32, (ROWS, LANES), 1)
    wide = xa.astype(F32)
    old = jnp.sum(jnp.where((lane >= 32) & (lane < 35), wide, 0.0), axis=1, keepdims=True)
    return lane, wide, old


def with_row_potential(lane, wide, pot):
    high, middle, low = split3(pot)
    new = jnp.where(lane == 32, high, jnp.where(lane == 33, middle, jnp.where(lane == 34, low, wide)))
    return new.astype(BF16)


def kernel_b(counts, xa_ref, yg_ref, gb_ref, l0, l1, l2, l3, g_ref, col_ref, ya_ref, za_ref, zb_ref, p_ref, q_ref, top_ref, sum_ref, weight_ref, low_ref, most_ref, acc_ref):
    _, count_here, count_next, member = around(counts)
    mine = row_blocks(count_here, count_next, member, 4)
    nb = (mine + 1) // 2
    nc = col_steps(count_next)

    def prepare(start, cols):
        logs = [ref[:, cols] for ref in (l0, l1, l2, l3)]
        top = jnp.maximum(jnp.maximum(logs[0], logs[1]), jnp.maximum(logs[2], logs[3]))
        total = sum(jnp.exp(one - top) for one in logs)
        ids = start + lax.broadcasted_iota(jnp.int32, (1, WIDE), 1)
        pot = jnp.where(ids < count_next, -DAMPING * (top + jnp.log(total)), 0.0)
        g_ref[:, cols] = pot
        write_augmented(ya_ref, start, yg_ref[:, cols], pot + gb_ref[:, cols], False)

    in_steps(yg_ref.shape[1], prepare)

    buffers = za_ref, zb_ref

    def quick():
        acc_ref[...] = jnp.zeros_like(acc_ref)

        def matmul_of(first_row):
            sum_ref[...] = jnp.zeros_like(sum_ref)
            return lambda c, start, size: scores(
                xa_ref[pl.ds(pl.multiple_of(first_row + start, size), size), :], ya_ref, c
            )

        def finish(start, rows):
            row = lax.broadcasted_iota(jnp.int32, (1, ROWS), 1)
            live = live_rows(start, member, count_here) & (row < rows)
            total = row_totals(sum_ref)
            low_ref[...] = jnp.minimum(low_ref[...], jnp.where(live, total, 1.0))
            pot = -DAMPING * (jnp.log(jnp.maximum(total, TINY)) - SHIFT)
            weight = jnp.where(live, jnp.exp(pot - SHIFT), 0.0)
            weight_ref[...] = spread(weight)
            most_ref[...] = jnp.maximum(most_ref[...], weight)

        two_stage(
            mine, nc, row_adder(sum_ref), finish, lambda c, kept: column_parts(c, [(kept[0], weight_ref)]),
            adder([acc_ref]), matmul_of, ((p_ref,), (q_ref,)),
        )

    def exact():
        acc_ref[...] = jnp.zeros_like(acc_ref)

        def row_visit(b, _):
            xa = xa_ref[pl.ds(aligned(b, ROWS), ROWS), :]
            lane, wide, old = row_potential(xa)
            live = old > 0.5 * MASKED
            top, total = row_lse(xa, ya_ref, nc, buffers, top_ref, sum_ref)
            pot = -DAMPING * (top + jnp.log(total) - SHIFT)
            xb = with_row_potential(lane, wide, jnp.where(live, pot + old - SHIFT, MASKED))
            piped(nc, lambda c: scores(xb, ya_ref, c), column_sums, *buffers, store=adder([acc_ref]))
            return 0

        lax.fori_loop(0, nb, row_visit, 0)

    def lost():
        total = jnp.sum(acc_ref[...], axis=0, keepdims=True)
        ids = lax.broadcasted_iota(jnp.int32, total.shape, 1)
        least = jnp.min(jnp.where((ids < count_next) & (nb > 0), total, 1.0))
        return least < jnp.max(most_ref[...]) * 2.0**-91

    most_ref[...] = jnp.zeros_like(most_ref)
    sweep(quick, exact, low_ref, lost)
    col_ref[...] = jnp.sum(acc_ref[...], axis=0, keepdims=True)


def kernel_c(
    counts, xa_ref, xt_ref, base_ref, yg_ref, gb_ref, g_ref, c0, c1, c2, c3,
    rows_ref, g2_ref, col_ref,
    ya_ref, za_ref, zb_ref, p_ref, w_ref, q_ref, v_ref, top_ref, sum_ref, push_ref, adj_ref, low_ref, cost_ref, weight_ref, xat_ref, acc_ref, acc0_ref, acc1_ref, acc2_ref,
):
    _, count_here, count_next, member = around(counts)
    mine = row_blocks(count_here, count_next, member, 4)
    nb = (mine + 1) // 2
    nc = col_steps(count_next)

    def prepare(start, cols):
        total = (c0[:, cols] + c1[:, cols]) + (c2[:, cols] + c3[:, cols])
        ids = start + lax.broadcasted_iota(jnp.int32, (1, WIDE), 1)
        log = jnp.log(jnp.maximum(total, TINY)) - g_ref[:, cols]
        pot = jnp.where(ids < count_next, -DAMPING * log, 0.0)
        g2_ref[:, cols] = pot
        write_augmented(ya_ref, start, yg_ref[:, cols], pot + gb_ref[:, cols], False)

    in_steps(yg_ref.shape[1], prepare)

    buffers = za_ref, zb_ref
    accs = acc0_ref, acc1_ref, acc2_ref

    ids = lax.broadcasted_iota(jnp.int32, g_ref.shape, 1)
    centre = jnp.sum(jnp.where(ids < count_next, g_ref[...], 0.0), axis=1, keepdims=True)
    centre = centre / (DAMPING * jnp.maximum(count_next, 1).astype(F32)) + 3.0
    cost_ref[...] = g2_ref[...] + (SHIFT - centre)

    line = lax.broadcasted_iota(jnp.int32, rows_ref.shape, 0)
    rows_ref[...] = jnp.where(line == 3, MASKED, 0.0)

    def close_rows(start, rows, row_log, mean_cost):
        rows_here = pl.ds(pl.multiple_of(start, LANES), ROWS)
        live = live_rows(start, member, count_here) & (lax.broadcasted_iota(jnp.int32, (1, ROWS), 1) < rows)
        pot = jnp.where(live, -DAMPING * row_log, 0.0)
        row_sum = jnp.where(live, jnp.exp(row_log + pot), 0.0)
        adjoint = jnp.where(live, mean_cost + centre, 0.0)
        full = jnp.where(live, pot + base_ref[:, rows_here] - SHIFT, MASKED)
        rows_ref[0:1, rows_here] = adjoint
        rows_ref[1:2, rows_here] = jnp.where(row_sum > 0.0, 1.0 / jnp.maximum(row_sum, TINY), 0.0)
        rows_ref[2:3, rows_here] = pot
        rows_ref[3:4, rows_here] = full
        return live, pot, adjoint, full

    def quick():
        acc_ref[...] = jnp.zeros_like(acc_ref)

        def matmul_of(first_row):
            sum_ref[...] = jnp.zeros_like(sum_ref)
            push_ref[...] = jnp.zeros_like(push_ref)
            return lambda c, start, size: scores(
                xa_ref[pl.ds(pl.multiple_of(first_row + start, size), size), :], ya_ref, c
            )

        def finish(start, rows):
            total = row_totals(sum_ref)
            safe = jnp.maximum(total, TINY)
            live, pot, adjoint, _ = close_rows(start, rows, jnp.log(safe) - SHIFT, row_totals(push_ref) / safe)
            low_ref[...] = jnp.minimum(low_ref[...], jnp.where(live, total, 1.0))
            weight = jnp.where(live, jnp.exp(pot - SHIFT), 0.0)
            row = lax.broadcasted_iota(jnp.int32, (16, ROWS), 0)
            packed = jnp.zeros((16, ROWS), F32)
            for k, piece in enumerate((*split2(weight), *split2(weight * adjoint))):
                packed = jnp.where(row == k, piece, packed)
            weight_ref[...] = packed.astype(BF16)

        def second(c, kept):
            weights = weight_ref[...]
            plan = jnp.dot(weights, kept[0][:, col_tile(c)], preferred_element_type=F32)
            cost = jnp.dot(weights, kept[1][:, col_tile(c)], preferred_element_type=F32)
            return plan, cost

        def store(c, sums):
            acc_ref[0:16, col_tile(c)] += sums[0]
            acc_ref[16:32, col_tile(c)] += sums[1]

        two_stage(
            mine, nc, row_adder(sum_ref, push_ref, cost_ref), finish, second, store, matmul_of,
            ((p_ref, w_ref), (q_ref, v_ref)),
        )
        acc0_ref[0:1, :] = acc_ref[0:1, :] + acc_ref[1:2, :]
        acc1_ref[0:1, :] = acc_ref[16:17, :] + acc_ref[17:18, :]
        acc2_ref[0:1, :] = acc_ref[2:3, :] + acc_ref[3:4, :]
        for ref in accs:
            ref[1:8, :] = jnp.zeros((7, ref.shape[1]), F32)

    def exact():
        for ref in accs:
            ref[...] = jnp.zeros_like(ref)

        def row_visit(b, _):
            xa = xa_ref[pl.ds(aligned(b, ROWS), ROWS), :]
            top, total, push = row_lse(xa, ya_ref, nc, buffers, top_ref, sum_ref, push_ref, cost_ref)
            _, pot, adjoint, full = close_rows(
                b * ROWS, ROWS, laid(top + jnp.log(total) - SHIFT), laid(push / total)
            )
            top_ref[...] = spread(pot - SHIFT)
            adj_ref[...] = spread(adjoint)
            write_augmented(xat_ref, 0, xt_ref[:, pl.ds(aligned(b, ROWS), ROWS)], full, True)
            xb = jnp.transpose(xat_ref[...]).astype(BF16)

            def work(c, z_ref, _):
                sums = [[jnp.zeros((8, LANES), F32) for _ in range(LTS)] for _ in range(3)]
                for rg in range(0, ROWS, 8):
                    pot_here = top_ref[rg : rg + 8, :]
                    adj_here = adj_ref[rg : rg + 8, :]
                    for lt in range(LTS):
                        tile = piece_of(z_ref, rg, lt, 8)
                        p = jnp.exp(tile)
                        sums[0][lt] = sums[0][lt] + p
                        sums[1][lt] = sums[1][lt] + p * (cost_ref[:, lane_tile(c, lt)] + (pot_here - tile))
                        sums[2][lt] = sums[2][lt] + p * adj_here
                return sums

            piped(nc, lambda c: scores(xb, ya_ref, c), work, *buffers, store=adder(accs))
            return 0

        lax.fori_loop(0, nb, row_visit, 0)

    sweep(quick, exact, low_ref)
    mass = jnp.sum(acc0_ref[...], axis=0, keepdims=True)
    slots = mass.shape[1]
    col_ref[:, 0:slots] = mass
    push = jnp.sum(acc1_ref[...], axis=0, keepdims=True)
    col_ref[:, slots : 2 * slots] = push + centre * mass
    col_ref[:, 2 * slots :] = jnp.sum(acc2_ref[...], axis=0, keepdims=True)


def kernel_d(
    counts, xt_ref, rows_ref, yg_ref, gb_ref, g2_ref, s0, s1, s2, s3,
    stat_ref, send_ref,
    ya_ref, xat_ref, xb_ref, p_ref, q_ref, first_ref, second_ref, weight_ref, acc_ref,
):
    _, count_here, count_next, member = around(counts)
    mine = row_blocks(count_here, count_next, member, 4)
    nb = (mine + 1) // 2
    nc = col_steps(count_next)
    slots = yg_ref.shape[1]
    local = xt_ref.shape[1]
    acc_ref[...] = jnp.zeros_like(acc_ref)

    def prepare(start, cols):
        mass, push, pulled = (
            (s0[:, part] + s1[:, part]) + (s2[:, part] + s3[:, part])
            for part in (pl.ds(start + k * slots, WIDE) for k in range(3))
        )
        inverse = jnp.where(mass > 0.0, 1.0 / jnp.maximum(mass, TINY), 0.0)
        pot = g2_ref[:, cols]
        stat_ref[0:1, cols] = pot + gb_ref[:, cols]
        stat_ref[1:2, cols] = push * inverse
        stat_ref[2:3, cols] = (push - DAMPING * pulled) * inverse
        stat_ref[3:4, cols] = inverse
        stat_ref[4:5, cols] = pot
        stat_ref[5:8, cols] = jnp.zeros((3, WIDE), F32)
        write_augmented(ya_ref, start, yg_ref[:, cols], pot + gb_ref[:, cols], False)

    in_steps(slots, prepare)
    for block in range(local // ROWS):
        @pl.when(2 * block < mine)
        def _():
            rows = slice(block * ROWS, (block + 1) * ROWS)
            write_augmented(xat_ref, 0, xt_ref[:, rows], rows_ref[3:4, rows], True)
            xb_ref[rows, :] = jnp.transpose(xat_ref[...]).astype(BF16)

    send_ref[:, slots : slots + local] = jnp.full((1, local), MASKED, F32)
    send_ref[:, slots + local :] = jnp.zeros((1, local), F32)

    def matmul_of(first_row):
        first_ref[...] = jnp.zeros_like(first_ref)
        second_ref[...] = jnp.zeros_like(second_ref)
        return lambda c, start, size: scores(
            xb_ref[pl.ds(pl.multiple_of(first_row + start, size), size), :], ya_ref, c
        )

    def sums(c, scores_of, kept, count):
        half = LANES
        for start in range(0, count, half):
            scored = scores_of(c, start, half)
            for rg in range(0, half, SUB):
                rows = slice(start + rg, start + rg + SUB)
                first = first_ref[rows, :]
                second = second_ref[rows, :]
                for lt in range(LTS):
                    p = jnp.exp(piece_of(scored, rg, lt))
                    kept[0][rows, lane_tile(c, lt)] = p
                    first = first + p * stat_ref[1:2, lane_tile(c, lt)]
                    second = second + p * stat_ref[2:3, lane_tile(c, lt)]
                first_ref[rows, :] = first
                second_ref[rows, :] = second

    def finish(start, rows):
        first, second = row_totals(first_ref), row_totals(second_ref)
        rows_here = pl.ds(pl.multiple_of(start, LANES), ROWS)
        start_adj, inverse, pot, full = (rows_ref[k : k + 1, rows_here] for k in range(4))
        middle_adj = start_adj - DAMPING * first * inverse
        last_adj = start_adj - DAMPING * second * inverse
        weight_ref[...] = spread(middle_adj)
        send_ref[:, pl.ds(pl.multiple_of(slots + start, LANES), ROWS)] = full
        send_ref[:, pl.ds(pl.multiple_of(slots + local + start, LANES), ROWS)] = 1.0 + DAMPING * last_adj - pot

    two_stage(
        mine, nc, sums, finish, lambda c, kept: column_parts(c, [(kept[0], weight_ref)]), adder([acc_ref]), matmul_of,
        ((p_ref,), (q_ref,)),
    )
    send_ref[:, 0:slots] = jnp.sum(acc_ref[...], axis=0, keepdims=True)


def kernel_f(counts, p0, p1, p2, p3, stat_ref, col_ref, early_ref, parts_ref):
    member = lax.axis_index("cell")
    slots = stat_ref.shape[1]
    local = early_ref.shape[1] - slots
    for k, ref in enumerate((p0, p1, p2, p3)):
        parts_ref[member ^ k] = ref[...]
    total = (p0[:, 0:slots] + p1[:, 0:slots]) + (p2[:, 0:slots] + p3[:, 0:slots])
    last = stat_ref[1:2, :] - DAMPING * total * stat_ref[3:4, :]
    col_ref[0:1, :] = stat_ref[0:1, :]
    col_ref[1:2, :] = DAMPING * last - stat_ref[4:5, :]
    for block in range(slots // LANES):
        owner, place = block % 4, block // 4
        lanes = slice(block * LANES, (block + 1) * LANES)
        for k in range(2):
            at = slots + k * local + place * LANES
            early_ref[k : k + 1, lanes] = parts_ref[owner, :, at : at + LANES]
    here = pl.ds(aligned(member, local), local)
    early_ref[:, slots:] = col_ref[:, here]


def kernel_e(
    counts, *refs, earlier,
):
    tall, wide = (COLS // 2, 2 * ROWS) if earlier else (COLS, ROWS)
    own_ref, rowpot_ref, other_ref, colpot_ref = refs[:4]
    local, slots = own_ref.shape[1], other_ref.shape[1]
    before, here, after, member = around(counts)
    if earlier:
        out_ref, xw_ref, tile_ref, ys_ref, beta_ref, za_ref, zb_ref, pull_ref, sum_ref = refs[4:]
        count_cols = before
        count_rows = jnp.clip(here - member * local, 0, local)
        nb = jnp.where(count_cols > 0, (count_rows + wide - 1) // wide, 0)
        pot_at = slots
    else:
        out_refs = refs[4:8]
        xw_ref, tile_ref, ys_ref, beta_ref, za_ref, zb_ref, pull_ref, sum_ref, out_ref = refs[8:]
        count_cols = after
        nb = (row_blocks(here, after, member, 4) + 1) // 2
        pot_at = slots
    nc = (count_cols + tall - 1) // tall
    out_ref[...] = jnp.zeros_like(out_ref)

    def prepare(c, _):
        cols = pl.ds(aligned(c, COLS), COLS)
        write_augmented(tile_ref, 0, other_ref[:, cols], colpot_ref[0:1, cols], False)
        ys_ref[cols, :] = jnp.transpose(tile_ref[...]).astype(BF16)
        beta_ref[cols, :] = jnp.transpose(jnp.broadcast_to(colpot_ref[1:2, cols], (LANES, COLS)))
        return 0

    @pl.when(nb > 0)
    def _():
        lax.fori_loop(0, col_steps(count_cols), prepare, 0)

    def row_visit(b, _):
        rows_here = pl.ds(aligned(b, wide), wide)
        own = own_ref[:, rows_here]
        pots = rowpot_ref[0:1, pl.ds(aligned(b + pot_at // wide, wide), wide)]
        write_augmented(xw_ref, 0, own, pots, True)
        xw = xw_ref[...]
        if earlier:
            alpha = rowpot_ref[1:2, pl.ds(aligned(b + pot_at // wide, wide), wide)]
        else:
            alpha = rowpot_ref[0:1, pl.ds(aligned(b + (pot_at + local) // wide, wide), wide)]
        sum_ref[...] = jnp.zeros_like(sum_ref)
        pull_ref[...] = jnp.zeros_like(pull_ref)

        def matmul(c):
            return jnp.dot(ys_ref[pl.ds(aligned(c, tall), tall), :], xw, preferred_element_type=F32)

        def work(c, z_ref, _):
            rounded = []
            sums = [jnp.zeros((8, LANES), F32) for _ in range(wide // LANES)]
            for jg in range(0, tall, 16):
                beta = beta_ref[pl.ds(pl.multiple_of(c * tall + jg, 16), 16), :]
                line = []
                for lt in range(wide // LANES):
                    tile = piece_of(z_ref, jg, lt, 16)
                    grad = jnp.exp(tile) * (tile + (alpha[:, lt * LANES : (lt + 1) * LANES] + beta))
                    sums[lt] = sums[lt] + (grad[0:8] + grad[8:16])
                    line.append(grad.astype(BF16))
                rounded.append(jnp.concatenate(line, axis=1))
            for lt in range(wide // LANES):
                sum_ref[:, lt * LANES : (lt + 1) * LANES] += sums[lt]
            feats = other_ref[:, pl.ds(aligned(c, tall), tall)]
            pull_ref[...] += jnp.dot(feats, jnp.concatenate(rounded, axis=0), preferred_element_type=F32)

        piped(nc, matmul, work, za_ref, zb_ref)
        total = jnp.sum(sum_ref[...], axis=0, keepdims=True)
        out_ref[:, rows_here] = 2.0 * (own.astype(F32) * total - pull_ref[...])
        return 0

    lax.fori_loop(0, nb, row_visit, 0)
    if not earlier:
        width = local // 4
        for k, ref in enumerate(out_refs):
            ref[...] = out_ref[:, pl.ds(pl.multiple_of((member ^ k) * width, LANES), width)]


def kernel_g(counts, target_ref, p0, p1, p2, p3, out_ref):
    member = lax.axis_index("cell")
    for k, ref in enumerate((p0, p1, p2, p3)):
        for i in range(ref.shape[1] // LANES):
            lanes = pl.ds(aligned(4 * i + (member ^ k), LANES), LANES)
            out_ref[:, lanes] = target_ref[:, lanes] + ref[:, i * LANES : (i + 1) * LANES]


def run(body, name, outs, scratch, limit, counts, *operands, flops=0, counts_out=False):
    vmem = pl.BlockSpec(memory_space=pltpu.VMEM)
    smem = pl.BlockSpec(memory_space=pltpu.SMEM)
    out_specs = jax.tree.map(lambda _: vmem, outs)
    if counts_out:
        out_specs = (smem, *out_specs[1:])
    return pl.pallas_call(
        body,
        name=name,
        out_shape=outs,
        in_specs=[smem] + [vmem] * len(operands),
        out_specs=out_specs,
        scratch_shapes=scratch,
        compiler_params=pltpu.CompilerParams(vmem_limit_bytes=limit * 1024 * 1024),
        cost_estimate=pl.CostEstimate(flops=flops, bytes_accessed=4_000_000, transcendentals=9_000_000),
    )(counts, *operands)


def shape(*dims, dtype=F32):
    return jax.ShapeDtypeStruct(dims, dtype)


def shifted(block, distance):
    size = lax.axis_size("tm")
    route = [(i - distance, i) for i in range(size) if 0 <= i - distance < size]
    return lax.ppermute(block, "tm", route)


def from_later(block, k):
    times, size = lax.axis_size("tm"), lax.axis_size("cell")
    route = [((t + 1) * size + (i ^ k), t * size + i) for t in range(times - 1) for i in range(size)]
    return lax.ppermute(block, ("tm", "cell"), route)


def swapped(block, k):
    return lax.ppermute(block, "cell", [(i, i ^ k) for i in range(lax.axis_size("cell"))])


def exchanged(block):
    near = swapped(block, 1)
    far = swapped(block, 2)
    return [block, near, far, swapped(far, 1)]


def per_device(embedding, counts):
    feat_dim, local = embedding.shape
    group = lax.axis_size("cell")
    slots = local * group

    ahead, ahead_far = from_later(embedding, 0), from_later(embedding, 2)
    source_parts = exchanged(embedding)
    target_parts = [ahead, swapped(ahead, 1), ahead_far, swapped(ahead_far, 1)]

    flops = 2 * local * slots * DEPTH
    aug = pltpu.VMEM((DEPTH, slots), BF16)
    narrow = pltpu.VMEM((ROWS, LANES), F32)
    flat = pltpu.VMEM((1, ROWS), F32)
    tile = pltpu.VMEM((DEPTH, ROWS), F32)
    wide = pltpu.VMEM((ROWS, slots), F32)
    half = pltpu.VMEM((ROWS, slots), BF16)
    turned_rows = pltpu.VMEM((16, ROWS), BF16)
    buffers = [pltpu.VMEM((ROWS, COLS), F32)] * 2
    long = pltpu.VMEM((8, slots), F32)
    counts, grouped, targets, dealt, xa, base, gb, log = run(
        kernel_a, "column_log",
        (
            shape(*counts.shape, dtype=jnp.int32),
            shape(feat_dim, slots, dtype=BF16), shape(feat_dim, slots, dtype=BF16), shape(feat_dim, local, dtype=BF16),
            shape(local, DEPTH, dtype=BF16), shape(1, local), shape(1, slots), shape(1, slots),
        ),
        [aug, pltpu.VMEM((DEPTH, local), F32), *buffers, long, long],
        16, counts, *source_parts, *target_parts, flops=flops, counts_out=True,
    )
    logs = exchanged(log)
    g1, col1 = run(
        kernel_b, "first_sweep",
        (shape(1, slots), shape(1, slots)),
        [aug, *buffers, wide, wide, narrow, narrow, narrow, flat, flat, long],
        24, counts, xa, targets, gb, *logs, flops=2 * flops,
    )
    grouped, col1 = lax.optimization_barrier((grouped, col1))
    earlier = shifted(grouped, 1)
    rows, g2, stats = run(
        kernel_c, "second_sweep",
        (shape(8, local), shape(1, slots), shape(1, 3 * slots)),
        [
            aug, *buffers, half, half, half, half, narrow, narrow, narrow, narrow, flat,
            pltpu.VMEM((1, slots), F32), turned_rows, tile, pltpu.VMEM((32, slots), F32), long, long, long,
        ],
        28, counts, xa, dealt, base, targets, gb, g1, *exchanged(col1), flops=2 * flops,
    )
    rows, earlier = lax.optimization_barrier((rows, earlier))
    stat, send = run(
        kernel_d, "adjoint",
        (shape(8, slots), shape(1, slots + 2 * local)),
        [aug, tile, pltpu.VMEM((local, DEPTH), BF16), wide, wide, narrow, narrow, narrow, long],
        24, counts, dealt, rows, targets, gb, g2, *exchanged(stats), flops=2 * flops,
    )
    col_pair, early = run(
        kernel_f, "assemble",
        (shape(2, slots), shape(2, slots + local)),
        [pltpu.VMEM((group, 1, slots + 2 * local), F32)],
        8, counts, *exchanged(send), stat,
    )
    early = shifted(early, 1)

    def scratch_e(tall, wide):
        return [
            pltpu.VMEM((DEPTH, wide), BF16), pltpu.VMEM((DEPTH, COLS), F32), pltpu.VMEM((slots, DEPTH), BF16),
            pltpu.VMEM((slots, LANES), F32), *[pltpu.VMEM((tall, wide), F32)] * 2,
            pltpu.VMEM((feat_dim, wide), F32), pltpu.VMEM((8, wide), F32),
        ]

    parts = run(
        functools.partial(kernel_e, earlier=False), "source_gradient", (shape(feat_dim, local // group),) * group,
        scratch_e(COLS, ROWS) + [pltpu.VMEM((feat_dim, local), F32)],
        16, counts, dealt, send, targets, col_pair, flops=2 * flops,
    )
    parts = [parts[0]] + [swapped(parts[k], k) for k in range(1, group)]
    target_grad = run(
        functools.partial(kernel_e, earlier=True), "target_gradient", shape(feat_dim, local),
        scratch_e(COLS // 2, 2 * ROWS),
        16, counts, embedding, early, earlier, early, flops=2 * flops,
    )
    return run(kernel_g, "total", shape(feat_dim, local), [], 8, counts, target_grad, *parts)


def solution(mesh):
    in_specs = (P(None, ("tm", "cell")), P())
    out_specs = P(None, ("tm", "cell"))
    return jax.shard_map(
        per_device, mesh=mesh, in_specs=in_specs, out_specs=out_specs, check_vma=False
    )
```

```python
import functools

import jax
import jax.numpy as jnp
from jax import lax
from jax.experimental import pallas as pl
from jax.experimental.pallas import tpu as pltpu
from jax.sharding import PartitionSpec as P

ENTROPY = 0.25
PENALTY = 5.0
DAMPING = PENALTY / (PENALTY + ENTROPY)
MASKED = -1e30
SQ_SCALE = 1.0 / ENTROPY
DOT_SCALE = 2.0 / ENTROPY
TINY = 1e-37
SHIFT = 44.0
LOWEST = 1e-24

ROWS = 256
COLS = 512
LANES = 128
DEPTH = 128
F32 = jnp.float32
BF16 = jnp.bfloat16


def split3(value):
    high = value.astype(BF16).astype(F32)
    rest = value - high
    middle = rest.astype(BF16).astype(F32)
    return high, middle, rest - middle


def write_augmented(out_ref, start, feats, pot, is_row):
    n = feats.shape[1]
    cols = pl.ds(start, n)
    scaled = feats.astype(F32) * DOT_SCALE if is_row else feats
    out_ref[0:32, cols] = scaled.astype(out_ref.dtype)
    first = 0 if is_row else 3
    ones_from = 3 if is_row else 0
    row = lax.broadcasted_iota(jnp.int32, (16, n), 0)
    tail = jnp.where((row >= ones_from) & (row < ones_from + 3), 1.0, 0.0)
    for k, piece in enumerate(split3(pot)):
        tail = jnp.where(row == first + k, piece, tail)
    out_ref[32:48, cols] = tail.astype(out_ref.dtype)
    out_ref[48:128, cols] = jnp.zeros((80, n), out_ref.dtype)


def square_sum(feats):
    wide = feats.astype(F32)
    return jnp.sum(wide * wide, axis=0, keepdims=True)


def live_pot(feats, start, count):
    ids = start + lax.broadcasted_iota(jnp.int32, (1, feats.shape[1]), 1)
    return jnp.where(ids < count, -SQ_SCALE * square_sum(feats), MASKED)


def aligned(index, size):
    return pl.multiple_of(index * size, size)


def around(counts):
    size = counts.shape[0]
    time, member = lax.axis_index("tm"), lax.axis_index("cell")
    before = jnp.where(time > 0, counts[jnp.maximum(time - 1, 0)], 0)
    after = jnp.where(time + 1 < size, counts[jnp.minimum(time + 1, size - 1)], 0)
    return before, counts[time], after, member


def row_blocks(count_here, count_next, member, group):
    blocks = pl.cdiv(count_here, LANES)
    mine = jnp.maximum((blocks - member + group - 1) // group, 0)
    return jnp.where(count_next > 0, mine, 0)


def live_rows(start, member, count, group=4):
    row = lax.broadcasted_iota(jnp.int32, (1, ROWS), 1)
    slot = (group * (start // LANES) + member) * LANES + row
    return slot + jnp.where(row >= LANES, (group - 1) * LANES, 0) < count


def col_steps(count):
    return (count + COLS - 1) // COLS


LTS = COLS // LANES
SUB = 32
WIDE = 1536


def scores(xa, ya_ref, c, cols=COLS):
    return jnp.dot(xa, ya_ref[:, pl.ds(aligned(c, cols), cols)], preferred_element_type=F32)


def piped(count, matmul, work, first_ref, second_ref, load=None, store=None):
    load = load or (lambda c: None)
    store = store or (lambda c, state: None)
    first_ref[...] = matmul(0)

    def pair(i, _):
        here, there = 2 * i, 2 * i + 1
        states = load(here), load(there)
        second_ref[...] = matmul(there)
        one = work(here, first_ref, states[0])
        first_ref[...] = matmul(jnp.minimum(there + 1, count - 1))
        two = work(there, second_ref, states[1])
        store(here, one)
        store(there, two)
        return 0

    lax.fori_loop(0, count // 2, pair, 0)

    @pl.when(count % 2 == 1)
    def _():
        store(count - 1, work(count - 1, first_ref, load(count - 1)))


def adder(acc_refs):
    def store(c, sums):
        for k, acc_ref in enumerate(acc_refs):
            lts = len(sums[k])
            for lt in range(lts):
                acc_ref[:, lane_tile(c, lt, lts)] += sums[k][lt]

    return store


def lane_tile(c, lt, lts=LTS):
    return pl.ds(aligned(c * lts + lt, LANES), LANES)


def piece_of(z_ref, rg, lt, size=SUB):
    return z_ref[rg : rg + size, lt * LANES : (lt + 1) * LANES]


def in_steps(total, visit):
    for start in range(0, total, WIDE):
        visit(start, slice(start, start + WIDE))


def kernel_a(
    counts, x0, x1, x2, x3, y0, y1, y2, y3,
    xg_ref, yg_ref, xt_ref, xa_ref, base_ref, gb_ref, log_ref,
    ya_ref, xat_ref, za_ref, zb_ref, top_ref, sum_ref,
):
    _, count_here, count_next, member = around(counts)
    group = 4
    mine = row_blocks(count_here, count_next, member, group)
    nb = (mine + 1) // 2
    nc = col_steps(count_next)
    local = x0.shape[1]
    for k, y_ref in enumerate((y0, y1, y2, y3)):
        yg_ref[:, pl.ds(aligned(member ^ k, local), local)] = y_ref[...]
    for k, x_ref in enumerate((x0, x1, x2, x3)):
        xg_ref[:, pl.ds(aligned(member ^ k, local), local)] = x_ref[...]
    sum_ref[...] = jnp.zeros_like(sum_ref)

    def prepare(start, cols):
        feats = yg_ref[:, cols]
        pot = live_pot(feats, start, count_next)
        gb_ref[:, cols] = pot
        write_augmented(ya_ref, start, feats, pot, False)

    in_steps(group * local, prepare)
    for k in range(local // LANES):
        lanes = slice(k * LANES, (k + 1) * LANES)
        block_id = group * k + member
        piece = xg_ref[:, pl.ds(aligned(block_id, LANES), LANES)]
        xt_ref[:, lanes] = piece
        pot = live_pot(piece, block_id * LANES, count_here) + SHIFT
        base_ref[:, lanes] = pot
        write_augmented(xat_ref, k * LANES, piece, pot, True)
        xa_ref[lanes, :] = jnp.transpose(xat_ref[:, lanes]).astype(BF16)

    def exact():
        top_ref[...] = jnp.full(top_ref.shape, MASKED, F32)
        sum_ref[...] = jnp.zeros_like(sum_ref)

        def row_visit(b, _):
            xa = xa_ref[pl.ds(aligned(b, ROWS), ROWS), :]

            def load(c):
                return [(top_ref[:, lane_tile(c, lt)], sum_ref[:, lane_tile(c, lt)]) for lt in range(LTS)]

            def work(c, z_ref, state):
                after = []
                for lt, (old, total) in enumerate(state):
                    tile = z_ref[:, lt * LANES : (lt + 1) * LANES].reshape(ROWS // 8, 8, LANES)
                    top = jnp.maximum(old, jnp.max(tile, axis=0))
                    total = total * jnp.exp(old - top) + jnp.sum(jnp.exp(tile - top[None]), axis=0)
                    after.append((top, total))
                return after

            def store(c, state):
                for lt, (top, total) in enumerate(state):
                    top_ref[:, lane_tile(c, lt)] = top
                    sum_ref[:, lane_tile(c, lt)] = total

            piped(nc, lambda c: scores(xa, ya_ref, c), work, za_ref, zb_ref, load, store)
            return 0

        lax.fori_loop(0, nb, row_visit, 0)
        tops = top_ref[...]
        top = jnp.max(tops, axis=0, keepdims=True)
        total = jnp.sum(sum_ref[...] * jnp.exp(tops - top), axis=0, keepdims=True)
        log_ref[...] = top + jnp.log(jnp.maximum(total, TINY)) - SHIFT

    def quick_rows(first_block, blocks):
        def tile_sums(c):
            totals = [jnp.zeros((8, LANES), F32) for _ in range(LTS)]
            for k in range(blocks):
                z = scores(xa_ref[pl.ds(aligned(first_block + k, LANES), LANES), :], ya_ref, c)
                for lt in range(LTS):
                    p = jnp.exp(z[:, lt * LANES : (lt + 1) * LANES])
                    totals[lt] = totals[lt] + jnp.sum(p.reshape(LANES // 8, 8, LANES), axis=0)
            return [totals]

        store = adder([sum_ref])

        def pair(i, _):
            one, two = tile_sums(2 * i), tile_sums(2 * i + 1)
            store(2 * i, one)
            store(2 * i + 1, two)
            return 0

        lax.fori_loop(0, nc // 2, pair, 0)

        @pl.when(nc % 2 == 1)
        def _():
            store(nc - 1, tile_sums(nc - 1))

    def quick_visit(b, _):
        quick_rows(2 * b, 2)
        return 0

    lax.fori_loop(0, mine // 2, quick_visit, 0)

    @pl.when(mine % 2 == 1)
    def _():
        quick_rows(mine - 1, 1)

    total = jnp.sum(sum_ref[...], axis=0, keepdims=True)
    log_ref[...] = jnp.where(total > 0.0, jnp.log(jnp.maximum(total, TINY)) - SHIFT, MASKED)
    ids = lax.broadcasted_iota(jnp.int32, total.shape, 1)
    lowest = jnp.min(jnp.where(ids < count_next, total, 1.0))

    @pl.when((lowest < LOWEST) & (nb > 0))
    def _():
        exact()


def column_sums(c, z_ref, _):
    rows, cols = z_ref.shape
    sums = []
    for lt in range(cols // LANES):
        p = jnp.exp(z_ref[:, lt * LANES : (lt + 1) * LANES])
        sums.append(jnp.sum(p.reshape(rows // 8, 8, LANES), axis=0))
    return [sums]


def row_adder(sum_ref, push_ref=None, g_ref=None):
    def first(c, scores_of, kept, count):
        half = LANES
        for start in range(0, count, half):
            scored = scores_of(c, start, half)
            for rg in range(0, half, SUB):
                rows = slice(start + rg, start + rg + SUB)
                total = sum_ref[rows, :]
                push = push_ref[rows, :] if push_ref is not None else None
                for lt in range(LTS):
                    z = piece_of(scored, rg, lt)
                    p = jnp.exp(z)
                    total = total + p
                    kept[0][rows, lane_tile(c, lt)] = p.astype(kept[0].dtype)
                    if push is not None:
                        part = p * (g_ref[:, lane_tile(c, lt)] - z)
                        push = push + part
                        kept[1][rows, lane_tile(c, lt)] = part.astype(kept[1].dtype)
                sum_ref[rows, :] = total
                if push is not None:
                    push_ref[rows, :] = push

    return first


def column_parts(c, plan):
    sums = [[jnp.zeros((8, LANES), F32) for _ in range(LTS)] for _ in plan]
    for rg in range(0, ROWS, 8):
        for k, (kept_ref, weight_ref) in enumerate(plan):
            scale = weight_ref[rg : rg + 8, :]
            for lt in range(LTS):
                sums[k][lt] = sums[k][lt] + scale * kept_ref[rg : rg + 8, lane_tile(c, lt)]
    return sums


def two_stage(mine, nc, first, finish, second, store, matmul_of, kept):
    nb = (mine + 1) // 2
    alone = mine % 2 == 1

    def in_pairs(visit, put):
        put = put or (lambda c, sums: None)

        def pair(i, _):
            one, two = visit(2 * i), visit(2 * i + 1)
            put(2 * i, one)
            put(2 * i + 1, two)
            return 0

        lax.fori_loop(0, nc // 2, pair, 0)

        @pl.when(nc % 2 == 1)
        def _():
            put(nc - 1, visit(nc - 1))

    def stage(start, now, before, rows=ROWS):
        scores_of = matmul_of(start)

        def visit(c):
            first(c, scores_of, now, rows)
            if rows < ROWS:
                for ref in now:
                    ref[rows:, col_tile(c)] = jnp.zeros((ROWS - rows, COLS), ref.dtype)
            return second(c, before) if before else None

        in_pairs(visit, store if before else None)
        finish(start, rows)

    def tail(before):
        in_pairs(lambda c: second(c, before), store)

    even, odd = kept

    @pl.when((nb > 0) & alone)
    def _():
        stage(0, even, None, LANES)

    @pl.when((nb > 0) & jnp.logical_not(alone))
    def _():
        stage(0, even, None)

    def visit(b, _):
        start = pl.multiple_of(b * ROWS - jnp.where(alone, LANES, 0), LANES)

        @pl.when(b % 2 == 1)
        def _():
            stage(start, odd, even)

        @pl.when(b % 2 == 0)
        def _():
            stage(start, even, odd)

        return 0

    lax.fori_loop(1, nb, visit, 0)

    @pl.when((nb > 0) & (nb % 2 == 1))
    def _():
        tail(even)

    @pl.when((nb > 0) & (nb % 2 == 0))
    def _():
        tail(odd)


def col_tile(c):
    return pl.ds(aligned(c, COLS), COLS)


def split2(value):
    high = value.astype(BF16).astype(F32)
    return high, value - high


def row_totals(ref):
    return jnp.sum(jnp.transpose(ref[...]), axis=0, keepdims=True)


def spread(row):
    return jnp.transpose(jnp.broadcast_to(row, (LANES, ROWS)))


def laid(column):
    return jnp.transpose(jnp.broadcast_to(column, (ROWS, LANES)))[0:1, :]


def sweep(quick, exact, low_ref, lost=None):
    low_ref[...] = jnp.ones_like(low_ref)
    quick()
    again = jnp.min(low_ref[...]) < LOWEST
    if lost is not None:
        again = again | lost()

    @pl.when(again)
    def _():
        exact()


def row_lse(xa, ya_ref, nc, buffers, top_ref, sum_ref, push_ref=None, g_ref=None):
    top_ref[...] = jnp.full(top_ref.shape, MASKED, F32)
    sum_ref[...] = jnp.zeros_like(sum_ref)
    if push_ref is not None:
        push_ref[...] = jnp.zeros_like(push_ref)

    def work(c, z_ref, _):
        for rg in range(0, ROWS, SUB):
            rows = slice(rg, rg + SUB)
            old = top_ref[rows, :]
            pieces = [piece_of(z_ref, rg, lt) for lt in range(LTS)]
            top = old
            for z in pieces:
                top = jnp.maximum(top, z)
            fade = jnp.exp(old - top)
            total = sum_ref[rows, :] * fade
            push = push_ref[rows, :] * fade if push_ref is not None else None
            for lt, z in enumerate(pieces):
                p = jnp.exp(z - top)
                total = total + p
                if push is not None:
                    push = push + p * (g_ref[:, lane_tile(c, lt)] - z)
            top_ref[rows, :] = top
            sum_ref[rows, :] = total
            if push is not None:
                push_ref[rows, :] = push

    piped(nc, lambda c: scores(xa, ya_ref, c), work, *buffers)
    tops = top_ref[...]
    top = jnp.max(tops, axis=1, keepdims=True)
    fade = jnp.exp(tops - top)
    total = jnp.sum(sum_ref[...] * fade, axis=1, keepdims=True)
    if push_ref is None:
        return top, total
    return top, total, jnp.sum(push_ref[...] * fade, axis=1, keepdims=True)


def row_potential(xa):
    lane = lax.broadcasted_iota(jnp.int32, (ROWS, LANES), 1)
    wide = xa.astype(F32)
    old = jnp.sum(jnp.where((lane >= 32) & (lane < 35), wide, 0.0), axis=1, keepdims=True)
    return lane, wide, old


def with_row_potential(lane, wide, pot):
    high, middle, low = split3(pot)
    new = jnp.where(lane == 32, high, jnp.where(lane == 33, middle, jnp.where(lane == 34, low, wide)))
    return new.astype(BF16)


def kernel_b(counts, xa_ref, yg_ref, gb_ref, l0, l1, l2, l3, g_ref, col_ref, ya_ref, za_ref, zb_ref, p_ref, q_ref, top_ref, sum_ref, weight_ref, low_ref, most_ref, acc_ref):
    _, count_here, count_next, member = around(counts)
    mine = row_blocks(count_here, count_next, member, 4)
    nb = (mine + 1) // 2
    nc = col_steps(count_next)

    def prepare(start, cols):
        logs = [ref[:, cols] for ref in (l0, l1, l2, l3)]
        top = jnp.maximum(jnp.maximum(logs[0], logs[1]), jnp.maximum(logs[2], logs[3]))
        total = sum(jnp.exp(one - top) for one in logs)
        ids = start + lax.broadcasted_iota(jnp.int32, (1, WIDE), 1)
        pot = jnp.where(ids < count_next, -DAMPING * (top + jnp.log(total)), 0.0)
        g_ref[:, cols] = pot
        write_augmented(ya_ref, start, yg_ref[:, cols], pot + gb_ref[:, cols], False)

    in_steps(yg_ref.shape[1], prepare)

    buffers = za_ref, zb_ref

    def quick():
        acc_ref[...] = jnp.zeros_like(acc_ref)

        def matmul_of(first_row):
            sum_ref[...] = jnp.zeros_like(sum_ref)
            return lambda c, start, size: scores(
                xa_ref[pl.ds(pl.multiple_of(first_row + start, size), size), :], ya_ref, c
            )

        def finish(start, rows):
            row = lax.broadcasted_iota(jnp.int32, (1, ROWS), 1)
            live = live_rows(start, member, count_here) & (row < rows)
            total = row_totals(sum_ref)
            low_ref[...] = jnp.minimum(low_ref[...], jnp.where(live, total, 1.0))
            pot = -DAMPING * (jnp.log(jnp.maximum(total, TINY)) - SHIFT)
            weight = jnp.where(live, jnp.exp(pot - SHIFT), 0.0)
            weight_ref[...] = spread(weight)
            most_ref[...] = jnp.maximum(most_ref[...], weight)

        two_stage(
            mine, nc, row_adder(sum_ref), finish, lambda c, kept: column_parts(c, [(kept[0], weight_ref)]),
            adder([acc_ref]), matmul_of, ((p_ref,), (q_ref,)),
        )

    def exact():
        acc_ref[...] = jnp.zeros_like(acc_ref)

        def row_visit(b, _):
            xa = xa_ref[pl.ds(aligned(b, ROWS), ROWS), :]
            lane, wide, old = row_potential(xa)
            live = old > 0.5 * MASKED
            top, total = row_lse(xa, ya_ref, nc, buffers, top_ref, sum_ref)
            pot = -DAMPING * (top + jnp.log(total) - SHIFT)
            xb = with_row_potential(lane, wide, jnp.where(live, pot + old - SHIFT, MASKED))
            piped(nc, lambda c: scores(xb, ya_ref, c), column_sums, *buffers, store=adder([acc_ref]))
            return 0

        lax.fori_loop(0, nb, row_visit, 0)

    def lost():
        total = jnp.sum(acc_ref[...], axis=0, keepdims=True)
        ids = lax.broadcasted_iota(jnp.int32, total.shape, 1)
        least = jnp.min(jnp.where((ids < count_next) & (nb > 0), total, 1.0))
        return least < jnp.max(most_ref[...]) * 2.0**-91

    most_ref[...] = jnp.zeros_like(most_ref)
    sweep(quick, exact, low_ref, lost)
    col_ref[...] = jnp.sum(acc_ref[...], axis=0, keepdims=True)


def kernel_c(
    counts, xa_ref, xt_ref, base_ref, yg_ref, gb_ref, g_ref, c0, c1, c2, c3,
    rows_ref, g2_ref, col_ref,
    ya_ref, za_ref, zb_ref, p_ref, w_ref, q_ref, v_ref, top_ref, sum_ref, push_ref, adj_ref, low_ref, cost_ref, weight_ref, xat_ref, acc_ref, acc0_ref, acc1_ref, acc2_ref,
):
    _, count_here, count_next, member = around(counts)
    mine = row_blocks(count_here, count_next, member, 4)
    nb = (mine + 1) // 2
    nc = col_steps(count_next)

    def prepare(start, cols):
        total = (c0[:, cols] + c1[:, cols]) + (c2[:, cols] + c3[:, cols])
        ids = start + lax.broadcasted_iota(jnp.int32, (1, WIDE), 1)
        log = jnp.log(jnp.maximum(total, TINY)) - g_ref[:, cols]
        pot = jnp.where(ids < count_next, -DAMPING * log, 0.0)
        g2_ref[:, cols] = pot
        write_augmented(ya_ref, start, yg_ref[:, cols], pot + gb_ref[:, cols], False)

    in_steps(yg_ref.shape[1], prepare)

    buffers = za_ref, zb_ref
    accs = acc0_ref, acc1_ref, acc2_ref

    ids = lax.broadcasted_iota(jnp.int32, g_ref.shape, 1)
    centre = jnp.sum(jnp.where(ids < count_next, g_ref[...], 0.0), axis=1, keepdims=True)
    centre = centre / (DAMPING * jnp.maximum(count_next, 1).astype(F32)) + 3.0
    cost_ref[...] = g2_ref[...] + (SHIFT - centre)

    line = lax.broadcasted_iota(jnp.int32, rows_ref.shape, 0)
    rows_ref[...] = jnp.where(line == 3, MASKED, 0.0)

    def close_rows(start, rows, row_log, mean_cost):
        rows_here = pl.ds(pl.multiple_of(start, LANES), ROWS)
        live = live_rows(start, member, count_here) & (lax.broadcasted_iota(jnp.int32, (1, ROWS), 1) < rows)
        pot = jnp.where(live, -DAMPING * row_log, 0.0)
        row_sum = jnp.where(live, jnp.exp(row_log + pot), 0.0)
        adjoint = jnp.where(live, mean_cost + centre, 0.0)
        full = jnp.where(live, pot + base_ref[:, rows_here] - SHIFT, MASKED)
        rows_ref[0:1, rows_here] = adjoint
        rows_ref[1:2, rows_here] = jnp.where(row_sum > 0.0, 1.0 / jnp.maximum(row_sum, TINY), 0.0)
        rows_ref[2:3, rows_here] = pot
        rows_ref[3:4, rows_here] = full
        return live, pot, adjoint, full

    def quick():
        acc_ref[...] = jnp.zeros_like(acc_ref)

        def matmul_of(first_row):
            sum_ref[...] = jnp.zeros_like(sum_ref)
            push_ref[...] = jnp.zeros_like(push_ref)
            return lambda c, start, size: scores(
                xa_ref[pl.ds(pl.multiple_of(first_row + start, size), size), :], ya_ref, c
            )

        def finish(start, rows):
            total = row_totals(sum_ref)
            safe = jnp.maximum(total, TINY)
            live, pot, adjoint, _ = close_rows(start, rows, jnp.log(safe) - SHIFT, row_totals(push_ref) / safe)
            low_ref[...] = jnp.minimum(low_ref[...], jnp.where(live, total, 1.0))
            weight = jnp.where(live, jnp.exp(pot - SHIFT), 0.0)
            row = lax.broadcasted_iota(jnp.int32, (16, ROWS), 0)
            packed = jnp.zeros((16, ROWS), F32)
            for k, piece in enumerate((*split2(weight), *split2(weight * adjoint))):
                packed = jnp.where(row == k, piece, packed)
            weight_ref[...] = packed.astype(BF16)

        def second(c, kept):
            weights = weight_ref[...]
            plan = jnp.dot(weights, kept[0][:, col_tile(c)], preferred_element_type=F32)
            cost = jnp.dot(weights, kept[1][:, col_tile(c)], preferred_element_type=F32)
            return plan, cost

        def store(c, sums):
            acc_ref[0:16, col_tile(c)] += sums[0]
            acc_ref[16:32, col_tile(c)] += sums[1]

        two_stage(
            mine, nc, row_adder(sum_ref, push_ref, cost_ref), finish, second, store, matmul_of,
            ((p_ref, w_ref), (q_ref, v_ref)),
        )
        acc0_ref[0:1, :] = acc_ref[0:1, :] + acc_ref[1:2, :]
        acc1_ref[0:1, :] = acc_ref[16:17, :] + acc_ref[17:18, :]
        acc2_ref[0:1, :] = acc_ref[2:3, :] + acc_ref[3:4, :]
        for ref in accs:
            ref[1:8, :] = jnp.zeros((7, ref.shape[1]), F32)

    def exact():
        for ref in accs:
            ref[...] = jnp.zeros_like(ref)

        def row_visit(b, _):
            xa = xa_ref[pl.ds(aligned(b, ROWS), ROWS), :]
            top, total, push = row_lse(xa, ya_ref, nc, buffers, top_ref, sum_ref, push_ref, cost_ref)
            _, pot, adjoint, full = close_rows(
                b * ROWS, ROWS, laid(top + jnp.log(total) - SHIFT), laid(push / total)
            )
            top_ref[...] = spread(pot - SHIFT)
            adj_ref[...] = spread(adjoint)
            write_augmented(xat_ref, 0, xt_ref[:, pl.ds(aligned(b, ROWS), ROWS)], full, True)
            xb = jnp.transpose(xat_ref[...]).astype(BF16)

            def work(c, z_ref, _):
                sums = [[jnp.zeros((8, LANES), F32) for _ in range(LTS)] for _ in range(3)]
                for rg in range(0, ROWS, 8):
                    pot_here = top_ref[rg : rg + 8, :]
                    adj_here = adj_ref[rg : rg + 8, :]
                    for lt in range(LTS):
                        tile = piece_of(z_ref, rg, lt, 8)
                        p = jnp.exp(tile)
                        sums[0][lt] = sums[0][lt] + p
                        sums[1][lt] = sums[1][lt] + p * (cost_ref[:, lane_tile(c, lt)] + (pot_here - tile))
                        sums[2][lt] = sums[2][lt] + p * adj_here
                return sums

            piped(nc, lambda c: scores(xb, ya_ref, c), work, *buffers, store=adder(accs))
            return 0

        lax.fori_loop(0, nb, row_visit, 0)

    sweep(quick, exact, low_ref)
    mass = jnp.sum(acc0_ref[...], axis=0, keepdims=True)
    slots = mass.shape[1]
    col_ref[:, 0:slots] = mass
    push = jnp.sum(acc1_ref[...], axis=0, keepdims=True)
    col_ref[:, slots : 2 * slots] = push + centre * mass
    col_ref[:, 2 * slots :] = jnp.sum(acc2_ref[...], axis=0, keepdims=True)


def kernel_d(
    counts, xt_ref, rows_ref, yg_ref, gb_ref, g2_ref, s0, s1, s2, s3,
    stat_ref, send_ref,
    ya_ref, xat_ref, xb_ref, p_ref, q_ref, first_ref, second_ref, weight_ref, acc_ref,
):
    _, count_here, count_next, member = around(counts)
    mine = row_blocks(count_here, count_next, member, 4)
    nb = (mine + 1) // 2
    nc = col_steps(count_next)
    slots = yg_ref.shape[1]
    local = xt_ref.shape[1]
    acc_ref[...] = jnp.zeros_like(acc_ref)

    def prepare(start, cols):
        mass, push, pulled = (
            (s0[:, part] + s1[:, part]) + (s2[:, part] + s3[:, part])
            for part in (pl.ds(start + k * slots, WIDE) for k in range(3))
        )
        inverse = jnp.where(mass > 0.0, 1.0 / jnp.maximum(mass, TINY), 0.0)
        pot = g2_ref[:, cols]
        stat_ref[0:1, cols] = pot + gb_ref[:, cols]
        stat_ref[1:2, cols] = push * inverse
        stat_ref[2:3, cols] = (push - DAMPING * pulled) * inverse
        stat_ref[3:4, cols] = inverse
        stat_ref[4:5, cols] = pot
        stat_ref[5:8, cols] = jnp.zeros((3, WIDE), F32)
        write_augmented(ya_ref, start, yg_ref[:, cols], pot + gb_ref[:, cols], False)

    in_steps(slots, prepare)
    for block in range(local // ROWS):
        @pl.when(2 * block < mine)
        def _():
            rows = slice(block * ROWS, (block + 1) * ROWS)
            write_augmented(xat_ref, 0, xt_ref[:, rows], rows_ref[3:4, rows], True)
            xb_ref[rows, :] = jnp.transpose(xat_ref[...]).astype(BF16)

    send_ref[:, slots : slots + local] = jnp.full((1, local), MASKED, F32)
    send_ref[:, slots + local :] = jnp.zeros((1, local), F32)

    def matmul_of(first_row):
        first_ref[...] = jnp.zeros_like(first_ref)
        second_ref[...] = jnp.zeros_like(second_ref)
        return lambda c, start, size: scores(
            xb_ref[pl.ds(pl.multiple_of(first_row + start, size), size), :], ya_ref, c
        )

    def sums(c, scores_of, kept, count):
        half = LANES
        for start in range(0, count, half):
            scored = scores_of(c, start, half)
            for rg in range(0, half, SUB):
                rows = slice(start + rg, start + rg + SUB)
                first = first_ref[rows, :]
                second = second_ref[rows, :]
                for lt in range(LTS):
                    p = jnp.exp(piece_of(scored, rg, lt))
                    kept[0][rows, lane_tile(c, lt)] = p
                    first = first + p * stat_ref[1:2, lane_tile(c, lt)]
                    second = second + p * stat_ref[2:3, lane_tile(c, lt)]
                first_ref[rows, :] = first
                second_ref[rows, :] = second

    def finish(start, rows):
        first, second = row_totals(first_ref), row_totals(second_ref)
        rows_here = pl.ds(pl.multiple_of(start, LANES), ROWS)
        start_adj, inverse, pot, full = (rows_ref[k : k + 1, rows_here] for k in range(4))
        middle_adj = start_adj - DAMPING * first * inverse
        last_adj = start_adj - DAMPING * second * inverse
        weight_ref[...] = spread(middle_adj)
        send_ref[:, pl.ds(pl.multiple_of(slots + start, LANES), ROWS)] = full
        send_ref[:, pl.ds(pl.multiple_of(slots + local + start, LANES), ROWS)] = 1.0 + DAMPING * last_adj - pot

    two_stage(
        mine, nc, sums, finish, lambda c, kept: column_parts(c, [(kept[0], weight_ref)]), adder([acc_ref]), matmul_of,
        ((p_ref,), (q_ref,)),
    )
    send_ref[:, 0:slots] = jnp.sum(acc_ref[...], axis=0, keepdims=True)


def kernel_f(counts, p0, p1, p2, p3, stat_ref, col_ref, early_ref, parts_ref):
    member = lax.axis_index("cell")
    slots = stat_ref.shape[1]
    local = early_ref.shape[1] - slots
    for k, ref in enumerate((p0, p1, p2, p3)):
        parts_ref[member ^ k] = ref[...]
    total = (p0[:, 0:slots] + p1[:, 0:slots]) + (p2[:, 0:slots] + p3[:, 0:slots])
    last = stat_ref[1:2, :] - DAMPING * total * stat_ref[3:4, :]
    col_ref[0:1, :] = stat_ref[0:1, :]
    col_ref[1:2, :] = DAMPING * last - stat_ref[4:5, :]
    for block in range(slots // LANES):
        owner, place = block % 4, block // 4
        lanes = slice(block * LANES, (block + 1) * LANES)
        for k in range(2):
            at = slots + k * local + place * LANES
            early_ref[k : k + 1, lanes] = parts_ref[owner, :, at : at + LANES]
    here = pl.ds(aligned(member, local), local)
    early_ref[:, slots:] = col_ref[:, here]


def kernel_e(
    counts, *refs, earlier,
):
    tall, wide = (COLS // 2, 2 * ROWS) if earlier else (COLS, ROWS)
    own_ref, rowpot_ref, other_ref, colpot_ref = refs[:4]
    local, slots = own_ref.shape[1], other_ref.shape[1]
    before, here, after, member = around(counts)
    if earlier:
        out_ref, xw_ref, tile_ref, ys_ref, beta_ref, za_ref, zb_ref, pull_ref, sum_ref = refs[4:]
        count_cols = before
        count_rows = jnp.clip(here - member * local, 0, local)
        nb = jnp.where(count_cols > 0, (count_rows + wide - 1) // wide, 0)
        pot_at = slots
    else:
        out_refs = refs[4:8]
        xw_ref, tile_ref, ys_ref, beta_ref, za_ref, zb_ref, pull_ref, sum_ref, out_ref = refs[8:]
        count_cols = after
        nb = (row_blocks(here, after, member, 4) + 1) // 2
        pot_at = slots
    nc = (count_cols + tall - 1) // tall
    out_ref[...] = jnp.zeros_like(out_ref)

    def prepare(c, _):
        cols = pl.ds(aligned(c, COLS), COLS)
        write_augmented(tile_ref, 0, other_ref[:, cols], colpot_ref[0:1, cols], False)
        ys_ref[cols, :] = jnp.transpose(tile_ref[...]).astype(BF16)
        beta_ref[cols, :] = jnp.transpose(jnp.broadcast_to(colpot_ref[1:2, cols], (LANES, COLS)))
        return 0

    @pl.when(nb > 0)
    def _():
        lax.fori_loop(0, col_steps(count_cols), prepare, 0)

    def row_visit(b, _):
        rows_here = pl.ds(aligned(b, wide), wide)
        own = own_ref[:, rows_here]
        pots = rowpot_ref[0:1, pl.ds(aligned(b + pot_at // wide, wide), wide)]
        write_augmented(xw_ref, 0, own, pots, True)
        xw = xw_ref[...]
        if earlier:
            alpha = rowpot_ref[1:2, pl.ds(aligned(b + pot_at // wide, wide), wide)]
        else:
            alpha = rowpot_ref[0:1, pl.ds(aligned(b + (pot_at + local) // wide, wide), wide)]
        sum_ref[...] = jnp.zeros_like(sum_ref)
        pull_ref[...] = jnp.zeros_like(pull_ref)

        def matmul(c):
            return jnp.dot(ys_ref[pl.ds(aligned(c, tall), tall), :], xw, preferred_element_type=F32)

        def work(c, z_ref, _):
            rounded = []
            sums = [jnp.zeros((8, LANES), F32) for _ in range(wide // LANES)]
            for jg in range(0, tall, 16):
                beta = beta_ref[pl.ds(pl.multiple_of(c * tall + jg, 16), 16), :]
                line = []
                for lt in range(wide // LANES):
                    tile = piece_of(z_ref, jg, lt, 16)
                    grad = jnp.exp(tile) * (tile + (alpha[:, lt * LANES : (lt + 1) * LANES] + beta))
                    sums[lt] = sums[lt] + (grad[0:8] + grad[8:16])
                    line.append(grad.astype(BF16))
                rounded.append(jnp.concatenate(line, axis=1))
            for lt in range(wide // LANES):
                sum_ref[:, lt * LANES : (lt + 1) * LANES] += sums[lt]
            feats = other_ref[:, pl.ds(aligned(c, tall), tall)]
            pull_ref[...] += jnp.dot(feats, jnp.concatenate(rounded, axis=0), preferred_element_type=F32)

        piped(nc, matmul, work, za_ref, zb_ref)
        total = jnp.sum(sum_ref[...], axis=0, keepdims=True)
        out_ref[:, rows_here] = 2.0 * (own.astype(F32) * total - pull_ref[...])
        return 0

    lax.fori_loop(0, nb, row_visit, 0)
    if not earlier:
        width = local // 4
        for k, ref in enumerate(out_refs):
            ref[...] = out_ref[:, pl.ds(pl.multiple_of((member ^ k) * width, LANES), width)]


def kernel_g(counts, target_ref, p0, p1, p2, p3, out_ref):
    member = lax.axis_index("cell")
    for k, ref in enumerate((p0, p1, p2, p3)):
        for i in range(ref.shape[1] // LANES):
            lanes = pl.ds(aligned(4 * i + (member ^ k), LANES), LANES)
            out_ref[:, lanes] = target_ref[:, lanes] + ref[:, i * LANES : (i + 1) * LANES]


def run(body, name, outs, scratch, limit, counts, *operands, flops=0):
    vmem = pl.BlockSpec(memory_space=pltpu.VMEM)
    return pl.pallas_call(
        body,
        name=name,
        out_shape=outs,
        in_specs=[pl.BlockSpec(memory_space=pltpu.SMEM)] + [vmem] * len(operands),
        out_specs=jax.tree.map(lambda _: vmem, outs),
        scratch_shapes=scratch,
        compiler_params=pltpu.CompilerParams(vmem_limit_bytes=limit * 1024 * 1024),
        cost_estimate=pl.CostEstimate(flops=flops, bytes_accessed=4_000_000, transcendentals=9_000_000),
    )(counts, *operands)


def shape(*dims, dtype=F32):
    return jax.ShapeDtypeStruct(dims, dtype)


def shifted(block, distance):
    size = lax.axis_size("tm")
    route = [(i - distance, i) for i in range(size) if 0 <= i - distance < size]
    return lax.ppermute(block, "tm", route)


def from_later(block, k):
    times, size = lax.axis_size("tm"), lax.axis_size("cell")
    route = [((t + 1) * size + (i ^ k), t * size + i) for t in range(times - 1) for i in range(size)]
    return lax.ppermute(block, ("tm", "cell"), route)


def swapped(block, k):
    return lax.ppermute(block, "cell", [(i, i ^ k) for i in range(lax.axis_size("cell"))])


def exchanged(block):
    near = swapped(block, 1)
    far = swapped(block, 2)
    return [block, near, far, swapped(far, 1)]


def per_device(embedding, counts):
    feat_dim, local = embedding.shape
    group = lax.axis_size("cell")
    slots = local * group

    counts = jnp.maximum(counts, lax.axis_index("cell") - group)
    source_parts = exchanged(embedding)
    source_parts[0] = swapped(source_parts[1], 1)
    ahead, ahead_far = from_later(embedding, 0), from_later(embedding, 2)
    target_parts = [ahead, swapped(ahead, 1), ahead_far, swapped(ahead_far, 1)]

    flops = 2 * local * slots * DEPTH
    aug = pltpu.VMEM((DEPTH, slots), BF16)
    narrow = pltpu.VMEM((ROWS, LANES), F32)
    flat = pltpu.VMEM((1, ROWS), F32)
    tile = pltpu.VMEM((DEPTH, ROWS), F32)
    wide = pltpu.VMEM((ROWS, slots), F32)
    half = pltpu.VMEM((ROWS, slots), BF16)
    turned_rows = pltpu.VMEM((16, ROWS), BF16)
    buffers = [pltpu.VMEM((ROWS, COLS), F32)] * 2
    long = pltpu.VMEM((8, slots), F32)
    grouped, targets, dealt, xa, base, gb, log = run(
        kernel_a, "column_log",
        (
            shape(feat_dim, slots, dtype=BF16), shape(feat_dim, slots, dtype=BF16), shape(feat_dim, local, dtype=BF16),
            shape(local, DEPTH, dtype=BF16), shape(1, local), shape(1, slots), shape(1, slots),
        ),
        [aug, pltpu.VMEM((DEPTH, local), F32), *buffers, long, long],
        16, counts, *source_parts, *target_parts, flops=flops,
    )
    logs = exchanged(log)
    g1, col1 = run(
        kernel_b, "first_sweep",
        (shape(1, slots), shape(1, slots)),
        [aug, *buffers, wide, wide, narrow, narrow, narrow, flat, flat, long],
        24, counts, xa, targets, gb, *logs, flops=2 * flops,
    )
    grouped, col1 = lax.optimization_barrier((grouped, col1))
    earlier = shifted(grouped, 1)
    rows, g2, stats = run(
        kernel_c, "second_sweep",
        (shape(8, local), shape(1, slots), shape(1, 3 * slots)),
        [
            aug, *buffers, half, half, half, half, narrow, narrow, narrow, narrow, flat,
            pltpu.VMEM((1, slots), F32), turned_rows, tile, pltpu.VMEM((32, slots), F32), long, long, long,
        ],
        28, counts, xa, dealt, base, targets, gb, g1, *exchanged(col1), flops=2 * flops,
    )
    rows, earlier = lax.optimization_barrier((rows, earlier))
    stat, send = run(
        kernel_d, "adjoint",
        (shape(8, slots), shape(1, slots + 2 * local)),
        [aug, tile, pltpu.VMEM((local, DEPTH), BF16), wide, wide, narrow, narrow, narrow, long],
        24, counts, dealt, rows, targets, gb, g2, *exchanged(stats), flops=2 * flops,
    )
    col_pair, early = run(
        kernel_f, "assemble",
        (shape(2, slots), shape(2, slots + local)),
        [pltpu.VMEM((group, 1, slots + 2 * local), F32)],
        8, counts, *exchanged(send), stat,
    )
    early = shifted(early, 1)

    def scratch_e(tall, wide):
        return [
            pltpu.VMEM((DEPTH, wide), BF16), pltpu.VMEM((DEPTH, COLS), F32), pltpu.VMEM((slots, DEPTH), BF16),
            pltpu.VMEM((slots, LANES), F32), *[pltpu.VMEM((tall, wide), F32)] * 2,
            pltpu.VMEM((feat_dim, wide), F32), pltpu.VMEM((8, wide), F32),
        ]

    parts = run(
        functools.partial(kernel_e, earlier=False), "source_gradient", (shape(feat_dim, local // group),) * group,
        scratch_e(COLS, ROWS) + [pltpu.VMEM((feat_dim, local), F32)],
        16, counts, dealt, send, targets, col_pair, flops=2 * flops,
    )
    parts = [parts[0]] + [swapped(parts[k], k) for k in range(1, group)]
    target_grad = run(
        functools.partial(kernel_e, earlier=True), "target_gradient", shape(feat_dim, local),
        scratch_e(COLS // 2, 2 * ROWS),
        16, counts, embedding, early, earlier, early, flops=2 * flops,
    )
    return run(kernel_g, "total", shape(feat_dim, local), [], 8, counts, target_grad, *parts)


def solution(mesh):
    in_specs = (P(None, ("tm", "cell")), P())
    out_specs = P(None, ("tm", "cell"))
    return jax.shard_map(
        per_device, mesh=mesh, in_specs=in_specs, out_specs=out_specs, check_vma=False
    )
```

```python
import functools

import jax
import jax.numpy as jnp
from jax import lax
from jax.experimental import pallas as pl
from jax.experimental.pallas import tpu as pltpu
from jax.sharding import PartitionSpec as P

ENTROPY = 0.25
PENALTY = 5.0
DAMPING = PENALTY / (PENALTY + ENTROPY)
MASKED = -1e30
SQ_SCALE = 1.0 / ENTROPY
DOT_SCALE = 2.0 / ENTROPY
TINY = 1e-37
SHIFT = 44.0
LOWEST = 1e-24

ROWS = 256
COLS = 512
LANES = 128
DEPTH = 128
F32 = jnp.float32
BF16 = jnp.bfloat16


def split3(value):
    high = value.astype(BF16).astype(F32)
    rest = value - high
    middle = rest.astype(BF16).astype(F32)
    return high, middle, rest - middle


def write_augmented(out_ref, start, feats, pot, is_row):
    n = feats.shape[1]
    cols = pl.ds(start, n)
    scaled = feats.astype(F32) * DOT_SCALE if is_row else feats
    out_ref[0:32, cols] = scaled.astype(out_ref.dtype)
    first = 0 if is_row else 3
    ones_from = 3 if is_row else 0
    row = lax.broadcasted_iota(jnp.int32, (16, n), 0)
    tail = jnp.where((row >= ones_from) & (row < ones_from + 3), 1.0, 0.0)
    for k, piece in enumerate(split3(pot)):
        tail = jnp.where(row == first + k, piece, tail)
    out_ref[32:48, cols] = tail.astype(out_ref.dtype)
    out_ref[48:128, cols] = jnp.zeros((80, n), out_ref.dtype)


def square_sum(feats):
    wide = feats.astype(F32)
    return jnp.sum(wide * wide, axis=0, keepdims=True)


def live_pot(feats, start, count):
    ids = start + lax.broadcasted_iota(jnp.int32, (1, feats.shape[1]), 1)
    return jnp.where(ids < count, -SQ_SCALE * square_sum(feats), MASKED)


def aligned(index, size):
    return pl.multiple_of(index * size, size)


def around(counts):
    size = counts.shape[0]
    time, member = lax.axis_index("tm"), lax.axis_index("cell")
    before = jnp.where(time > 0, counts[jnp.maximum(time - 1, 0)], 0)
    after = jnp.where(time + 1 < size, counts[jnp.minimum(time + 1, size - 1)], 0)
    return before, counts[time], after, member


def row_blocks(count_here, count_next, member, group):
    blocks = pl.cdiv(count_here, LANES)
    mine = jnp.maximum((blocks - member + group - 1) // group, 0)
    return jnp.where(count_next > 0, mine, 0)


def live_rows(start, member, count, group=4):
    row = lax.broadcasted_iota(jnp.int32, (1, ROWS), 1)
    slot = (group * (start // LANES) + member) * LANES + row
    return slot + jnp.where(row >= LANES, (group - 1) * LANES, 0) < count


def col_steps(count):
    return (count + COLS - 1) // COLS


LTS = COLS // LANES
SUB = 32
WIDE = 1536


def scores(xa, ya_ref, c, cols=COLS):
    return jnp.dot(xa, ya_ref[:, pl.ds(aligned(c, cols), cols)], preferred_element_type=F32)


def piped(count, matmul, work, first_ref, second_ref, load=None, store=None):
    load = load or (lambda c: None)
    store = store or (lambda c, state: None)
    first_ref[...] = matmul(0)

    def pair(i, _):
        here, there = 2 * i, 2 * i + 1
        states = load(here), load(there)
        second_ref[...] = matmul(there)
        one = work(here, first_ref, states[0])
        first_ref[...] = matmul(jnp.minimum(there + 1, count - 1))
        two = work(there, second_ref, states[1])
        store(here, one)
        store(there, two)
        return 0

    lax.fori_loop(0, count // 2, pair, 0)

    @pl.when(count % 2 == 1)
    def _():
        store(count - 1, work(count - 1, first_ref, load(count - 1)))


def adder(acc_refs):
    def store(c, sums):
        for k, acc_ref in enumerate(acc_refs):
            lts = len(sums[k])
            for lt in range(lts):
                acc_ref[:, lane_tile(c, lt, lts)] += sums[k][lt]

    return store


def lane_tile(c, lt, lts=LTS):
    return pl.ds(aligned(c * lts + lt, LANES), LANES)


def piece_of(z_ref, rg, lt, size=SUB):
    return z_ref[rg : rg + size, lt * LANES : (lt + 1) * LANES]


def in_steps(total, visit):
    for start in range(0, total, WIDE):
        visit(start, slice(start, start + WIDE))


def kernel_a(
    counts, x0, x1, x2, x3, y0, y1, y2, y3,
    xg_ref, yg_ref, xt_ref, xa_ref, base_ref, gb_ref, log_ref,
    ya_ref, xat_ref, za_ref, zb_ref, top_ref, sum_ref,
):
    _, count_here, count_next, member = around(counts)
    group = 4
    mine = row_blocks(count_here, count_next, member, group)
    nb = (mine + 1) // 2
    nc = col_steps(count_next)
    local = x0.shape[1]
    for k, y_ref in enumerate((y0, y1, y2, y3)):
        yg_ref[:, pl.ds(aligned(member ^ k, local), local)] = y_ref[...]
    for k, x_ref in enumerate((x0, x1, x2, x3)):
        xg_ref[:, pl.ds(aligned(member ^ k, local), local)] = x_ref[...]
    sum_ref[...] = jnp.zeros_like(sum_ref)

    def prepare(start, cols):
        feats = yg_ref[:, cols]
        pot = live_pot(feats, start, count_next)
        gb_ref[:, cols] = pot
        write_augmented(ya_ref, start, feats, pot, False)

    in_steps(group * local, prepare)
    for k in range(local // LANES):
        lanes = slice(k * LANES, (k + 1) * LANES)
        block_id = group * k + member
        piece = xg_ref[:, pl.ds(aligned(block_id, LANES), LANES)]
        xt_ref[:, lanes] = piece
        pot = live_pot(piece, block_id * LANES, count_here) + SHIFT
        base_ref[:, lanes] = pot
        write_augmented(xat_ref, k * LANES, piece, pot, True)
        xa_ref[lanes, :] = jnp.transpose(xat_ref[:, lanes]).astype(BF16)

    def exact():
        top_ref[...] = jnp.full(top_ref.shape, MASKED, F32)
        sum_ref[...] = jnp.zeros_like(sum_ref)

        def row_visit(b, _):
            xa = xa_ref[pl.ds(aligned(b, ROWS), ROWS), :]

            def load(c):
                return [(top_ref[:, lane_tile(c, lt)], sum_ref[:, lane_tile(c, lt)]) for lt in range(LTS)]

            def work(c, z_ref, state):
                after = []
                for lt, (old, total) in enumerate(state):
                    tile = z_ref[:, lt * LANES : (lt + 1) * LANES].reshape(ROWS // 8, 8, LANES)
                    top = jnp.maximum(old, jnp.max(tile, axis=0))
                    total = total * jnp.exp(old - top) + jnp.sum(jnp.exp(tile - top[None]), axis=0)
                    after.append((top, total))
                return after

            def store(c, state):
                for lt, (top, total) in enumerate(state):
                    top_ref[:, lane_tile(c, lt)] = top
                    sum_ref[:, lane_tile(c, lt)] = total

            piped(nc, lambda c: scores(xa, ya_ref, c), work, za_ref, zb_ref, load, store)
            return 0

        lax.fori_loop(0, nb, row_visit, 0)
        tops = top_ref[...]
        top = jnp.max(tops, axis=0, keepdims=True)
        total = jnp.sum(sum_ref[...] * jnp.exp(tops - top), axis=0, keepdims=True)
        log_ref[...] = top + jnp.log(jnp.maximum(total, TINY)) - SHIFT

    def quick_rows(first_block, blocks):
        def tile_sums(c):
            totals = [jnp.zeros((8, LANES), F32) for _ in range(LTS)]
            for k in range(blocks):
                z = scores(xa_ref[pl.ds(aligned(first_block + k, LANES), LANES), :], ya_ref, c)
                for lt in range(LTS):
                    p = jnp.exp(z[:, lt * LANES : (lt + 1) * LANES])
                    totals[lt] = totals[lt] + jnp.sum(p.reshape(LANES // 8, 8, LANES), axis=0)
            return [totals]

        over_tiles(nc, tile_sums, adder([sum_ref]))

    def quick_visit(b, _):
        quick_rows(2 * b, 2)
        return 0

    lax.fori_loop(0, mine // 2, quick_visit, 0)

    @pl.when(mine % 2 == 1)
    def _():
        quick_rows(mine - 1, 1)

    total = jnp.sum(sum_ref[...], axis=0, keepdims=True)
    log_ref[...] = jnp.where(total > 0.0, jnp.log(jnp.maximum(total, TINY)) - SHIFT, MASKED)
    ids = lax.broadcasted_iota(jnp.int32, total.shape, 1)
    lowest = jnp.min(jnp.where(ids < count_next, total, 1.0))

    @pl.when((lowest < LOWEST) & (nb > 0))
    def _():
        exact()


def column_sums(c, z_ref, _):
    rows, cols = z_ref.shape
    sums = []
    for lt in range(cols // LANES):
        p = jnp.exp(z_ref[:, lt * LANES : (lt + 1) * LANES])
        sums.append(jnp.sum(p.reshape(rows // 8, 8, LANES), axis=0))
    return [sums]


def row_adder(sum_ref, push_ref=None, g_ref=None):
    def first(c, scores_of, kept, count):
        half = LANES
        for start in range(0, count, half):
            scored = scores_of(c, start, half)
            for rg in range(0, half, SUB):
                rows = slice(start + rg, start + rg + SUB)
                total = sum_ref[rows, :]
                push = push_ref[rows, :] if push_ref is not None else None
                for lt in range(LTS):
                    z = piece_of(scored, rg, lt)
                    p = jnp.exp(z)
                    total = total + p
                    kept[0][rows, lane_tile(c, lt)] = p.astype(kept[0].dtype)
                    if push is not None:
                        part = p * (g_ref[:, lane_tile(c, lt)] - z)
                        push = push + part
                        kept[1][rows, lane_tile(c, lt)] = part.astype(kept[1].dtype)
                sum_ref[rows, :] = total
                if push is not None:
                    push_ref[rows, :] = push

    return first


def column_parts(c, plan):
    sums = [[jnp.zeros((8, LANES), F32) for _ in range(LTS)] for _ in plan]
    for rg in range(0, ROWS, 8):
        for k, (kept_ref, weight_ref) in enumerate(plan):
            scale = weight_ref[rg : rg + 8, :]
            for lt in range(LTS):
                sums[k][lt] = sums[k][lt] + scale * kept_ref[rg : rg + 8, lane_tile(c, lt)]
    return sums


def over_tiles(count, visit, put=None):
    put = put or (lambda c, sums: None)

    def body(tiles):
        for c, sums in [(c, visit(c)) for c in tiles]:
            put(c, sums)

    def four(i, _):
        body([4 * i + k for k in range(4)])
        return 0

    lax.fori_loop(0, count // 4, four, 0)

    @pl.when(count % 4 >= 2)
    def _():
        first = count // 4 * 4
        body([first, first + 1])

    @pl.when(count % 2 == 1)
    def _():
        body([count - 1])


def two_stage(mine, nc, first, finish, second, store, matmul_of, kept):
    nb = (mine + 1) // 2
    alone = mine % 2 == 1

    def stage(start, now, before, rows=ROWS):
        scores_of = matmul_of(start)

        def visit(c):
            first(c, scores_of, now, rows)
            if rows < ROWS:
                for ref in now:
                    ref[rows:, col_tile(c)] = jnp.zeros((ROWS - rows, COLS), ref.dtype)
            return second(c, before) if before else None

        over_tiles(nc, visit, store if before else None)
        finish(start, rows)

    def tail(before):
        over_tiles(nc, lambda c: second(c, before), store)

    even, odd = kept

    @pl.when((nb > 0) & alone)
    def _():
        stage(0, even, None, LANES)

    @pl.when((nb > 0) & jnp.logical_not(alone))
    def _():
        stage(0, even, None)

    def visit(b, _):
        start = pl.multiple_of(b * ROWS - jnp.where(alone, LANES, 0), LANES)

        @pl.when(b % 2 == 1)
        def _():
            stage(start, odd, even)

        @pl.when(b % 2 == 0)
        def _():
            stage(start, even, odd)

        return 0

    lax.fori_loop(1, nb, visit, 0)

    @pl.when((nb > 0) & (nb % 2 == 1))
    def _():
        tail(even)

    @pl.when((nb > 0) & (nb % 2 == 0))
    def _():
        tail(odd)


def col_tile(c):
    return pl.ds(aligned(c, COLS), COLS)


def split2(value):
    high = value.astype(BF16).astype(F32)
    return high, value - high


def row_totals(ref):
    return jnp.sum(jnp.transpose(ref[...]), axis=0, keepdims=True)


def spread(row):
    return jnp.transpose(jnp.broadcast_to(row, (LANES, ROWS)))


def laid(column):
    return jnp.transpose(jnp.broadcast_to(column, (ROWS, LANES)))[0:1, :]


def sweep(quick, exact, low_ref, lost=None):
    low_ref[...] = jnp.ones_like(low_ref)
    quick()
    again = jnp.min(low_ref[...]) < LOWEST
    if lost is not None:
        again = again | lost()

    @pl.when(again)
    def _():
        exact()


def row_lse(xa, ya_ref, nc, buffers, top_ref, sum_ref, push_ref=None, g_ref=None):
    top_ref[...] = jnp.full(top_ref.shape, MASKED, F32)
    sum_ref[...] = jnp.zeros_like(sum_ref)
    if push_ref is not None:
        push_ref[...] = jnp.zeros_like(push_ref)

    def work(c, z_ref, _):
        for rg in range(0, ROWS, SUB):
            rows = slice(rg, rg + SUB)
            old = top_ref[rows, :]
            pieces = [piece_of(z_ref, rg, lt) for lt in range(LTS)]
            top = old
            for z in pieces:
                top = jnp.maximum(top, z)
            fade = jnp.exp(old - top)
            total = sum_ref[rows, :] * fade
            push = push_ref[rows, :] * fade if push_ref is not None else None
            for lt, z in enumerate(pieces):
                p = jnp.exp(z - top)
                total = total + p
                if push is not None:
                    push = push + p * (g_ref[:, lane_tile(c, lt)] - z)
            top_ref[rows, :] = top
            sum_ref[rows, :] = total
            if push is not None:
                push_ref[rows, :] = push

    piped(nc, lambda c: scores(xa, ya_ref, c), work, *buffers)
    tops = top_ref[...]
    top = jnp.max(tops, axis=1, keepdims=True)
    fade = jnp.exp(tops - top)
    total = jnp.sum(sum_ref[...] * fade, axis=1, keepdims=True)
    if push_ref is None:
        return top, total
    return top, total, jnp.sum(push_ref[...] * fade, axis=1, keepdims=True)


def row_potential(xa):
    lane = lax.broadcasted_iota(jnp.int32, (ROWS, LANES), 1)
    wide = xa.astype(F32)
    old = jnp.sum(jnp.where((lane >= 32) & (lane < 35), wide, 0.0), axis=1, keepdims=True)
    return lane, wide, old


def with_row_potential(lane, wide, pot):
    high, middle, low = split3(pot)
    new = jnp.where(lane == 32, high, jnp.where(lane == 33, middle, jnp.where(lane == 34, low, wide)))
    return new.astype(BF16)


def kernel_b(counts, xa_ref, yg_ref, gb_ref, l0, l1, l2, l3, g_ref, col_ref, ya_ref, za_ref, zb_ref, p_ref, q_ref, top_ref, sum_ref, weight_ref, low_ref, most_ref, acc_ref):
    _, count_here, count_next, member = around(counts)
    mine = row_blocks(count_here, count_next, member, 4)
    nb = (mine + 1) // 2
    nc = col_steps(count_next)

    def prepare(start, cols):
        logs = [ref[:, cols] for ref in (l0, l1, l2, l3)]
        top = jnp.maximum(jnp.maximum(logs[0], logs[1]), jnp.maximum(logs[2], logs[3]))
        total = sum(jnp.exp(one - top) for one in logs)
        ids = start + lax.broadcasted_iota(jnp.int32, (1, WIDE), 1)
        pot = jnp.where(ids < count_next, -DAMPING * (top + jnp.log(total)), 0.0)
        g_ref[:, cols] = pot
        write_augmented(ya_ref, start, yg_ref[:, cols], pot + gb_ref[:, cols], False)

    in_steps(yg_ref.shape[1], prepare)

    buffers = za_ref, zb_ref

    def quick():
        acc_ref[...] = jnp.zeros_like(acc_ref)

        def matmul_of(first_row):
            sum_ref[...] = jnp.zeros_like(sum_ref)
            return lambda c, start, size: scores(
                xa_ref[pl.ds(pl.multiple_of(first_row + start, size), size), :], ya_ref, c
            )

        def finish(start, rows):
            row = lax.broadcasted_iota(jnp.int32, (1, ROWS), 1)
            live = live_rows(start, member, count_here) & (row < rows)
            total = row_totals(sum_ref)
            low_ref[...] = jnp.minimum(low_ref[...], jnp.where(live, total, 1.0))
            pot = -DAMPING * (jnp.log(jnp.maximum(total, TINY)) - SHIFT)
            weight = jnp.where(live, jnp.exp(pot - SHIFT), 0.0)
            weight_ref[...] = spread(weight)
            most_ref[...] = jnp.maximum(most_ref[...], weight)

        two_stage(
            mine, nc, row_adder(sum_ref), finish, lambda c, kept: column_parts(c, [(kept[0], weight_ref)]),
            adder([acc_ref]), matmul_of, ((p_ref,), (q_ref,)),
        )

    def exact():
        acc_ref[...] = jnp.zeros_like(acc_ref)

        def row_visit(b, _):
            xa = xa_ref[pl.ds(aligned(b, ROWS), ROWS), :]
            lane, wide, old = row_potential(xa)
            live = old > 0.5 * MASKED
            top, total = row_lse(xa, ya_ref, nc, buffers, top_ref, sum_ref)
            pot = -DAMPING * (top + jnp.log(total) - SHIFT)
            xb = with_row_potential(lane, wide, jnp.where(live, pot + old - SHIFT, MASKED))
            piped(nc, lambda c: scores(xb, ya_ref, c), column_sums, *buffers, store=adder([acc_ref]))
            return 0

        lax.fori_loop(0, nb, row_visit, 0)

    def lost():
        total = jnp.sum(acc_ref[...], axis=0, keepdims=True)
        ids = lax.broadcasted_iota(jnp.int32, total.shape, 1)
        least = jnp.min(jnp.where((ids < count_next) & (nb > 0), total, 1.0))
        return least < jnp.max(most_ref[...]) * 2.0**-91

    most_ref[...] = jnp.zeros_like(most_ref)
    sweep(quick, exact, low_ref, lost)
    col_ref[...] = jnp.sum(acc_ref[...], axis=0, keepdims=True)


def kernel_c(
    counts, xa_ref, xt_ref, base_ref, yg_ref, gb_ref, g_ref, c0, c1, c2, c3,
    rows_ref, g2_ref, col_ref,
    ya_ref, za_ref, zb_ref, p_ref, w_ref, q_ref, v_ref, top_ref, sum_ref, push_ref, adj_ref, low_ref, cost_ref, weight_ref, xat_ref, acc_ref, acc0_ref, acc1_ref, acc2_ref,
):
    _, count_here, count_next, member = around(counts)
    mine = row_blocks(count_here, count_next, member, 4)
    nb = (mine + 1) // 2
    nc = col_steps(count_next)

    def prepare(start, cols):
        total = (c0[:, cols] + c1[:, cols]) + (c2[:, cols] + c3[:, cols])
        ids = start + lax.broadcasted_iota(jnp.int32, (1, WIDE), 1)
        log = jnp.log(jnp.maximum(total, TINY)) - g_ref[:, cols]
        pot = jnp.where(ids < count_next, -DAMPING * log, 0.0)
        g2_ref[:, cols] = pot
        write_augmented(ya_ref, start, yg_ref[:, cols], pot + gb_ref[:, cols], False)

    in_steps(yg_ref.shape[1], prepare)

    buffers = za_ref, zb_ref
    accs = acc0_ref, acc1_ref, acc2_ref

    ids = lax.broadcasted_iota(jnp.int32, g_ref.shape, 1)
    centre = jnp.sum(jnp.where(ids < count_next, g_ref[...], 0.0), axis=1, keepdims=True)
    centre = centre / (DAMPING * jnp.maximum(count_next, 1).astype(F32)) + 3.0
    cost_ref[...] = g2_ref[...] + (SHIFT - centre)

    line = lax.broadcasted_iota(jnp.int32, rows_ref.shape, 0)
    rows_ref[...] = jnp.where(line == 3, MASKED, 0.0)

    def close_rows(start, rows, row_log, mean_cost):
        rows_here = pl.ds(pl.multiple_of(start, LANES), ROWS)
        live = live_rows(start, member, count_here) & (lax.broadcasted_iota(jnp.int32, (1, ROWS), 1) < rows)
        pot = jnp.where(live, -DAMPING * row_log, 0.0)
        row_sum = jnp.where(live, jnp.exp(row_log + pot), 0.0)
        adjoint = jnp.where(live, mean_cost + centre, 0.0)
        full = jnp.where(live, pot + base_ref[:, rows_here] - SHIFT, MASKED)
        rows_ref[0:1, rows_here] = adjoint
        rows_ref[1:2, rows_here] = jnp.where(row_sum > 0.0, 1.0 / jnp.maximum(row_sum, TINY), 0.0)
        rows_ref[2:3, rows_here] = pot
        rows_ref[3:4, rows_here] = full
        return live, pot, adjoint, full

    def quick():
        acc_ref[...] = jnp.zeros_like(acc_ref)

        def matmul_of(first_row):
            sum_ref[...] = jnp.zeros_like(sum_ref)
            push_ref[...] = jnp.zeros_like(push_ref)
            return lambda c, start, size: scores(
                xa_ref[pl.ds(pl.multiple_of(first_row + start, size), size), :], ya_ref, c
            )

        def finish(start, rows):
            total = row_totals(sum_ref)
            safe = jnp.maximum(total, TINY)
            live, pot, adjoint, _ = close_rows(start, rows, jnp.log(safe) - SHIFT, row_totals(push_ref) / safe)
            low_ref[...] = jnp.minimum(low_ref[...], jnp.where(live, total, 1.0))
            weight = jnp.where(live, jnp.exp(pot - SHIFT), 0.0)
            row = lax.broadcasted_iota(jnp.int32, (16, ROWS), 0)
            packed = jnp.zeros((16, ROWS), F32)
            for k, piece in enumerate((*split2(weight), *split2(weight * adjoint))):
                packed = jnp.where(row == k, piece, packed)
            weight_ref[...] = packed.astype(BF16)

        def second(c, kept):
            weights = weight_ref[...]
            plan = jnp.dot(weights, kept[0][:, col_tile(c)], preferred_element_type=F32)
            cost = jnp.dot(weights, kept[1][:, col_tile(c)], preferred_element_type=F32)
            return plan, cost

        def store(c, sums):
            acc_ref[0:16, col_tile(c)] += sums[0]
            acc_ref[16:32, col_tile(c)] += sums[1]

        two_stage(
            mine, nc, row_adder(sum_ref, push_ref, cost_ref), finish, second, store, matmul_of,
            ((p_ref, w_ref), (q_ref, v_ref)),
        )
        acc0_ref[0:1, :] = acc_ref[0:1, :] + acc_ref[1:2, :]
        acc1_ref[0:1, :] = acc_ref[16:17, :] + acc_ref[17:18, :]
        acc2_ref[0:1, :] = acc_ref[2:3, :] + acc_ref[3:4, :]
        for ref in accs:
            ref[1:8, :] = jnp.zeros((7, ref.shape[1]), F32)

    def exact():
        for ref in accs:
            ref[...] = jnp.zeros_like(ref)

        def row_visit(b, _):
            xa = xa_ref[pl.ds(aligned(b, ROWS), ROWS), :]
            top, total, push = row_lse(xa, ya_ref, nc, buffers, top_ref, sum_ref, push_ref, cost_ref)
            _, pot, adjoint, full = close_rows(
                b * ROWS, ROWS, laid(top + jnp.log(total) - SHIFT), laid(push / total)
            )
            top_ref[...] = spread(pot - SHIFT)
            adj_ref[...] = spread(adjoint)
            write_augmented(xat_ref, 0, xt_ref[:, pl.ds(aligned(b, ROWS), ROWS)], full, True)
            xb = jnp.transpose(xat_ref[...]).astype(BF16)

            def work(c, z_ref, _):
                sums = [[jnp.zeros((8, LANES), F32) for _ in range(LTS)] for _ in range(3)]
                for rg in range(0, ROWS, 8):
                    pot_here = top_ref[rg : rg + 8, :]
                    adj_here = adj_ref[rg : rg + 8, :]
                    for lt in range(LTS):
                        tile = piece_of(z_ref, rg, lt, 8)
                        p = jnp.exp(tile)
                        sums[0][lt] = sums[0][lt] + p
                        sums[1][lt] = sums[1][lt] + p * (cost_ref[:, lane_tile(c, lt)] + (pot_here - tile))
                        sums[2][lt] = sums[2][lt] + p * adj_here
                return sums

            piped(nc, lambda c: scores(xb, ya_ref, c), work, *buffers, store=adder(accs))
            return 0

        lax.fori_loop(0, nb, row_visit, 0)

    sweep(quick, exact, low_ref)
    mass = jnp.sum(acc0_ref[...], axis=0, keepdims=True)
    slots = mass.shape[1]
    col_ref[:, 0:slots] = mass
    push = jnp.sum(acc1_ref[...], axis=0, keepdims=True)
    col_ref[:, slots : 2 * slots] = push + centre * mass
    col_ref[:, 2 * slots :] = jnp.sum(acc2_ref[...], axis=0, keepdims=True)


def kernel_d(
    counts, xt_ref, rows_ref, yg_ref, gb_ref, g2_ref, s0, s1, s2, s3,
    stat_ref, send_ref,
    ya_ref, xat_ref, xb_ref, p_ref, q_ref, first_ref, second_ref, weight_ref, acc_ref,
):
    _, count_here, count_next, member = around(counts)
    mine = row_blocks(count_here, count_next, member, 4)
    nb = (mine + 1) // 2
    nc = col_steps(count_next)
    slots = yg_ref.shape[1]
    local = xt_ref.shape[1]
    acc_ref[...] = jnp.zeros_like(acc_ref)

    def prepare(start, cols):
        mass, push, pulled = (
            (s0[:, part] + s1[:, part]) + (s2[:, part] + s3[:, part])
            for part in (pl.ds(start + k * slots, WIDE) for k in range(3))
        )
        inverse = jnp.where(mass > 0.0, 1.0 / jnp.maximum(mass, TINY), 0.0)
        pot = g2_ref[:, cols]
        stat_ref[0:1, cols] = pot + gb_ref[:, cols]
        stat_ref[1:2, cols] = push * inverse
        stat_ref[2:3, cols] = (push - DAMPING * pulled) * inverse
        stat_ref[3:4, cols] = inverse
        stat_ref[4:5, cols] = pot
        stat_ref[5:8, cols] = jnp.zeros((3, WIDE), F32)
        write_augmented(ya_ref, start, yg_ref[:, cols], pot + gb_ref[:, cols], False)

    in_steps(slots, prepare)
    for block in range(local // ROWS):
        @pl.when(2 * block < mine)
        def _():
            rows = slice(block * ROWS, (block + 1) * ROWS)
            write_augmented(xat_ref, 0, xt_ref[:, rows], rows_ref[3:4, rows], True)
            xb_ref[rows, :] = jnp.transpose(xat_ref[...]).astype(BF16)

    send_ref[:, slots : slots + local] = jnp.full((1, local), MASKED, F32)
    send_ref[:, slots + local :] = jnp.zeros((1, local), F32)

    def matmul_of(first_row):
        first_ref[...] = jnp.zeros_like(first_ref)
        second_ref[...] = jnp.zeros_like(second_ref)
        return lambda c, start, size: scores(
            xb_ref[pl.ds(pl.multiple_of(first_row + start, size), size), :], ya_ref, c
        )

    def sums(c, scores_of, kept, count):
        half = LANES
        for start in range(0, count, half):
            scored = scores_of(c, start, half)
            for rg in range(0, half, SUB):
                rows = slice(start + rg, start + rg + SUB)
                first = first_ref[rows, :]
                second = second_ref[rows, :]
                for lt in range(LTS):
                    p = jnp.exp(piece_of(scored, rg, lt))
                    kept[0][rows, lane_tile(c, lt)] = p
                    first = first + p * stat_ref[1:2, lane_tile(c, lt)]
                    second = second + p * stat_ref[2:3, lane_tile(c, lt)]
                first_ref[rows, :] = first
                second_ref[rows, :] = second

    def finish(start, rows):
        first, second = row_totals(first_ref), row_totals(second_ref)
        rows_here = pl.ds(pl.multiple_of(start, LANES), ROWS)
        start_adj, inverse, pot, full = (rows_ref[k : k + 1, rows_here] for k in range(4))
        middle_adj = start_adj - DAMPING * first * inverse
        last_adj = start_adj - DAMPING * second * inverse
        weight_ref[...] = spread(middle_adj)
        send_ref[:, pl.ds(pl.multiple_of(slots + start, LANES), ROWS)] = full
        send_ref[:, pl.ds(pl.multiple_of(slots + local + start, LANES), ROWS)] = 1.0 + DAMPING * last_adj - pot

    two_stage(
        mine, nc, sums, finish, lambda c, kept: column_parts(c, [(kept[0], weight_ref)]), adder([acc_ref]), matmul_of,
        ((p_ref,), (q_ref,)),
    )
    send_ref[:, 0:slots] = jnp.sum(acc_ref[...], axis=0, keepdims=True)


def kernel_f(counts, p0, p1, p2, p3, stat_ref, col_ref, early_ref, parts_ref):
    member = lax.axis_index("cell")
    slots = stat_ref.shape[1]
    local = early_ref.shape[1] - slots
    for k, ref in enumerate((p0, p1, p2, p3)):
        parts_ref[member ^ k] = ref[...]
    total = (p0[:, 0:slots] + p1[:, 0:slots]) + (p2[:, 0:slots] + p3[:, 0:slots])
    last = stat_ref[1:2, :] - DAMPING * total * stat_ref[3:4, :]
    col_ref[0:1, :] = stat_ref[0:1, :]
    col_ref[1:2, :] = DAMPING * last - stat_ref[4:5, :]
    for block in range(slots // LANES):
        owner, place = block % 4, block // 4
        lanes = slice(block * LANES, (block + 1) * LANES)
        for k in range(2):
            at = slots + k * local + place * LANES
            early_ref[k : k + 1, lanes] = parts_ref[owner, :, at : at + LANES]
    here = pl.ds(aligned(member, local), local)
    early_ref[:, slots:] = col_ref[:, here]


def kernel_e(
    counts, *refs, earlier,
):
    tall, wide = (COLS // 2, 2 * ROWS) if earlier else (COLS, ROWS)
    own_ref, rowpot_ref, other_ref, colpot_ref = refs[:4]
    local, slots = own_ref.shape[1], other_ref.shape[1]
    before, here, after, member = around(counts)
    if earlier:
        out_ref, xw_ref, tile_ref, ys_ref, beta_ref, za_ref, zb_ref, pull_ref, sum_ref = refs[4:]
        count_cols = before
        count_rows = jnp.clip(here - member * local, 0, local)
        nb = jnp.where(count_cols > 0, (count_rows + wide - 1) // wide, 0)
        pot_at = slots
    else:
        out_refs = refs[4:8]
        xw_ref, tile_ref, ys_ref, beta_ref, za_ref, zb_ref, pull_ref, sum_ref, out_ref = refs[8:]
        count_cols = after
        nb = (row_blocks(here, after, member, 4) + 1) // 2
        pot_at = slots
    nc = (count_cols + tall - 1) // tall
    out_ref[...] = jnp.zeros_like(out_ref)

    def prepare(c, _):
        cols = pl.ds(aligned(c, COLS), COLS)
        write_augmented(tile_ref, 0, other_ref[:, cols], colpot_ref[0:1, cols], False)
        ys_ref[cols, :] = jnp.transpose(tile_ref[...]).astype(BF16)
        beta_ref[cols, :] = jnp.transpose(jnp.broadcast_to(colpot_ref[1:2, cols], (LANES, COLS)))
        return 0

    @pl.when(nb > 0)
    def _():
        lax.fori_loop(0, col_steps(count_cols), prepare, 0)

    def row_visit(b, _):
        rows_here = pl.ds(aligned(b, wide), wide)
        own = own_ref[:, rows_here]
        pots = rowpot_ref[0:1, pl.ds(aligned(b + pot_at // wide, wide), wide)]
        write_augmented(xw_ref, 0, own, pots, True)
        xw = xw_ref[...]
        if earlier:
            alpha = rowpot_ref[1:2, pl.ds(aligned(b + pot_at // wide, wide), wide)]
        else:
            alpha = rowpot_ref[0:1, pl.ds(aligned(b + (pot_at + local) // wide, wide), wide)]
        sum_ref[...] = jnp.zeros_like(sum_ref)
        pull_ref[...] = jnp.zeros_like(pull_ref)

        def matmul(c):
            return jnp.dot(ys_ref[pl.ds(aligned(c, tall), tall), :], xw, preferred_element_type=F32)

        def work(c, z_ref, _):
            rounded = []
            sums = [jnp.zeros((8, LANES), F32) for _ in range(wide // LANES)]
            for jg in range(0, tall, 16):
                beta = beta_ref[pl.ds(pl.multiple_of(c * tall + jg, 16), 16), :]
                line = []
                for lt in range(wide // LANES):
                    tile = piece_of(z_ref, jg, lt, 16)
                    grad = jnp.exp(tile) * (tile + (alpha[:, lt * LANES : (lt + 1) * LANES] + beta))
                    sums[lt] = sums[lt] + (grad[0:8] + grad[8:16])
                    line.append(grad.astype(BF16))
                rounded.append(jnp.concatenate(line, axis=1))
            for lt in range(wide // LANES):
                sum_ref[:, lt * LANES : (lt + 1) * LANES] += sums[lt]
            feats = other_ref[:, pl.ds(aligned(c, tall), tall)]
            pull_ref[...] += jnp.dot(feats, jnp.concatenate(rounded, axis=0), preferred_element_type=F32)

        piped(nc, matmul, work, za_ref, zb_ref)
        total = jnp.sum(sum_ref[...], axis=0, keepdims=True)
        out_ref[:, rows_here] = 2.0 * (own.astype(F32) * total - pull_ref[...])
        return 0

    lax.fori_loop(0, nb, row_visit, 0)
    if not earlier:
        width = local // 4
        for k, ref in enumerate(out_refs):
            ref[...] = out_ref[:, pl.ds(pl.multiple_of((member ^ k) * width, LANES), width)]


def kernel_g(counts, target_ref, p0, p1, p2, p3, out_ref):
    member = lax.axis_index("cell")
    for k, ref in enumerate((p0, p1, p2, p3)):
        for i in range(ref.shape[1] // LANES):
            lanes = pl.ds(aligned(4 * i + (member ^ k), LANES), LANES)
            out_ref[:, lanes] = target_ref[:, lanes] + ref[:, i * LANES : (i + 1) * LANES]


def run(body, name, outs, scratch, limit, counts, *operands, flops=0):
    vmem = pl.BlockSpec(memory_space=pltpu.VMEM)
    return pl.pallas_call(
        body,
        name=name,
        out_shape=outs,
        in_specs=[pl.BlockSpec(memory_space=pltpu.SMEM)] + [vmem] * len(operands),
        out_specs=jax.tree.map(lambda _: vmem, outs),
        scratch_shapes=scratch,
        compiler_params=pltpu.CompilerParams(vmem_limit_bytes=limit * 1024 * 1024),
        cost_estimate=pl.CostEstimate(flops=flops, bytes_accessed=4_000_000, transcendentals=9_000_000),
    )(counts, *operands)


def shape(*dims, dtype=F32):
    return jax.ShapeDtypeStruct(dims, dtype)


def shifted(block, distance):
    size = lax.axis_size("tm")
    route = [(i - distance, i) for i in range(size) if 0 <= i - distance < size]
    return lax.ppermute(block, "tm", route)


def from_later(block, k):
    times, size = lax.axis_size("tm"), lax.axis_size("cell")
    route = [((t + 1) * size + (i ^ k), t * size + i) for t in range(times - 1) for i in range(size)]
    return lax.ppermute(block, ("tm", "cell"), route)


def swapped(block, k):
    return lax.ppermute(block, "cell", [(i, i ^ k) for i in range(lax.axis_size("cell"))])


def exchanged(block):
    near = swapped(block, 1)
    far = swapped(block, 2)
    return [block, near, far, swapped(far, 1)]


def per_device(embedding, counts):
    feat_dim, local = embedding.shape
    group = lax.axis_size("cell")
    slots = local * group

    counts = jnp.maximum(counts, lax.axis_index("cell") - group)
    source_parts = exchanged(embedding)
    source_parts[0] = swapped(source_parts[1], 1)
    ahead, ahead_far = from_later(embedding, 0), from_later(embedding, 2)
    target_parts = [ahead, swapped(ahead, 1), ahead_far, swapped(ahead_far, 1)]

    flops = 2 * local * slots * DEPTH
    aug = pltpu.VMEM((DEPTH, slots), BF16)
    narrow = pltpu.VMEM((ROWS, LANES), F32)
    flat = pltpu.VMEM((1, ROWS), F32)
    tile = pltpu.VMEM((DEPTH, ROWS), F32)
    wide = pltpu.VMEM((ROWS, slots), F32)
    half = pltpu.VMEM((ROWS, slots), BF16)
    turned_rows = pltpu.VMEM((16, ROWS), BF16)
    buffers = [pltpu.VMEM((ROWS, COLS), F32)] * 2
    long = pltpu.VMEM((8, slots), F32)
    grouped, targets, dealt, xa, base, gb, log = run(
        kernel_a, "column_log",
        (
            shape(feat_dim, slots, dtype=BF16), shape(feat_dim, slots, dtype=BF16), shape(feat_dim, local, dtype=BF16),
            shape(local, DEPTH, dtype=BF16), shape(1, local), shape(1, slots), shape(1, slots),
        ),
        [aug, pltpu.VMEM((DEPTH, local), F32), *buffers, long, long],
        16, counts, *source_parts, *target_parts, flops=flops,
    )
    logs = exchanged(log)
    g1, col1 = run(
        kernel_b, "first_sweep",
        (shape(1, slots), shape(1, slots)),
        [aug, *buffers, wide, wide, narrow, narrow, narrow, flat, flat, long],
        24, counts, xa, targets, gb, *logs, flops=2 * flops,
    )
    grouped, col1 = lax.optimization_barrier((grouped, col1))
    earlier = shifted(grouped, 1)
    rows, g2, stats = run(
        kernel_c, "second_sweep",
        (shape(8, local), shape(1, slots), shape(1, 3 * slots)),
        [
            aug, *buffers, half, half, half, half, narrow, narrow, narrow, narrow, flat,
            pltpu.VMEM((1, slots), F32), turned_rows, tile, pltpu.VMEM((32, slots), F32), long, long, long,
        ],
        28, counts, xa, dealt, base, targets, gb, g1, *exchanged(col1), flops=2 * flops,
    )
    rows, earlier = lax.optimization_barrier((rows, earlier))
    stat, send = run(
        kernel_d, "adjoint",
        (shape(8, slots), shape(1, slots + 2 * local)),
        [aug, tile, pltpu.VMEM((local, DEPTH), BF16), wide, wide, narrow, narrow, narrow, long],
        24, counts, dealt, rows, targets, gb, g2, *exchanged(stats), flops=2 * flops,
    )
    col_pair, early = run(
        kernel_f, "assemble",
        (shape(2, slots), shape(2, slots + local)),
        [pltpu.VMEM((group, 1, slots + 2 * local), F32)],
        8, counts, *exchanged(send), stat,
    )
    early = shifted(early, 1)

    def scratch_e(tall, wide):
        return [
            pltpu.VMEM((DEPTH, wide), BF16), pltpu.VMEM((DEPTH, COLS), F32), pltpu.VMEM((slots, DEPTH), BF16),
            pltpu.VMEM((slots, LANES), F32), *[pltpu.VMEM((tall, wide), F32)] * 2,
            pltpu.VMEM((feat_dim, wide), F32), pltpu.VMEM((8, wide), F32),
        ]

    parts = run(
        functools.partial(kernel_e, earlier=False), "source_gradient", (shape(feat_dim, local // group),) * group,
        scratch_e(COLS, ROWS) + [pltpu.VMEM((feat_dim, local), F32)],
        16, counts, dealt, send, targets, col_pair, flops=2 * flops,
    )
    parts = [parts[0]] + [swapped(parts[k], k) for k in range(1, group)]
    target_grad = run(
        functools.partial(kernel_e, earlier=True), "target_gradient", shape(feat_dim, local),
        scratch_e(COLS // 2, 2 * ROWS),
        16, counts, embedding, early, earlier, early, flops=2 * flops,
    )
    return run(kernel_g, "total", shape(feat_dim, local), [], 8, counts, target_grad, *parts)


def solution(mesh):
    in_specs = (P(None, ("tm", "cell")), P())
    out_specs = P(None, ("tm", "cell"))
    return jax.shard_map(
        per_device, mesh=mesh, in_specs=in_specs, out_specs=out_specs, check_vma=False
    )
```

```python
import functools

import jax
import jax.numpy as jnp
from jax import lax
from jax.experimental import pallas as pl
from jax.experimental.pallas import tpu as pltpu
from jax.sharding import PartitionSpec as P

ENTROPY = 0.25
PENALTY = 5.0
DAMPING = PENALTY / (PENALTY + ENTROPY)
MASKED = -1e30
SQ_SCALE = 1.0 / ENTROPY
DOT_SCALE = 2.0 / ENTROPY
TINY = 1e-37
SHIFT = 44.0
LOWEST = 1e-24

ROWS = 256
COLS = 512
LANES = 128
DEPTH = 128
F32 = jnp.float32
BF16 = jnp.bfloat16


def split3(value):
    high = value.astype(BF16).astype(F32)
    rest = value - high
    middle = rest.astype(BF16).astype(F32)
    return high, middle, rest - middle


def write_augmented(out_ref, start, feats, pot, is_row):
    n = feats.shape[1]
    cols = pl.ds(start, n)
    scaled = feats.astype(F32) * DOT_SCALE if is_row else feats
    out_ref[0:32, cols] = scaled.astype(out_ref.dtype)
    first = 0 if is_row else 3
    ones_from = 3 if is_row else 0
    row = lax.broadcasted_iota(jnp.int32, (16, n), 0)
    tail = jnp.where((row >= ones_from) & (row < ones_from + 3), 1.0, 0.0)
    for k, piece in enumerate(split3(pot)):
        tail = jnp.where(row == first + k, piece, tail)
    out_ref[32:48, cols] = tail.astype(out_ref.dtype)
    out_ref[48:128, cols] = jnp.zeros((80, n), out_ref.dtype)


def square_sum(feats):
    wide = feats.astype(F32)
    return jnp.sum(wide * wide, axis=0, keepdims=True)


def live_pot(feats, start, count):
    ids = start + lax.broadcasted_iota(jnp.int32, (1, feats.shape[1]), 1)
    return jnp.where(ids < count, -SQ_SCALE * square_sum(feats), MASKED)


def aligned(index, size):
    return pl.multiple_of(index * size, size)


def around(counts):
    size = counts.shape[0]
    time, member = lax.axis_index("tm"), lax.axis_index("cell")
    before = jnp.where(time > 0, counts[jnp.maximum(time - 1, 0)], 0)
    after = jnp.where(time + 1 < size, counts[jnp.minimum(time + 1, size - 1)], 0)
    return before, counts[time], after, member


def row_blocks(count_here, count_next, member, group):
    blocks = pl.cdiv(count_here, LANES)
    mine = jnp.maximum((blocks - member + group - 1) // group, 0)
    return jnp.where(count_next > 0, mine, 0)


def live_rows(start, member, count, group=4):
    row = lax.broadcasted_iota(jnp.int32, (1, ROWS), 1)
    slot = (group * (start // LANES) + member) * LANES + row
    return slot + jnp.where(row >= LANES, (group - 1) * LANES, 0) < count


def col_steps(count):
    return (count + COLS - 1) // COLS


LTS = COLS // LANES
SUB = 32
WIDE = 1536


def scores(xa, ya_ref, c, cols=COLS):
    return jnp.dot(xa, ya_ref[:, pl.ds(aligned(c, cols), cols)], preferred_element_type=F32)


def piped(count, matmul, work, first_ref, second_ref, load=None, store=None, most=2):
    load = load or (lambda c: None)
    store = store or (lambda c, state: None)
    first_ref[...] = matmul(0)

    def body(start, tiles):
        refs = first_ref, second_ref
        states = [load(start + k) for k in range(tiles)]
        for k in range(tiles):
            refs[(k + 1) % 2][...] = matmul(jnp.minimum(start + k + 1, count - 1))
            states[k] = work(start + k, refs[k % 2], states[k])
        for k in range(tiles):
            store(start + k, states[k])

    def full(i, _):
        body(most * i, most)
        return 0

    lax.fori_loop(0, count // most, full, 0)
    size = most // 2
    while size >= 2:
        part = size

        @pl.when(count % (2 * part) >= part)
        def _():
            body(count // (2 * part) * (2 * part), part)

        size //= 2

    @pl.when(count % 2 == 1)
    def _():
        store(count - 1, work(count - 1, first_ref, load(count - 1)))


def adder(acc_refs):
    def store(c, sums):
        for k, acc_ref in enumerate(acc_refs):
            lts = len(sums[k])
            for lt in range(lts):
                acc_ref[:, lane_tile(c, lt, lts)] += sums[k][lt]

    return store


def lane_tile(c, lt, lts=LTS):
    return pl.ds(aligned(c * lts + lt, LANES), LANES)


def piece_of(z_ref, rg, lt, size=SUB):
    return z_ref[rg : rg + size, lt * LANES : (lt + 1) * LANES]


def in_steps(total, visit):
    for start in range(0, total, WIDE):
        visit(start, slice(start, start + WIDE))


def kernel_a(
    counts, x0, x1, x2, x3, y0, y1, y2, y3,
    xg_ref, yg_ref, xt_ref, xa_ref, base_ref, gb_ref, log_ref,
    ya_ref, xat_ref, za_ref, zb_ref, top_ref, sum_ref,
):
    _, count_here, count_next, member = around(counts)
    group = 4
    mine = row_blocks(count_here, count_next, member, group)
    nb = (mine + 1) // 2
    nc = col_steps(count_next)
    local = x0.shape[1]
    for k, y_ref in enumerate((y0, y1, y2, y3)):
        yg_ref[:, pl.ds(aligned(member ^ k, local), local)] = y_ref[...]
    for k, x_ref in enumerate((x0, x1, x2, x3)):
        xg_ref[:, pl.ds(aligned(member ^ k, local), local)] = x_ref[...]
    sum_ref[...] = jnp.zeros_like(sum_ref)

    def prepare(start, cols):
        feats = yg_ref[:, cols]
        pot = live_pot(feats, start, count_next)
        gb_ref[:, cols] = pot
        write_augmented(ya_ref, start, feats, pot, False)

    in_steps(group * local, prepare)
    for k in range(local // LANES):
        lanes = slice(k * LANES, (k + 1) * LANES)
        block_id = group * k + member
        piece = xg_ref[:, pl.ds(aligned(block_id, LANES), LANES)]
        xt_ref[:, lanes] = piece
        pot = live_pot(piece, block_id * LANES, count_here) + SHIFT
        base_ref[:, lanes] = pot
        write_augmented(xat_ref, k * LANES, piece, pot, True)
        xa_ref[lanes, :] = jnp.transpose(xat_ref[:, lanes]).astype(BF16)

    def exact():
        top_ref[...] = jnp.full(top_ref.shape, MASKED, F32)
        sum_ref[...] = jnp.zeros_like(sum_ref)

        def row_visit(b, _):
            xa = xa_ref[pl.ds(aligned(b, ROWS), ROWS), :]

            def load(c):
                return [(top_ref[:, lane_tile(c, lt)], sum_ref[:, lane_tile(c, lt)]) for lt in range(LTS)]

            def work(c, z_ref, state):
                after = []
                for lt, (old, total) in enumerate(state):
                    tile = z_ref[:, lt * LANES : (lt + 1) * LANES].reshape(ROWS // 8, 8, LANES)
                    top = jnp.maximum(old, jnp.max(tile, axis=0))
                    total = total * jnp.exp(old - top) + jnp.sum(jnp.exp(tile - top[None]), axis=0)
                    after.append((top, total))
                return after

            def store(c, state):
                for lt, (top, total) in enumerate(state):
                    top_ref[:, lane_tile(c, lt)] = top
                    sum_ref[:, lane_tile(c, lt)] = total

            piped(nc, lambda c: scores(xa, ya_ref, c), work, za_ref, zb_ref, load, store)
            return 0

        lax.fori_loop(0, nb, row_visit, 0)
        tops = top_ref[...]
        top = jnp.max(tops, axis=0, keepdims=True)
        total = jnp.sum(sum_ref[...] * jnp.exp(tops - top), axis=0, keepdims=True)
        log_ref[...] = top + jnp.log(jnp.maximum(total, TINY)) - SHIFT

    def quick_rows(first_block, blocks):
        def tile_sums(c):
            totals = [jnp.zeros((8, LANES), F32) for _ in range(LTS)]
            for k in range(blocks):
                z = scores(xa_ref[pl.ds(aligned(first_block + k, LANES), LANES), :], ya_ref, c)
                for lt in range(LTS):
                    p = jnp.exp(z[:, lt * LANES : (lt + 1) * LANES])
                    totals[lt] = totals[lt] + jnp.sum(p.reshape(LANES // 8, 8, LANES), axis=0)
            return [totals]

        over_tiles(nc, tile_sums, adder([sum_ref]), most=8)

    def quick_visit(b, _):
        quick_rows(2 * b, 2)
        return 0

    lax.fori_loop(0, mine // 2, quick_visit, 0)

    @pl.when(mine % 2 == 1)
    def _():
        quick_rows(mine - 1, 1)

    total = jnp.sum(sum_ref[...], axis=0, keepdims=True)
    log_ref[...] = jnp.where(total > 0.0, jnp.log(jnp.maximum(total, TINY)) - SHIFT, MASKED)
    ids = lax.broadcasted_iota(jnp.int32, total.shape, 1)
    lowest = jnp.min(jnp.where(ids < count_next, total, 1.0))

    @pl.when((lowest < LOWEST) & (nb > 0))
    def _():
        exact()


def column_sums(c, z_ref, _):
    rows, cols = z_ref.shape
    sums = []
    for lt in range(cols // LANES):
        p = jnp.exp(z_ref[:, lt * LANES : (lt + 1) * LANES])
        sums.append(jnp.sum(p.reshape(rows // 8, 8, LANES), axis=0))
    return [sums]


def row_adder(sum_ref, push_ref=None, g_ref=None):
    def first(c, scores_of, kept, count):
        half = LANES
        for start in range(0, count, half):
            scored = scores_of(c, start, half)
            for rg in range(0, half, SUB):
                rows = slice(start + rg, start + rg + SUB)
                total = sum_ref[rows, :]
                push = push_ref[rows, :] if push_ref is not None else None
                for lt in range(LTS):
                    z = piece_of(scored, rg, lt)
                    p = jnp.exp(z)
                    total = total + p
                    kept[0][rows, lane_tile(c, lt)] = p.astype(kept[0].dtype)
                    if push is not None:
                        part = p * (g_ref[:, lane_tile(c, lt)] - z)
                        push = push + part
                        kept[1][rows, lane_tile(c, lt)] = part.astype(kept[1].dtype)
                sum_ref[rows, :] = total
                if push is not None:
                    push_ref[rows, :] = push

    return first


def column_parts(c, plan):
    sums = [[jnp.zeros((8, LANES), F32) for _ in range(LTS)] for _ in plan]
    for rg in range(0, ROWS, 8):
        for k, (kept_ref, weight_ref) in enumerate(plan):
            scale = weight_ref[rg : rg + 8, :]
            for lt in range(LTS):
                sums[k][lt] = sums[k][lt] + scale * kept_ref[rg : rg + 8, lane_tile(c, lt)]
    return sums


def over_tiles(count, visit, put=None, most=4):
    put = put or (lambda c, sums: None)

    def body(tiles):
        for c, sums in [(c, visit(c)) for c in tiles]:
            put(c, sums)

    def full(i, _):
        body([most * i + k for k in range(most)])
        return 0

    lax.fori_loop(0, count // most, full, 0)
    size = most // 2
    while size >= 1:
        part = size

        @pl.when(count % (2 * part) >= part)
        def _():
            first = count // (2 * part) * (2 * part)
            body([first + k for k in range(part)])

        size //= 2


def two_stage(mine, nc, first, finish, second, store, matmul_of, kept):
    nb = (mine + 1) // 2
    alone = mine % 2 == 1

    def stage(start, now, before, rows=ROWS):
        scores_of = matmul_of(start)

        def visit(c):
            first(c, scores_of, now, rows)
            if rows < ROWS:
                for ref in now:
                    ref[rows:, col_tile(c)] = jnp.zeros((ROWS - rows, COLS), ref.dtype)
            return second(c, before) if before else None

        over_tiles(nc, visit, store if before else None)
        finish(start, rows)

    def tail(before):
        over_tiles(nc, lambda c: second(c, before), store)

    even, odd = kept

    @pl.when((nb > 0) & alone)
    def _():
        stage(0, even, None, LANES)

    @pl.when((nb > 0) & jnp.logical_not(alone))
    def _():
        stage(0, even, None)

    def visit(b, _):
        start = pl.multiple_of(b * ROWS - jnp.where(alone, LANES, 0), LANES)

        @pl.when(b % 2 == 1)
        def _():
            stage(start, odd, even)

        @pl.when(b % 2 == 0)
        def _():
            stage(start, even, odd)

        return 0

    lax.fori_loop(1, nb, visit, 0)

    @pl.when((nb > 0) & (nb % 2 == 1))
    def _():
        tail(even)

    @pl.when((nb > 0) & (nb % 2 == 0))
    def _():
        tail(odd)


def col_tile(c):
    return pl.ds(aligned(c, COLS), COLS)


def split2(value):
    high = value.astype(BF16).astype(F32)
    return high, value - high


def row_totals(ref):
    return jnp.sum(jnp.transpose(ref[...]), axis=0, keepdims=True)


def spread(row):
    return jnp.transpose(jnp.broadcast_to(row, (LANES, ROWS)))


def laid(column):
    return jnp.transpose(jnp.broadcast_to(column, (ROWS, LANES)))[0:1, :]


def sweep(quick, exact, low_ref, lost=None):
    low_ref[...] = jnp.ones_like(low_ref)
    quick()
    again = jnp.min(low_ref[...]) < LOWEST
    if lost is not None:
        again = again | lost()

    @pl.when(again)
    def _():
        exact()


def row_lse(xa, ya_ref, nc, buffers, top_ref, sum_ref, push_ref=None, g_ref=None):
    top_ref[...] = jnp.full(top_ref.shape, MASKED, F32)
    sum_ref[...] = jnp.zeros_like(sum_ref)
    if push_ref is not None:
        push_ref[...] = jnp.zeros_like(push_ref)

    def work(c, z_ref, _):
        for rg in range(0, ROWS, SUB):
            rows = slice(rg, rg + SUB)
            old = top_ref[rows, :]
            pieces = [piece_of(z_ref, rg, lt) for lt in range(LTS)]
            top = old
            for z in pieces:
                top = jnp.maximum(top, z)
            fade = jnp.exp(old - top)
            total = sum_ref[rows, :] * fade
            push = push_ref[rows, :] * fade if push_ref is not None else None
            for lt, z in enumerate(pieces):
                p = jnp.exp(z - top)
                total = total + p
                if push is not None:
                    push = push + p * (g_ref[:, lane_tile(c, lt)] - z)
            top_ref[rows, :] = top
            sum_ref[rows, :] = total
            if push is not None:
                push_ref[rows, :] = push

    piped(nc, lambda c: scores(xa, ya_ref, c), work, *buffers)
    tops = top_ref[...]
    top = jnp.max(tops, axis=1, keepdims=True)
    fade = jnp.exp(tops - top)
    total = jnp.sum(sum_ref[...] * fade, axis=1, keepdims=True)
    if push_ref is None:
        return top, total
    return top, total, jnp.sum(push_ref[...] * fade, axis=1, keepdims=True)


def row_potential(xa):
    lane = lax.broadcasted_iota(jnp.int32, (ROWS, LANES), 1)
    wide = xa.astype(F32)
    old = jnp.sum(jnp.where((lane >= 32) & (lane < 35), wide, 0.0), axis=1, keepdims=True)
    return lane, wide, old


def with_row_potential(lane, wide, pot):
    high, middle, low = split3(pot)
    new = jnp.where(lane == 32, high, jnp.where(lane == 33, middle, jnp.where(lane == 34, low, wide)))
    return new.astype(BF16)


def kernel_b(counts, xa_ref, yg_ref, gb_ref, l0, l1, l2, l3, g_ref, col_ref, ya_ref, za_ref, zb_ref, p_ref, q_ref, top_ref, sum_ref, weight_ref, low_ref, most_ref, acc_ref):
    _, count_here, count_next, member = around(counts)
    mine = row_blocks(count_here, count_next, member, 4)
    nb = (mine + 1) // 2
    nc = col_steps(count_next)

    def prepare(start, cols):
        logs = [ref[:, cols] for ref in (l0, l1, l2, l3)]
        top = jnp.maximum(jnp.maximum(logs[0], logs[1]), jnp.maximum(logs[2], logs[3]))
        total = sum(jnp.exp(one - top) for one in logs)
        ids = start + lax.broadcasted_iota(jnp.int32, (1, WIDE), 1)
        pot = jnp.where(ids < count_next, -DAMPING * (top + jnp.log(total)), 0.0)
        g_ref[:, cols] = pot
        write_augmented(ya_ref, start, yg_ref[:, cols], pot + gb_ref[:, cols], False)

    in_steps(yg_ref.shape[1], prepare)

    buffers = za_ref, zb_ref

    def quick():
        acc_ref[...] = jnp.zeros_like(acc_ref)

        def matmul_of(first_row):
            sum_ref[...] = jnp.zeros_like(sum_ref)
            return lambda c, start, size: scores(
                xa_ref[pl.ds(pl.multiple_of(first_row + start, size), size), :], ya_ref, c
            )

        def finish(start, rows):
            row = lax.broadcasted_iota(jnp.int32, (1, ROWS), 1)
            live = live_rows(start, member, count_here) & (row < rows)
            total = row_totals(sum_ref)
            low_ref[...] = jnp.minimum(low_ref[...], jnp.where(live, total, 1.0))
            pot = -DAMPING * (jnp.log(jnp.maximum(total, TINY)) - SHIFT)
            weight = jnp.where(live, jnp.exp(pot - SHIFT), 0.0)
            weight_ref[...] = spread(weight)
            most_ref[...] = jnp.maximum(most_ref[...], weight)

        two_stage(
            mine, nc, row_adder(sum_ref), finish, lambda c, kept: column_parts(c, [(kept[0], weight_ref)]),
            adder([acc_ref]), matmul_of, ((p_ref,), (q_ref,)),
        )

    def exact():
        acc_ref[...] = jnp.zeros_like(acc_ref)

        def row_visit(b, _):
            xa = xa_ref[pl.ds(aligned(b, ROWS), ROWS), :]
            lane, wide, old = row_potential(xa)
            live = old > 0.5 * MASKED
            top, total = row_lse(xa, ya_ref, nc, buffers, top_ref, sum_ref)
            pot = -DAMPING * (top + jnp.log(total) - SHIFT)
            xb = with_row_potential(lane, wide, jnp.where(live, pot + old - SHIFT, MASKED))
            piped(nc, lambda c: scores(xb, ya_ref, c), column_sums, *buffers, store=adder([acc_ref]))
            return 0

        lax.fori_loop(0, nb, row_visit, 0)

    def lost():
        total = jnp.sum(acc_ref[...], axis=0, keepdims=True)
        ids = lax.broadcasted_iota(jnp.int32, total.shape, 1)
        least = jnp.min(jnp.where((ids < count_next) & (nb > 0), total, 1.0))
        return least < jnp.max(most_ref[...]) * 2.0**-91

    most_ref[...] = jnp.zeros_like(most_ref)
    sweep(quick, exact, low_ref, lost)
    col_ref[...] = jnp.sum(acc_ref[...], axis=0, keepdims=True)


def kernel_c(
    counts, xa_ref, xt_ref, base_ref, yg_ref, gb_ref, g_ref, c0, c1, c2, c3,
    rows_ref, g2_ref, col_ref,
    ya_ref, za_ref, zb_ref, p_ref, w_ref, q_ref, v_ref, top_ref, sum_ref, push_ref, adj_ref, low_ref, cost_ref, weight_ref, xat_ref, acc_ref, acc0_ref, acc1_ref, acc2_ref,
):
    _, count_here, count_next, member = around(counts)
    mine = row_blocks(count_here, count_next, member, 4)
    nb = (mine + 1) // 2
    nc = col_steps(count_next)

    def prepare(start, cols):
        total = (c0[:, cols] + c1[:, cols]) + (c2[:, cols] + c3[:, cols])
        ids = start + lax.broadcasted_iota(jnp.int32, (1, WIDE), 1)
        log = jnp.log(jnp.maximum(total, TINY)) - g_ref[:, cols]
        pot = jnp.where(ids < count_next, -DAMPING * log, 0.0)
        g2_ref[:, cols] = pot
        write_augmented(ya_ref, start, yg_ref[:, cols], pot + gb_ref[:, cols], False)

    in_steps(yg_ref.shape[1], prepare)

    buffers = za_ref, zb_ref
    accs = acc0_ref, acc1_ref, acc2_ref

    ids = lax.broadcasted_iota(jnp.int32, g_ref.shape, 1)
    centre = jnp.sum(jnp.where(ids < count_next, g_ref[...], 0.0), axis=1, keepdims=True)
    centre = centre / (DAMPING * jnp.maximum(count_next, 1).astype(F32)) + 3.0
    cost_ref[...] = g2_ref[...] + (SHIFT - centre)

    line = lax.broadcasted_iota(jnp.int32, rows_ref.shape, 0)
    rows_ref[...] = jnp.where(line == 3, MASKED, 0.0)

    def close_rows(start, rows, row_log, mean_cost):
        rows_here = pl.ds(pl.multiple_of(start, LANES), ROWS)
        live = live_rows(start, member, count_here) & (lax.broadcasted_iota(jnp.int32, (1, ROWS), 1) < rows)
        pot = jnp.where(live, -DAMPING * row_log, 0.0)
        row_sum = jnp.where(live, jnp.exp(row_log + pot), 0.0)
        adjoint = jnp.where(live, mean_cost + centre, 0.0)
        full = jnp.where(live, pot + base_ref[:, rows_here] - SHIFT, MASKED)
        rows_ref[0:1, rows_here] = adjoint
        rows_ref[1:2, rows_here] = jnp.where(row_sum > 0.0, 1.0 / jnp.maximum(row_sum, TINY), 0.0)
        rows_ref[2:3, rows_here] = pot
        rows_ref[3:4, rows_here] = full
        return live, pot, adjoint, full

    def quick():
        acc_ref[...] = jnp.zeros_like(acc_ref)

        def matmul_of(first_row):
            sum_ref[...] = jnp.zeros_like(sum_ref)
            push_ref[...] = jnp.zeros_like(push_ref)
            return lambda c, start, size: scores(
                xa_ref[pl.ds(pl.multiple_of(first_row + start, size), size), :], ya_ref, c
            )

        def finish(start, rows):
            total = row_totals(sum_ref)
            safe = jnp.maximum(total, TINY)
            live, pot, adjoint, _ = close_rows(start, rows, jnp.log(safe) - SHIFT, row_totals(push_ref) / safe)
            low_ref[...] = jnp.minimum(low_ref[...], jnp.where(live, total, 1.0))
            weight = jnp.where(live, jnp.exp(pot - SHIFT), 0.0)
            row = lax.broadcasted_iota(jnp.int32, (16, ROWS), 0)
            packed = jnp.zeros((16, ROWS), F32)
            for k, piece in enumerate((*split2(weight), *split2(weight * adjoint))):
                packed = jnp.where(row == k, piece, packed)
            weight_ref[...] = packed.astype(BF16)

        def second(c, kept):
            weights = weight_ref[...]
            plan = jnp.dot(weights, kept[0][:, col_tile(c)], preferred_element_type=F32)
            cost = jnp.dot(weights, kept[1][:, col_tile(c)], preferred_element_type=F32)
            return plan, cost

        def store(c, sums):
            acc_ref[0:16, col_tile(c)] += sums[0]
            acc_ref[16:32, col_tile(c)] += sums[1]

        two_stage(
            mine, nc, row_adder(sum_ref, push_ref, cost_ref), finish, second, store, matmul_of,
            ((p_ref, w_ref), (q_ref, v_ref)),
        )
        acc0_ref[0:1, :] = acc_ref[0:1, :] + acc_ref[1:2, :]
        acc1_ref[0:1, :] = acc_ref[16:17, :] + acc_ref[17:18, :]
        acc2_ref[0:1, :] = acc_ref[2:3, :] + acc_ref[3:4, :]
        for ref in accs:
            ref[1:8, :] = jnp.zeros((7, ref.shape[1]), F32)

    def exact():
        for ref in accs:
            ref[...] = jnp.zeros_like(ref)

        def row_visit(b, _):
            xa = xa_ref[pl.ds(aligned(b, ROWS), ROWS), :]
            top, total, push = row_lse(xa, ya_ref, nc, buffers, top_ref, sum_ref, push_ref, cost_ref)
            _, pot, adjoint, full = close_rows(
                b * ROWS, ROWS, laid(top + jnp.log(total) - SHIFT), laid(push / total)
            )
            top_ref[...] = spread(pot - SHIFT)
            adj_ref[...] = spread(adjoint)
            write_augmented(xat_ref, 0, xt_ref[:, pl.ds(aligned(b, ROWS), ROWS)], full, True)
            xb = jnp.transpose(xat_ref[...]).astype(BF16)

            def work(c, z_ref, _):
                sums = [[jnp.zeros((8, LANES), F32) for _ in range(LTS)] for _ in range(3)]
                for rg in range(0, ROWS, 8):
                    pot_here = top_ref[rg : rg + 8, :]
                    adj_here = adj_ref[rg : rg + 8, :]
                    for lt in range(LTS):
                        tile = piece_of(z_ref, rg, lt, 8)
                        p = jnp.exp(tile)
                        sums[0][lt] = sums[0][lt] + p
                        sums[1][lt] = sums[1][lt] + p * (cost_ref[:, lane_tile(c, lt)] + (pot_here - tile))
                        sums[2][lt] = sums[2][lt] + p * adj_here
                return sums

            piped(nc, lambda c: scores(xb, ya_ref, c), work, *buffers, store=adder(accs))
            return 0

        lax.fori_loop(0, nb, row_visit, 0)

    sweep(quick, exact, low_ref)
    mass = jnp.sum(acc0_ref[...], axis=0, keepdims=True)
    slots = mass.shape[1]
    col_ref[:, 0:slots] = mass
    push = jnp.sum(acc1_ref[...], axis=0, keepdims=True)
    col_ref[:, slots : 2 * slots] = push + centre * mass
    col_ref[:, 2 * slots :] = jnp.sum(acc2_ref[...], axis=0, keepdims=True)


def kernel_d(
    counts, xt_ref, rows_ref, yg_ref, gb_ref, g2_ref, s0, s1, s2, s3,
    stat_ref, send_ref,
    ya_ref, xat_ref, xb_ref, p_ref, q_ref, first_ref, second_ref, weight_ref, acc_ref,
):
    _, count_here, count_next, member = around(counts)
    mine = row_blocks(count_here, count_next, member, 4)
    nb = (mine + 1) // 2
    nc = col_steps(count_next)
    slots = yg_ref.shape[1]
    local = xt_ref.shape[1]
    acc_ref[...] = jnp.zeros_like(acc_ref)

    def prepare(start, cols):
        mass, push, pulled = (
            (s0[:, part] + s1[:, part]) + (s2[:, part] + s3[:, part])
            for part in (pl.ds(start + k * slots, WIDE) for k in range(3))
        )
        inverse = jnp.where(mass > 0.0, 1.0 / jnp.maximum(mass, TINY), 0.0)
        pot = g2_ref[:, cols]
        stat_ref[0:1, cols] = pot + gb_ref[:, cols]
        stat_ref[1:2, cols] = push * inverse
        stat_ref[2:3, cols] = (push - DAMPING * pulled) * inverse
        stat_ref[3:4, cols] = inverse
        stat_ref[4:5, cols] = pot
        stat_ref[5:8, cols] = jnp.zeros((3, WIDE), F32)
        write_augmented(ya_ref, start, yg_ref[:, cols], pot + gb_ref[:, cols], False)

    in_steps(slots, prepare)
    for block in range(local // ROWS):
        @pl.when(2 * block < mine)
        def _():
            rows = slice(block * ROWS, (block + 1) * ROWS)
            write_augmented(xat_ref, 0, xt_ref[:, rows], rows_ref[3:4, rows], True)
            xb_ref[rows, :] = jnp.transpose(xat_ref[...]).astype(BF16)

    send_ref[:, slots : slots + local] = jnp.full((1, local), MASKED, F32)
    send_ref[:, slots + local :] = jnp.zeros((1, local), F32)

    def matmul_of(first_row):
        first_ref[...] = jnp.zeros_like(first_ref)
        second_ref[...] = jnp.zeros_like(second_ref)
        return lambda c, start, size: scores(
            xb_ref[pl.ds(pl.multiple_of(first_row + start, size), size), :], ya_ref, c
        )

    def sums(c, scores_of, kept, count):
        half = LANES
        for start in range(0, count, half):
            scored = scores_of(c, start, half)
            for rg in range(0, half, SUB):
                rows = slice(start + rg, start + rg + SUB)
                first = first_ref[rows, :]
                second = second_ref[rows, :]
                for lt in range(LTS):
                    p = jnp.exp(piece_of(scored, rg, lt))
                    kept[0][rows, lane_tile(c, lt)] = p
                    first = first + p * stat_ref[1:2, lane_tile(c, lt)]
                    second = second + p * stat_ref[2:3, lane_tile(c, lt)]
                first_ref[rows, :] = first
                second_ref[rows, :] = second

    def finish(start, rows):
        first, second = row_totals(first_ref), row_totals(second_ref)
        rows_here = pl.ds(pl.multiple_of(start, LANES), ROWS)
        start_adj, inverse, pot, full = (rows_ref[k : k + 1, rows_here] for k in range(4))
        middle_adj = start_adj - DAMPING * first * inverse
        last_adj = start_adj - DAMPING * second * inverse
        weight_ref[...] = spread(middle_adj)
        send_ref[:, pl.ds(pl.multiple_of(slots + start, LANES), ROWS)] = full
        send_ref[:, pl.ds(pl.multiple_of(slots + local + start, LANES), ROWS)] = 1.0 + DAMPING * last_adj - pot

    two_stage(
        mine, nc, sums, finish, lambda c, kept: column_parts(c, [(kept[0], weight_ref)]), adder([acc_ref]), matmul_of,
        ((p_ref,), (q_ref,)),
    )
    send_ref[:, 0:slots] = jnp.sum(acc_ref[...], axis=0, keepdims=True)


def kernel_f(counts, p0, p1, p2, p3, stat_ref, col_ref, early_ref, parts_ref):
    member = lax.axis_index("cell")
    slots = stat_ref.shape[1]
    local = early_ref.shape[1] - slots
    for k, ref in enumerate((p0, p1, p2, p3)):
        parts_ref[member ^ k] = ref[...]
    total = (p0[:, 0:slots] + p1[:, 0:slots]) + (p2[:, 0:slots] + p3[:, 0:slots])
    last = stat_ref[1:2, :] - DAMPING * total * stat_ref[3:4, :]
    col_ref[0:1, :] = stat_ref[0:1, :]
    col_ref[1:2, :] = DAMPING * last - stat_ref[4:5, :]
    for block in range(slots // LANES):
        owner, place = block % 4, block // 4
        lanes = slice(block * LANES, (block + 1) * LANES)
        for k in range(2):
            at = slots + k * local + place * LANES
            early_ref[k : k + 1, lanes] = parts_ref[owner, :, at : at + LANES]
    here = pl.ds(aligned(member, local), local)
    early_ref[:, slots:] = col_ref[:, here]


def kernel_e(
    counts, *refs, earlier,
):
    tall, wide = (COLS // 2, 2 * ROWS) if earlier else (COLS, ROWS)
    own_ref, rowpot_ref, other_ref, colpot_ref = refs[:4]
    local, slots = own_ref.shape[1], other_ref.shape[1]
    before, here, after, member = around(counts)
    if earlier:
        out_ref, xw_ref, tile_ref, ys_ref, beta_ref, za_ref, zb_ref, pull_ref, sum_ref = refs[4:]
        count_cols = before
        count_rows = jnp.clip(here - member * local, 0, local)
        nb = jnp.where(count_cols > 0, (count_rows + wide - 1) // wide, 0)
        pot_at = slots
    else:
        out_refs = refs[4:8]
        xw_ref, tile_ref, ys_ref, beta_ref, za_ref, zb_ref, pull_ref, sum_ref, out_ref = refs[8:]
        count_cols = after
        nb = (row_blocks(here, after, member, 4) + 1) // 2
        pot_at = slots
    nc = (count_cols + tall - 1) // tall
    out_ref[...] = jnp.zeros_like(out_ref)

    def prepare(c, _):
        cols = pl.ds(aligned(c, COLS), COLS)
        write_augmented(tile_ref, 0, other_ref[:, cols], colpot_ref[0:1, cols], False)
        ys_ref[cols, :] = jnp.transpose(tile_ref[...]).astype(BF16)
        beta_ref[cols, :] = jnp.transpose(jnp.broadcast_to(colpot_ref[1:2, cols], (LANES, COLS)))
        return 0

    @pl.when(nb > 0)
    def _():
        lax.fori_loop(0, col_steps(count_cols), prepare, 0)

    def row_visit(b, _):
        rows_here = pl.ds(aligned(b, wide), wide)
        own = own_ref[:, rows_here]
        pots = rowpot_ref[0:1, pl.ds(aligned(b + pot_at // wide, wide), wide)]
        write_augmented(xw_ref, 0, own, pots, True)
        xw = xw_ref[...]
        if earlier:
            alpha = rowpot_ref[1:2, pl.ds(aligned(b + pot_at // wide, wide), wide)]
        else:
            alpha = rowpot_ref[0:1, pl.ds(aligned(b + (pot_at + local) // wide, wide), wide)]
        sum_ref[...] = jnp.zeros_like(sum_ref)
        pull_ref[...] = jnp.zeros_like(pull_ref)

        def matmul(c):
            return jnp.dot(ys_ref[pl.ds(aligned(c, tall), tall), :], xw, preferred_element_type=F32)

        def work(c, z_ref, _):
            rounded = []
            sums = [jnp.zeros((8, LANES), F32) for _ in range(wide // LANES)]
            for jg in range(0, tall, 16):
                beta = beta_ref[pl.ds(pl.multiple_of(c * tall + jg, 16), 16), :]
                line = []
                for lt in range(wide // LANES):
                    tile = piece_of(z_ref, jg, lt, 16)
                    grad = jnp.exp(tile) * (tile + (alpha[:, lt * LANES : (lt + 1) * LANES] + beta))
                    sums[lt] = sums[lt] + (grad[0:8] + grad[8:16])
                    line.append(grad.astype(BF16))
                rounded.append(jnp.concatenate(line, axis=1))
            for lt in range(wide // LANES):
                sum_ref[:, lt * LANES : (lt + 1) * LANES] += sums[lt]
            feats = other_ref[:, pl.ds(aligned(c, tall), tall)]
            pull_ref[...] += jnp.dot(feats, jnp.concatenate(rounded, axis=0), preferred_element_type=F32)

        piped(nc, matmul, work, za_ref, zb_ref, most=4)
        total = jnp.sum(sum_ref[...], axis=0, keepdims=True)
        out_ref[:, rows_here] = 2.0 * (own.astype(F32) * total - pull_ref[...])
        return 0

    lax.fori_loop(0, nb, row_visit, 0)
    if not earlier:
        width = local // 4
        for k, ref in enumerate(out_refs):
            ref[...] = out_ref[:, pl.ds(pl.multiple_of((member ^ k) * width, LANES), width)]


def kernel_g(counts, target_ref, p0, p1, p2, p3, out_ref):
    member = lax.axis_index("cell")
    for k, ref in enumerate((p0, p1, p2, p3)):
        for i in range(ref.shape[1] // LANES):
            lanes = pl.ds(aligned(4 * i + (member ^ k), LANES), LANES)
            out_ref[:, lanes] = target_ref[:, lanes] + ref[:, i * LANES : (i + 1) * LANES]


def run(body, name, outs, scratch, limit, counts, *operands, flops=0):
    vmem = pl.BlockSpec(memory_space=pltpu.VMEM)
    return pl.pallas_call(
        body,
        name=name,
        out_shape=outs,
        in_specs=[pl.BlockSpec(memory_space=pltpu.SMEM)] + [vmem] * len(operands),
        out_specs=jax.tree.map(lambda _: vmem, outs),
        scratch_shapes=scratch,
        compiler_params=pltpu.CompilerParams(vmem_limit_bytes=limit * 1024 * 1024),
        cost_estimate=pl.CostEstimate(flops=flops, bytes_accessed=4_000_000, transcendentals=9_000_000),
    )(counts, *operands)


def shape(*dims, dtype=F32):
    return jax.ShapeDtypeStruct(dims, dtype)


def shifted(block, distance):
    size = lax.axis_size("tm")
    route = [(i - distance, i) for i in range(size) if 0 <= i - distance < size]
    return lax.ppermute(block, "tm", route)


def from_later(block, k):
    times, size = lax.axis_size("tm"), lax.axis_size("cell")
    route = [((t + 1) * size + (i ^ k), t * size + i) for t in range(times - 1) for i in range(size)]
    return lax.ppermute(block, ("tm", "cell"), route)


def swapped(block, k):
    return lax.ppermute(block, "cell", [(i, i ^ k) for i in range(lax.axis_size("cell"))])


def exchanged(block):
    near = swapped(block, 1)
    far = swapped(block, 2)
    return [block, near, far, swapped(far, 1)]


def per_device(embedding, counts):
    feat_dim, local = embedding.shape
    group = lax.axis_size("cell")
    slots = local * group

    counts = jnp.maximum(counts, lax.axis_index("cell") - group)
    source_parts = exchanged(embedding)
    source_parts[0] = swapped(source_parts[1], 1)
    ahead, ahead_far = from_later(embedding, 0), from_later(embedding, 2)
    target_parts = [ahead, swapped(ahead, 1), ahead_far, swapped(ahead_far, 1)]

    flops = 2 * local * slots * DEPTH
    aug = pltpu.VMEM((DEPTH, slots), BF16)
    narrow = pltpu.VMEM((ROWS, LANES), F32)
    flat = pltpu.VMEM((1, ROWS), F32)
    tile = pltpu.VMEM((DEPTH, ROWS), F32)
    wide = pltpu.VMEM((ROWS, slots), F32)
    half = pltpu.VMEM((ROWS, slots), BF16)
    turned_rows = pltpu.VMEM((16, ROWS), BF16)
    buffers = [pltpu.VMEM((ROWS, COLS), F32)] * 2
    long = pltpu.VMEM((8, slots), F32)
    grouped, targets, dealt, xa, base, gb, log = run(
        kernel_a, "column_log",
        (
            shape(feat_dim, slots, dtype=BF16), shape(feat_dim, slots, dtype=BF16), shape(feat_dim, local, dtype=BF16),
            shape(local, DEPTH, dtype=BF16), shape(1, local), shape(1, slots), shape(1, slots),
        ),
        [aug, pltpu.VMEM((DEPTH, local), F32), *buffers, long, long],
        16, counts, *source_parts, *target_parts, flops=flops,
    )
    logs = exchanged(log)
    g1, col1 = run(
        kernel_b, "first_sweep",
        (shape(1, slots), shape(1, slots)),
        [aug, *buffers, wide, wide, narrow, narrow, narrow, flat, flat, long],
        24, counts, xa, targets, gb, *logs, flops=2 * flops,
    )
    grouped, col1 = lax.optimization_barrier((grouped, col1))
    earlier = shifted(grouped, 1)
    rows, g2, stats = run(
        kernel_c, "second_sweep",
        (shape(8, local), shape(1, slots), shape(1, 3 * slots)),
        [
            aug, *buffers, half, half, half, half, narrow, narrow, narrow, narrow, flat,
            pltpu.VMEM((1, slots), F32), turned_rows, tile, pltpu.VMEM((32, slots), F32), long, long, long,
        ],
        28, counts, xa, dealt, base, targets, gb, g1, *exchanged(col1), flops=2 * flops,
    )
    rows, earlier = lax.optimization_barrier((rows, earlier))
    stat, send = run(
        kernel_d, "adjoint",
        (shape(8, slots), shape(1, slots + 2 * local)),
        [aug, tile, pltpu.VMEM((local, DEPTH), BF16), wide, wide, narrow, narrow, narrow, long],
        24, counts, dealt, rows, targets, gb, g2, *exchanged(stats), flops=2 * flops,
    )
    col_pair, early = run(
        kernel_f, "assemble",
        (shape(2, slots), shape(2, slots + local)),
        [pltpu.VMEM((group, 1, slots + 2 * local), F32)],
        8, counts, *exchanged(send), stat,
    )
    early = shifted(early, 1)

    def scratch_e(tall, wide):
        return [
            pltpu.VMEM((DEPTH, wide), BF16), pltpu.VMEM((DEPTH, COLS), F32), pltpu.VMEM((slots, DEPTH), BF16),
            pltpu.VMEM((slots, LANES), F32), *[pltpu.VMEM((tall, wide), F32)] * 2,
            pltpu.VMEM((feat_dim, wide), F32), pltpu.VMEM((8, wide), F32),
        ]

    parts = run(
        functools.partial(kernel_e, earlier=False), "source_gradient", (shape(feat_dim, local // group),) * group,
        scratch_e(COLS, ROWS) + [pltpu.VMEM((feat_dim, local), F32)],
        16, counts, dealt, send, targets, col_pair, flops=2 * flops,
    )
    parts = [parts[0]] + [swapped(parts[k], k) for k in range(1, group)]
    target_grad = run(
        functools.partial(kernel_e, earlier=True), "target_gradient", shape(feat_dim, local),
        scratch_e(COLS // 2, 2 * ROWS),
        16, counts, embedding, early, earlier, early, flops=2 * flops,
    )
    return run(kernel_g, "total", shape(feat_dim, local), [], 8, counts, target_grad, *parts)


def solution(mesh):
    in_specs = (P(None, ("tm", "cell")), P())
    out_specs = P(None, ("tm", "cell"))
    return jax.shard_map(
        per_device, mesh=mesh, in_specs=in_specs, out_specs=out_specs, check_vma=False
    )
```
